32 devices in a mesh: section: 2 (over x), group: 4 (over z), dp: 4 (over y, core).
Axes of the slice: x: 2, y: 2, z: 4, core: 2. Of those that a mesh axis runs over, the one named last changes fastest.
Arguments:
- inputs_x: bfloat16 [32, 128, 1536], P(('group', 'dp')), may hold values from -6 to 6
- cotangent: bfloat16 [32, 128, 1536], P(('group', 'dp')), may hold values from -6 to 6
- lengths: int32 [32], P(('group', 'dp')), may hold values from 32 to 128, as said below
- attn_gain: bfloat16 [2, 1536], P('section', ('group', 'dp')), may hold values from 0.099609375 to 1.8984375
- qkv_weight: bfloat16 [2, 1536, 3072], P('section', ('group', 'dp')), may hold values from -0.15625 to 0.15625
- out_weight: bfloat16 [2, 1536, 1536], P('section', ('group', 'dp')), may hold values from -0.4375 to 0.4375
- ffn_gain: bfloat16 [2, 1536], P('section', ('group', 'dp')), may hold values from 0.099609375 to 1.8984375
- gate_up: bfloat16 [2, 1536, 8192], P('section', ('group', 'dp')), may hold values from -0.15625 to 0.15625
- down_weight: bfloat16 [2, 4096, 1536], P('section', ('group', 'dp')), may hold values from -0.09375 to 0.09375
Outputs:
- section_out: bfloat16 [2, 32, 128, 1536], P('section', ('group', 'dp'))
- input_grads: float32 [2, 32, 128, 1536], P('section', ('group', 'dp'))
- attn_gain_grad: float32 [2, 1536], P('section', 'group')
- qkv_grad: float32 [2, 1536, 3072], P('section', 'group')
- out_grad: float32 [2, 1536, 1536], P('section', 'group')
- ffn_gain_grad: float32 [2, 1536], P('section', 'group')
- gate_up_grad: float32 [2, 1536, 8192], P('section', 'group')
- down_grad: float32 [2, 4096, 1536], P('section', 'group')
The draws below stay inside these ranges and needn't reach their ends.
Inputs may be any that keep to these rules, and one draw needn't show every extreme that they name: Sequence b occupies slots 0 to lengths[b] - 1; the rest of its 128 slots is padding. Some sequence is 128 long and some 32 long in every draw.
All inputs are finite; a program needn't handle non-finite values.
Results may differ from the reference program's by a relative error of at most 0.029.
Values may be sent and summed in bfloat16 or wider, within the bound.
A program may use at most 256 MiB of HBM per device.

```python
import math
import jax
import jax.numpy as jnp
from jax import lax

D = 1536
H = 16
KVH = 8
HD = 96
FF = 4096
SLOTS = 128
LMIN = 32
BATCH = 32


def draw_lengths(key, part):
    key = jax.random.fold_in(key, 7)
    key_values, key_order = jax.random.split(key)
    values = jax.random.randint(key_values, (BATCH,), LMIN, SLOTS + 1)
    order = jax.random.permutation(key_order, BATCH)
    values = values.at[order[0]].set(SLOTS).at[order[1]].set(LMIN)
    return values.astype(jnp.int32)


def shard_levels(key, extent, cuts, least, top_value):
    level = 1.0
    for dim, shards_of in cuts:
        steps = jax.random.uniform(jax.random.fold_in(jax.random.fold_in(key, 6), dim), (shards_of,), jnp.float32, least / len(cuts), top_value / len(cuts))
        level = level * jnp.repeat(jnp.exp(steps), extent[dim] // shards_of).reshape((-1,) + (1,) * (len(extent) - 1 - dim))
    return level


def gaussian(key, dims, scale, limit, shards=(), kind=jnp.bfloat16):
    entries = jax.random.normal(key, dims, jnp.float32) * scale
    if len(shards) > 0:
        entries = shard_levels(key, dims, shards, -0.22, 0.18) * entries
    return jnp.clip(entries, min=-limit, max=limit).astype(kind)


def setup_inputs(seed: int = 0) -> dict:
    keys = jax.random.split(jax.random.key(seed), 10)
    return {
        "inputs_x": gaussian(keys[0], (BATCH, SLOTS, D), 1.0, 6.0, ((0, 16),)),
        "cotangent": gaussian(keys[1], (BATCH, SLOTS, D), 1.0, 6.0, ((0, 16),)),
        "lengths": draw_lengths(jax.random.fold_in(keys[9], 71), 0),
        "attn_gain": jnp.clip(1.0 + 0.18 * jax.random.normal(keys[3], (2, D), jnp.float32), 0.099609375, 1.8984375).astype(jnp.bfloat16),
        "qkv_weight": gaussian(keys[4], (2, D, (H + 2 * KVH) * HD), D ** -0.5, 0.15625, ((0, 2), (1, 16))),
        "out_weight": gaussian(keys[5], (2, H * HD, D), (H * HD // 8) ** -0.5, 0.4375, ((0, 2), (1, 16))),
        "ffn_gain": jnp.clip(1.0 + 0.18 * jax.random.normal(keys[6], (2, D), jnp.float32), 0.099609375, 1.8984375).astype(jnp.bfloat16),
        "gate_up": gaussian(keys[7], (2, D, 2 * FF), D ** -0.5, 0.15625, ((0, 2), (1, 16))),
        "down_weight": gaussian(keys[8], (2, FF, D), FF ** -0.5, 0.09375, ((0, 2), (1, 16))),
    }


@jax.custom_vjp
def low(v):
    return lax.optimization_barrier(v.astype(jnp.bfloat16)).astype(jnp.float32)

@jax.custom_vjp
def low_back(v):
    return v

def low_keep(v):
    return (low(v), None)

def low_pass(kept, grad):
    return (grad,)

def back_keep(v):
    return (v, None)

def back_low(kept, grad):
    return (low(grad),)
low.defvjp(low_keep, low_pass)
low_back.defvjp(back_keep, back_low)
norm_eps = 1e-05
rope_base = 100000.0
masked_score = -1e+30
topmost_precision = lax.Precision.HIGHEST

def rope_tables(slot_count, head_width):
    half_width = head_width // 2
    frequency = rope_base ** (-(jnp.arange(half_width, dtype=jnp.float32) * 2.0 / head_width))
    angles = jnp.arange(slot_count, dtype=jnp.float32)[:, None] * frequency[None, :]
    return (jnp.cos(angles), jnp.sin(angles))

def rotate(vector, cosines, sine_table):
    half_width = vector.shape[-1] // 2
    front_half = vector[..., :half_width]
    back_half = vector[..., half_width:]
    cos_wide = cosines[:, None, :]
    sin_wide = sine_table[:, None, :]
    return jnp.concatenate([front_half * cos_wide - back_half * sin_wide, back_half * cos_wide + front_half * sin_wide], -1)

def norm_scale(vector):
    return lax.rsqrt(lax.optimization_barrier(jnp.mean(vector * vector, -1, keepdims=True)) + norm_eps)

def allowed_keys(lengths, slot_count):
    position = jnp.arange(slot_count, dtype=jnp.int32)
    causal = position[None, :] <= position[:, None]
    return causal[None] & (position[None, None, :] < lengths[:, None, None])

def layer(weights, input_rows, lengths):
    gain_one, qkv_w, output_weight, gain_two, gate_up_w, down_w = weights
    row_count, slot_count, width = input_rows.shape
    groups = H // KVH
    score_scale = HD ** (-0.5)
    cosines, sine_table = rope_tables(slot_count, HD)
    normed_one = low(input_rows * norm_scale(input_rows) * gain_one)
    qkv_all = low_back(jnp.einsum('rsd,de->rse', normed_one, qkv_w, precision=topmost_precision))
    query_heads = qkv_all[..., :H * HD].reshape(row_count, slot_count, H, HD)
    query_heads = low(rotate(query_heads, cosines, sine_table)).reshape(row_count, slot_count, KVH, groups, HD)
    key_heads = qkv_all[..., H * HD:(H + KVH) * HD].reshape(row_count, slot_count, KVH, HD)
    key_heads = low(rotate(key_heads, cosines, sine_table))
    value_heads = low(qkv_all[..., (H + KVH) * HD:].reshape(row_count, slot_count, KVH, HD))
    scores = low_back(jnp.einsum('rqkgh,rpkh->rkgqp', query_heads, key_heads, precision=topmost_precision) * score_scale)
    allowed = allowed_keys(lengths, slot_count)
    scores = jnp.where(allowed[:, None, None], scores, masked_score)
    row_max = lax.optimization_barrier(jnp.max(scores, -1, keepdims=True))
    log_total = row_max + jnp.log(lax.optimization_barrier(jnp.sum(jnp.exp(scores - row_max), -1, keepdims=True)))
    prob_low = low(jnp.exp(scores - log_total))
    attention_result = jnp.einsum('rkgqp,rpkh->rqkgh', prob_low, value_heads, precision=topmost_precision)
    attention_result = low_back(low(attention_result.reshape(row_count, slot_count, H * HD)))
    after_attention = input_rows + low_back(jnp.einsum('vao,oj->vaj', attention_result, output_weight, precision=topmost_precision))
    normed_two = low(after_attention * norm_scale(after_attention) * gain_two)
    gated = low_back(jnp.einsum('rsd,de->rse', normed_two, gate_up_w, precision=topmost_precision))
    hidden = low(jax.nn.silu(gated[..., :FF]) * gated[..., FF:])
    result = after_attention + low_back(jnp.einsum('rsf,fd->rsd', hidden, down_w, precision=topmost_precision))
    position = jnp.arange(slot_count, dtype=jnp.int32)
    pad_mask = (position[None, :] < lengths[:, None]).astype(input_rows.dtype)
    return result * pad_mask[..., None]

def block(params, input_rows, extra_term, lengths):
    layer_one = tuple((weight[0] for weight in params))
    layer_two = tuple((weight[1] for weight in params))
    hidden_one = low(layer(layer_one, input_rows, lengths))
    hidden_two = layer(layer_two, low_back(hidden_one + extra_term), lengths)
    return (hidden_one, hidden_two)

def reference(inputs_x, cotangent, lengths, attn_gain, qkv_weight, out_weight, ffn_gain, gate_up, down_weight):
    params = tuple((weight.astype(jnp.float32) for weight in (attn_gain, qkv_weight, out_weight, ffn_gain, gate_up, down_weight)))
    inputs_f = inputs_x.astype(jnp.float32)
    cot_f = cotangent.astype(jnp.float32)
    row_total = inputs_f.shape[0]
    block_rows = math.gcd(row_total, max(1, 4096 // SLOTS))
    block_count = row_total // block_rows
    checked = jax.checkpoint(block)

    def whole_model(params, inputs_f, extra_term):

        def by_blocks(array):
            return array.reshape((block_count, block_rows) + array.shape[1:])

        def one_block(operand):
            return checked(params, operand[0], operand[1], operand[2])
        hidden_one, hidden_two = lax.map(one_block, (by_blocks(inputs_f), by_blocks(extra_term), by_blocks(lengths)))
        return (hidden_one.reshape(inputs_f.shape), hidden_two.reshape(inputs_f.shape))
    extra_term = jnp.zeros_like(inputs_f)
    (hidden_one, hidden_two), pull_back = jax.vjp(whole_model, params, inputs_f, extra_term)
    param_grads, input_grad, extra_grad = pull_back((jnp.zeros_like(hidden_one), cot_f))
    section_out = jnp.stack([hidden_one, hidden_two]).astype(jnp.bfloat16)
    input_grads = jnp.stack([input_grad, extra_grad])
    return (section_out, input_grads, param_grads[0], param_grads[1], param_grads[2], param_grads[3], param_grads[4], param_grads[5])
```

```python
import jax
import jax.numpy as jnp
from jax import lax
from jax.sharding import PartitionSpec as P

H = 16
KVH = 8
HD = 96
FF = 4096


norm_eps = 1e-05
rope_base = 100000.0
masked_score = -1e30


def passed_along(value, axis, by):
    length = lax.axis_size(axis)
    pairs = [(i, i + by) for i in range(length) if 0 <= i + by < length]
    return lax.ppermute(value, axis, pairs)


def rope_tables(slot_count, head_width):
    half_width = head_width // 2
    frequency = rope_base ** (-(jnp.arange(half_width, dtype=jnp.float32) * 2.0 / head_width))
    angles = jnp.arange(slot_count, dtype=jnp.float32)[:, None] * frequency[None, :]
    return (jnp.cos(angles), jnp.sin(angles))


def rotate(vector, cosines, sine_table):
    half_width = vector.shape[-1] // 2
    front_half = vector[..., :half_width]
    back_half = vector[..., half_width:]
    cos_wide = cosines[:, None, :]
    sin_wide = sine_table[:, None, :]
    return jnp.concatenate(
        [
            front_half * cos_wide - back_half * sin_wide,
            back_half * cos_wide + front_half * sin_wide,
        ],
        -1,
    )


def norm_scale(vector):
    return lax.rsqrt(jnp.mean(vector * vector, -1, keepdims=True) + norm_eps)


def allowed_keys(lengths, slot_count):
    position = jnp.arange(slot_count, dtype=jnp.int32)
    causal = position[None, :] <= position[:, None]
    return causal[None] & (position[None, None, :] < lengths[:, None, None])


def padding(lengths, slot_count):
    position = jnp.arange(slot_count, dtype=jnp.int32)
    return (position[None, :] < lengths[:, None]).astype(jnp.float32)[..., None]


def norm_back(vector, scale, gain, grad_normed):
    scaled = grad_normed * gain.astype(jnp.float32)
    gain_grad = jnp.sum(grad_normed * vector * scale, axis=(0, 1))
    grad_vector = scale * scaled - vector * (scale * scale * scale) * jnp.mean(
        vector * scaled, -1, keepdims=True
    )
    return (gain_grad, grad_vector)


def score_block(query_heads, key_heads, lengths):
    slot_count = query_heads.shape[1]
    scores = jnp.einsum(
        "rqkgh,rpkh->rkgqp", query_heads, key_heads, preferred_element_type=jnp.float32
    ) * HD ** (-0.5)
    allowed = allowed_keys(lengths, slot_count)
    return jnp.where(allowed[:, None, None], scores, masked_score)


def forward_layer(weights, input_rows, lengths):
    gain_one, qkv_w, output_weight, gain_two, gate_up_w, down_w = weights
    row_count, slot_count, width = input_rows.shape
    groups = H // KVH
    cosines, sine_table = rope_tables(slot_count, HD)
    scale_one = norm_scale(input_rows)
    normed_one = (input_rows * scale_one * gain_one.astype(jnp.float32)).astype(jnp.bfloat16)
    qkv_all = jnp.einsum("rsd,de->rse", normed_one, qkv_w, preferred_element_type=jnp.float32)
    query_heads = rotate(
        qkv_all[..., : H * HD].reshape(row_count, slot_count, H, HD), cosines, sine_table
    )
    query_heads = query_heads.astype(jnp.bfloat16).reshape(row_count, slot_count, KVH, groups, HD)
    key_heads = rotate(
        qkv_all[..., H * HD : (H + KVH) * HD].reshape(row_count, slot_count, KVH, HD),
        cosines,
        sine_table,
    )
    key_heads = key_heads.astype(jnp.bfloat16)
    value_heads = (
        qkv_all[..., (H + KVH) * HD :].reshape(row_count, slot_count, KVH, HD).astype(jnp.bfloat16)
    )
    scores = score_block(query_heads, key_heads, lengths)
    row_max = jnp.max(scores, -1, keepdims=True)
    log_total = row_max + jnp.log(jnp.sum(jnp.exp(scores - row_max), -1, keepdims=True))
    prob_low = jnp.exp(scores - log_total).astype(jnp.bfloat16)
    attention_result = jnp.einsum(
        "rkgqp,rpkh->rqkgh", prob_low, value_heads, preferred_element_type=jnp.float32
    )
    attention_result = attention_result.astype(jnp.bfloat16).reshape(row_count, slot_count, H * HD)
    after_attention = input_rows + jnp.einsum(
        "vao,oj->vaj", attention_result, output_weight, preferred_element_type=jnp.float32
    )
    scale_two = norm_scale(after_attention)
    normed_two = (after_attention * scale_two * gain_two.astype(jnp.float32)).astype(jnp.bfloat16)
    gated = jnp.einsum("rsd,de->rse", normed_two, gate_up_w, preferred_element_type=jnp.float32)
    hidden = (jax.nn.silu(gated[..., :FF]) * gated[..., FF:]).astype(jnp.bfloat16)
    result = after_attention + jnp.einsum(
        "rsf,fd->rsd", hidden, down_w, preferred_element_type=jnp.float32
    )
    result = result * padding(lengths, slot_count)
    kept_state = (
        input_rows,
        scale_one,
        normed_one,
        query_heads,
        key_heads,
        value_heads,
        log_total,
        attention_result,
        after_attention,
        scale_two,
        normed_two,
        gated,
        hidden,
        lengths,
    )
    return (result, kept_state)


def backward_layer(weights, kept_state, grad_out):
    gain_one, qkv_w, output_weight, gain_two, gate_up_w, down_w = weights
    (
        input_rows,
        scale_one,
        normed_one,
        query_heads,
        key_heads,
        value_heads,
        log_total,
        attention_result,
        after_attention,
        scale_two,
        normed_two,
        gated,
        hidden,
        lengths,
    ) = kept_state
    row_count, slot_count, width = input_rows.shape
    groups = H // KVH
    score_scale = HD ** (-0.5)
    cosines, sine_table = rope_tables(slot_count, HD)
    grad_masked = grad_out * padding(lengths, slot_count)
    grad_low = grad_masked.astype(jnp.bfloat16)
    grad_hidden = jnp.einsum("rsd,fd->rsf", grad_low, down_w, preferred_element_type=jnp.float32)
    gate_part = gated[..., :FF]
    up_part = gated[..., FF:]
    sigmoid_gate = jax.nn.sigmoid(gate_part)
    grad_gate = grad_hidden * up_part * sigmoid_gate * (1.0 + gate_part * (1.0 - sigmoid_gate))
    grad_up = grad_hidden * (gate_part * sigmoid_gate)
    grad_gated = jnp.concatenate([grad_gate, grad_up], -1).astype(jnp.bfloat16)
    grad_normed_two = jnp.einsum(
        "rse,de->rsd", grad_gated, gate_up_w, preferred_element_type=jnp.float32
    )
    ffn_gain_part, grad_norm_two = norm_back(after_attention, scale_two, gain_two, grad_normed_two)
    grad_after = grad_masked + grad_norm_two
    gradient_after_lowered = grad_after.astype(jnp.bfloat16)
    attention_gradient = jnp.einsum(
        "vol,el->voe", gradient_after_lowered, output_weight, preferred_element_type=jnp.float32
    )
    attention_gradient = attention_gradient.astype(jnp.bfloat16).reshape(
        row_count, slot_count, KVH, groups, HD
    )
    scores = score_block(query_heads, key_heads, lengths)
    prob_full = jnp.exp(scores - log_total)
    prob_low = prob_full.astype(jnp.bfloat16)
    grad_values = jnp.einsum(
        "rkgqp,rqkgh->rpkh", prob_low, attention_gradient, preferred_element_type=jnp.float32
    )
    grad_probs = jnp.einsum(
        "rqkgh,rpkh->rkgqp", attention_gradient, value_heads, preferred_element_type=jnp.float32
    )
    row_dot = jnp.sum(prob_full * grad_probs, -1, keepdims=True)
    grad_scores = (prob_full * (grad_probs - row_dot)).astype(jnp.bfloat16)
    grad_query = (
        jnp.einsum("rkgqp,rpkh->rqkgh", grad_scores, key_heads, preferred_element_type=jnp.float32)
        * score_scale
    )
    grad_query = rotate(grad_query.reshape(row_count, slot_count, H, HD), cosines, -sine_table)
    grad_keys = (
        jnp.einsum(
            "rkgqp,rqkgh->rpkh", grad_scores, query_heads, preferred_element_type=jnp.float32
        )
        * score_scale
    )
    grad_keys = rotate(grad_keys, cosines, -sine_table)
    grad_qkv = jnp.concatenate(
        [
            grad_query.reshape(row_count, slot_count, H * HD),
            grad_keys.reshape(row_count, slot_count, KVH * HD),
            grad_values.reshape(row_count, slot_count, KVH * HD),
        ],
        -1,
    ).astype(jnp.bfloat16)
    grad_normed_one = jnp.einsum("rse,de->rsd", grad_qkv, qkv_w, preferred_element_type=jnp.float32)
    attn_gain_part, grad_norm_one = norm_back(input_rows, scale_one, gain_one, grad_normed_one)
    grad_inputs = grad_after + grad_norm_one
    return (
        grad_inputs,
        (attn_gain_part, ffn_gain_part, grad_low, grad_gated, gradient_after_lowered, grad_qkv),
    )


def weight_grads(kept_state, operands):
    (
        input_rows,
        scale_one,
        normed_one,
        query_heads,
        key_heads,
        value_heads,
        log_total,
        attention_result,
        after_attention,
        scale_two,
        normed_two,
        gated,
        hidden,
        lengths,
    ) = kept_state
    attn_gain_part, ffn_gain_part, grad_low, grad_gated, gradient_after_lowered, grad_qkv = operands
    down_part = jnp.einsum("rsf,rsd->fd", hidden, grad_low, preferred_element_type=jnp.float32)
    gate_up_part = jnp.einsum(
        "rsd,rse->de", normed_two, grad_gated, preferred_element_type=jnp.float32
    )
    out_part = jnp.einsum(
        "jvl,jvc->lc", attention_result, gradient_after_lowered, preferred_element_type=jnp.float32
    )
    qkv_part = jnp.einsum("rsd,rse->de", normed_one, grad_qkv, preferred_element_type=jnp.float32)
    return (attn_gain_part, qkv_part, out_part, ffn_gain_part, gate_up_part, down_part)


def body(
    inputs_x, cotangent, lengths, attn_gain, qkv_weight, out_weight, ffn_gain, gate_up, down_weight
):
    is_first = lax.axis_index("section") == 0
    weights = tuple(
        (
            whole[0]
            for whole in (
                lax.all_gather(attn_gain, ("group", "dp"), axis=1, tiled=True),
                lax.all_gather(qkv_weight, ("group", "dp"), axis=1, tiled=True),
                lax.all_gather(out_weight, ("group", "dp"), axis=1, tiled=True),
                lax.all_gather(ffn_gain, ("group", "dp"), axis=1, tiled=True),
                lax.all_gather(gate_up, ("group", "dp"), axis=1, tiled=True),
                lax.all_gather(down_weight, ("group", "dp"), axis=1, tiled=True),
            )
        )
    )
    inputs_f = inputs_x.astype(jnp.float32)
    cotangent_f = cotangent.astype(jnp.float32)
    first_out, _ = forward_layer(weights, inputs_f, lengths)
    recv_act = passed_along(first_out.astype(jnp.bfloat16), "section", 1)
    layer_in = jnp.where(is_first, inputs_f, recv_act.astype(jnp.float32))
    result, kept_state = forward_layer(weights, layer_in, lengths)
    section_out = result.astype(jnp.bfloat16)[None]
    second_dx, _ = backward_layer(weights, kept_state, cotangent_f)
    recv_grad = passed_along(second_dx.astype(jnp.bfloat16), "section", -1)
    grad_in = jnp.where(is_first, recv_grad.astype(jnp.float32), cotangent_f)
    grad_x, operands = backward_layer(weights, kept_state, grad_in)
    input_grads = jnp.where(
        is_first, grad_x, grad_x.astype(jnp.bfloat16).astype(jnp.float32)
    )[None]
    totals = weight_grads(kept_state, operands)
    reduced = []
    for total in totals:
        piece = lax.psum_scatter(
            total.astype(jnp.bfloat16), ("group", "dp"), scatter_dimension=0, tiled=True
        )
        reduced.append(lax.all_gather(piece, "dp", axis=0, tiled=True).astype(jnp.float32))
    return (section_out, input_grads) + tuple((shard_sum[None] for shard_sum in reduced))


def solution(mesh):
    placed = (
        P(("group", "dp"), None, None),
        P(("group", "dp"), None, None),
        P(("group", "dp")),
        P("section", ("group", "dp")),
        P("section", ("group", "dp"), None),
        P("section", ("group", "dp"), None),
        P("section", ("group", "dp")),
        P("section", ("group", "dp"), None),
        P("section", ("group", "dp"), None),
    )
    return jax.shard_map(
        body,
        mesh=mesh,
        in_specs=placed,
        out_specs=(
            P("section", ("group", "dp"), None, None),
            P("section", ("group", "dp"), None, None),
            P("section", "group"),
            P("section", "group", None),
            P("section", "group", None),
            P("section", "group"),
            P("section", "group", None),
            P("section", "group", None),
        ),
        check_vma=False,
    )
```

```python
import functools

import jax
import jax.numpy as jnp
from jax import lax
from jax.experimental import pallas as pl
from jax.experimental.pallas import tpu as pltpu
from jax.sharding import PartitionSpec as P

H = 16
KVH = 8
HD = 96
FF = 4096


norm_eps = 1e-05
rope_base = 100000.0
masked_score = -1e30


def passed_along(value, axis, by):
    length = lax.axis_size(axis)
    pairs = [(i, i + by) for i in range(length) if 0 <= i + by < length]
    return lax.ppermute(value, axis, pairs)


def rope_tables(slot_count, head_width):
    half_width = head_width // 2
    frequency = rope_base ** (-(jnp.arange(half_width, dtype=jnp.float32) * 2.0 / head_width))
    angles = jnp.arange(slot_count, dtype=jnp.float32)[:, None] * frequency[None, :]
    return (jnp.cos(angles), jnp.sin(angles))


def rotate(vector, cosines, sine_table):
    half_width = vector.shape[-1] // 2
    front_half = vector[..., :half_width]
    back_half = vector[..., half_width:]
    cos_wide = cosines[:, None, :]
    sin_wide = sine_table[:, None, :]
    return jnp.concatenate(
        [
            front_half * cos_wide - back_half * sin_wide,
            back_half * cos_wide + front_half * sin_wide,
        ],
        -1,
    )


def norm_scale(vector):
    return lax.rsqrt(jnp.mean(vector * vector, -1, keepdims=True) + norm_eps)


def allowed_keys(lengths, slot_count):
    position = jnp.arange(slot_count, dtype=jnp.int32)
    causal = position[None, :] <= position[:, None]
    return causal[None] & (position[None, None, :] < lengths[:, None, None])


def padding(lengths, slot_count):
    position = jnp.arange(slot_count, dtype=jnp.int32)
    return (position[None, :] < lengths[:, None]).astype(jnp.float32)[..., None]


def norm_back(vector, scale, gain, grad_normed):
    scaled = grad_normed * gain.astype(jnp.float32)
    gain_grad = jnp.sum(grad_normed * vector * scale, axis=(0, 1))
    grad_vector = scale * scaled - vector * (scale * scale * scale) * jnp.mean(
        vector * scaled, -1, keepdims=True
    )
    return (gain_grad, grad_vector)


def score_block(query_heads, key_heads, lengths):
    slot_count = query_heads.shape[1]
    scores = jnp.einsum(
        "rqkgh,rpkh->rkgqp", query_heads, key_heads, preferred_element_type=jnp.float32
    ) * HD ** (-0.5)
    allowed = allowed_keys(lengths, slot_count)
    return jnp.where(allowed[:, None, None], scores, masked_score)


def forward_layer(weights, input_rows, lengths):
    gain_one, qkv_w, output_weight, gain_two, gate_up_w, down_w = weights
    row_count, slot_count, width = input_rows.shape
    groups = H // KVH
    cosines, sine_table = rope_tables(slot_count, HD)
    scale_one = norm_scale(input_rows)
    normed_one = (input_rows * scale_one * gain_one.astype(jnp.float32)).astype(jnp.bfloat16)
    qkv_all = jnp.einsum("rsd,de->rse", normed_one, qkv_w, preferred_element_type=jnp.float32)
    query_heads = rotate(
        qkv_all[..., : H * HD].reshape(row_count, slot_count, H, HD), cosines, sine_table
    )
    query_heads = query_heads.astype(jnp.bfloat16).reshape(row_count, slot_count, KVH, groups, HD)
    key_heads = rotate(
        qkv_all[..., H * HD : (H + KVH) * HD].reshape(row_count, slot_count, KVH, HD),
        cosines,
        sine_table,
    )
    key_heads = key_heads.astype(jnp.bfloat16)
    value_heads = (
        qkv_all[..., (H + KVH) * HD :].reshape(row_count, slot_count, KVH, HD).astype(jnp.bfloat16)
    )
    scores = score_block(query_heads, key_heads, lengths)
    row_max = jnp.max(scores, -1, keepdims=True)
    log_total = row_max + jnp.log(jnp.sum(jnp.exp(scores - row_max), -1, keepdims=True))
    prob_low = jnp.exp(scores - log_total).astype(jnp.bfloat16)
    attention_result = jnp.einsum(
        "rkgqp,rpkh->rqkgh", prob_low, value_heads, preferred_element_type=jnp.float32
    )
    attention_result = attention_result.astype(jnp.bfloat16).reshape(row_count, slot_count, H * HD)
    after_attention = input_rows + jnp.einsum(
        "vao,oj->vaj", attention_result, output_weight, preferred_element_type=jnp.float32
    )
    scale_two = norm_scale(after_attention)
    normed_two = (after_attention * scale_two * gain_two.astype(jnp.float32)).astype(jnp.bfloat16)
    gated = jnp.einsum("rsd,de->rse", normed_two, gate_up_w, preferred_element_type=jnp.float32)
    hidden = (jax.nn.silu(gated[..., :FF]) * gated[..., FF:]).astype(jnp.bfloat16)
    result = after_attention + jnp.einsum(
        "rsf,fd->rsd", hidden, down_w, preferred_element_type=jnp.float32
    )
    result = result * padding(lengths, slot_count)
    kept_state = (
        input_rows,
        scale_one,
        normed_one,
        query_heads,
        key_heads,
        value_heads,
        log_total,
        attention_result,
        after_attention,
        scale_two,
        normed_two,
        gated,
        hidden,
        lengths,
    )
    return (result, kept_state)


def backward_layer(weights, kept_state, grad_out):
    gain_one, qkv_w, output_weight, gain_two, gate_up_w, down_w = weights
    (
        input_rows,
        scale_one,
        normed_one,
        query_heads,
        key_heads,
        value_heads,
        log_total,
        attention_result,
        after_attention,
        scale_two,
        normed_two,
        gated,
        hidden,
        lengths,
    ) = kept_state
    row_count, slot_count, width = input_rows.shape
    groups = H // KVH
    score_scale = HD ** (-0.5)
    cosines, sine_table = rope_tables(slot_count, HD)
    grad_masked = grad_out * padding(lengths, slot_count)
    grad_low = grad_masked.astype(jnp.bfloat16)
    grad_hidden = jnp.einsum("rsd,fd->rsf", grad_low, down_w, preferred_element_type=jnp.float32)
    gate_part = gated[..., :FF]
    up_part = gated[..., FF:]
    sigmoid_gate = jax.nn.sigmoid(gate_part)
    grad_gate = grad_hidden * up_part * sigmoid_gate * (1.0 + gate_part * (1.0 - sigmoid_gate))
    grad_up = grad_hidden * (gate_part * sigmoid_gate)
    grad_gated = jnp.concatenate([grad_gate, grad_up], -1).astype(jnp.bfloat16)
    grad_normed_two = jnp.einsum(
        "rse,de->rsd", grad_gated, gate_up_w, preferred_element_type=jnp.float32
    )
    ffn_gain_part, grad_norm_two = norm_back(after_attention, scale_two, gain_two, grad_normed_two)
    grad_after = grad_masked + grad_norm_two
    gradient_after_lowered = grad_after.astype(jnp.bfloat16)
    attention_gradient = jnp.einsum(
        "vol,el->voe", gradient_after_lowered, output_weight, preferred_element_type=jnp.float32
    )
    attention_gradient = attention_gradient.astype(jnp.bfloat16).reshape(
        row_count, slot_count, KVH, groups, HD
    )
    scores = score_block(query_heads, key_heads, lengths)
    prob_full = jnp.exp(scores - log_total)
    prob_low = prob_full.astype(jnp.bfloat16)
    grad_values = jnp.einsum(
        "rkgqp,rqkgh->rpkh", prob_low, attention_gradient, preferred_element_type=jnp.float32
    )
    grad_probs = jnp.einsum(
        "rqkgh,rpkh->rkgqp", attention_gradient, value_heads, preferred_element_type=jnp.float32
    )
    row_dot = jnp.sum(prob_full * grad_probs, -1, keepdims=True)
    grad_scores = (prob_full * (grad_probs - row_dot)).astype(jnp.bfloat16)
    grad_query = (
        jnp.einsum("rkgqp,rpkh->rqkgh", grad_scores, key_heads, preferred_element_type=jnp.float32)
        * score_scale
    )
    grad_query = rotate(grad_query.reshape(row_count, slot_count, H, HD), cosines, -sine_table)
    grad_keys = (
        jnp.einsum(
            "rkgqp,rqkgh->rpkh", grad_scores, query_heads, preferred_element_type=jnp.float32
        )
        * score_scale
    )
    grad_keys = rotate(grad_keys, cosines, -sine_table)
    grad_qkv = jnp.concatenate(
        [
            grad_query.reshape(row_count, slot_count, H * HD),
            grad_keys.reshape(row_count, slot_count, KVH * HD),
            grad_values.reshape(row_count, slot_count, KVH * HD),
        ],
        -1,
    ).astype(jnp.bfloat16)
    grad_normed_one = jnp.einsum("rse,de->rsd", grad_qkv, qkv_w, preferred_element_type=jnp.float32)
    attn_gain_part, grad_norm_one = norm_back(input_rows, scale_one, gain_one, grad_normed_one)
    grad_inputs = grad_after + grad_norm_one
    return (
        grad_inputs,
        (attn_gain_part, ffn_gain_part, grad_low, grad_gated, gradient_after_lowered, grad_qkv),
    )


def turned(array):
    return array.reshape(-1, array.shape[-1]).T


def flat(array):
    return array.reshape(-1, array.shape[-1])


MESH = pl.DeviceIdType.MESH
LANES = 128


def grad_plan(groups, dp, tokens, width, hidden, qkv_cols):
    pairs = dp // 2
    block = width // groups
    down_block = hidden // groups
    gate_cols = 2 * hidden // 2 // pairs
    qkv_part = qkv_cols // 2 // pairs
    pieces_gate = gate_cols // LANES
    pieces_qkv = qkv_part // LANES
    pieces = pieces_gate + pieces_qkv
    z_rows = LANES
    while down_block % z_rows or block % z_rows:
        z_rows //= 2
    row_chunks = (down_block + block) // z_rows
    half = width // 2
    z_split = max(1, pieces // row_chunks)
    while half % (z_split * LANES):
        z_split -= 1
    return dict(
        groups=groups, pairs=pairs, tokens=tokens, width=width, hidden=hidden, qkv_cols=qkv_cols, block=block,
        down_block=down_block, gate_cols=gate_cols, qkv_part=qkv_part, pieces_gate=pieces_gate, pieces=pieces,
        z_rows=z_rows, z_split=z_split, z_cols=half // z_split, z_pieces=row_chunks * z_split,
        down_chunks=down_block // z_rows, half=half,
    )


YS_RING = 4
HOP = 2
LEAD = 2


def grad_kernel(
    plan, at, ot, n2t, n1t, dz, dy, dg, dq, outy, outz,
    LT, RH, YS, YR, YRT, YLT, ZRT, ZLT, ZX,
    own_sem, xs, xr, ys_s, ys_r, yr_s, yr_r, yl_s, yl_r, zr_s, zr_r, zl_s, zl_r,
    zx_s, zx_r, ag_s, ag_r, sib_s, sib_r, lo,
):
    G, A, T = plan["groups"], plan["pairs"], plan["tokens"]
    width, hidden, half = plan["width"], plan["hidden"], plan["half"]
    block, nY, nZ = plan["block"], plan["pieces"], plan["z_pieces"]
    zr, zc = plan["z_rows"], plan["z_cols"]
    s, z, d = lax.axis_index("section"), lax.axis_index("group"), lax.axis_index("dp")
    c, a = lax.rem(d, 2), lax.div(d, 2)
    sib = (s, z, 2 * a + 1 - c)
    right, left = (s, z + 1, d), (s, z - 1, d)

    def peer(k):
        return (s, z, 2 * lax.rem(a + k, A) + c)

    def remote(src, dst, ss, rs, dev):
        return pltpu.make_async_remote_copy(
            src_ref=src, dst_ref=dst, send_sem=ss, recv_sem=rs, device_id=dev, device_id_type=MESH
        )

    barrier = pltpu.get_barrier_semaphore()
    for dev in [sib, (s, lax.rem(z + 1, G), d), (s, lax.rem(z + G - 1, G), d)] + [peer(k) for k in range(1, A)]:
        pl.semaphore_signal(barrier, inc=1, device_id=dev, device_id_type=MESH)
    pl.semaphore_wait(barrier, A + 2)

    lhs = [(at, 0, hidden), (ot, hidden, width), (n2t, hidden + width, width), (n1t, hidden + 2 * width, width)]
    rhs = [(dz, 0, half), (dy, half, half), (dg, width, hidden), (dq, width + hidden, plan["qkv_cols"] // 2)]
    order = [(0, 0), (2, 2), (1, 1), (3, 3)]
    own, cross = {}, {}
    for i, (ref, row, rows) in enumerate(lhs):
        own[0, i] = pltpu.make_async_copy(ref, LT.at[pl.ds(row, rows), pl.ds(0, T)], own_sem.at[i])
        cross[0, i] = remote(ref, LT.at[pl.ds(row, rows), pl.ds(T, T)], xs.at[i], xr.at[i], sib)
    for i, (ref, col, cols) in enumerate(rhs):
        mine = pl.ds(pl.multiple_of(c * cols, LANES), cols)
        theirs = pl.ds(pl.multiple_of((1 - c) * cols, LANES), cols)
        own[1, i] = pltpu.make_async_copy(ref.at[:, mine], RH.at[pl.ds(0, T), pl.ds(col, cols)], own_sem.at[4 + i])
        cross[1, i] = remote(ref.at[:, theirs], RH.at[pl.ds(T, T), pl.ds(col, cols)], xs.at[4 + i], xr.at[4 + i], sib)
    for i, _ in order:
        for side in (0, 1):
            own[side, i].start()
            cross[side, i].start()

    def operands_here(i):
        for side in (0, 1):
            own[side, i].wait()
            cross[side, i].wait_recv()

    def product(row, rows, col, cols):
        return jnp.dot(
            LT[pl.ds(row, rows), :], RH[:, pl.ds(col, cols)], preferred_element_type=jnp.float32
        )

    def y_product(q, which, b):
        is_gate = q < plan["pieces_gate"]
        row = jnp.where(is_gate, hidden + width, hidden + 2 * width) + b * block
        col = jnp.where(
            is_gate,
            width + which * plan["gate_cols"] + q * LANES,
            width + hidden + which * plan["qkv_part"] + (q - plan["pieces_gate"]) * LANES,
        )
        return product(pl.multiple_of(row, 16), block, pl.multiple_of(col, LANES), LANES)

    def z_product(p, b):
        r, h = lax.div(p, plan["z_split"]), lax.rem(p, plan["z_split"])
        is_down = r < plan["down_chunks"]
        row = jnp.where(
            is_down, b * plan["down_block"] + r * zr, hidden + b * block + (r - plan["down_chunks"]) * zr
        )
        col = jnp.where(is_down, 0, half) + h * zc
        return product(pl.multiple_of(row, 16), zr, pl.multiple_of(col, LANES), zc)

    def y_out(q, part, core):
        is_gate = q < plan["pieces_gate"]
        col = jnp.where(
            is_gate,
            core * hidden + part * plan["gate_cols"] + q * LANES,
            2 * hidden + core * (plan["qkv_cols"] // 2) + part * plan["qkv_part"] + (q - plan["pieces_gate"]) * LANES,
        )
        return outy.at[:, pl.ds(pl.multiple_of(col, LANES), LANES)]

    def z_out(p, core):
        r, h = lax.div(p, plan["z_split"]), lax.rem(p, plan["z_split"])
        return outz.at[
            pl.ds(pl.multiple_of(r * zr, 16), zr), pl.ds(pl.multiple_of(core * half + h * zc, LANES), zc)
        ]

    def y_send(q, k):
        return remote(YS.at[lax.rem(q, YS_RING), k - 1], YR.at[q, k - 1], ys_s.at[q, k - 1], ys_r.at[q, k - 1], peer(k))

    def line_copies(slots_r, slots_l, r_s, r_r, l_s, l_r, first_r, first_l, p):
        out_r, in_r, out_l, in_l = [], [], [], []
        for k in range(G):
            if k < G - 1:
                src = first_r(p) if k == 0 else slots_r.at[p, pl.ds(k, G - 1 - k)]
                out_r.append((k, remote(src, slots_r.at[p, pl.ds(k, G - 1 - k)], r_s.at[p], r_r.at[p], right)))
                held = slots_l.at[p, pl.ds(0, k + 1)]
                in_l.append((k, remote(held, held, l_s.at[p], l_r.at[p], left)))
            if k > 0:
                src = first_l(p) if k == G - 1 else slots_l.at[p, pl.ds(0, k)]
                out_l.append((k, remote(src, slots_l.at[p, pl.ds(0, k)], l_s.at[p], l_r.at[p], left)))
                held = slots_r.at[p, pl.ds(k - 1, G - k)]
                in_r.append((k, remote(held, held, r_s.at[p], r_r.at[p], right)))
        return out_r, in_r, out_l, in_l

    def at_place(copies, act):
        for k, copy in copies:
            @pl.when(z == k)
            def _(copy=copy):
                act(copy)

    def y_line(q):
        return line_copies(
            YRT, YLT, yr_s, yr_r, yl_s, yl_r,
            lambda q: YR.at[q, 0, pl.ds(1, G - 1)], lambda q: YR.at[q, 0, pl.ds(0, G - 1)], q,
        )

    def z_line(p):
        return line_copies(
            ZRT, ZLT, zr_s, zr_r, zl_s, zl_r,
            lambda p: ZRT.at[p, pl.ds(0, G - 1)], lambda p: ZLT.at[p, pl.ds(0, G - 1)], p,
        )

    def zx_copy(p, k):
        return remote(ZX.at[p, a], ZX.at[p, a], zx_s.at[p, k - 1], zx_r.at[p, k - 1], peer(k))

    def ag_copy(q, k):
        return remote(YR.at[q, 0, z], y_out(q, a, c), ag_s.at[q, k - 1], ag_r.at[q, k - 1], peer(k))

    def sib_own(q):
        return remote(YR.at[q, 0, z], y_out(q, a, c), sib_s.at[q, 0], sib_r.at[q, 0], sib)

    def sib_pass(q, k):
        part = lax.rem(a + A - k, A)
        return remote(y_out(q, part, c), y_out(q, part, c), sib_s.at[q, k], sib_r.at[q, k], sib)

    def own_y(q):
        return pltpu.make_async_copy(YR.at[q, 0, z], y_out(q, a, c), lo.at[q])

    def own_z(p):
        return pltpu.make_async_copy(ZX.at[p, a], z_out(p, c), lo.at[nY + p])

    def sib_z(p):
        return remote(ZX.at[p, a], z_out(p, c), sib_s.at[nY + p, 0], sib_r.at[nY + p, 0], sib)

    f32, bf16 = jnp.float32, jnp.bfloat16
    far = jnp.maximum(z, G - 1 - z)

    def live(index, count):
        return (index >= 0) & (index < count)

    def step(t, carry):
        @pl.when(t == 0)
        def _():
            operands_here(0)
            operands_here(2)

        @pl.when(t == 1)
        def _():
            operands_here(1)
            operands_here(3)

        q1 = t

        @pl.when(live(q1, nY))
        def _():
            for k in range(1, A):
                @pl.when(q1 >= YS_RING)
                def _():
                    y_send(q1 - YS_RING, k).wait_send()

                @pl.loop(0, G)
                def _(b):
                    YS[lax.rem(q1, YS_RING), k - 1, b] = y_product(q1, lax.rem(a + k, A), b).astype(bf16)

                y_send(q1, k).start()

        pr = t - HOP * z

        @pl.when(live(pr, nZ))
        def _():
            out_r, in_r, _, _ = z_line(pr)
            at_place(in_r, lambda copy: copy.wait_recv())

            @pl.loop(0, G)
            def _(b):
                @pl.when((b > z) & (z > 0))
                def _():
                    ZRT[pr, b - 1] = (z_product(pr, b) + ZRT[pr, b - 1].astype(f32)).astype(bf16)

                @pl.when((b > z) & (z == 0))
                def _():
                    ZRT[pr, b - 1] = z_product(pr, b).astype(bf16)

            at_place(out_r, lambda copy: copy.start())

        pL = t - HOP * (G - 1 - z)

        @pl.when(live(pL, nZ))
        def _():
            _, _, out_l, in_l = z_line(pL)
            at_place(in_l, lambda copy: copy.wait_recv())

            @pl.loop(0, G)
            def _(b):
                @pl.when((b < z) & (z < G - 1))
                def _():
                    ZLT[pL, b] = (z_product(pL, b) + ZLT[pL, b].astype(f32)).astype(bf16)

                @pl.when((b < z) & (z == G - 1))
                def _():
                    ZLT[pL, b] = z_product(pL, b).astype(bf16)

            at_place(out_l, lambda copy: copy.start())

        q2 = t - LEAD

        @pl.when(live(q2, nY))
        def _():
            for k in range(1, A):
                y_send(q2, k).wait_recv()

            @pl.loop(0, G)
            def _(b):
                total = y_product(q2, a, b)
                for k in range(1, A):
                    total += YR[q2, k - 1, b].astype(f32)
                YR[q2, 0, b] = total.astype(bf16)

        qr = t - LEAD - HOP * z

        @pl.when(live(qr, nY))
        def _():
            out_r, in_r, _, _ = y_line(qr)
            at_place(in_r, lambda copy: copy.wait_recv())

            @pl.loop(0, G)
            def _(b):
                @pl.when((b > z) & (z > 0))
                def _():
                    YRT[qr, b - 1] = (YR[qr, 0, b].astype(f32) + YRT[qr, b - 1].astype(f32)).astype(bf16)

            at_place(out_r, lambda copy: copy.start())

        qL = t - LEAD - HOP * (G - 1 - z)

        @pl.when(live(qL, nY))
        def _():
            _, _, out_l, in_l = y_line(qL)
            at_place(in_l, lambda copy: copy.wait_recv())

            @pl.loop(0, G)
            def _(b):
                @pl.when((b < z) & (z < G - 1))
                def _():
                    YLT[qL, b] = (YR[qL, 0, b].astype(f32) + YLT[qL, b].astype(f32)).astype(bf16)

            at_place(out_l, lambda copy: copy.start())

        pf = t - HOP * far

        @pl.when(live(pf, nZ))
        def _():
            mine = z_product(pf, z)
            from_left = ZRT[pf, jnp.maximum(z - 1, 0)].astype(f32)
            from_right = ZLT[pf, jnp.minimum(z, G - 2)].astype(f32)
            mine = mine + jnp.where(z > 0, from_left, 0.0) + jnp.where(z < G - 1, from_right, 0.0)
            ZX[pf, a] = mine.astype(bf16)
            for k in range(1, A):
                zx_copy(pf, k).start()

        pg = t - HOP * far - LEAD

        @pl.when(live(pg, nZ))
        def _():
            for k in range(1, A):
                remote(
                    ZX.at[pg, lax.rem(a + A - k, A)], ZX.at[pg, lax.rem(a + A - k, A)],
                    zx_s.at[pg, k - 1], zx_r.at[pg, k - 1], peer(k),
                ).wait_recv()
            total = ZX[pg, 0].astype(f32)
            for k in range(1, A):
                total += ZX[pg, k].astype(f32)
            for k in range(1, A):
                zx_copy(pg, k).wait_send()
            ZX[pg, a] = total.astype(bf16)
            own_z(pg).start()
            sib_z(pg).start()

        qf = t - LEAD - HOP * far

        @pl.when(live(qf, nY))
        def _():
            total = YR[qf, 0, z].astype(f32)
            from_left = YRT[qf, jnp.maximum(z - 1, 0)].astype(f32)
            from_right = YLT[qf, jnp.minimum(z, G - 2)].astype(f32)
            total = total + jnp.where(z > 0, from_left, 0.0) + jnp.where(z < G - 1, from_right, 0.0)
            YR[qf, 0, z] = total.astype(bf16)
            for k in range(1, A):
                ag_copy(qf, k).start()
            own_y(qf).start()
            sib_own(qf).start()

        qg = t - LEAD - HOP * far - LEAD

        @pl.when(live(qg, nY))
        def _():
            for k in range(1, A):
                here = y_out(qg, lax.rem(a + A - k, A), c)
                remote(here, here, ag_s.at[qg, k - 1], ag_r.at[qg, k - 1], peer(k)).wait_recv()
                sib_pass(qg, k).start()

        return carry

    steps = max(nY, nZ) + 2 * LEAD + HOP * (G - 1)
    lax.fori_loop(0, steps, step, 0)

    for i in range(4):
        for side in (0, 1):
            cross[side, i].wait_send()

    def drain_y(q, carry):
        for k in range(1, A):
            @pl.when(q >= nY - YS_RING)
            def _():
                y_send(q, k).wait_send()

            ag_copy(q, k).wait_send()
            sib_pass(q, k).wait_send()
            there = y_out(q, lax.rem(a + A - k, A), 1 - c)
            remote(there, there, sib_s.at[q, k], sib_r.at[q, k], sib).wait_recv()
        out_r, _, out_l, _ = y_line(q)
        at_place(out_r, lambda copy: copy.wait_send())
        at_place(out_l, lambda copy: copy.wait_send())
        own_y(q).wait()
        sib_own(q).wait_send()
        there = y_out(q, a, 1 - c)
        remote(there, there, sib_s.at[q, 0], sib_r.at[q, 0], sib).wait_recv()
        return carry

    lax.fori_loop(0, nY, drain_y, 0)

    def drain_z(p, carry):
        out_r, _, out_l, _ = z_line(p)
        at_place(out_r, lambda copy: copy.wait_send())
        at_place(out_l, lambda copy: copy.wait_send())
        own_z(p).wait()
        sib_z(p).wait_send()
        there = z_out(p, 1 - c)
        remote(there, there, sib_s.at[nY + p, 0], sib_r.at[nY + p, 0], sib).wait_recv()
        return carry

    lax.fori_loop(0, nZ, drain_z, 0)


def summed_grads(groups, dp, at, ot, n2t, n1t, dz, dy, dg, dq):
    hidden, tokens = at.shape
    width, qkv_cols = ot.shape[0], dq.shape[1]
    plan = grad_plan(groups, dp, tokens, width, hidden, qkv_cols)
    G, A, nY, nZ = groups, plan["pairs"], plan["pieces"], plan["z_pieces"]
    block, zr, zc = plan["block"], plan["z_rows"], plan["z_cols"]
    bf16, DMA = jnp.bfloat16, pltpu.SemaphoreType.DMA
    any_space = pl.BlockSpec(memory_space=pl.ANY)
    return pl.pallas_call(
        functools.partial(grad_kernel, plan),
        out_shape=(
            jax.ShapeDtypeStruct((block, 2 * hidden + qkv_cols), bf16),
            jax.ShapeDtypeStruct((plan["down_block"] + block, width), bf16),
        ),
        in_specs=[any_space] * 8,
        out_specs=(any_space, any_space),
        scratch_shapes=[
            pltpu.VMEM((hidden + 3 * width, 2 * tokens), bf16),
            pltpu.VMEM((2 * tokens, width + hidden + qkv_cols // 2), bf16),
            pltpu.VMEM((YS_RING, A - 1, G, block, LANES), bf16),
            pltpu.VMEM((nY, A - 1, G, block, LANES), bf16),
            pltpu.VMEM((nY, G - 1, block, LANES), bf16),
            pltpu.VMEM((nY, G - 1, block, LANES), bf16),
            pltpu.VMEM((nZ, G - 1, zr, zc), bf16),
            pltpu.VMEM((nZ, G - 1, zr, zc), bf16),
            pltpu.VMEM((nZ, A, zr, zc), bf16),
            DMA((8,)), DMA((8,)), DMA((8,)),
            DMA((nY, A - 1)), DMA((nY, A - 1)),
            DMA((nY,)), DMA((nY,)), DMA((nY,)), DMA((nY,)),
            DMA((nZ,)), DMA((nZ,)), DMA((nZ,)), DMA((nZ,)),
            DMA((nZ, A - 1)), DMA((nZ, A - 1)),
            DMA((nY, A - 1)), DMA((nY, A - 1)),
            DMA((nY + nZ, A)), DMA((nY + nZ, A)),
            DMA((nY + nZ,)),
        ],
        compiler_params=pltpu.CompilerParams(
            collective_id=3, has_side_effects=True, vmem_limit_bytes=63 * 1024 * 1024
        ),
        cost_estimate=pl.CostEstimate(
            flops=2 * 2 * tokens * (width * (2 * hidden + qkv_cols + width) + hidden * width) // 2,
            bytes_accessed=40_000_000, transcendentals=0,
        ),
    )(at, ot, n2t, n1t, dz, dy, dg, dq)


def body(
    inputs_x, cotangent, lengths, attn_gain, qkv_weight, out_weight, ffn_gain, gate_up, down_weight
):
    is_first = lax.axis_index("section") == 0
    everyone = ("group", "dp")
    gains = lax.all_gather(jnp.concatenate([attn_gain, ffn_gain], 0), everyone)
    gains = gains.transpose(1, 0, 2).reshape(2, -1)
    weights = (
        gains[0],
        lax.all_gather(qkv_weight[0], everyone, axis=0, tiled=True),
        lax.all_gather(out_weight[0], everyone, axis=0, tiled=True),
        gains[1],
        lax.all_gather(gate_up[0], everyone, axis=0, tiled=True),
        lax.all_gather(down_weight[0], everyone, axis=0, tiled=True),
    )
    inputs_f = inputs_x.astype(jnp.float32)
    cotangent_f = cotangent.astype(jnp.float32)
    first_out, _ = forward_layer(weights, inputs_f, lengths)
    recv_act = passed_along(first_out.astype(jnp.bfloat16), "section", 1)
    layer_in = jnp.where(is_first, inputs_f, recv_act.astype(jnp.float32))
    result, kept_state = forward_layer(weights, layer_in, lengths)
    section_out = result.astype(jnp.bfloat16)[None]
    second_dx, _ = backward_layer(weights, kept_state, cotangent_f)
    recv_grad = passed_along(second_dx.astype(jnp.bfloat16), "section", -1)
    grad_in = jnp.where(is_first, recv_grad.astype(jnp.float32), cotangent_f)
    grad_x, operands = backward_layer(weights, kept_state, grad_in)
    input_grads = jnp.where(
        is_first, grad_x, grad_x.astype(jnp.bfloat16).astype(jnp.float32)
    )[None]
    (_, _, normed_one, _, _, _, _, attention_result, _, _, normed_two, _, hidden, _) = kept_state
    attn_gain_part, ffn_gain_part, grad_low, grad_gated, gradient_after_lowered, grad_qkv = operands
    gain_parts = lax.all_gather(jnp.stack([attn_gain_part, ffn_gain_part]), ("group", "dp"))
    gate_qkv_sum, down_out_sum = summed_grads(
        lax.axis_size("group"),
        lax.axis_size("dp"),
        turned(hidden),
        turned(attention_result),
        turned(normed_two),
        turned(normed_one),
        flat(grad_low),
        flat(gradient_after_lowered),
        flat(grad_gated),
        flat(grad_qkv),
    )
    gain_cols = attn_gain.shape[1] * lax.axis_size("dp")
    gain_sums = lax.dynamic_slice_in_dim(
        jnp.sum(gain_parts, 0), lax.axis_index("group") * gain_cols, gain_cols, 1
    )
    gate_width = gate_up.shape[2]
    down_rows = down_weight.shape[1] * lax.axis_size("dp")
    reduced = (
        gain_sums[0],
        gate_qkv_sum[:, gate_width:].astype(jnp.float32),
        down_out_sum[down_rows:].astype(jnp.float32),
        gain_sums[1],
        gate_qkv_sum[:, :gate_width].astype(jnp.float32),
        down_out_sum[:down_rows].astype(jnp.float32),
    )
    return (section_out, input_grads) + tuple((shard_sum[None] for shard_sum in reduced))


def solution(mesh):
    placed = (
        P(("group", "dp"), None, None),
        P(("group", "dp"), None, None),
        P(("group", "dp")),
        P("section", ("group", "dp")),
        P("section", ("group", "dp"), None),
        P("section", ("group", "dp"), None),
        P("section", ("group", "dp")),
        P("section", ("group", "dp"), None),
        P("section", ("group", "dp"), None),
    )
    return jax.shard_map(
        body,
        mesh=mesh,
        in_specs=placed,
        out_specs=(
            P("section", ("group", "dp"), None, None),
            P("section", ("group", "dp"), None, None),
            P("section", "group"),
            P("section", "group", None),
            P("section", "group", None),
            P("section", "group"),
            P("section", "group", None),
            P("section", "group", None),
        ),
        check_vma=False,
    )
```

```python
import functools

import jax
import jax.numpy as jnp
from jax import lax
from jax.experimental import pallas as pl
from jax.experimental.pallas import tpu as pltpu
from jax.sharding import PartitionSpec as P

H = 16
KVH = 8
HD = 96
FF = 4096


norm_eps = 1e-05
rope_base = 100000.0
masked_score = -1e30


def passed_along(value, axis, by):
    length = lax.axis_size(axis)
    pairs = [(i, i + by) for i in range(length) if 0 <= i + by < length]
    return lax.ppermute(value, axis, pairs)


def rope_tables(slot_count, head_width):
    half_width = head_width // 2
    frequency = rope_base ** (-(jnp.arange(half_width, dtype=jnp.float32) * 2.0 / head_width))
    angles = jnp.arange(slot_count, dtype=jnp.float32)[:, None] * frequency[None, :]
    return (jnp.cos(angles), jnp.sin(angles))


def rotate(vector, cosines, sine_table):
    half_width = vector.shape[-1] // 2
    front_half = vector[..., :half_width]
    back_half = vector[..., half_width:]
    cos_wide = cosines[:, None, :]
    sin_wide = sine_table[:, None, :]
    return jnp.concatenate(
        [
            front_half * cos_wide - back_half * sin_wide,
            back_half * cos_wide + front_half * sin_wide,
        ],
        -1,
    )


def norm_scale(vector):
    return lax.rsqrt(jnp.mean(vector * vector, -1, keepdims=True) + norm_eps)


def allowed_keys(lengths, slot_count):
    position = jnp.arange(slot_count, dtype=jnp.int32)
    causal = position[None, :] <= position[:, None]
    return causal[None] & (position[None, None, :] < lengths[:, None, None])


def padding(lengths, slot_count):
    position = jnp.arange(slot_count, dtype=jnp.int32)
    return (position[None, :] < lengths[:, None]).astype(jnp.float32)[..., None]


def norm_back(vector, scale, gain, grad_normed):
    scaled = grad_normed * gain.astype(jnp.float32)
    gain_grad = jnp.sum(grad_normed * vector * scale, axis=(0, 1))
    grad_vector = scale * scaled - vector * (scale * scale * scale) * jnp.mean(
        vector * scaled, -1, keepdims=True
    )
    return (gain_grad, grad_vector)


def score_block(query_heads, key_heads, lengths):
    slot_count = query_heads.shape[1]
    scores = jnp.einsum(
        "rqkgh,rpkh->rkgqp", query_heads, key_heads, preferred_element_type=jnp.float32
    ) * HD ** (-0.5)
    allowed = allowed_keys(lengths, slot_count)
    return jnp.where(allowed[:, None, None], scores, masked_score)


def forward_layer(weights, input_rows, lengths):
    gain_one, qkv_w, output_weight, gain_two, gate_up_w, down_w = weights
    row_count, slot_count, width = input_rows.shape
    groups = H // KVH
    cosines, sine_table = rope_tables(slot_count, HD)
    scale_one = norm_scale(input_rows)
    normed_one = (input_rows * scale_one * gain_one.astype(jnp.float32)).astype(jnp.bfloat16)
    qkv_all = jnp.einsum("rsd,de->rse", normed_one, qkv_w, preferred_element_type=jnp.float32)
    query_heads = rotate(
        qkv_all[..., : H * HD].reshape(row_count, slot_count, H, HD), cosines, sine_table
    )
    query_heads = query_heads.astype(jnp.bfloat16).reshape(row_count, slot_count, KVH, groups, HD)
    key_heads = rotate(
        qkv_all[..., H * HD : (H + KVH) * HD].reshape(row_count, slot_count, KVH, HD),
        cosines,
        sine_table,
    )
    key_heads = key_heads.astype(jnp.bfloat16)
    value_heads = (
        qkv_all[..., (H + KVH) * HD :].reshape(row_count, slot_count, KVH, HD).astype(jnp.bfloat16)
    )
    scores = score_block(query_heads, key_heads, lengths)
    row_max = jnp.max(scores, -1, keepdims=True)
    log_total = row_max + jnp.log(jnp.sum(jnp.exp(scores - row_max), -1, keepdims=True))
    prob_low = jnp.exp(scores - log_total).astype(jnp.bfloat16)
    attention_result = jnp.einsum(
        "rkgqp,rpkh->rqkgh", prob_low, value_heads, preferred_element_type=jnp.float32
    )
    attention_result = attention_result.astype(jnp.bfloat16).reshape(row_count, slot_count, H * HD)
    after_attention = input_rows + jnp.einsum(
        "vao,oj->vaj", attention_result, output_weight, preferred_element_type=jnp.float32
    )
    scale_two = norm_scale(after_attention)
    normed_two = (after_attention * scale_two * gain_two.astype(jnp.float32)).astype(jnp.bfloat16)
    gated = jnp.einsum("rsd,de->rse", normed_two, gate_up_w, preferred_element_type=jnp.float32)
    hidden = (jax.nn.silu(gated[..., :FF]) * gated[..., FF:]).astype(jnp.bfloat16)
    result = after_attention + jnp.einsum(
        "rsf,fd->rsd", hidden, down_w, preferred_element_type=jnp.float32
    )
    result = result * padding(lengths, slot_count)
    kept_state = (
        input_rows,
        scale_one,
        normed_one,
        query_heads,
        key_heads,
        value_heads,
        log_total,
        attention_result,
        after_attention,
        scale_two,
        normed_two,
        gated,
        hidden,
        lengths,
    )
    return (result, kept_state)


def backward_layer(weights, kept_state, grad_out):
    gain_one, qkv_w, output_weight, gain_two, gate_up_w, down_w = weights
    (
        input_rows,
        scale_one,
        normed_one,
        query_heads,
        key_heads,
        value_heads,
        log_total,
        attention_result,
        after_attention,
        scale_two,
        normed_two,
        gated,
        hidden,
        lengths,
    ) = kept_state
    row_count, slot_count, width = input_rows.shape
    groups = H // KVH
    score_scale = HD ** (-0.5)
    cosines, sine_table = rope_tables(slot_count, HD)
    grad_masked = grad_out * padding(lengths, slot_count)
    grad_low = grad_masked.astype(jnp.bfloat16)
    grad_hidden = jnp.einsum("rsd,fd->rsf", grad_low, down_w, preferred_element_type=jnp.float32)
    gate_part = gated[..., :FF]
    up_part = gated[..., FF:]
    sigmoid_gate = jax.nn.sigmoid(gate_part)
    grad_gate = grad_hidden * up_part * sigmoid_gate * (1.0 + gate_part * (1.0 - sigmoid_gate))
    grad_up = grad_hidden * (gate_part * sigmoid_gate)
    grad_gated = jnp.concatenate([grad_gate, grad_up], -1).astype(jnp.bfloat16)
    grad_normed_two = jnp.einsum(
        "rse,de->rsd", grad_gated, gate_up_w, preferred_element_type=jnp.float32
    )
    ffn_gain_part, grad_norm_two = norm_back(after_attention, scale_two, gain_two, grad_normed_two)
    grad_after = grad_masked + grad_norm_two
    gradient_after_lowered = grad_after.astype(jnp.bfloat16)
    attention_gradient = jnp.einsum(
        "vol,el->voe", gradient_after_lowered, output_weight, preferred_element_type=jnp.float32
    )
    attention_gradient = attention_gradient.astype(jnp.bfloat16).reshape(
        row_count, slot_count, KVH, groups, HD
    )
    scores = score_block(query_heads, key_heads, lengths)
    prob_full = jnp.exp(scores - log_total)
    prob_low = prob_full.astype(jnp.bfloat16)
    grad_values = jnp.einsum(
        "rkgqp,rqkgh->rpkh", prob_low, attention_gradient, preferred_element_type=jnp.float32
    )
    grad_probs = jnp.einsum(
        "rqkgh,rpkh->rkgqp", attention_gradient, value_heads, preferred_element_type=jnp.float32
    )
    row_dot = jnp.sum(prob_full * grad_probs, -1, keepdims=True)
    grad_scores = (prob_full * (grad_probs - row_dot)).astype(jnp.bfloat16)
    grad_query = (
        jnp.einsum("rkgqp,rpkh->rqkgh", grad_scores, key_heads, preferred_element_type=jnp.float32)
        * score_scale
    )
    grad_query = rotate(grad_query.reshape(row_count, slot_count, H, HD), cosines, -sine_table)
    grad_keys = (
        jnp.einsum(
            "rkgqp,rqkgh->rpkh", grad_scores, query_heads, preferred_element_type=jnp.float32
        )
        * score_scale
    )
    grad_keys = rotate(grad_keys, cosines, -sine_table)
    grad_qkv = jnp.concatenate(
        [
            grad_query.reshape(row_count, slot_count, H * HD),
            grad_keys.reshape(row_count, slot_count, KVH * HD),
            grad_values.reshape(row_count, slot_count, KVH * HD),
        ],
        -1,
    ).astype(jnp.bfloat16)
    grad_normed_one = jnp.einsum("rse,de->rsd", grad_qkv, qkv_w, preferred_element_type=jnp.float32)
    attn_gain_part, grad_norm_one = norm_back(input_rows, scale_one, gain_one, grad_normed_one)
    grad_inputs = grad_after + grad_norm_one
    return (
        grad_inputs,
        (attn_gain_part, ffn_gain_part, grad_low, grad_gated, gradient_after_lowered, grad_qkv),
    )


def turned(array):
    return array.reshape(-1, array.shape[-1]).T


def flat(array):
    return array.reshape(-1, array.shape[-1])


MESH = pl.DeviceIdType.MESH
LANES = 128


def grad_plan(groups, dp, tokens, width, hidden, qkv_cols):
    pairs = dp // 2
    block = width // groups
    down_block = hidden // groups
    gate_cols = 2 * hidden // 2 // pairs
    qkv_part = qkv_cols // 2 // pairs
    pieces_gate = gate_cols // LANES
    pieces_qkv = qkv_part // LANES
    pieces = pieces_gate + pieces_qkv
    z_rows = LANES
    while down_block % z_rows or block % z_rows:
        z_rows //= 2
    row_chunks = (down_block + block) // z_rows
    half = width // 2
    z_split = max(1, pieces // row_chunks)
    while half % (z_split * LANES):
        z_split -= 1
    return dict(
        groups=groups, pairs=pairs, tokens=tokens, width=width, hidden=hidden, qkv_cols=qkv_cols, block=block,
        down_block=down_block, gate_cols=gate_cols, qkv_part=qkv_part, pieces_gate=pieces_gate, pieces=pieces,
        z_rows=z_rows, z_split=z_split, z_cols=half // z_split, z_pieces=row_chunks * z_split,
        down_chunks=down_block // z_rows, half=half,
    )


YS_RING = 4
HOP = 2
LEAD = 2


def grad_kernel(
    plan, at, ot, n2t, n1t, dz, dy, dg, dq, gp, outy, outz, outg,
    LT, RH, YS, YR, YRT, YLT, ZRT, ZLT, ZX,
    own_sem, xs, xr, ys_s, ys_r, yr_s, yr_r, yl_s, yl_r, zr_s, zr_r, zl_s, zl_r,
    zx_s, zx_r, ag_s, ag_r, sib_s, sib_r, lo,
    GC, GA, GS, GR, GL, gc_sem, ga_s, ga_r, gr_sem, gl_sem,
):
    G, A, T = plan["groups"], plan["pairs"], plan["tokens"]
    width, hidden, half = plan["width"], plan["hidden"], plan["half"]
    block, nY, nZ = plan["block"], plan["pieces"], plan["z_pieces"]
    zr, zc = plan["z_rows"], plan["z_cols"]
    s, z, d = lax.axis_index("section"), lax.axis_index("group"), lax.axis_index("dp")
    c, a = lax.rem(d, 2), lax.div(d, 2)
    sib = (s, z, 2 * a + 1 - c)
    right, left = (s, z + 1, d), (s, z - 1, d)

    def peer(k):
        return (s, z, 2 * lax.rem(a + k, A) + c)

    def remote(src, dst, ss, rs, dev):
        return pltpu.make_async_remote_copy(
            src_ref=src, dst_ref=dst, send_sem=ss, recv_sem=rs, device_id=dev, device_id_type=MESH
        )

    barrier = pltpu.get_barrier_semaphore()
    for dev in [sib, (s, lax.rem(z + 1, G), d), (s, lax.rem(z + G - 1, G), d)] + [peer(k) for k in range(1, A)]:
        pl.semaphore_signal(barrier, inc=1, device_id=dev, device_id_type=MESH)
    pl.semaphore_wait(barrier, A + 2)

    lhs = [(at, 0, hidden), (ot, hidden, width), (n2t, hidden + width, width), (n1t, hidden + 2 * width, width)]
    rhs = [(dz, 0, half), (dy, half, half), (dg, width, hidden), (dq, width + hidden, plan["qkv_cols"] // 2)]
    order = [(0, 0), (2, 2), (1, 1), (3, 3)]
    own, cross = {}, {}
    for i, (ref, row, rows) in enumerate(lhs):
        own[0, i] = pltpu.make_async_copy(ref, LT.at[pl.ds(row, rows), pl.ds(0, T)], own_sem.at[i])
        cross[0, i] = remote(ref, LT.at[pl.ds(row, rows), pl.ds(T, T)], xs.at[i], xr.at[i], sib)
    for i, (ref, col, cols) in enumerate(rhs):
        mine = pl.ds(pl.multiple_of(c * cols, LANES), cols)
        theirs = pl.ds(pl.multiple_of((1 - c) * cols, LANES), cols)
        own[1, i] = pltpu.make_async_copy(ref.at[:, mine], RH.at[pl.ds(0, T), pl.ds(col, cols)], own_sem.at[4 + i])
        cross[1, i] = remote(ref.at[:, theirs], RH.at[pl.ds(T, T), pl.ds(col, cols)], xs.at[4 + i], xr.at[4 + i], sib)
    for i, _ in order:
        for side in (0, 1):
            own[side, i].start()
            cross[side, i].start()

    def operands_here(i):
        for side in (0, 1):
            own[side, i].wait()
            cross[side, i].wait_recv()

    def product(row, rows, col, cols):
        return jnp.dot(
            LT[pl.ds(row, rows), :], RH[:, pl.ds(col, cols)], preferred_element_type=jnp.float32
        )

    def y_product(q, which, b):
        is_gate = q < plan["pieces_gate"]
        row = jnp.where(is_gate, hidden + width, hidden + 2 * width) + b * block
        col = jnp.where(
            is_gate,
            width + which * plan["gate_cols"] + q * LANES,
            width + hidden + which * plan["qkv_part"] + (q - plan["pieces_gate"]) * LANES,
        )
        return product(pl.multiple_of(row, 16), block, pl.multiple_of(col, LANES), LANES)

    def z_product(p, b):
        r, h = lax.div(p, plan["z_split"]), lax.rem(p, plan["z_split"])
        is_down = r < plan["down_chunks"]
        row = jnp.where(
            is_down, b * plan["down_block"] + r * zr, hidden + b * block + (r - plan["down_chunks"]) * zr
        )
        col = jnp.where(is_down, 0, half) + h * zc
        return product(pl.multiple_of(row, 16), zr, pl.multiple_of(col, LANES), zc)

    def y_out(q, part, core):
        is_gate = q < plan["pieces_gate"]
        col = jnp.where(
            is_gate,
            core * hidden + part * plan["gate_cols"] + q * LANES,
            2 * hidden + core * (plan["qkv_cols"] // 2) + part * plan["qkv_part"] + (q - plan["pieces_gate"]) * LANES,
        )
        return outy.at[:, pl.ds(pl.multiple_of(col, LANES), LANES)]

    def z_out(p, core):
        r, h = lax.div(p, plan["z_split"]), lax.rem(p, plan["z_split"])
        return outz.at[
            pl.ds(pl.multiple_of(r * zr, 16), zr), pl.ds(pl.multiple_of(core * half + h * zc, LANES), zc)
        ]

    def y_send(q, k):
        return remote(YS.at[lax.rem(q, YS_RING), k - 1], YR.at[q, k - 1], ys_s.at[q, k - 1], ys_r.at[q, k - 1], peer(k))

    def line_copies(slots_r, slots_l, r_s, r_r, l_s, l_r, first_r, first_l, p):
        out_r, in_r, out_l, in_l = [], [], [], []
        for k in range(G):
            if k < G - 1:
                src = first_r(p) if k == 0 else slots_r.at[p, pl.ds(k, G - 1 - k)]
                out_r.append((k, remote(src, slots_r.at[p, pl.ds(k, G - 1 - k)], r_s.at[p], r_r.at[p], right)))
                held = slots_l.at[p, pl.ds(0, k + 1)]
                in_l.append((k, remote(held, held, l_s.at[p], l_r.at[p], left)))
            if k > 0:
                src = first_l(p) if k == G - 1 else slots_l.at[p, pl.ds(0, k)]
                out_l.append((k, remote(src, slots_l.at[p, pl.ds(0, k)], l_s.at[p], l_r.at[p], left)))
                held = slots_r.at[p, pl.ds(k - 1, G - k)]
                in_r.append((k, remote(held, held, r_s.at[p], r_r.at[p], right)))
        return out_r, in_r, out_l, in_l

    def at_place(copies, act):
        for k, copy in copies:
            @pl.when(z == k)
            def _(copy=copy):
                act(copy)

    def y_line(q):
        return line_copies(
            YRT, YLT, yr_s, yr_r, yl_s, yl_r,
            lambda q: YR.at[q, 0, pl.ds(1, G - 1)], lambda q: YR.at[q, 0, pl.ds(0, G - 1)], q,
        )

    def z_line(p):
        return line_copies(
            ZRT, ZLT, zr_s, zr_r, zl_s, zl_r,
            lambda p: ZRT.at[p, pl.ds(0, G - 1)], lambda p: ZLT.at[p, pl.ds(0, G - 1)], p,
        )

    def zx_copy(p, k):
        return remote(ZX.at[p, a], ZX.at[p, a], zx_s.at[p, k - 1], zx_r.at[p, k - 1], peer(k))

    def ag_copy(q, k):
        return remote(YR.at[q, 0, z], y_out(q, a, c), ag_s.at[q, k - 1], ag_r.at[q, k - 1], peer(k))

    def sib_own(q):
        return remote(YR.at[q, 0, z], y_out(q, a, c), sib_s.at[q, 0], sib_r.at[q, 0], sib)

    def sib_pass(q, k):
        part = lax.rem(a + A - k, A)
        return remote(y_out(q, part, c), y_out(q, part, c), sib_s.at[q, k], sib_r.at[q, k], sib)

    def own_y(q):
        return pltpu.make_async_copy(YR.at[q, 0, z], y_out(q, a, c), lo.at[q])

    def own_z(p):
        return pltpu.make_async_copy(ZX.at[p, a], z_out(p, c), lo.at[nY + p])

    def sib_z(p):
        return remote(ZX.at[p, a], z_out(p, c), sib_s.at[nY + p, 0], sib_r.at[nY + p, 0], sib)

    f32, bf16 = jnp.float32, jnp.bfloat16
    far = jnp.maximum(z, G - 1 - z)

    def live(index, count):
        return (index >= 0) & (index < count)

    def gain_core():
        return remote(gp, GC, gc_sem.at[0], gc_sem.at[1], sib)

    def gain_part(k):
        return remote(GA.at[a], GA.at[a], ga_s.at[k - 1], ga_r.at[k - 1], peer(k))

    def gain_right():
        return remote(GS.at[1], GR, gr_sem.at[0], gr_sem.at[1], right)

    def gain_left():
        return remote(GS.at[2], GL, gl_sem.at[0], gl_sem.at[1], left)

    def gain_step(t):
        @pl.when(t == 0)
        def _():
            gain_core().start()

        @pl.when(t == 1)
        def _():
            gain_core().wait_recv()
            GA[a] = gp[...] + GC[...]
            for k in range(1, A):
                gain_part(k).start()

        @pl.when(t == 2)
        def _():
            for k in range(1, A):
                remote(
                    GA.at[lax.rem(a + A - k, A)], GA.at[lax.rem(a + A - k, A)], ga_s.at[k - 1], ga_r.at[k - 1], peer(k)
                ).wait_recv()
            total = GA[0]
            for k in range(1, A):
                total += GA[k]
            GS[0] = total

        @pl.when(t == 2 + HOP * z)
        def _():
            @pl.when(z > 0)
            def _():
                gain_right().wait_recv()
                GS[1] = GS[0] + GR[...]

            @pl.when(z == 0)
            def _():
                GS[1] = GS[0]

            @pl.when(z < G - 1)
            def _():
                gain_right().start()

        @pl.when(t == 2 + HOP * (G - 1 - z))
        def _():
            @pl.when(z < G - 1)
            def _():
                gain_left().wait_recv()
                GS[2] = GS[0] + GL[...]

            @pl.when(z == G - 1)
            def _():
                GS[2] = GS[0]

            @pl.when(z > 0)
            def _():
                gain_left().start()

        @pl.when(t == 3 + HOP * (G - 1))
        def _():
            outg[...] = GS[1] + jnp.where(z < G - 1, GL[...], 0.0)

    def step(t, carry):
        gain_step(t)

        @pl.when(t == 0)
        def _():
            operands_here(0)
            operands_here(2)

        @pl.when(t == 1)
        def _():
            operands_here(1)
            operands_here(3)

        q1 = t

        @pl.when(live(q1, nY))
        def _():
            for k in range(1, A):
                @pl.when(q1 >= YS_RING)
                def _():
                    y_send(q1 - YS_RING, k).wait_send()

                @pl.loop(0, G)
                def _(b):
                    YS[lax.rem(q1, YS_RING), k - 1, b] = y_product(q1, lax.rem(a + k, A), b).astype(bf16)

                y_send(q1, k).start()

        pr = t - HOP * z

        @pl.when(live(pr, nZ))
        def _():
            out_r, in_r, _, _ = z_line(pr)
            at_place(in_r, lambda copy: copy.wait_recv())

            @pl.loop(0, G)
            def _(b):
                @pl.when((b > z) & (z > 0))
                def _():
                    ZRT[pr, b - 1] = (z_product(pr, b) + ZRT[pr, b - 1].astype(f32)).astype(bf16)

                @pl.when((b > z) & (z == 0))
                def _():
                    ZRT[pr, b - 1] = z_product(pr, b).astype(bf16)

            at_place(out_r, lambda copy: copy.start())

        pL = t - HOP * (G - 1 - z)

        @pl.when(live(pL, nZ))
        def _():
            _, _, out_l, in_l = z_line(pL)
            at_place(in_l, lambda copy: copy.wait_recv())

            @pl.loop(0, G)
            def _(b):
                @pl.when((b < z) & (z < G - 1))
                def _():
                    ZLT[pL, b] = (z_product(pL, b) + ZLT[pL, b].astype(f32)).astype(bf16)

                @pl.when((b < z) & (z == G - 1))
                def _():
                    ZLT[pL, b] = z_product(pL, b).astype(bf16)

            at_place(out_l, lambda copy: copy.start())

        q2 = t - LEAD

        @pl.when(live(q2, nY))
        def _():
            for k in range(1, A):
                y_send(q2, k).wait_recv()

            @pl.loop(0, G)
            def _(b):
                total = y_product(q2, a, b)
                for k in range(1, A):
                    total += YR[q2, k - 1, b].astype(f32)
                YR[q2, 0, b] = total.astype(bf16)

        qr = t - LEAD - HOP * z

        @pl.when(live(qr, nY))
        def _():
            out_r, in_r, _, _ = y_line(qr)
            at_place(in_r, lambda copy: copy.wait_recv())

            @pl.loop(0, G)
            def _(b):
                @pl.when((b > z) & (z > 0))
                def _():
                    YRT[qr, b - 1] = (YR[qr, 0, b].astype(f32) + YRT[qr, b - 1].astype(f32)).astype(bf16)

            at_place(out_r, lambda copy: copy.start())

        qL = t - LEAD - HOP * (G - 1 - z)

        @pl.when(live(qL, nY))
        def _():
            _, _, out_l, in_l = y_line(qL)
            at_place(in_l, lambda copy: copy.wait_recv())

            @pl.loop(0, G)
            def _(b):
                @pl.when((b < z) & (z < G - 1))
                def _():
                    YLT[qL, b] = (YR[qL, 0, b].astype(f32) + YLT[qL, b].astype(f32)).astype(bf16)

            at_place(out_l, lambda copy: copy.start())

        pf = t - HOP * far

        @pl.when(live(pf, nZ))
        def _():
            mine = z_product(pf, z)
            from_left = ZRT[pf, jnp.maximum(z - 1, 0)].astype(f32)
            from_right = ZLT[pf, jnp.minimum(z, G - 2)].astype(f32)
            mine = mine + jnp.where(z > 0, from_left, 0.0) + jnp.where(z < G - 1, from_right, 0.0)
            ZX[pf, a] = mine.astype(bf16)
            for k in range(1, A):
                zx_copy(pf, k).start()

        pg = t - HOP * far - LEAD

        @pl.when(live(pg, nZ))
        def _():
            for k in range(1, A):
                remote(
                    ZX.at[pg, lax.rem(a + A - k, A)], ZX.at[pg, lax.rem(a + A - k, A)],
                    zx_s.at[pg, k - 1], zx_r.at[pg, k - 1], peer(k),
                ).wait_recv()
            total = ZX[pg, 0].astype(f32)
            for k in range(1, A):
                total += ZX[pg, k].astype(f32)
            for k in range(1, A):
                zx_copy(pg, k).wait_send()
            ZX[pg, a] = total.astype(bf16)
            own_z(pg).start()
            sib_z(pg).start()

        qf = t - LEAD - HOP * far

        @pl.when(live(qf, nY))
        def _():
            total = YR[qf, 0, z].astype(f32)
            from_left = YRT[qf, jnp.maximum(z - 1, 0)].astype(f32)
            from_right = YLT[qf, jnp.minimum(z, G - 2)].astype(f32)
            total = total + jnp.where(z > 0, from_left, 0.0) + jnp.where(z < G - 1, from_right, 0.0)
            YR[qf, 0, z] = total.astype(bf16)
            for k in range(1, A):
                ag_copy(qf, k).start()
            own_y(qf).start()
            sib_own(qf).start()

        qg = t - LEAD - HOP * far - LEAD

        @pl.when(live(qg, nY))
        def _():
            for k in range(1, A):
                here = y_out(qg, lax.rem(a + A - k, A), c)
                remote(here, here, ag_s.at[qg, k - 1], ag_r.at[qg, k - 1], peer(k)).wait_recv()
                sib_pass(qg, k).start()

        return carry

    steps = max(nY, nZ) + 2 * LEAD + HOP * (G - 1)
    lax.fori_loop(0, steps, step, 0)

    gain_core().wait_send()
    for k in range(1, A):
        gain_part(k).wait_send()

    @pl.when(z < G - 1)
    def _():
        gain_right().wait_send()

    @pl.when(z > 0)
    def _():
        gain_left().wait_send()

    for i in range(4):
        for side in (0, 1):
            cross[side, i].wait_send()

    def drain_y(q, carry):
        for k in range(1, A):
            @pl.when(q >= nY - YS_RING)
            def _():
                y_send(q, k).wait_send()

            ag_copy(q, k).wait_send()
            sib_pass(q, k).wait_send()
            there = y_out(q, lax.rem(a + A - k, A), 1 - c)
            remote(there, there, sib_s.at[q, k], sib_r.at[q, k], sib).wait_recv()
        out_r, _, out_l, _ = y_line(q)
        at_place(out_r, lambda copy: copy.wait_send())
        at_place(out_l, lambda copy: copy.wait_send())
        own_y(q).wait()
        sib_own(q).wait_send()
        there = y_out(q, a, 1 - c)
        remote(there, there, sib_s.at[q, 0], sib_r.at[q, 0], sib).wait_recv()
        return carry

    lax.fori_loop(0, nY, drain_y, 0)

    def drain_z(p, carry):
        out_r, _, out_l, _ = z_line(p)
        at_place(out_r, lambda copy: copy.wait_send())
        at_place(out_l, lambda copy: copy.wait_send())
        own_z(p).wait()
        sib_z(p).wait_send()
        there = z_out(p, 1 - c)
        remote(there, there, sib_s.at[nY + p, 0], sib_r.at[nY + p, 0], sib).wait_recv()
        return carry

    lax.fori_loop(0, nZ, drain_z, 0)


def summed_grads(groups, dp, at, ot, n2t, n1t, dz, dy, dg, dq, gain_parts):
    hidden, tokens = at.shape
    width, qkv_cols = ot.shape[0], dq.shape[1]
    plan = grad_plan(groups, dp, tokens, width, hidden, qkv_cols)
    G, A, nY, nZ = groups, plan["pairs"], plan["pieces"], plan["z_pieces"]
    block, zr, zc = plan["block"], plan["z_rows"], plan["z_cols"]
    bf16, DMA = jnp.bfloat16, pltpu.SemaphoreType.DMA
    any_space = pl.BlockSpec(memory_space=pl.ANY)
    in_vmem, f32, gain_shape = pl.BlockSpec(memory_space=pltpu.VMEM), jnp.float32, gain_parts.shape
    return pl.pallas_call(
        functools.partial(grad_kernel, plan),
        out_shape=(
            jax.ShapeDtypeStruct((block, 2 * hidden + qkv_cols), bf16),
            jax.ShapeDtypeStruct((plan["down_block"] + block, width), bf16),
            jax.ShapeDtypeStruct(gain_parts.shape, f32),
        ),
        in_specs=[any_space] * 8 + [in_vmem],
        out_specs=(any_space, any_space, in_vmem),
        scratch_shapes=[
            pltpu.VMEM((hidden + 3 * width, 2 * tokens), bf16),
            pltpu.VMEM((2 * tokens, width + hidden + qkv_cols // 2), bf16),
            pltpu.VMEM((YS_RING, A - 1, G, block, LANES), bf16),
            pltpu.VMEM((nY, A - 1, G, block, LANES), bf16),
            pltpu.VMEM((nY, G - 1, block, LANES), bf16),
            pltpu.VMEM((nY, G - 1, block, LANES), bf16),
            pltpu.VMEM((nZ, G - 1, zr, zc), bf16),
            pltpu.VMEM((nZ, G - 1, zr, zc), bf16),
            pltpu.VMEM((nZ, A, zr, zc), bf16),
            DMA((8,)), DMA((8,)), DMA((8,)),
            DMA((nY, A - 1)), DMA((nY, A - 1)),
            DMA((nY,)), DMA((nY,)), DMA((nY,)), DMA((nY,)),
            DMA((nZ,)), DMA((nZ,)), DMA((nZ,)), DMA((nZ,)),
            DMA((nZ, A - 1)), DMA((nZ, A - 1)),
            DMA((nY, A - 1)), DMA((nY, A - 1)),
            DMA((nY + nZ, A)), DMA((nY + nZ, A)),
            DMA((nY + nZ,)),
            pltpu.VMEM(gain_shape, f32),
            pltpu.VMEM((A,) + gain_shape, f32),
            pltpu.VMEM((3,) + gain_shape, f32),
            pltpu.VMEM(gain_shape, f32),
            pltpu.VMEM(gain_shape, f32),
            DMA((2,)), DMA((max(A - 1, 1),)), DMA((max(A - 1, 1),)), DMA((2,)), DMA((2,)),
        ],
        compiler_params=pltpu.CompilerParams(
            collective_id=3, has_side_effects=True, vmem_limit_bytes=63 * 1024 * 1024
        ),
        cost_estimate=pl.CostEstimate(
            flops=2 * 2 * tokens * (width * (2 * hidden + qkv_cols + width) + hidden * width) // 2,
            bytes_accessed=40_000_000, transcendentals=0,
        ),
    )(at, ot, n2t, n1t, dz, dy, dg, dq, gain_parts)


W_HOP = 2
gather_families = (
    (1, True, False),
    (2, True, True),
    (1, True, False),
    (8, True, False),
    (4, False, False),
)


def gather_kernel(groups, pairs, families, *refs):
    G, A, F = groups, pairs, len(families)
    shards, wholes = refs[:F], refs[F : 2 * F]
    sems = refs[2 * F :]
    s, z, d = lax.axis_index("section"), lax.axis_index("group"), lax.axis_index("dp")
    c, a = lax.rem(d, 2), lax.div(d, 2)
    sib = (s, z, 2 * a + 1 - c)
    right, left = (s, z + 1, d), (s, z - 1, d)

    def peer(part):
        return (s, z, 2 * part + c)

    barrier = pltpu.get_barrier_semaphore()
    others = [peer(lax.rem(a + k, A)) for k in range(1, A)]
    for dev in [sib, (s, lax.rem(z + 1, G), d), (s, lax.rem(z + G - 1, G), d)] + others:
        pl.semaphore_signal(barrier, inc=1, device_id=dev, device_id_type=MESH)
    pl.semaphore_wait(barrier, A + 2)

    def cut(f, ref, i):
        pieces, by_columns, _ = families[f]
        rows, cols = ref.shape
        if pieces == 1:
            return ref
        if by_columns:
            size = cols // pieces
            return ref.at[:, pl.ds(pl.multiple_of(i * size, 128), size)]
        size = rows // pieces
        return ref.at[pl.ds(pl.multiple_of(i * size, 16), size), :]

    def placed(f, i, o, part, core):
        return cut(f, wholes[f].at[(o * A + part) * 2 + core], i)

    def copy(f, i, o, part, kind, index, dev, own=False, core=None):
        core = c if core is None else core
        there = placed(f, i, o, part, core)
        src = cut(f, shards[f], i) if own else there
        send, recv = sems[f * 9 + 2 * kind], sems[f * 9 + 2 * kind + 1]
        return pltpu.make_async_remote_copy(
            src_ref=src, dst_ref=there, send_sem=send.at[index], recv_sem=recv.at[index], device_id=dev, device_id_type=MESH
        )

    def to_right(f, i, o, part, own=False):
        return copy(f, i, o, part, 0, (i, o, lax.rem(part + A - a, A)), right, own)

    def to_left(f, i, o, part, own=False):
        return copy(f, i, o, part, 1, (i, o, lax.rem(part + A - a, A)), left, own)

    def to_part(f, i, o, k, own=False):
        return copy(f, i, o, a, 2, (i, o, k - 1), peer(lax.rem(a + k, A)), own)

    def from_part(f, i, o, k):
        return copy(f, i, o, lax.rem(a + A - k, A), 2, (i, o, k - 1), peer(lax.rem(a + A - k, A)))

    def to_core(f, i, o, part, own=False):
        return copy(f, i, o, part, 3, (i, o, lax.rem(part + A - a, A)), sib, own)

    def from_core(f, i, o, k):
        part = lax.rem(a + k, A)
        return copy(f, i, o, part, 3, (i, o, k), sib, core=1 - c)

    def own_copy(f, i):
        return pltpu.make_async_copy(cut(f, shards[f], i), placed(f, i, z, a, c), sems[f * 9 + 8].at[i])

    def along(f, i, o, part, own, go_right, go_left):
        if go_right:
            @pl.when(z < G - 1)
            def _():
                to_right(f, i, o, part, own).start()
        if go_left:
            @pl.when(z > 0)
            def _():
                to_left(f, i, o, part, own).start()

    first = []
    total = 0
    for pieces, _, _ in families:
        first.append(total)
        total += pieces

    def step(t, carry):
        for f, (pieces, _, parts_first) in enumerate(families):
            i0 = t - first[f]

            @pl.when((i0 >= 0) & (i0 < pieces))
            def _(f=f, i0=i0):
                along(f, i0, z, a, True, True, True)
                for k in range(1, A):
                    to_part(f, i0, z, k, True).start()
                to_core(f, i0, z, a, True).start()
                own_copy(f, i0).start()

        for f, (pieces, _, parts_first) in enumerate(families):
            for h in range(G):
                for k in range(A if parts_first else 1):
                    if h == 0:
                        continue
                    i = t - first[f] - W_HOP * h - (W_HOP if k > 0 else 0)
                    part = lax.rem(a + k, A)
                    for sign in (-1, 1):
                        o = z + sign * h

                        @pl.when((i >= 0) & (i < pieces) & (o >= 0) & (o < G))
                        def _(f=f, i=i, o=o, part=part, sign=sign, parts_first=parts_first):
                            if sign < 0:
                                to_right(f, i, o, part).wait_recv()
                                along(f, i, o, part, False, True, False)
                            else:
                                to_left(f, i, o, part).wait_recv()
                                along(f, i, o, part, False, False, True)
                            if not parts_first:
                                for j in range(1, A):
                                    to_part(f, i, o, j).start()
                            to_core(f, i, o, part).start()

                if parts_first and h > 0:
                    continue
                i = t - first[f] - W_HOP * (h + 1)
                for sign in (-1, 1) if h else (1,):
                    o = z + sign * h

                    @pl.when((i >= 0) & (i < pieces) & (o >= 0) & (o < G))
                    def _(f=f, i=i, o=o, parts_first=parts_first):
                        for k in range(1, A):
                            from_part(f, i, o, k).wait_recv()
                            part = lax.rem(a + A - k, A)
                            if parts_first:
                                along(f, i, o, part, False, True, True)
                            to_core(f, i, o, part).start()
        return carry

    lax.fori_loop(0, total + W_HOP * (G + 1), step, 0)

    for f, (pieces, _, parts_first) in enumerate(families):
        def drain(i, carry, f=f, parts_first=parts_first):
            own_copy(f, i).wait()

            def by_group(o, carry):
                for k in range(A):
                    part = lax.rem(a + k, A)
                    to_core(f, i, o, part).wait_send()
                    from_core(f, i, o, k).wait_recv()
                    if parts_first or k == 0:
                        @pl.when((z < G - 1) & (o <= z))
                        def _(part=part):
                            to_right(f, i, o, part).wait_send()

                        @pl.when((z > 0) & (o >= z))
                        def _(part=part):
                            to_left(f, i, o, part).wait_send()
                for k in range(1, A):
                    if parts_first:
                        @pl.when(o == z)
                        def _(k=k):
                            to_part(f, i, o, k).wait_send()
                    else:
                        to_part(f, i, o, k).wait_send()
                return carry

            return lax.fori_loop(0, G, by_group, carry)

        lax.fori_loop(0, pieces, drain, 0)


def gathered(groups, dp, shards, families):
    A, DMA = dp // 2, pltpu.SemaphoreType.DMA
    any_space = pl.BlockSpec(memory_space=pl.ANY)
    scratch = []
    for pieces, _, parts_first in families:
        on_line = (pieces, groups, A if parts_first else 1)
        scratch += [DMA(on_line)] * 4 + [DMA((pieces, groups, max(A - 1, 1)))] * 2 + [DMA((pieces, groups, A))] * 2
        scratch += [DMA((pieces,))]
    return pl.pallas_call(
        functools.partial(gather_kernel, groups, A, families),
        out_shape=tuple(jax.ShapeDtypeStruct((groups * dp,) + x.shape, x.dtype) for x in shards),
        in_specs=[any_space] * len(shards),
        out_specs=(any_space,) * len(shards),
        scratch_shapes=scratch,
        compiler_params=pltpu.CompilerParams(collective_id=5, has_side_effects=True),
    )(*shards)


def body(
    inputs_x, cotangent, lengths, attn_gain, qkv_weight, out_weight, ffn_gain, gate_up, down_weight
):
    is_first = lax.axis_index("section") == 0
    gains = jnp.concatenate([attn_gain, ffn_gain], 0)
    gains = jnp.pad(gains, ((0, 14), (0, -gains.shape[1] % 128)))
    gains, qkv_all, out_all, gate_up_all, down_all = gathered(
        lax.axis_size("group"),
        lax.axis_size("dp"),
        (gains, qkv_weight[0], out_weight[0], gate_up[0], down_weight[0]),
        gather_families,
    )
    gain_part = attn_gain.shape[1]
    weights = (
        gains[:, 0, :gain_part].reshape(-1),
        flat(qkv_all),
        flat(out_all),
        gains[:, 1, :gain_part].reshape(-1),
        flat(gate_up_all),
        flat(down_all),
    )
    inputs_f = inputs_x.astype(jnp.float32)
    cotangent_f = cotangent.astype(jnp.float32)
    first_out, _ = forward_layer(weights, inputs_f, lengths)
    recv_act = passed_along(first_out.astype(jnp.bfloat16), "section", 1)
    layer_in = jnp.where(is_first, inputs_f, recv_act.astype(jnp.float32))
    result, kept_state = forward_layer(weights, layer_in, lengths)
    section_out = result.astype(jnp.bfloat16)[None]
    second_dx, _ = backward_layer(weights, kept_state, cotangent_f)
    recv_grad = passed_along(second_dx.astype(jnp.bfloat16), "section", -1)
    recv_grad, section_out = lax.optimization_barrier((recv_grad, section_out))
    grad_in = jnp.where(is_first, recv_grad.astype(jnp.float32), cotangent_f)
    grad_x, operands = backward_layer(weights, kept_state, grad_in)
    input_grads = jnp.where(
        is_first, grad_x, grad_x.astype(jnp.bfloat16).astype(jnp.float32)
    )[None]
    (_, _, normed_one, _, _, _, _, attention_result, _, _, normed_two, _, hidden, _) = kept_state
    attn_gain_part, ffn_gain_part, grad_low, grad_gated, gradient_after_lowered, grad_qkv = operands
    gain_parts = jnp.pad(jnp.stack([attn_gain_part, ffn_gain_part]), ((0, 6), (0, 0)))
    gate_qkv_sum, down_out_sum, gain_sums = summed_grads(
        lax.axis_size("group"),
        lax.axis_size("dp"),
        turned(hidden),
        turned(attention_result),
        turned(normed_two),
        turned(normed_one),
        flat(grad_low),
        flat(gradient_after_lowered),
        flat(grad_gated),
        flat(grad_qkv),
        gain_parts,
    )
    gain_cols = attn_gain.shape[1] * lax.axis_size("dp")
    gain_sums = lax.dynamic_slice_in_dim(
        gain_sums, lax.axis_index("group") * gain_cols, gain_cols, 1
    )
    gate_width = gate_up.shape[2]
    down_rows = down_weight.shape[1] * lax.axis_size("dp")
    reduced = (
        gain_sums[0],
        gate_qkv_sum[:, gate_width:].astype(jnp.float32),
        down_out_sum[down_rows:].astype(jnp.float32),
        gain_sums[1],
        gate_qkv_sum[:, :gate_width].astype(jnp.float32),
        down_out_sum[:down_rows].astype(jnp.float32),
    )
    return (section_out, input_grads) + tuple((shard_sum[None] for shard_sum in reduced))


def solution(mesh):
    placed = (
        P(("group", "dp"), None, None),
        P(("group", "dp"), None, None),
        P(("group", "dp")),
        P("section", ("group", "dp")),
        P("section", ("group", "dp"), None),
        P("section", ("group", "dp"), None),
        P("section", ("group", "dp")),
        P("section", ("group", "dp"), None),
        P("section", ("group", "dp"), None),
    )
    return jax.shard_map(
        body,
        mesh=mesh,
        in_specs=placed,
        out_specs=(
            P("section", ("group", "dp"), None, None),
            P("section", ("group", "dp"), None, None),
            P("section", "group"),
            P("section", "group", None),
            P("section", "group", None),
            P("section", "group"),
            P("section", "group", None),
            P("section", "group", None),
        ),
        check_vma=False,
    )
```

```python
import functools

import jax
import jax.numpy as jnp
from jax import lax
from jax.experimental import pallas as pl
from jax.experimental.pallas import tpu as pltpu
from jax.sharding import PartitionSpec as P

H = 16
KVH = 8
HD = 96
FF = 4096


norm_eps = 1e-05
rope_base = 100000.0
masked_score = -1e30
across = (((1,), (1,)), ((), ()))


def passed_along(value, axis, by):
    length = lax.axis_size(axis)
    pairs = [(i, i + by) for i in range(length) if 0 <= i + by < length]
    return lax.ppermute(value, axis, pairs)


def rope_tables(slot_count, head_width):
    half_width = head_width // 2
    frequency = rope_base ** (-(jnp.arange(half_width, dtype=jnp.float32) * 2.0 / head_width))
    angles = jnp.arange(slot_count, dtype=jnp.float32)[:, None] * frequency[None, :]
    return (jnp.cos(angles), jnp.sin(angles))


def rotate(vector, cosines, sine_table):
    half_width = vector.shape[-1] // 2
    front_half = vector[..., :half_width]
    back_half = vector[..., half_width:]
    cos_wide = cosines[:, None, :]
    sin_wide = sine_table[:, None, :]
    return jnp.concatenate(
        [
            front_half * cos_wide - back_half * sin_wide,
            back_half * cos_wide + front_half * sin_wide,
        ],
        -1,
    )


def norm_scale(vector):
    return lax.rsqrt(jnp.mean(vector * vector, -1, keepdims=True) + norm_eps)


def allowed_keys(lengths, slot_count):
    position = jnp.arange(slot_count, dtype=jnp.int32)
    causal = position[None, :] <= position[:, None]
    return causal[None] & (position[None, None, :] < lengths[:, None, None])


def padding(lengths, slot_count):
    position = jnp.arange(slot_count, dtype=jnp.int32)
    return (position[None, :] < lengths[:, None]).astype(jnp.float32)[..., None]


def norm_back(vector, scale, gain, grad_normed):
    scaled = grad_normed * gain.astype(jnp.float32)
    gain_grad = jnp.sum(grad_normed * vector * scale, axis=(0, 1))
    grad_vector = scale * scaled - vector * (scale * scale * scale) * jnp.mean(
        vector * scaled, -1, keepdims=True
    )
    return (gain_grad, grad_vector)


def score_block(query_heads, key_heads, lengths):
    slot_count = query_heads.shape[1]
    scores = jnp.einsum(
        "rqkgh,rpkh->rkgqp", query_heads, key_heads, preferred_element_type=jnp.float32
    ) * HD ** (-0.5)
    allowed = allowed_keys(lengths, slot_count)
    return jnp.where(allowed[:, None, None], scores, masked_score)


def attention_forward(weights, input_rows, lengths):
    gain_one, qkv_w, output_weight = weights[:3]
    row_count, slot_count, width = input_rows.shape
    groups = H // KVH
    cosines, sine_table = rope_tables(slot_count, HD)
    scale_one = norm_scale(input_rows)
    normed_one = (input_rows * scale_one * gain_one.astype(jnp.float32)).astype(jnp.bfloat16)
    qkv_all = jnp.einsum("rsd,de->rse", normed_one, qkv_w, preferred_element_type=jnp.float32)
    query_heads = rotate(
        qkv_all[..., : H * HD].reshape(row_count, slot_count, H, HD), cosines, sine_table
    )
    query_heads = query_heads.astype(jnp.bfloat16).reshape(row_count, slot_count, KVH, groups, HD)
    key_heads = rotate(
        qkv_all[..., H * HD : (H + KVH) * HD].reshape(row_count, slot_count, KVH, HD),
        cosines,
        sine_table,
    )
    key_heads = key_heads.astype(jnp.bfloat16)
    value_heads = (
        qkv_all[..., (H + KVH) * HD :].reshape(row_count, slot_count, KVH, HD).astype(jnp.bfloat16)
    )
    scores = score_block(query_heads, key_heads, lengths)
    row_max = jnp.max(scores, -1, keepdims=True)
    log_total = row_max + jnp.log(jnp.sum(jnp.exp(scores - row_max), -1, keepdims=True))
    prob_low = jnp.exp(scores - log_total).astype(jnp.bfloat16)
    attention_result = jnp.einsum(
        "rkgqp,rpkh->rqkgh", prob_low, value_heads, preferred_element_type=jnp.float32
    )
    attention_result = attention_result.astype(jnp.bfloat16).reshape(row_count, slot_count, H * HD)
    after_attention = input_rows + jnp.einsum(
        "vao,oj->vaj", attention_result, output_weight, preferred_element_type=jnp.float32
    )
    kept_state = (
        input_rows,
        scale_one,
        normed_one,
        query_heads,
        key_heads,
        value_heads,
        log_total,
        attention_result,
        lengths,
    )
    return (after_attention, kept_state)


def attention_backward(weights, kept_state, grad_after, gradient_after_lowered):
    gain_one, qkv_w, output_weight = weights[:3]
    (
        input_rows,
        scale_one,
        normed_one,
        query_heads,
        key_heads,
        value_heads,
        log_total,
        attention_result,
        lengths,
    ) = kept_state
    row_count, slot_count, width = input_rows.shape
    groups = H // KVH
    score_scale = HD ** (-0.5)
    cosines, sine_table = rope_tables(slot_count, HD)
    attention_gradient = jnp.einsum(
        "vol,el->voe", gradient_after_lowered, output_weight, preferred_element_type=jnp.float32
    )
    attention_gradient = attention_gradient.astype(jnp.bfloat16).reshape(
        row_count, slot_count, KVH, groups, HD
    )
    scores = score_block(query_heads, key_heads, lengths)
    prob_full = jnp.exp(scores - log_total)
    prob_low = prob_full.astype(jnp.bfloat16)
    grad_values = jnp.einsum(
        "rkgqp,rqkgh->rpkh", prob_low, attention_gradient, preferred_element_type=jnp.float32
    )
    grad_probs = jnp.einsum(
        "rqkgh,rpkh->rkgqp", attention_gradient, value_heads, preferred_element_type=jnp.float32
    )
    row_dot = jnp.sum(prob_full * grad_probs, -1, keepdims=True)
    grad_scores = (prob_full * (grad_probs - row_dot)).astype(jnp.bfloat16)
    grad_query = (
        jnp.einsum("rkgqp,rpkh->rqkgh", grad_scores, key_heads, preferred_element_type=jnp.float32)
        * score_scale
    )
    grad_query = rotate(grad_query.reshape(row_count, slot_count, H, HD), cosines, -sine_table)
    grad_keys = (
        jnp.einsum(
            "rkgqp,rqkgh->rpkh", grad_scores, query_heads, preferred_element_type=jnp.float32
        )
        * score_scale
    )
    grad_keys = rotate(grad_keys, cosines, -sine_table)
    grad_qkv = jnp.concatenate(
        [
            grad_query.reshape(row_count, slot_count, H * HD),
            grad_keys.reshape(row_count, slot_count, KVH * HD),
            grad_values.reshape(row_count, slot_count, KVH * HD),
        ],
        -1,
    ).astype(jnp.bfloat16)
    grad_normed_one = jnp.einsum("rse,de->rsd", grad_qkv, qkv_w, preferred_element_type=jnp.float32)
    attn_gain_part, grad_norm_one = norm_back(input_rows, scale_one, gain_one, grad_normed_one)
    return (grad_after + grad_norm_one, attn_gain_part, grad_qkv)


FF_CHUNK = 512
across = (((1,), (1,)), ((), ()))


def scaled_norm(value, gain):
    scale = lax.rsqrt(jnp.mean(value * value, -1, keepdims=True) + norm_eps)
    return scale, (value * scale * gain).astype(jnp.bfloat16)


def ffn_forward_kernel(y, gain, mask, wg, wu, wd, out, n2, acc):
    j = pl.program_id(0)

    @pl.when(j == 0)
    def _():
        n2[...] = scaled_norm(y[...], gain[...])[1]
        acc[...] = y[...]

    gate = jnp.dot(n2[...], wg[...], preferred_element_type=jnp.float32)
    up = jnp.dot(n2[...], wu[...], preferred_element_type=jnp.float32)
    hidden = (gate / (1.0 + jnp.exp(-gate)) * up).astype(jnp.bfloat16)
    acc[...] += jnp.dot(hidden, wd[...], preferred_element_type=jnp.float32)

    @pl.when(j == pl.num_programs(0) - 1)
    def _():
        out[...] = (acc[...] * mask[...]).astype(jnp.bfloat16)


def ffn_specs(tokens, width, hidden):
    steps = hidden // FF_CHUNK
    whole = pl.BlockSpec((tokens, width), lambda j: (0, 0))
    row = pl.BlockSpec((1, width), lambda j: (0, 0))
    weights = [
        pl.BlockSpec((width, FF_CHUNK), lambda j: (0, j)),
        pl.BlockSpec((width, FF_CHUNK), lambda j: (0, j + steps)),
        pl.BlockSpec((FF_CHUNK, width), lambda j: (j, 0)),
    ]
    return steps, whole, row, weights


def ffn_forward(y, gain, mask, gate_up_w, down_w):
    tokens, width = y.shape
    hidden = down_w.shape[0]
    steps, whole, row, weights = ffn_specs(tokens, width, hidden)
    return pl.pallas_call(
        ffn_forward_kernel,
        grid=(steps,),
        out_shape=jax.ShapeDtypeStruct((tokens, width), jnp.bfloat16),
        in_specs=[whole, row, pl.BlockSpec((tokens, 1), lambda j: (0, 0))] + weights,
        out_specs=whole,
        scratch_shapes=[pltpu.VMEM((tokens, width), jnp.bfloat16), pltpu.VMEM((tokens, width), jnp.float32)],
        compiler_params=pltpu.CompilerParams(vmem_limit_bytes=40 * 1024 * 1024),
        cost_estimate=pl.CostEstimate(
            flops=6 * tokens * width * hidden, bytes_accessed=6 * width * hidden, transcendentals=tokens * hidden
        ),
    )(y, gain, mask, gate_up_w, gate_up_w, down_w)


def ffn_backward_kernel(keep, y, dz, gain, mask, wg, wu, wd, dy, dyb, gain_grad, *rest):
    if keep:
        at, dgate, dup, n2t, out, n2, scale, acc, zacc = rest
    else:
        n2, scale, acc = rest
    j = pl.program_id(0)
    bf16, f32 = jnp.bfloat16, jnp.float32

    @pl.when(j == 0)
    def _():
        r, n = scaled_norm(y[...], gain[...])
        n2[...] = n
        scale[...] = r
        acc[...] = jnp.zeros_like(acc)
        if keep:
            n2t[...] = n.T
            zacc[...] = y[...]

    gate = jnp.dot(n2[...], wg[...], preferred_element_type=f32)
    up = jnp.dot(n2[...], wu[...], preferred_element_type=f32)
    grad = lax.dot_general(dz[...], wd[...], across, preferred_element_type=f32)
    sig = 1.0 / (1.0 + jnp.exp(-gate))
    silu = gate * sig
    grad_gate = (grad * up * sig * (1.0 + gate * (1.0 - sig))).astype(bf16)
    grad_up = (grad * silu).astype(bf16)
    if keep:
        hidden = (silu * up).astype(bf16)
        at[...] = hidden.T
        dgate[...] = grad_gate
        dup[...] = grad_up
        zacc[...] += jnp.dot(hidden, wd[...], preferred_element_type=f32)
    acc[...] += lax.dot_general(grad_gate, wg[...], across, preferred_element_type=f32) + lax.dot_general(
        grad_up, wu[...], across, preferred_element_type=f32
    )

    @pl.when(j == pl.num_programs(0) - 1)
    def _():
        value, r, grad_normed = y[...], scale[...], acc[...]
        scaled = grad_normed * gain[...]
        gain_grad[...] = jnp.sum(grad_normed * value * r, axis=0, keepdims=True)
        inner = jnp.mean(value * scaled, -1, keepdims=True)
        total = dz[...].astype(f32) + r * scaled - value * (r * r * r) * inner
        dy[...] = total
        dyb[...] = total.astype(bf16)
        if keep:
            out[...] = (zacc[...] * mask[...]).astype(bf16)


def ffn_backward(y, dz, gain, mask, gate_up_w, down_w, keep):
    tokens, width = y.shape
    hidden = down_w.shape[0]
    steps, whole, row, weights = ffn_specs(tokens, width, hidden)
    shape, bf16, f32 = jax.ShapeDtypeStruct, jnp.bfloat16, jnp.float32
    outs = [shape((tokens, width), f32), shape((tokens, width), bf16), shape((1, width), f32)]
    out_specs = [whole, whole, row]
    scratch = [pltpu.VMEM((tokens, width), bf16), pltpu.VMEM((tokens, 1), f32), pltpu.VMEM((tokens, width), f32)]
    if keep:
        part = pl.BlockSpec((tokens, FF_CHUNK), lambda j: (0, j))
        outs += [
            shape((hidden, tokens), bf16), shape((tokens, hidden), bf16), shape((tokens, hidden), bf16),
            shape((width, tokens), bf16), shape((tokens, width), bf16),
        ]
        out_specs += [
            pl.BlockSpec((FF_CHUNK, tokens), lambda j: (j, 0)), part, part,
            pl.BlockSpec((width, tokens), lambda j: (0, 0)), whole,
        ]
        scratch += [pltpu.VMEM((tokens, width), f32)]
    return pl.pallas_call(
        functools.partial(ffn_backward_kernel, keep),
        grid=(steps,),
        out_shape=tuple(outs),
        in_specs=[whole, whole, row, pl.BlockSpec((tokens, 1), lambda j: (0, 0))] + weights,
        out_specs=tuple(out_specs),
        scratch_shapes=scratch,
        compiler_params=pltpu.CompilerParams(vmem_limit_bytes=48 * 1024 * 1024),
        cost_estimate=pl.CostEstimate(
            flops=10 * tokens * width * hidden, bytes_accessed=6 * width * hidden, transcendentals=tokens * hidden
        ),
    )(y, dz, gain, mask, gate_up_w, gate_up_w, down_w)


def turned(array):
    return array.reshape(-1, array.shape[-1]).T


def flat(array):
    return array.reshape(-1, array.shape[-1])


MESH = pl.DeviceIdType.MESH
LANES = 128


def grad_plan(groups, dp, tokens, width, hidden, qkv_cols):
    pairs = dp // 2
    block = width // groups
    down_block = hidden // groups
    gate_cols = 2 * hidden // 2 // pairs
    qkv_part = qkv_cols // 2 // pairs
    pieces_gate = gate_cols // LANES
    pieces_qkv = qkv_part // LANES
    pieces = pieces_gate + pieces_qkv
    z_rows = LANES
    while down_block % z_rows or block % z_rows:
        z_rows //= 2
    row_chunks = (down_block + block) // z_rows
    half = width // 2
    z_split = max(1, pieces // row_chunks)
    while half % (z_split * LANES):
        z_split -= 1
    return dict(
        groups=groups, pairs=pairs, tokens=tokens, width=width, hidden=hidden, qkv_cols=qkv_cols, block=block,
        down_block=down_block, gate_cols=gate_cols, qkv_part=qkv_part, pieces_gate=pieces_gate, pieces=pieces,
        z_rows=z_rows, z_split=z_split, z_cols=half // z_split, z_pieces=row_chunks * z_split,
        down_chunks=down_block // z_rows, half=half,
    )


YS_RING = 4
HOP = 2
LEAD = 2


def grad_kernel(
    plan, at, ot, n2t, n1t, dz, dy, dgate, dup, dq, gp, outy, outz, outg,
    LT, RH, YS, YR, YRT, YLT, ZRT, ZLT, ZX,
    own_sem, xs, xr, ys_s, ys_r, yr_s, yr_r, yl_s, yl_r, zr_s, zr_r, zl_s, zl_r,
    zx_s, zx_r, ag_s, ag_r, sib_s, sib_r, lo,
    GC, GA, GS, GR, GL, gc_sem, ga_s, ga_r, gr_sem, gl_sem,
):
    G, A, T = plan["groups"], plan["pairs"], plan["tokens"]
    width, hidden, half = plan["width"], plan["hidden"], plan["half"]
    block, nY, nZ = plan["block"], plan["pieces"], plan["z_pieces"]
    zr, zc = plan["z_rows"], plan["z_cols"]
    s, z, d = lax.axis_index("section"), lax.axis_index("group"), lax.axis_index("dp")
    c, a = lax.rem(d, 2), lax.div(d, 2)
    sib = (s, z, 2 * a + 1 - c)
    right, left = (s, z + 1, d), (s, z - 1, d)

    def peer(k):
        return (s, z, 2 * lax.rem(a + k, A) + c)

    def remote(src, dst, ss, rs, dev):
        return pltpu.make_async_remote_copy(
            src_ref=src, dst_ref=dst, send_sem=ss, recv_sem=rs, device_id=dev, device_id_type=MESH
        )

    barrier = pltpu.get_barrier_semaphore()
    for dev in [sib, (s, lax.rem(z + 1, G), d), (s, lax.rem(z + G - 1, G), d)] + [peer(k) for k in range(1, A)]:
        pl.semaphore_signal(barrier, inc=1, device_id=dev, device_id_type=MESH)
    pl.semaphore_wait(barrier, A + 2)

    lhs = [(at, 0, hidden), (ot, hidden, width), (n2t, hidden + width, width), (n1t, hidden + 2 * width, width)]
    rhs = [(dz, 0, half), (dy, half, half), (None, width, hidden), (dq, width + hidden, plan["qkv_cols"] // 2)]
    order = [(0, 0), (2, 2), (1, 1), (3, 3)]
    own, cross = {}, {}
    for i, (ref, row, rows) in enumerate(lhs):
        own[0, i] = pltpu.make_async_copy(ref, LT.at[pl.ds(row, rows), pl.ds(0, T)], own_sem.at[i])
        cross[0, i] = remote(ref, LT.at[pl.ds(row, rows), pl.ds(T, T)], xs.at[i], xr.at[i], sib)
    for i, (ref, col, cols) in enumerate(rhs):
        if ref is None:
            continue
        mine = pl.ds(pl.multiple_of(c * cols, LANES), cols)
        theirs = pl.ds(pl.multiple_of((1 - c) * cols, LANES), cols)
        own[1, i] = pltpu.make_async_copy(ref.at[:, mine], RH.at[pl.ds(0, T), pl.ds(col, cols)], own_sem.at[4 + i])
        cross[1, i] = remote(ref.at[:, theirs], RH.at[pl.ds(T, T), pl.ds(col, cols)], xs.at[4 + i], xr.at[4 + i], sib)
    col, cols = rhs[2][1:]
    for core, (mine, theirs) in enumerate(((dgate, dup), (dup, dgate))):
        own[1, 2, core] = pltpu.make_async_copy(mine, RH.at[pl.ds(0, T), pl.ds(col, cols)], own_sem.at[6])
        cross[1, 2, core] = remote(theirs, RH.at[pl.ds(T, T), pl.ds(col, cols)], xs.at[6], xr.at[6], sib)
    own[1, 2], cross[1, 2] = own[1, 2, 0], cross[1, 2, 0]
    for i, _ in order:
        for side in (0, 1):
            if (side, i) == (1, 2):
                for core in (0, 1):
                    @pl.when(c == core)
                    def _(core=core):
                        own[1, 2, core].start()
                        cross[1, 2, core].start()
            else:
                own[side, i].start()
                cross[side, i].start()

    def operands_here(i):
        for side in (0, 1):
            own[side, i].wait()
            cross[side, i].wait_recv()

    def product(row, rows, col, cols):
        return jnp.dot(
            LT[pl.ds(row, rows), :], RH[:, pl.ds(col, cols)], preferred_element_type=jnp.float32
        )

    def y_product(q, which, b):
        is_gate = q < plan["pieces_gate"]
        row = jnp.where(is_gate, hidden + width, hidden + 2 * width) + b * block
        col = jnp.where(
            is_gate,
            width + which * plan["gate_cols"] + q * LANES,
            width + hidden + which * plan["qkv_part"] + (q - plan["pieces_gate"]) * LANES,
        )
        return product(pl.multiple_of(row, 16), block, pl.multiple_of(col, LANES), LANES)

    def z_product(p, b):
        r, h = lax.div(p, plan["z_split"]), lax.rem(p, plan["z_split"])
        is_down = r < plan["down_chunks"]
        row = jnp.where(
            is_down, b * plan["down_block"] + r * zr, hidden + b * block + (r - plan["down_chunks"]) * zr
        )
        col = jnp.where(is_down, 0, half) + h * zc
        return product(pl.multiple_of(row, 16), zr, pl.multiple_of(col, LANES), zc)

    def y_out(q, part, core):
        is_gate = q < plan["pieces_gate"]
        col = jnp.where(
            is_gate,
            core * hidden + part * plan["gate_cols"] + q * LANES,
            2 * hidden + core * (plan["qkv_cols"] // 2) + part * plan["qkv_part"] + (q - plan["pieces_gate"]) * LANES,
        )
        return outy.at[:, pl.ds(pl.multiple_of(col, LANES), LANES)]

    def z_out(p, core):
        r, h = lax.div(p, plan["z_split"]), lax.rem(p, plan["z_split"])
        return outz.at[
            pl.ds(pl.multiple_of(r * zr, 16), zr), pl.ds(pl.multiple_of(core * half + h * zc, LANES), zc)
        ]

    def y_send(q, k):
        return remote(YS.at[lax.rem(q, YS_RING), k - 1], YR.at[q, k - 1], ys_s.at[q, k - 1], ys_r.at[q, k - 1], peer(k))

    def line_copies(slots_r, slots_l, r_s, r_r, l_s, l_r, first_r, first_l, p):
        out_r, in_r, out_l, in_l = [], [], [], []
        for k in range(G):
            if k < G - 1:
                src = first_r(p) if k == 0 else slots_r.at[p, pl.ds(k, G - 1 - k)]
                out_r.append((k, remote(src, slots_r.at[p, pl.ds(k, G - 1 - k)], r_s.at[p], r_r.at[p], right)))
                held = slots_l.at[p, pl.ds(0, k + 1)]
                in_l.append((k, remote(held, held, l_s.at[p], l_r.at[p], left)))
            if k > 0:
                src = first_l(p) if k == G - 1 else slots_l.at[p, pl.ds(0, k)]
                out_l.append((k, remote(src, slots_l.at[p, pl.ds(0, k)], l_s.at[p], l_r.at[p], left)))
                held = slots_r.at[p, pl.ds(k - 1, G - k)]
                in_r.append((k, remote(held, held, r_s.at[p], r_r.at[p], right)))
        return out_r, in_r, out_l, in_l

    def at_place(copies, act):
        for k, copy in copies:
            @pl.when(z == k)
            def _(copy=copy):
                act(copy)

    def y_line(q):
        return line_copies(
            YRT, YLT, yr_s, yr_r, yl_s, yl_r,
            lambda q: YR.at[q, 0, pl.ds(1, G - 1)], lambda q: YR.at[q, 0, pl.ds(0, G - 1)], q,
        )

    def z_line(p):
        return line_copies(
            ZRT, ZLT, zr_s, zr_r, zl_s, zl_r,
            lambda p: ZRT.at[p, pl.ds(0, G - 1)], lambda p: ZLT.at[p, pl.ds(0, G - 1)], p,
        )

    def zx_copy(p, k):
        return remote(ZX.at[p, a], ZX.at[p, a], zx_s.at[p, k - 1], zx_r.at[p, k - 1], peer(k))

    def ag_copy(q, k):
        return remote(YR.at[q, 0, z], y_out(q, a, c), ag_s.at[q, k - 1], ag_r.at[q, k - 1], peer(k))

    def sib_own(q):
        return remote(YR.at[q, 0, z], y_out(q, a, c), sib_s.at[q, 0], sib_r.at[q, 0], sib)

    def sib_pass(q, k):
        part = lax.rem(a + A - k, A)
        return remote(y_out(q, part, c), y_out(q, part, c), sib_s.at[q, k], sib_r.at[q, k], sib)

    def own_y(q):
        return pltpu.make_async_copy(YR.at[q, 0, z], y_out(q, a, c), lo.at[q])

    def own_z(p):
        return pltpu.make_async_copy(ZX.at[p, a], z_out(p, c), lo.at[nY + p])

    def sib_z(p):
        return remote(ZX.at[p, a], z_out(p, c), sib_s.at[nY + p, 0], sib_r.at[nY + p, 0], sib)

    f32, bf16 = jnp.float32, jnp.bfloat16
    far = jnp.maximum(z, G - 1 - z)

    def live(index, count):
        return (index >= 0) & (index < count)

    def gain_core():
        return remote(gp, GC, gc_sem.at[0], gc_sem.at[1], sib)

    def gain_part(k):
        return remote(GA.at[a], GA.at[a], ga_s.at[k - 1], ga_r.at[k - 1], peer(k))

    def gain_right():
        return remote(GS.at[1], GR, gr_sem.at[0], gr_sem.at[1], right)

    def gain_left():
        return remote(GS.at[2], GL, gl_sem.at[0], gl_sem.at[1], left)

    def gain_step(t):
        @pl.when(t == 0)
        def _():
            gain_core().start()

        @pl.when(t == 1)
        def _():
            gain_core().wait_recv()
            GA[a] = gp[...] + GC[...]
            for k in range(1, A):
                gain_part(k).start()

        @pl.when(t == 2)
        def _():
            for k in range(1, A):
                remote(
                    GA.at[lax.rem(a + A - k, A)], GA.at[lax.rem(a + A - k, A)], ga_s.at[k - 1], ga_r.at[k - 1], peer(k)
                ).wait_recv()
            total = GA[0]
            for k in range(1, A):
                total += GA[k]
            GS[0] = total

        @pl.when(t == 2 + HOP * z)
        def _():
            @pl.when(z > 0)
            def _():
                gain_right().wait_recv()
                GS[1] = GS[0] + GR[...]

            @pl.when(z == 0)
            def _():
                GS[1] = GS[0]

            @pl.when(z < G - 1)
            def _():
                gain_right().start()

        @pl.when(t == 2 + HOP * (G - 1 - z))
        def _():
            @pl.when(z < G - 1)
            def _():
                gain_left().wait_recv()
                GS[2] = GS[0] + GL[...]

            @pl.when(z == G - 1)
            def _():
                GS[2] = GS[0]

            @pl.when(z > 0)
            def _():
                gain_left().start()

        @pl.when(t == 3 + HOP * (G - 1))
        def _():
            outg[...] = GS[1] + jnp.where(z < G - 1, GL[...], 0.0)

    def step(t, carry):
        gain_step(t)

        @pl.when(t == 0)
        def _():
            operands_here(0)
            operands_here(2)

        @pl.when(t == 1)
        def _():
            operands_here(1)
            operands_here(3)

        q1 = t

        @pl.when(live(q1, nY))
        def _():
            for k in range(1, A):
                @pl.when(q1 >= YS_RING)
                def _():
                    y_send(q1 - YS_RING, k).wait_send()

                @pl.loop(0, G)
                def _(b):
                    YS[lax.rem(q1, YS_RING), k - 1, b] = y_product(q1, lax.rem(a + k, A), b).astype(bf16)

                y_send(q1, k).start()

        pr = t - HOP * z

        @pl.when(live(pr, nZ))
        def _():
            out_r, in_r, _, _ = z_line(pr)
            at_place(in_r, lambda copy: copy.wait_recv())

            @pl.loop(0, G)
            def _(b):
                @pl.when((b > z) & (z > 0))
                def _():
                    ZRT[pr, b - 1] = (z_product(pr, b) + ZRT[pr, b - 1].astype(f32)).astype(bf16)

                @pl.when((b > z) & (z == 0))
                def _():
                    ZRT[pr, b - 1] = z_product(pr, b).astype(bf16)

            at_place(out_r, lambda copy: copy.start())

        pL = t - HOP * (G - 1 - z)

        @pl.when(live(pL, nZ))
        def _():
            _, _, out_l, in_l = z_line(pL)
            at_place(in_l, lambda copy: copy.wait_recv())

            @pl.loop(0, G)
            def _(b):
                @pl.when((b < z) & (z < G - 1))
                def _():
                    ZLT[pL, b] = (z_product(pL, b) + ZLT[pL, b].astype(f32)).astype(bf16)

                @pl.when((b < z) & (z == G - 1))
                def _():
                    ZLT[pL, b] = z_product(pL, b).astype(bf16)

            at_place(out_l, lambda copy: copy.start())

        q2 = t - LEAD

        @pl.when(live(q2, nY))
        def _():
            for k in range(1, A):
                y_send(q2, k).wait_recv()

            @pl.loop(0, G)
            def _(b):
                total = y_product(q2, a, b)
                for k in range(1, A):
                    total += YR[q2, k - 1, b].astype(f32)
                YR[q2, 0, b] = total.astype(bf16)

        qr = t - LEAD - HOP * z

        @pl.when(live(qr, nY))
        def _():
            out_r, in_r, _, _ = y_line(qr)
            at_place(in_r, lambda copy: copy.wait_recv())

            @pl.loop(0, G)
            def _(b):
                @pl.when((b > z) & (z > 0))
                def _():
                    YRT[qr, b - 1] = (YR[qr, 0, b].astype(f32) + YRT[qr, b - 1].astype(f32)).astype(bf16)

            at_place(out_r, lambda copy: copy.start())

        qL = t - LEAD - HOP * (G - 1 - z)

        @pl.when(live(qL, nY))
        def _():
            _, _, out_l, in_l = y_line(qL)
            at_place(in_l, lambda copy: copy.wait_recv())

            @pl.loop(0, G)
            def _(b):
                @pl.when((b < z) & (z < G - 1))
                def _():
                    YLT[qL, b] = (YR[qL, 0, b].astype(f32) + YLT[qL, b].astype(f32)).astype(bf16)

            at_place(out_l, lambda copy: copy.start())

        pf = t - HOP * far

        @pl.when(live(pf, nZ))
        def _():
            mine = z_product(pf, z)
            from_left = ZRT[pf, jnp.maximum(z - 1, 0)].astype(f32)
            from_right = ZLT[pf, jnp.minimum(z, G - 2)].astype(f32)
            mine = mine + jnp.where(z > 0, from_left, 0.0) + jnp.where(z < G - 1, from_right, 0.0)
            ZX[pf, a] = mine.astype(bf16)
            for k in range(1, A):
                zx_copy(pf, k).start()

        pg = t - HOP * far - LEAD

        @pl.when(live(pg, nZ))
        def _():
            for k in range(1, A):
                remote(
                    ZX.at[pg, lax.rem(a + A - k, A)], ZX.at[pg, lax.rem(a + A - k, A)],
                    zx_s.at[pg, k - 1], zx_r.at[pg, k - 1], peer(k),
                ).wait_recv()
            total = ZX[pg, 0].astype(f32)
            for k in range(1, A):
                total += ZX[pg, k].astype(f32)
            for k in range(1, A):
                zx_copy(pg, k).wait_send()
            ZX[pg, a] = total.astype(bf16)
            own_z(pg).start()
            sib_z(pg).start()

        qf = t - LEAD - HOP * far

        @pl.when(live(qf, nY))
        def _():
            total = YR[qf, 0, z].astype(f32)
            from_left = YRT[qf, jnp.maximum(z - 1, 0)].astype(f32)
            from_right = YLT[qf, jnp.minimum(z, G - 2)].astype(f32)
            total = total + jnp.where(z > 0, from_left, 0.0) + jnp.where(z < G - 1, from_right, 0.0)
            YR[qf, 0, z] = total.astype(bf16)
            for k in range(1, A):
                ag_copy(qf, k).start()
            own_y(qf).start()
            sib_own(qf).start()

        qg = t - LEAD - HOP * far - LEAD

        @pl.when(live(qg, nY))
        def _():
            for k in range(1, A):
                here = y_out(qg, lax.rem(a + A - k, A), c)
                remote(here, here, ag_s.at[qg, k - 1], ag_r.at[qg, k - 1], peer(k)).wait_recv()
                sib_pass(qg, k).start()

        return carry

    steps = max(nY, nZ) + 2 * LEAD + HOP * (G - 1)
    lax.fori_loop(0, steps, step, 0)

    gain_core().wait_send()
    for k in range(1, A):
        gain_part(k).wait_send()

    @pl.when(z < G - 1)
    def _():
        gain_right().wait_send()

    @pl.when(z > 0)
    def _():
        gain_left().wait_send()

    for i in range(4):
        for side in (0, 1):
            cross[side, i].wait_send()

    def drain_y(q, carry):
        for k in range(1, A):
            @pl.when(q >= nY - YS_RING)
            def _():
                y_send(q, k).wait_send()

            ag_copy(q, k).wait_send()
            sib_pass(q, k).wait_send()
            there = y_out(q, lax.rem(a + A - k, A), 1 - c)
            remote(there, there, sib_s.at[q, k], sib_r.at[q, k], sib).wait_recv()
        out_r, _, out_l, _ = y_line(q)
        at_place(out_r, lambda copy: copy.wait_send())
        at_place(out_l, lambda copy: copy.wait_send())
        own_y(q).wait()
        sib_own(q).wait_send()
        there = y_out(q, a, 1 - c)
        remote(there, there, sib_s.at[q, 0], sib_r.at[q, 0], sib).wait_recv()
        return carry

    lax.fori_loop(0, nY, drain_y, 0)

    def drain_z(p, carry):
        out_r, _, out_l, _ = z_line(p)
        at_place(out_r, lambda copy: copy.wait_send())
        at_place(out_l, lambda copy: copy.wait_send())
        own_z(p).wait()
        sib_z(p).wait_send()
        there = z_out(p, 1 - c)
        remote(there, there, sib_s.at[nY + p, 0], sib_r.at[nY + p, 0], sib).wait_recv()
        return carry

    lax.fori_loop(0, nZ, drain_z, 0)


def summed_grads(groups, dp, at, ot, n2t, n1t, dz, dy, dgate, dup, dq, gain_parts):
    hidden, tokens = at.shape
    width, qkv_cols = ot.shape[0], dq.shape[1]
    plan = grad_plan(groups, dp, tokens, width, hidden, qkv_cols)
    G, A, nY, nZ = groups, plan["pairs"], plan["pieces"], plan["z_pieces"]
    block, zr, zc = plan["block"], plan["z_rows"], plan["z_cols"]
    bf16, DMA = jnp.bfloat16, pltpu.SemaphoreType.DMA
    any_space = pl.BlockSpec(memory_space=pl.ANY)
    in_vmem, f32, gain_shape = pl.BlockSpec(memory_space=pltpu.VMEM), jnp.float32, gain_parts.shape
    return pl.pallas_call(
        functools.partial(grad_kernel, plan),
        out_shape=(
            jax.ShapeDtypeStruct((block, 2 * hidden + qkv_cols), bf16),
            jax.ShapeDtypeStruct((plan["down_block"] + block, width), bf16),
            jax.ShapeDtypeStruct(gain_parts.shape, f32),
        ),
        in_specs=[any_space] * 9 + [in_vmem],
        out_specs=(any_space, any_space, in_vmem),
        scratch_shapes=[
            pltpu.VMEM((hidden + 3 * width, 2 * tokens), bf16),
            pltpu.VMEM((2 * tokens, width + hidden + qkv_cols // 2), bf16),
            pltpu.VMEM((YS_RING, A - 1, G, block, LANES), bf16),
            pltpu.VMEM((nY, A - 1, G, block, LANES), bf16),
            pltpu.VMEM((nY, G - 1, block, LANES), bf16),
            pltpu.VMEM((nY, G - 1, block, LANES), bf16),
            pltpu.VMEM((nZ, G - 1, zr, zc), bf16),
            pltpu.VMEM((nZ, G - 1, zr, zc), bf16),
            pltpu.VMEM((nZ, A, zr, zc), bf16),
            DMA((8,)), DMA((8,)), DMA((8,)),
            DMA((nY, A - 1)), DMA((nY, A - 1)),
            DMA((nY,)), DMA((nY,)), DMA((nY,)), DMA((nY,)),
            DMA((nZ,)), DMA((nZ,)), DMA((nZ,)), DMA((nZ,)),
            DMA((nZ, A - 1)), DMA((nZ, A - 1)),
            DMA((nY, A - 1)), DMA((nY, A - 1)),
            DMA((nY + nZ, A)), DMA((nY + nZ, A)),
            DMA((nY + nZ,)),
            pltpu.VMEM(gain_shape, f32),
            pltpu.VMEM((A,) + gain_shape, f32),
            pltpu.VMEM((3,) + gain_shape, f32),
            pltpu.VMEM(gain_shape, f32),
            pltpu.VMEM(gain_shape, f32),
            DMA((2,)), DMA((max(A - 1, 1),)), DMA((max(A - 1, 1),)), DMA((2,)), DMA((2,)),
        ],
        compiler_params=pltpu.CompilerParams(
            collective_id=3, has_side_effects=True, vmem_limit_bytes=63 * 1024 * 1024
        ),
        cost_estimate=pl.CostEstimate(
            flops=2 * 2 * tokens * (width * (2 * hidden + qkv_cols + width) + hidden * width) // 2,
            bytes_accessed=40_000_000, transcendentals=0,
        ),
    )(at, ot, n2t, n1t, dz, dy, dgate, dup, dq, gain_parts)


W_HOP = 2
gather_families = (
    (1, True, False),
    (2, True, True),
    (1, True, False),
    (8, True, False),
    (4, False, False),
)


def gather_kernel(groups, pairs, families, *refs):
    G, A, F = groups, pairs, len(families)
    shards, wholes = refs[:F], refs[F : 2 * F]
    sems = refs[2 * F :]
    s, z, d = lax.axis_index("section"), lax.axis_index("group"), lax.axis_index("dp")
    c, a = lax.rem(d, 2), lax.div(d, 2)
    sib = (s, z, 2 * a + 1 - c)
    right, left = (s, z + 1, d), (s, z - 1, d)

    def peer(part):
        return (s, z, 2 * part + c)

    barrier = pltpu.get_barrier_semaphore()
    others = [peer(lax.rem(a + k, A)) for k in range(1, A)]
    for dev in [sib, (s, lax.rem(z + 1, G), d), (s, lax.rem(z + G - 1, G), d)] + others:
        pl.semaphore_signal(barrier, inc=1, device_id=dev, device_id_type=MESH)
    pl.semaphore_wait(barrier, A + 2)

    def cut(f, ref, i):
        pieces, by_columns, _ = families[f]
        rows, cols = ref.shape
        if pieces == 1:
            return ref
        if by_columns:
            size = cols // pieces
            return ref.at[:, pl.ds(pl.multiple_of(i * size, 128), size)]
        size = rows // pieces
        return ref.at[pl.ds(pl.multiple_of(i * size, 16), size), :]

    def placed(f, i, o, part, core):
        return cut(f, wholes[f].at[(o * A + part) * 2 + core], i)

    def copy(f, i, o, part, kind, index, dev, own=False, core=None):
        core = c if core is None else core
        there = placed(f, i, o, part, core)
        src = cut(f, shards[f], i) if own else there
        send, recv = sems[f * 9 + 2 * kind], sems[f * 9 + 2 * kind + 1]
        return pltpu.make_async_remote_copy(
            src_ref=src, dst_ref=there, send_sem=send.at[index], recv_sem=recv.at[index], device_id=dev, device_id_type=MESH
        )

    def to_right(f, i, o, part, own=False):
        return copy(f, i, o, part, 0, (i, o, lax.rem(part + A - a, A)), right, own)

    def to_left(f, i, o, part, own=False):
        return copy(f, i, o, part, 1, (i, o, lax.rem(part + A - a, A)), left, own)

    def to_part(f, i, o, k, own=False):
        return copy(f, i, o, a, 2, (i, o, k - 1), peer(lax.rem(a + k, A)), own)

    def from_part(f, i, o, k):
        return copy(f, i, o, lax.rem(a + A - k, A), 2, (i, o, k - 1), peer(lax.rem(a + A - k, A)))

    def to_core(f, i, o, part, own=False):
        return copy(f, i, o, part, 3, (i, o, lax.rem(part + A - a, A)), sib, own)

    def from_core(f, i, o, k):
        part = lax.rem(a + k, A)
        return copy(f, i, o, part, 3, (i, o, k), sib, core=1 - c)

    def own_copy(f, i):
        return pltpu.make_async_copy(cut(f, shards[f], i), placed(f, i, z, a, c), sems[f * 9 + 8].at[i])

    def along(f, i, o, part, own, go_right, go_left):
        if go_right:
            @pl.when(z < G - 1)
            def _():
                to_right(f, i, o, part, own).start()
        if go_left:
            @pl.when(z > 0)
            def _():
                to_left(f, i, o, part, own).start()

    first = []
    total = 0
    for pieces, _, _ in families:
        first.append(total)
        total += pieces

    def step(t, carry):
        for f, (pieces, _, parts_first) in enumerate(families):
            i0 = t - first[f]

            @pl.when((i0 >= 0) & (i0 < pieces))
            def _(f=f, i0=i0):
                along(f, i0, z, a, True, True, True)
                for k in range(1, A):
                    to_part(f, i0, z, k, True).start()
                to_core(f, i0, z, a, True).start()
                own_copy(f, i0).start()

        for f, (pieces, _, parts_first) in enumerate(families):
            for h in range(G):
                for k in range(A if parts_first else 1):
                    if h == 0:
                        continue
                    i = t - first[f] - W_HOP * h - (W_HOP if k > 0 else 0)
                    part = lax.rem(a + k, A)
                    for sign in (-1, 1):
                        o = z + sign * h

                        @pl.when((i >= 0) & (i < pieces) & (o >= 0) & (o < G))
                        def _(f=f, i=i, o=o, part=part, sign=sign, parts_first=parts_first):
                            if sign < 0:
                                to_right(f, i, o, part).wait_recv()
                                along(f, i, o, part, False, True, False)
                            else:
                                to_left(f, i, o, part).wait_recv()
                                along(f, i, o, part, False, False, True)
                            if not parts_first:
                                for j in range(1, A):
                                    to_part(f, i, o, j).start()
                            to_core(f, i, o, part).start()

                if parts_first and h > 0:
                    continue
                i = t - first[f] - W_HOP * (h + 1)
                for sign in (-1, 1) if h else (1,):
                    o = z + sign * h

                    @pl.when((i >= 0) & (i < pieces) & (o >= 0) & (o < G))
                    def _(f=f, i=i, o=o, parts_first=parts_first):
                        for k in range(1, A):
                            from_part(f, i, o, k).wait_recv()
                            part = lax.rem(a + A - k, A)
                            if parts_first:
                                along(f, i, o, part, False, True, True)
                            to_core(f, i, o, part).start()
        return carry

    lax.fori_loop(0, total + W_HOP * (G + 1), step, 0)

    for f, (pieces, _, parts_first) in enumerate(families):
        def drain(i, carry, f=f, parts_first=parts_first):
            own_copy(f, i).wait()

            def by_group(o, carry):
                for k in range(A):
                    part = lax.rem(a + k, A)
                    to_core(f, i, o, part).wait_send()
                    from_core(f, i, o, k).wait_recv()
                    if parts_first or k == 0:
                        @pl.when((z < G - 1) & (o <= z))
                        def _(part=part):
                            to_right(f, i, o, part).wait_send()

                        @pl.when((z > 0) & (o >= z))
                        def _(part=part):
                            to_left(f, i, o, part).wait_send()
                for k in range(1, A):
                    if parts_first:
                        @pl.when(o == z)
                        def _(k=k):
                            to_part(f, i, o, k).wait_send()
                    else:
                        to_part(f, i, o, k).wait_send()
                return carry

            return lax.fori_loop(0, G, by_group, carry)

        lax.fori_loop(0, pieces, drain, 0)


def gathered(groups, dp, shards, families):
    A, DMA = dp // 2, pltpu.SemaphoreType.DMA
    any_space = pl.BlockSpec(memory_space=pl.ANY)
    scratch = []
    for pieces, _, parts_first in families:
        on_line = (pieces, groups, A if parts_first else 1)
        scratch += [DMA(on_line)] * 4 + [DMA((pieces, groups, max(A - 1, 1)))] * 2 + [DMA((pieces, groups, A))] * 2
        scratch += [DMA((pieces,))]
    return pl.pallas_call(
        functools.partial(gather_kernel, groups, A, families),
        out_shape=tuple(jax.ShapeDtypeStruct((groups * dp,) + x.shape, x.dtype) for x in shards),
        in_specs=[any_space] * len(shards),
        out_specs=(any_space,) * len(shards),
        scratch_shapes=scratch,
        compiler_params=pltpu.CompilerParams(collective_id=5, has_side_effects=True),
    )(*shards)


def body(
    inputs_x, cotangent, lengths, attn_gain, qkv_weight, out_weight, ffn_gain, gate_up, down_weight
):
    is_first = lax.axis_index("section") == 0
    gains = jnp.concatenate([attn_gain, ffn_gain], 0)
    gains = jnp.pad(gains, ((0, 14), (0, -gains.shape[1] % 128)))
    gains, qkv_all, out_all, gate_up_all, down_all = gathered(
        lax.axis_size("group"),
        lax.axis_size("dp"),
        (gains, qkv_weight[0], out_weight[0], gate_up[0], down_weight[0]),
        gather_families,
    )
    gain_part = attn_gain.shape[1]
    weights = (
        gains[:, 0, :gain_part].reshape(-1),
        flat(qkv_all),
        flat(out_all),
        gains[:, 1, :gain_part].reshape(-1),
        flat(gate_up_all),
        flat(down_all),
    )
    slots = inputs_x.shape[1]
    inputs_f = inputs_x.astype(jnp.float32)
    mask = padding(lengths, slots)
    mask_rows = mask.reshape(-1, 1)
    ffn_gain_row = weights[3].astype(jnp.float32).reshape(1, -1)
    gate_up_w, down_w = weights[4:]
    dz_given = (cotangent.astype(jnp.float32) * mask).astype(jnp.bfloat16)
    after_one, _ = attention_forward(weights, inputs_f, lengths)
    first_out = ffn_forward(flat(after_one), ffn_gain_row, mask_rows, gate_up_w, down_w)
    recv_act = passed_along(first_out, "section", 1).reshape(inputs_x.shape)
    layer_in = jnp.where(is_first, inputs_f, recv_act.astype(jnp.float32))
    after, kept_state = attention_forward(weights, layer_in, lengths)
    dy, dy_low, _ = ffn_backward(
        flat(after), flat(dz_given), ffn_gain_row, mask_rows, gate_up_w, down_w, False
    )
    second_dx, _, _ = attention_backward(
        weights, kept_state, dy.reshape(inputs_x.shape), dy_low.reshape(inputs_x.shape)
    )
    recv_grad = passed_along(second_dx.astype(jnp.bfloat16), "section", -1)
    normed_one, attention_result = kept_state[2], kept_state[7]
    attention_turned, normed_turned = turned(attention_result), turned(normed_one)
    recv_grad, attention_turned, normed_turned = lax.optimization_barrier(
        (recv_grad, attention_turned, normed_turned)
    )
    dz = jnp.where(is_first, (recv_grad.astype(jnp.float32) * mask).astype(jnp.bfloat16), dz_given)
    dz = flat(dz)
    dy, dy_low, ffn_gain_part, hidden_turned, grad_gate, grad_up, normed_two_turned, result = ffn_backward(
        flat(after), dz, ffn_gain_row, mask_rows, gate_up_w, down_w, True
    )
    grad_x, attn_gain_part, grad_qkv = attention_backward(
        weights, kept_state, dy.reshape(inputs_x.shape), dy_low.reshape(inputs_x.shape)
    )
    section_out = result.reshape((1,) + inputs_x.shape)
    input_grads = jnp.where(
        is_first, grad_x, grad_x.astype(jnp.bfloat16).astype(jnp.float32)
    )[None]
    gain_parts = jnp.pad(
        jnp.concatenate([attn_gain_part[None], ffn_gain_part], 0), ((0, 6), (0, 0))
    )
    gate_qkv_sum, down_out_sum, gain_sums = summed_grads(
        lax.axis_size("group"),
        lax.axis_size("dp"),
        hidden_turned,
        attention_turned,
        normed_two_turned,
        normed_turned,
        dz,
        dy_low,
        grad_gate,
        grad_up,
        flat(grad_qkv),
        gain_parts,
    )
    gain_cols = attn_gain.shape[1] * lax.axis_size("dp")
    gain_sums = lax.dynamic_slice_in_dim(
        gain_sums, lax.axis_index("group") * gain_cols, gain_cols, 1
    )
    gate_width = gate_up.shape[2]
    down_rows = down_weight.shape[1] * lax.axis_size("dp")
    reduced = (
        gain_sums[0],
        gate_qkv_sum[:, gate_width:].astype(jnp.float32),
        down_out_sum[down_rows:].astype(jnp.float32),
        gain_sums[1],
        gate_qkv_sum[:, :gate_width].astype(jnp.float32),
        down_out_sum[:down_rows].astype(jnp.float32),
    )
    return (section_out, input_grads) + tuple((shard_sum[None] for shard_sum in reduced))


def solution(mesh):
    placed = (
        P(("group", "dp"), None, None),
        P(("group", "dp"), None, None),
        P(("group", "dp")),
        P("section", ("group", "dp")),
        P("section", ("group", "dp"), None),
        P("section", ("group", "dp"), None),
        P("section", ("group", "dp")),
        P("section", ("group", "dp"), None),
        P("section", ("group", "dp"), None),
    )
    return jax.shard_map(
        body,
        mesh=mesh,
        in_specs=placed,
        out_specs=(
            P("section", ("group", "dp"), None, None),
            P("section", ("group", "dp"), None, None),
            P("section", "group"),
            P("section", "group", None),
            P("section", "group", None),
            P("section", "group"),
            P("section", "group", None),
            P("section", "group", None),
        ),
        check_vma=False,
    )
```

```python
import functools

import jax
import jax.numpy as jnp
from jax import lax
from jax.experimental import pallas as pl
from jax.experimental.pallas import tpu as pltpu
from jax.sharding import PartitionSpec as P

H = 16
KVH = 8
HD = 96
FF = 4096


norm_eps = 1e-05
rope_base = 100000.0
masked_score = -1e30
across = (((1,), (1,)), ((), ()))


def passed_along(value, axis, by):
    length = lax.axis_size(axis)
    pairs = [(i, i + by) for i in range(length) if 0 <= i + by < length]
    return lax.ppermute(value, axis, pairs)


def rope_tables(slot_count, head_width):
    half_width = head_width // 2
    frequency = rope_base ** (-(jnp.arange(half_width, dtype=jnp.float32) * 2.0 / head_width))
    angles = jnp.arange(slot_count, dtype=jnp.float32)[:, None] * frequency[None, :]
    return (jnp.cos(angles), jnp.sin(angles))


def rotate(vector, cosines, sine_table):
    half_width = vector.shape[-1] // 2
    front_half = vector[..., :half_width]
    back_half = vector[..., half_width:]
    cos_wide = cosines[:, None, :]
    sin_wide = sine_table[:, None, :]
    return jnp.concatenate(
        [
            front_half * cos_wide - back_half * sin_wide,
            back_half * cos_wide + front_half * sin_wide,
        ],
        -1,
    )


def norm_scale(vector):
    return lax.rsqrt(jnp.mean(vector * vector, -1, keepdims=True) + norm_eps)


def allowed_keys(lengths, slot_count):
    position = jnp.arange(slot_count, dtype=jnp.int32)
    causal = position[None, :] <= position[:, None]
    return causal[None] & (position[None, None, :] < lengths[:, None, None])


def padding(lengths, slot_count):
    position = jnp.arange(slot_count, dtype=jnp.int32)
    return (position[None, :] < lengths[:, None]).astype(jnp.float32)[..., None]


def norm_back(vector, scale, gain, grad_normed):
    scaled = grad_normed * gain.astype(jnp.float32)
    gain_grad = jnp.sum(grad_normed * vector * scale, axis=(0, 1))
    grad_vector = scale * scaled - vector * (scale * scale * scale) * jnp.mean(
        vector * scaled, -1, keepdims=True
    )
    return (gain_grad, grad_vector)


def score_block(query_heads, key_heads, lengths):
    slot_count = query_heads.shape[1]
    scores = jnp.einsum(
        "rqkgh,rpkh->rkgqp", query_heads, key_heads, preferred_element_type=jnp.float32
    ) * HD ** (-0.5)
    allowed = allowed_keys(lengths, slot_count)
    return jnp.where(allowed[:, None, None], scores, masked_score)


def attention_forward(weights, input_rows, lengths):
    gain_one, qkv_w, output_weight = weights[:3]
    row_count, slot_count, width = input_rows.shape
    groups = H // KVH
    cosines, sine_table = rope_tables(slot_count, HD)
    scale_one = norm_scale(input_rows)
    normed_one = (input_rows * scale_one * gain_one.astype(jnp.float32)).astype(jnp.bfloat16)
    qkv_all = jnp.einsum("rsd,de->rse", normed_one, qkv_w, preferred_element_type=jnp.float32)
    query_heads = rotate(
        qkv_all[..., : H * HD].reshape(row_count, slot_count, H, HD), cosines, sine_table
    )
    query_heads = query_heads.astype(jnp.bfloat16).reshape(row_count, slot_count, KVH, groups, HD)
    key_heads = rotate(
        qkv_all[..., H * HD : (H + KVH) * HD].reshape(row_count, slot_count, KVH, HD),
        cosines,
        sine_table,
    )
    key_heads = key_heads.astype(jnp.bfloat16)
    value_heads = (
        qkv_all[..., (H + KVH) * HD :].reshape(row_count, slot_count, KVH, HD).astype(jnp.bfloat16)
    )
    scores = score_block(query_heads, key_heads, lengths)
    row_max = jnp.max(scores, -1, keepdims=True)
    log_total = row_max + jnp.log(jnp.sum(jnp.exp(scores - row_max), -1, keepdims=True))
    prob_low = jnp.exp(scores - log_total).astype(jnp.bfloat16)
    attention_result = jnp.einsum(
        "rkgqp,rpkh->rqkgh", prob_low, value_heads, preferred_element_type=jnp.float32
    )
    attention_result = attention_result.astype(jnp.bfloat16).reshape(row_count, slot_count, H * HD)
    after_attention = input_rows + jnp.einsum(
        "vao,oj->vaj", attention_result, output_weight, preferred_element_type=jnp.float32
    )
    kept_state = (
        input_rows,
        scale_one,
        normed_one,
        query_heads,
        key_heads,
        value_heads,
        log_total,
        attention_result,
        lengths,
    )
    return (after_attention, kept_state)


def attention_backward(weights, kept_state, grad_after, gradient_after_lowered):
    gain_one, qkv_w, output_weight = weights[:3]
    (
        input_rows,
        scale_one,
        normed_one,
        query_heads,
        key_heads,
        value_heads,
        log_total,
        attention_result,
        lengths,
    ) = kept_state
    row_count, slot_count, width = input_rows.shape
    groups = H // KVH
    score_scale = HD ** (-0.5)
    cosines, sine_table = rope_tables(slot_count, HD)
    attention_gradient = jnp.einsum(
        "vol,el->voe", gradient_after_lowered, output_weight, preferred_element_type=jnp.float32
    )
    attention_gradient = attention_gradient.astype(jnp.bfloat16).reshape(
        row_count, slot_count, KVH, groups, HD
    )
    scores = score_block(query_heads, key_heads, lengths)
    prob_full = jnp.exp(scores - log_total)
    prob_low = prob_full.astype(jnp.bfloat16)
    grad_values = jnp.einsum(
        "rkgqp,rqkgh->rpkh", prob_low, attention_gradient, preferred_element_type=jnp.float32
    )
    grad_probs = jnp.einsum(
        "rqkgh,rpkh->rkgqp", attention_gradient, value_heads, preferred_element_type=jnp.float32
    )
    row_dot = jnp.sum(prob_full * grad_probs, -1, keepdims=True)
    grad_scores = (prob_full * (grad_probs - row_dot)).astype(jnp.bfloat16)
    grad_query = (
        jnp.einsum("rkgqp,rpkh->rqkgh", grad_scores, key_heads, preferred_element_type=jnp.float32)
        * score_scale
    )
    grad_query = rotate(grad_query.reshape(row_count, slot_count, H, HD), cosines, -sine_table)
    grad_keys = (
        jnp.einsum(
            "rkgqp,rqkgh->rpkh", grad_scores, query_heads, preferred_element_type=jnp.float32
        )
        * score_scale
    )
    grad_keys = rotate(grad_keys, cosines, -sine_table)
    grad_qkv = jnp.concatenate(
        [
            grad_query.reshape(row_count, slot_count, H * HD),
            grad_keys.reshape(row_count, slot_count, KVH * HD),
            grad_values.reshape(row_count, slot_count, KVH * HD),
        ],
        -1,
    ).astype(jnp.bfloat16)
    grad_normed_one = jnp.einsum("rse,de->rsd", grad_qkv, qkv_w, preferred_element_type=jnp.float32)
    attn_gain_part, grad_norm_one = norm_back(input_rows, scale_one, gain_one, grad_normed_one)
    return (grad_after + grad_norm_one, attn_gain_part, grad_qkv)


FF_CHUNK = 512
across = (((1,), (1,)), ((), ()))


def scaled_norm(value, gain):
    scale = lax.rsqrt(jnp.mean(value * value, -1, keepdims=True) + norm_eps)
    return scale, (value * scale * gain).astype(jnp.bfloat16)


def ffn_forward_kernel(y, gain, mask, wg, wu, wd, out, n2, acc):
    j = pl.program_id(0)

    @pl.when(j == 0)
    def _():
        n2[...] = scaled_norm(y[...], gain[...])[1]
        acc[...] = y[...]

    gate = jnp.dot(n2[...], wg[...], preferred_element_type=jnp.float32)
    up = jnp.dot(n2[...], wu[...], preferred_element_type=jnp.float32)
    hidden = (gate / (1.0 + jnp.exp(-gate)) * up).astype(jnp.bfloat16)
    acc[...] += jnp.dot(hidden, wd[...], preferred_element_type=jnp.float32)

    @pl.when(j == pl.num_programs(0) - 1)
    def _():
        out[...] = (acc[...] * mask[...]).astype(jnp.bfloat16)


def ffn_specs(tokens, width, hidden):
    steps = hidden // FF_CHUNK
    whole = pl.BlockSpec((tokens, width), lambda j: (0, 0))
    row = pl.BlockSpec((1, width), lambda j: (0, 0))
    weights = [
        pl.BlockSpec((width, FF_CHUNK), lambda j: (0, j)),
        pl.BlockSpec((width, FF_CHUNK), lambda j: (0, j + steps)),
        pl.BlockSpec((FF_CHUNK, width), lambda j: (j, 0)),
    ]
    return steps, whole, row, weights


def ffn_forward(y, gain, mask, gate_up_w, down_w):
    tokens, width = y.shape
    hidden = down_w.shape[0]
    steps, whole, row, weights = ffn_specs(tokens, width, hidden)
    return pl.pallas_call(
        ffn_forward_kernel,
        grid=(steps,),
        out_shape=jax.ShapeDtypeStruct((tokens, width), jnp.bfloat16),
        in_specs=[whole, row, pl.BlockSpec((tokens, 1), lambda j: (0, 0))] + weights,
        out_specs=whole,
        scratch_shapes=[pltpu.VMEM((tokens, width), jnp.bfloat16), pltpu.VMEM((tokens, width), jnp.float32)],
        compiler_params=pltpu.CompilerParams(vmem_limit_bytes=40 * 1024 * 1024),
        cost_estimate=pl.CostEstimate(
            flops=6 * tokens * width * hidden, bytes_accessed=6 * width * hidden, transcendentals=tokens * hidden
        ),
    )(y, gain, mask, gate_up_w, gate_up_w, down_w)


def ffn_backward_kernel(keep, y, dz, gain, mask, wg, wu, wd, dy, dyb, gain_grad, *rest):
    if keep:
        at, dgate, dup, n2t, out, n2, scale, acc, zacc = rest
    else:
        n2, scale, acc = rest
    j = pl.program_id(0)
    bf16, f32 = jnp.bfloat16, jnp.float32

    @pl.when(j == 0)
    def _():
        r, n = scaled_norm(y[...], gain[...])
        n2[...] = n
        scale[...] = r
        acc[...] = jnp.zeros_like(acc)
        if keep:
            n2t[...] = n.T
            zacc[...] = y[...]

    gate = jnp.dot(n2[...], wg[...], preferred_element_type=f32)
    up = jnp.dot(n2[...], wu[...], preferred_element_type=f32)
    grad = lax.dot_general(dz[...], wd[...], across, preferred_element_type=f32)
    sig = 1.0 / (1.0 + jnp.exp(-gate))
    silu = gate * sig
    grad_gate = (grad * up * sig * (1.0 + gate * (1.0 - sig))).astype(bf16)
    grad_up = (grad * silu).astype(bf16)
    if keep:
        hidden = (silu * up).astype(bf16)
        at[...] = hidden.T
        dgate[...] = grad_gate
        dup[...] = grad_up
        zacc[...] += jnp.dot(hidden, wd[...], preferred_element_type=f32)
    acc[...] += lax.dot_general(grad_gate, wg[...], across, preferred_element_type=f32) + lax.dot_general(
        grad_up, wu[...], across, preferred_element_type=f32
    )

    @pl.when(j == pl.num_programs(0) - 1)
    def _():
        value, r, grad_normed = y[...], scale[...], acc[...]
        scaled = grad_normed * gain[...]
        gain_grad[...] = jnp.sum(grad_normed * value * r, axis=0, keepdims=True)
        inner = jnp.mean(value * scaled, -1, keepdims=True)
        total = dz[...].astype(f32) + r * scaled - value * (r * r * r) * inner
        dy[...] = total
        dyb[...] = total.astype(bf16)
        if keep:
            out[...] = (zacc[...] * mask[...]).astype(bf16)


def ffn_backward(y, dz, gain, mask, gate_up_w, down_w, keep):
    tokens, width = y.shape
    hidden = down_w.shape[0]
    steps, whole, row, weights = ffn_specs(tokens, width, hidden)
    shape, bf16, f32 = jax.ShapeDtypeStruct, jnp.bfloat16, jnp.float32
    outs = [shape((tokens, width), f32), shape((tokens, width), bf16), shape((1, width), f32)]
    out_specs = [whole, whole, row]
    scratch = [pltpu.VMEM((tokens, width), bf16), pltpu.VMEM((tokens, 1), f32), pltpu.VMEM((tokens, width), f32)]
    if keep:
        part = pl.BlockSpec((tokens, FF_CHUNK), lambda j: (0, j))
        outs += [
            shape((hidden, tokens), bf16), shape((tokens, hidden), bf16), shape((tokens, hidden), bf16),
            shape((width, tokens), bf16), shape((tokens, width), bf16),
        ]
        out_specs += [
            pl.BlockSpec((FF_CHUNK, tokens), lambda j: (j, 0)), part, part,
            pl.BlockSpec((width, tokens), lambda j: (0, 0)), whole,
        ]
        scratch += [pltpu.VMEM((tokens, width), f32)]
    return pl.pallas_call(
        functools.partial(ffn_backward_kernel, keep),
        grid=(steps,),
        out_shape=tuple(outs),
        in_specs=[whole, whole, row, pl.BlockSpec((tokens, 1), lambda j: (0, 0))] + weights,
        out_specs=tuple(out_specs),
        scratch_shapes=scratch,
        compiler_params=pltpu.CompilerParams(vmem_limit_bytes=48 * 1024 * 1024),
        cost_estimate=pl.CostEstimate(
            flops=10 * tokens * width * hidden, bytes_accessed=6 * width * hidden, transcendentals=tokens * hidden
        ),
    )(y, dz, gain, mask, gate_up_w, gate_up_w, down_w)


def turned(array):
    return array.reshape(-1, array.shape[-1]).T


def flat(array):
    return array.reshape(-1, array.shape[-1])


MESH = pl.DeviceIdType.MESH
LANES = 128


def grad_plan(groups, dp, tokens, width, hidden, qkv_cols):
    pairs = dp // 2
    block = width // groups
    down_block = hidden // groups
    gate_cols = 2 * hidden // 2 // pairs
    qkv_part = qkv_cols // 2 // pairs
    pieces_gate = gate_cols // LANES
    pieces_qkv = qkv_part // LANES
    pieces = pieces_gate + pieces_qkv
    z_rows = LANES
    while down_block % z_rows or block % z_rows:
        z_rows //= 2
    row_chunks = (down_block + block) // z_rows
    half = width // 2
    z_split = max(1, pieces // row_chunks)
    while half % (z_split * LANES):
        z_split -= 1
    return dict(
        groups=groups, pairs=pairs, tokens=tokens, width=width, hidden=hidden, qkv_cols=qkv_cols, block=block,
        down_block=down_block, gate_cols=gate_cols, qkv_part=qkv_part, pieces_gate=pieces_gate, pieces=pieces,
        z_rows=z_rows, z_split=z_split, z_cols=half // z_split, z_pieces=row_chunks * z_split,
        down_chunks=down_block // z_rows, half=half,
    )


YS_RING = 4
HOP = 2
LEAD = 2


def grad_kernel(
    plan, at, ot, n2t, n1t, dz, dy, dgate, dup, dq, gp, outy, outz, outg,
    LT, RH, YS, YR, YRT, YLT, ZRT, ZLT, ZX,
    own_sem, xs, xr, ys_s, ys_r, yr_s, yr_r, yl_s, yl_r, zr_s, zr_r, zl_s, zl_r,
    zx_s, zx_r, ag_s, ag_r, sib_s, sib_r, lo,
    GC, GA, GS, GR, GL, gc_sem, ga_s, ga_r, gr_sem, gl_sem,
):
    G, A, T = plan["groups"], plan["pairs"], plan["tokens"]
    width, hidden, half = plan["width"], plan["hidden"], plan["half"]
    block, nY, nZ = plan["block"], plan["pieces"], plan["z_pieces"]
    zr, zc = plan["z_rows"], plan["z_cols"]
    s, z, d = lax.axis_index("section"), lax.axis_index("group"), lax.axis_index("dp")
    c, a = lax.rem(d, 2), lax.div(d, 2)
    sib = (s, z, 2 * a + 1 - c)
    right, left = (s, z + 1, d), (s, z - 1, d)

    def peer(k):
        return (s, z, 2 * lax.rem(a + k, A) + c)

    def remote(src, dst, ss, rs, dev):
        return pltpu.make_async_remote_copy(
            src_ref=src, dst_ref=dst, send_sem=ss, recv_sem=rs, device_id=dev, device_id_type=MESH
        )

    barrier = pltpu.get_barrier_semaphore()
    for dev in [sib, (s, lax.rem(z + 1, G), d), (s, lax.rem(z + G - 1, G), d)] + [peer(k) for k in range(1, A)]:
        pl.semaphore_signal(barrier, inc=1, device_id=dev, device_id_type=MESH)
    pl.semaphore_wait(barrier, A + 2)

    lhs = [(at, 0, hidden), (ot, hidden, width), (n2t, hidden + width, width), (n1t, hidden + 2 * width, width)]
    rhs = [(dz, 0, half), (dy, half, half), (None, width, hidden), (dq, width + hidden, plan["qkv_cols"] // 2)]
    order = [(0, 0), (2, 2), (1, 1), (3, 3)]
    own, cross = {}, {}
    for i, (ref, row, rows) in enumerate(lhs):
        own[0, i] = pltpu.make_async_copy(ref, LT.at[pl.ds(row, rows), pl.ds(0, T)], own_sem.at[i])
        cross[0, i] = remote(ref, LT.at[pl.ds(row, rows), pl.ds(T, T)], xs.at[i], xr.at[i], sib)
    for i, (ref, col, cols) in enumerate(rhs):
        if ref is None:
            continue
        mine = pl.ds(pl.multiple_of(c * cols, LANES), cols)
        theirs = pl.ds(pl.multiple_of((1 - c) * cols, LANES), cols)
        own[1, i] = pltpu.make_async_copy(ref.at[:, mine], RH.at[pl.ds(0, T), pl.ds(col, cols)], own_sem.at[4 + i])
        cross[1, i] = remote(ref.at[:, theirs], RH.at[pl.ds(T, T), pl.ds(col, cols)], xs.at[4 + i], xr.at[4 + i], sib)
    col, cols = rhs[2][1:]
    for core, (mine, theirs) in enumerate(((dgate, dup), (dup, dgate))):
        own[1, 2, core] = pltpu.make_async_copy(mine, RH.at[pl.ds(0, T), pl.ds(col, cols)], own_sem.at[6])
        cross[1, 2, core] = remote(theirs, RH.at[pl.ds(T, T), pl.ds(col, cols)], xs.at[6], xr.at[6], sib)
    own[1, 2], cross[1, 2] = own[1, 2, 0], cross[1, 2, 0]
    for i, _ in order:
        for side in (0, 1):
            if (side, i) == (1, 2):
                for core in (0, 1):
                    @pl.when(c == core)
                    def _(core=core):
                        own[1, 2, core].start()
                        cross[1, 2, core].start()
            else:
                own[side, i].start()
                cross[side, i].start()

    def operands_here(i):
        for side in (0, 1):
            own[side, i].wait()
            cross[side, i].wait_recv()

    def product(row, rows, col, cols):
        return jnp.dot(
            LT[pl.ds(row, rows), :], RH[:, pl.ds(col, cols)], preferred_element_type=jnp.float32
        )

    def y_product(q, which, b):
        is_gate = q < plan["pieces_gate"]
        row = jnp.where(is_gate, hidden + width, hidden + 2 * width) + b * block
        col = jnp.where(
            is_gate,
            width + which * plan["gate_cols"] + q * LANES,
            width + hidden + which * plan["qkv_part"] + (q - plan["pieces_gate"]) * LANES,
        )
        return product(pl.multiple_of(row, 16), block, pl.multiple_of(col, LANES), LANES)

    def z_product(p, b):
        r, h = lax.div(p, plan["z_split"]), lax.rem(p, plan["z_split"])
        is_down = r < plan["down_chunks"]
        row = jnp.where(
            is_down, b * plan["down_block"] + r * zr, hidden + b * block + (r - plan["down_chunks"]) * zr
        )
        col = jnp.where(is_down, 0, half) + h * zc
        return product(pl.multiple_of(row, 16), zr, pl.multiple_of(col, LANES), zc)

    def y_out(q, part, core):
        is_gate = q < plan["pieces_gate"]
        col = jnp.where(
            is_gate,
            core * hidden + part * plan["gate_cols"] + q * LANES,
            2 * hidden + core * (plan["qkv_cols"] // 2) + part * plan["qkv_part"] + (q - plan["pieces_gate"]) * LANES,
        )
        return outy.at[:, pl.ds(pl.multiple_of(col, LANES), LANES)]

    def z_out(p, core):
        r, h = lax.div(p, plan["z_split"]), lax.rem(p, plan["z_split"])
        return outz.at[
            pl.ds(pl.multiple_of(r * zr, 16), zr), pl.ds(pl.multiple_of(core * half + h * zc, LANES), zc)
        ]

    def y_send(q, k):
        return remote(YS.at[lax.rem(q, YS_RING), k - 1], YR.at[q, k - 1], ys_s.at[q, k - 1], ys_r.at[q, k - 1], peer(k))

    def line_copies(slots_r, slots_l, r_s, r_r, l_s, l_r, first_r, first_l, p):
        out_r, in_r, out_l, in_l = [], [], [], []
        for k in range(G):
            if k < G - 1:
                src = first_r(p) if k == 0 else slots_r.at[p, pl.ds(k, G - 1 - k)]
                out_r.append((k, remote(src, slots_r.at[p, pl.ds(k, G - 1 - k)], r_s.at[p], r_r.at[p], right)))
                held = slots_l.at[p, pl.ds(0, k + 1)]
                in_l.append((k, remote(held, held, l_s.at[p], l_r.at[p], left)))
            if k > 0:
                src = first_l(p) if k == G - 1 else slots_l.at[p, pl.ds(0, k)]
                out_l.append((k, remote(src, slots_l.at[p, pl.ds(0, k)], l_s.at[p], l_r.at[p], left)))
                held = slots_r.at[p, pl.ds(k - 1, G - k)]
                in_r.append((k, remote(held, held, r_s.at[p], r_r.at[p], right)))
        return out_r, in_r, out_l, in_l

    def at_place(copies, act):
        for k, copy in copies:
            @pl.when(z == k)
            def _(copy=copy):
                act(copy)

    def y_line(q):
        return line_copies(
            YRT, YLT, yr_s, yr_r, yl_s, yl_r,
            lambda q: YR.at[q, 0, pl.ds(1, G - 1)], lambda q: YR.at[q, 0, pl.ds(0, G - 1)], q,
        )

    def z_line(p):
        return line_copies(
            ZRT, ZLT, zr_s, zr_r, zl_s, zl_r,
            lambda p: ZRT.at[p, pl.ds(0, G - 1)], lambda p: ZLT.at[p, pl.ds(0, G - 1)], p,
        )

    def zx_copy(p, k):
        return remote(ZX.at[p, a], ZX.at[p, a], zx_s.at[p, k - 1], zx_r.at[p, k - 1], peer(k))

    def ag_copy(q, k):
        return remote(YR.at[q, 0, z], y_out(q, a, c), ag_s.at[q, k - 1], ag_r.at[q, k - 1], peer(k))

    def sib_own(q):
        return remote(YR.at[q, 0, z], y_out(q, a, c), sib_s.at[q, 0], sib_r.at[q, 0], sib)

    def sib_pass(q, k):
        part = lax.rem(a + A - k, A)
        return remote(y_out(q, part, c), y_out(q, part, c), sib_s.at[q, k], sib_r.at[q, k], sib)

    def own_y(q):
        return pltpu.make_async_copy(YR.at[q, 0, z], y_out(q, a, c), lo.at[q])

    def own_z(p):
        return pltpu.make_async_copy(ZX.at[p, a], z_out(p, c), lo.at[nY + p])

    def sib_z(p):
        return remote(ZX.at[p, a], z_out(p, c), sib_s.at[nY + p, 0], sib_r.at[nY + p, 0], sib)

    f32, bf16 = jnp.float32, jnp.bfloat16
    far = jnp.maximum(z, G - 1 - z)

    def live(index, count):
        return (index >= 0) & (index < count)

    def gain_core():
        return remote(gp, GC, gc_sem.at[0], gc_sem.at[1], sib)

    def gain_part(k):
        return remote(GA.at[a], GA.at[a], ga_s.at[k - 1], ga_r.at[k - 1], peer(k))

    def gain_right():
        return remote(GS.at[1], GR, gr_sem.at[0], gr_sem.at[1], right)

    def gain_left():
        return remote(GS.at[2], GL, gl_sem.at[0], gl_sem.at[1], left)

    def gain_step(t):
        @pl.when(t == 0)
        def _():
            gain_core().start()

        @pl.when(t == 1)
        def _():
            gain_core().wait_recv()
            GA[a] = gp[...] + GC[...]
            for k in range(1, A):
                gain_part(k).start()

        @pl.when(t == 2)
        def _():
            for k in range(1, A):
                remote(
                    GA.at[lax.rem(a + A - k, A)], GA.at[lax.rem(a + A - k, A)], ga_s.at[k - 1], ga_r.at[k - 1], peer(k)
                ).wait_recv()
            total = GA[0]
            for k in range(1, A):
                total += GA[k]
            GS[0] = total

        @pl.when(t == 2 + HOP * z)
        def _():
            @pl.when(z > 0)
            def _():
                gain_right().wait_recv()
                GS[1] = GS[0] + GR[...]

            @pl.when(z == 0)
            def _():
                GS[1] = GS[0]

            @pl.when(z < G - 1)
            def _():
                gain_right().start()

        @pl.when(t == 2 + HOP * (G - 1 - z))
        def _():
            @pl.when(z < G - 1)
            def _():
                gain_left().wait_recv()
                GS[2] = GS[0] + GL[...]

            @pl.when(z == G - 1)
            def _():
                GS[2] = GS[0]

            @pl.when(z > 0)
            def _():
                gain_left().start()

        @pl.when(t == 3 + HOP * (G - 1))
        def _():
            outg[...] = GS[1] + jnp.where(z < G - 1, GL[...], 0.0)

    def step(t, carry):
        gain_step(t)

        @pl.when(t == 0)
        def _():
            operands_here(0)
            operands_here(2)

        @pl.when(t == 1)
        def _():
            operands_here(1)
            operands_here(3)

        q1 = t

        @pl.when(live(q1, nY))
        def _():
            for k in range(1, A):
                @pl.when(q1 >= YS_RING)
                def _():
                    y_send(q1 - YS_RING, k).wait_send()

                @pl.loop(0, G)
                def _(b):
                    YS[lax.rem(q1, YS_RING), k - 1, b] = y_product(q1, lax.rem(a + k, A), b).astype(bf16)

                y_send(q1, k).start()

        pr = t - HOP * z

        @pl.when(live(pr, nZ))
        def _():
            out_r, in_r, _, _ = z_line(pr)
            at_place(in_r, lambda copy: copy.wait_recv())

            @pl.loop(0, G)
            def _(b):
                @pl.when((b > z) & (z > 0))
                def _():
                    ZRT[pr, b - 1] = (z_product(pr, b) + ZRT[pr, b - 1].astype(f32)).astype(bf16)

                @pl.when((b > z) & (z == 0))
                def _():
                    ZRT[pr, b - 1] = z_product(pr, b).astype(bf16)

            at_place(out_r, lambda copy: copy.start())

        pL = t - HOP * (G - 1 - z)

        @pl.when(live(pL, nZ))
        def _():
            _, _, out_l, in_l = z_line(pL)
            at_place(in_l, lambda copy: copy.wait_recv())

            @pl.loop(0, G)
            def _(b):
                @pl.when((b < z) & (z < G - 1))
                def _():
                    ZLT[pL, b] = (z_product(pL, b) + ZLT[pL, b].astype(f32)).astype(bf16)

                @pl.when((b < z) & (z == G - 1))
                def _():
                    ZLT[pL, b] = z_product(pL, b).astype(bf16)

            at_place(out_l, lambda copy: copy.start())

        q2 = t - LEAD

        @pl.when(live(q2, nY))
        def _():
            for k in range(1, A):
                y_send(q2, k).wait_recv()

            @pl.loop(0, G)
            def _(b):
                total = y_product(q2, a, b)
                for k in range(1, A):
                    total += YR[q2, k - 1, b].astype(f32)
                YR[q2, 0, b] = total.astype(bf16)

        qr = t - LEAD - HOP * z

        @pl.when(live(qr, nY))
        def _():
            out_r, in_r, _, _ = y_line(qr)
            at_place(in_r, lambda copy: copy.wait_recv())

            @pl.loop(0, G)
            def _(b):
                @pl.when((b > z) & (z > 0))
                def _():
                    YRT[qr, b - 1] = (YR[qr, 0, b].astype(f32) + YRT[qr, b - 1].astype(f32)).astype(bf16)

            at_place(out_r, lambda copy: copy.start())

        qL = t - LEAD - HOP * (G - 1 - z)

        @pl.when(live(qL, nY))
        def _():
            _, _, out_l, in_l = y_line(qL)
            at_place(in_l, lambda copy: copy.wait_recv())

            @pl.loop(0, G)
            def _(b):
                @pl.when((b < z) & (z < G - 1))
                def _():
                    YLT[qL, b] = (YR[qL, 0, b].astype(f32) + YLT[qL, b].astype(f32)).astype(bf16)

            at_place(out_l, lambda copy: copy.start())

        pf = t - HOP * far

        @pl.when(live(pf, nZ))
        def _():
            mine = z_product(pf, z)
            from_left = ZRT[pf, jnp.maximum(z - 1, 0)].astype(f32)
            from_right = ZLT[pf, jnp.minimum(z, G - 2)].astype(f32)
            mine = mine + jnp.where(z > 0, from_left, 0.0) + jnp.where(z < G - 1, from_right, 0.0)
            ZX[pf, a] = mine.astype(bf16)
            for k in range(1, A):
                zx_copy(pf, k).start()

        pg = t - HOP * far - LEAD

        @pl.when(live(pg, nZ))
        def _():
            for k in range(1, A):
                remote(
                    ZX.at[pg, lax.rem(a + A - k, A)], ZX.at[pg, lax.rem(a + A - k, A)],
                    zx_s.at[pg, k - 1], zx_r.at[pg, k - 1], peer(k),
                ).wait_recv()
            total = ZX[pg, 0].astype(f32)
            for k in range(1, A):
                total += ZX[pg, k].astype(f32)
            for k in range(1, A):
                zx_copy(pg, k).wait_send()
            ZX[pg, a] = total.astype(bf16)
            own_z(pg).start()
            sib_z(pg).start()

        qf = t - LEAD - HOP * far

        @pl.when(live(qf, nY))
        def _():
            total = YR[qf, 0, z].astype(f32)
            from_left = YRT[qf, jnp.maximum(z - 1, 0)].astype(f32)
            from_right = YLT[qf, jnp.minimum(z, G - 2)].astype(f32)
            total = total + jnp.where(z > 0, from_left, 0.0) + jnp.where(z < G - 1, from_right, 0.0)
            YR[qf, 0, z] = total.astype(bf16)
            for k in range(1, A):
                ag_copy(qf, k).start()
            own_y(qf).start()
            sib_own(qf).start()

        qg = t - LEAD - HOP * far - LEAD

        @pl.when(live(qg, nY))
        def _():
            for k in range(1, A):
                here = y_out(qg, lax.rem(a + A - k, A), c)
                remote(here, here, ag_s.at[qg, k - 1], ag_r.at[qg, k - 1], peer(k)).wait_recv()
                sib_pass(qg, k).start()

        return carry

    steps = max(nY, nZ) + 2 * LEAD + HOP * (G - 1)
    lax.fori_loop(0, steps, step, 0)

    gain_core().wait_send()
    for k in range(1, A):
        gain_part(k).wait_send()

    @pl.when(z < G - 1)
    def _():
        gain_right().wait_send()

    @pl.when(z > 0)
    def _():
        gain_left().wait_send()

    for i in range(4):
        for side in (0, 1):
            cross[side, i].wait_send()

    def drain_y(q, carry):
        for k in range(1, A):
            @pl.when(q >= nY - YS_RING)
            def _():
                y_send(q, k).wait_send()

            ag_copy(q, k).wait_send()
            sib_pass(q, k).wait_send()
            there = y_out(q, lax.rem(a + A - k, A), 1 - c)
            remote(there, there, sib_s.at[q, k], sib_r.at[q, k], sib).wait_recv()
        out_r, _, out_l, _ = y_line(q)
        at_place(out_r, lambda copy: copy.wait_send())
        at_place(out_l, lambda copy: copy.wait_send())
        own_y(q).wait()
        sib_own(q).wait_send()
        there = y_out(q, a, 1 - c)
        remote(there, there, sib_s.at[q, 0], sib_r.at[q, 0], sib).wait_recv()
        return carry

    lax.fori_loop(0, nY, drain_y, 0)

    def drain_z(p, carry):
        out_r, _, out_l, _ = z_line(p)
        at_place(out_r, lambda copy: copy.wait_send())
        at_place(out_l, lambda copy: copy.wait_send())
        own_z(p).wait()
        sib_z(p).wait_send()
        there = z_out(p, 1 - c)
        remote(there, there, sib_s.at[nY + p, 0], sib_r.at[nY + p, 0], sib).wait_recv()
        return carry

    lax.fori_loop(0, nZ, drain_z, 0)


def summed_grads(groups, dp, at, ot, n2t, n1t, dz, dy, dgate, dup, dq, gain_parts):
    hidden, tokens = at.shape
    width, qkv_cols = ot.shape[0], dq.shape[1]
    plan = grad_plan(groups, dp, tokens, width, hidden, qkv_cols)
    G, A, nY, nZ = groups, plan["pairs"], plan["pieces"], plan["z_pieces"]
    block, zr, zc = plan["block"], plan["z_rows"], plan["z_cols"]
    bf16, DMA = jnp.bfloat16, pltpu.SemaphoreType.DMA
    any_space = pl.BlockSpec(memory_space=pl.ANY)
    in_vmem, f32, gain_shape = pl.BlockSpec(memory_space=pltpu.VMEM), jnp.float32, gain_parts.shape
    return pl.pallas_call(
        functools.partial(grad_kernel, plan),
        out_shape=(
            jax.ShapeDtypeStruct((block, 2 * hidden + qkv_cols), bf16),
            jax.ShapeDtypeStruct((plan["down_block"] + block, width), bf16),
            jax.ShapeDtypeStruct(gain_parts.shape, f32),
        ),
        in_specs=[any_space] * 9 + [in_vmem],
        out_specs=(any_space, any_space, in_vmem),
        scratch_shapes=[
            pltpu.VMEM((hidden + 3 * width, 2 * tokens), bf16),
            pltpu.VMEM((2 * tokens, width + hidden + qkv_cols // 2), bf16),
            pltpu.VMEM((YS_RING, A - 1, G, block, LANES), bf16),
            pltpu.VMEM((nY, A - 1, G, block, LANES), bf16),
            pltpu.VMEM((nY, G - 1, block, LANES), bf16),
            pltpu.VMEM((nY, G - 1, block, LANES), bf16),
            pltpu.VMEM((nZ, G - 1, zr, zc), bf16),
            pltpu.VMEM((nZ, G - 1, zr, zc), bf16),
            pltpu.VMEM((nZ, A, zr, zc), bf16),
            DMA((8,)), DMA((8,)), DMA((8,)),
            DMA((nY, A - 1)), DMA((nY, A - 1)),
            DMA((nY,)), DMA((nY,)), DMA((nY,)), DMA((nY,)),
            DMA((nZ,)), DMA((nZ,)), DMA((nZ,)), DMA((nZ,)),
            DMA((nZ, A - 1)), DMA((nZ, A - 1)),
            DMA((nY, A - 1)), DMA((nY, A - 1)),
            DMA((nY + nZ, A)), DMA((nY + nZ, A)),
            DMA((nY + nZ,)),
            pltpu.VMEM(gain_shape, f32),
            pltpu.VMEM((A,) + gain_shape, f32),
            pltpu.VMEM((3,) + gain_shape, f32),
            pltpu.VMEM(gain_shape, f32),
            pltpu.VMEM(gain_shape, f32),
            DMA((2,)), DMA((max(A - 1, 1),)), DMA((max(A - 1, 1),)), DMA((2,)), DMA((2,)),
        ],
        compiler_params=pltpu.CompilerParams(
            collective_id=3, has_side_effects=True, vmem_limit_bytes=63 * 1024 * 1024
        ),
        cost_estimate=pl.CostEstimate(
            flops=2 * 2 * tokens * (width * (2 * hidden + qkv_cols + width) + hidden * width) // 2,
            bytes_accessed=40_000_000, transcendentals=0,
        ),
    )(at, ot, n2t, n1t, dz, dy, dgate, dup, dq, gain_parts)


W_HOP = 5
gather_families = (
    (1, True, False),
    (2, True, True),
    (1, True, False),
    (8, True, False),
    (4, False, False),
)


def gather_kernel(groups, pairs, families, *refs):
    G, A, F = groups, pairs, len(families)
    shards, wholes = refs[:F], refs[F : 2 * F]
    sems = refs[2 * F :]
    s, z, d = lax.axis_index("section"), lax.axis_index("group"), lax.axis_index("dp")
    c, a = lax.rem(d, 2), lax.div(d, 2)
    sib = (s, z, 2 * a + 1 - c)
    right, left = (s, z + 1, d), (s, z - 1, d)

    def peer(part):
        return (s, z, 2 * part + c)

    barrier = pltpu.get_barrier_semaphore()
    others = [peer(lax.rem(a + k, A)) for k in range(1, A)]
    for dev in [sib, (s, lax.rem(z + 1, G), d), (s, lax.rem(z + G - 1, G), d)] + others:
        pl.semaphore_signal(barrier, inc=1, device_id=dev, device_id_type=MESH)
    pl.semaphore_wait(barrier, A + 2)

    def cut(f, ref, i):
        pieces, by_columns, _ = families[f]
        rows, cols = ref.shape
        if pieces == 1:
            return ref
        if by_columns:
            size = cols // pieces
            return ref.at[:, pl.ds(pl.multiple_of(i * size, 128), size)]
        size = rows // pieces
        return ref.at[pl.ds(pl.multiple_of(i * size, 16), size), :]

    def placed(f, i, o, part, core):
        return cut(f, wholes[f].at[(o * A + part) * 2 + core], i)

    def copy(f, i, o, part, kind, index, dev, own=False, core=None):
        core = c if core is None else core
        there = placed(f, i, o, part, core)
        src = cut(f, shards[f], i) if own else there
        send, recv = sems[f * 9 + 2 * kind], sems[f * 9 + 2 * kind + 1]
        return pltpu.make_async_remote_copy(
            src_ref=src, dst_ref=there, send_sem=send.at[index], recv_sem=recv.at[index], device_id=dev, device_id_type=MESH
        )

    def to_right(f, i, o, part, own=False):
        return copy(f, i, o, part, 0, (i, o, lax.rem(part + A - a, A)), right, own)

    def to_left(f, i, o, part, own=False):
        return copy(f, i, o, part, 1, (i, o, lax.rem(part + A - a, A)), left, own)

    def to_part(f, i, o, k, own=False):
        return copy(f, i, o, a, 2, (i, o, k - 1), peer(lax.rem(a + k, A)), own)

    def from_part(f, i, o, k):
        return copy(f, i, o, lax.rem(a + A - k, A), 2, (i, o, k - 1), peer(lax.rem(a + A - k, A)))

    def to_core(f, i, o, part, own=False):
        return copy(f, i, o, part, 3, (i, o, lax.rem(part + A - a, A)), sib, own)

    def from_core(f, i, o, k):
        part = lax.rem(a + k, A)
        return copy(f, i, o, part, 3, (i, o, k), sib, core=1 - c)

    def own_copy(f, i):
        return pltpu.make_async_copy(cut(f, shards[f], i), placed(f, i, z, a, c), sems[f * 9 + 8].at[i])

    def along(f, i, o, part, own, go_right, go_left):
        if go_right:
            @pl.when(z < G - 1)
            def _():
                to_right(f, i, o, part, own).start()
        if go_left:
            @pl.when(z > 0)
            def _():
                to_left(f, i, o, part, own).start()

    first = []
    total = 0
    for pieces, _, _ in families:
        first.append(total)
        total += pieces

    def step(t, carry):
        for f, (pieces, _, parts_first) in enumerate(families):
            i0 = t - first[f]

            @pl.when((i0 >= 0) & (i0 < pieces))
            def _(f=f, i0=i0):
                along(f, i0, z, a, True, True, True)
                for k in range(1, A):
                    to_part(f, i0, z, k, True).start()
                to_core(f, i0, z, a, True).start()
                own_copy(f, i0).start()

        for f, (pieces, _, parts_first) in enumerate(families):
            for h in range(G):
                for k in range(A if parts_first else 1):
                    if h == 0:
                        continue
                    i = t - first[f] - W_HOP * h - (W_HOP if k > 0 else 0)
                    part = lax.rem(a + k, A)
                    for sign in (-1, 1):
                        o = z + sign * h

                        @pl.when((i >= 0) & (i < pieces) & (o >= 0) & (o < G))
                        def _(f=f, i=i, o=o, part=part, sign=sign, parts_first=parts_first):
                            if sign < 0:
                                to_right(f, i, o, part).wait_recv()
                                along(f, i, o, part, False, True, False)
                            else:
                                to_left(f, i, o, part).wait_recv()
                                along(f, i, o, part, False, False, True)
                            if not parts_first:
                                for j in range(1, A):
                                    to_part(f, i, o, j).start()
                            to_core(f, i, o, part).start()

                if parts_first and h > 0:
                    continue
                i = t - first[f] - W_HOP * (h + 1)
                for sign in (-1, 1) if h else (1,):
                    o = z + sign * h

                    @pl.when((i >= 0) & (i < pieces) & (o >= 0) & (o < G))
                    def _(f=f, i=i, o=o, parts_first=parts_first):
                        for k in range(1, A):
                            from_part(f, i, o, k).wait_recv()
                            part = lax.rem(a + A - k, A)
                            if parts_first:
                                along(f, i, o, part, False, True, True)
                            to_core(f, i, o, part).start()
        return carry

    lax.fori_loop(0, total + W_HOP * (G + 1), step, 0)

    for f, (pieces, _, parts_first) in enumerate(families):
        def drain(i, carry, f=f, parts_first=parts_first):
            own_copy(f, i).wait()

            def by_group(o, carry):
                for k in range(A):
                    part = lax.rem(a + k, A)
                    to_core(f, i, o, part).wait_send()
                    from_core(f, i, o, k).wait_recv()
                    if parts_first or k == 0:
                        @pl.when((z < G - 1) & (o <= z))
                        def _(part=part):
                            to_right(f, i, o, part).wait_send()

                        @pl.when((z > 0) & (o >= z))
                        def _(part=part):
                            to_left(f, i, o, part).wait_send()
                for k in range(1, A):
                    if parts_first:
                        @pl.when(o == z)
                        def _(k=k):
                            to_part(f, i, o, k).wait_send()
                    else:
                        to_part(f, i, o, k).wait_send()
                return carry

            return lax.fori_loop(0, G, by_group, carry)

        lax.fori_loop(0, pieces, drain, 0)


def gathered(groups, dp, shards, families):
    A, DMA = dp // 2, pltpu.SemaphoreType.DMA
    any_space = pl.BlockSpec(memory_space=pl.ANY)
    scratch = []
    for pieces, _, parts_first in families:
        on_line = (pieces, groups, A if parts_first else 1)
        scratch += [DMA(on_line)] * 4 + [DMA((pieces, groups, max(A - 1, 1)))] * 2 + [DMA((pieces, groups, A))] * 2
        scratch += [DMA((pieces,))]
    return pl.pallas_call(
        functools.partial(gather_kernel, groups, A, families),
        out_shape=tuple(jax.ShapeDtypeStruct((groups * dp,) + x.shape, x.dtype) for x in shards),
        in_specs=[any_space] * len(shards),
        out_specs=(any_space,) * len(shards),
        scratch_shapes=scratch,
        compiler_params=pltpu.CompilerParams(collective_id=5, has_side_effects=True),
    )(*shards)


def body(
    inputs_x, cotangent, lengths, attn_gain, qkv_weight, out_weight, ffn_gain, gate_up, down_weight
):
    is_first = lax.axis_index("section") == 0
    gains = jnp.concatenate([attn_gain, ffn_gain], 0)
    gains = jnp.pad(gains, ((0, 14), (0, -gains.shape[1] % 128)))
    gains, qkv_all, out_all, gate_up_all, down_all = gathered(
        lax.axis_size("group"),
        lax.axis_size("dp"),
        (gains, qkv_weight[0], out_weight[0], gate_up[0], down_weight[0]),
        gather_families,
    )
    gain_part = attn_gain.shape[1]
    weights = (
        gains[:, 0, :gain_part].reshape(-1),
        flat(qkv_all),
        flat(out_all),
        gains[:, 1, :gain_part].reshape(-1),
        flat(gate_up_all),
        flat(down_all),
    )
    slots = inputs_x.shape[1]
    inputs_f = inputs_x.astype(jnp.float32)
    mask = padding(lengths, slots)
    mask_rows = mask.reshape(-1, 1)
    ffn_gain_row = weights[3].astype(jnp.float32).reshape(1, -1)
    gate_up_w, down_w = weights[4:]
    dz_given = (cotangent.astype(jnp.float32) * mask).astype(jnp.bfloat16)
    after_one, _ = attention_forward(weights, inputs_f, lengths)
    first_out = ffn_forward(flat(after_one), ffn_gain_row, mask_rows, gate_up_w, down_w)
    recv_act = passed_along(first_out, "section", 1).reshape(inputs_x.shape)
    layer_in = jnp.where(is_first, inputs_f, recv_act.astype(jnp.float32))
    after, kept_state = attention_forward(weights, layer_in, lengths)
    dy, dy_low, _ = ffn_backward(
        flat(after), flat(dz_given), ffn_gain_row, mask_rows, gate_up_w, down_w, False
    )
    second_dx, _, _ = attention_backward(
        weights, kept_state, dy.reshape(inputs_x.shape), dy_low.reshape(inputs_x.shape)
    )
    recv_grad = passed_along(second_dx.astype(jnp.bfloat16), "section", -1)
    normed_one, attention_result = kept_state[2], kept_state[7]
    attention_turned, normed_turned = turned(attention_result), turned(normed_one)
    recv_grad, attention_turned, normed_turned = lax.optimization_barrier(
        (recv_grad, attention_turned, normed_turned)
    )
    dz = jnp.where(is_first, (recv_grad.astype(jnp.float32) * mask).astype(jnp.bfloat16), dz_given)
    dz = flat(dz)
    dy, dy_low, ffn_gain_part, hidden_turned, grad_gate, grad_up, normed_two_turned, result = ffn_backward(
        flat(after), dz, ffn_gain_row, mask_rows, gate_up_w, down_w, True
    )
    grad_x, attn_gain_part, grad_qkv = attention_backward(
        weights, kept_state, dy.reshape(inputs_x.shape), dy_low.reshape(inputs_x.shape)
    )
    section_out = result.reshape((1,) + inputs_x.shape)
    input_grads = jnp.where(
        is_first, grad_x, grad_x.astype(jnp.bfloat16).astype(jnp.float32)
    )[None]
    gain_parts = jnp.pad(
        jnp.concatenate([attn_gain_part[None], ffn_gain_part], 0), ((0, 6), (0, 0))
    )
    gate_qkv_sum, down_out_sum, gain_sums = summed_grads(
        lax.axis_size("group"),
        lax.axis_size("dp"),
        hidden_turned,
        attention_turned,
        normed_two_turned,
        normed_turned,
        dz,
        dy_low,
        grad_gate,
        grad_up,
        flat(grad_qkv),
        gain_parts,
    )
    gain_cols = attn_gain.shape[1] * lax.axis_size("dp")
    gain_sums = lax.dynamic_slice_in_dim(
        gain_sums, lax.axis_index("group") * gain_cols, gain_cols, 1
    )
    gate_width = gate_up.shape[2]
    down_rows = down_weight.shape[1] * lax.axis_size("dp")
    reduced = (
        gain_sums[0],
        gate_qkv_sum[:, gate_width:].astype(jnp.float32),
        down_out_sum[down_rows:].astype(jnp.float32),
        gain_sums[1],
        gate_qkv_sum[:, :gate_width].astype(jnp.float32),
        down_out_sum[:down_rows].astype(jnp.float32),
    )
    return (section_out, input_grads) + tuple((shard_sum[None] for shard_sum in reduced))


def solution(mesh):
    placed = (
        P(("group", "dp"), None, None),
        P(("group", "dp"), None, None),
        P(("group", "dp")),
        P("section", ("group", "dp")),
        P("section", ("group", "dp"), None),
        P("section", ("group", "dp"), None),
        P("section", ("group", "dp")),
        P("section", ("group", "dp"), None),
        P("section", ("group", "dp"), None),
    )
    return jax.shard_map(
        body,
        mesh=mesh,
        in_specs=placed,
        out_specs=(
            P("section", ("group", "dp"), None, None),
            P("section", ("group", "dp"), None, None),
            P("section", "group"),
            P("section", "group", None),
            P("section", "group", None),
            P("section", "group"),
            P("section", "group", None),
            P("section", "group", None),
        ),
        check_vma=False,
    )
```

```python
import functools

import jax
import jax.numpy as jnp
from jax import lax
from jax.experimental import pallas as pl
from jax.experimental.pallas import tpu as pltpu
from jax.sharding import PartitionSpec as P

H = 16
KVH = 8
HD = 96


norm_eps = 1e-05
rope_base = 100000.0
masked_score = -1e30
across = (((1,), (1,)), ((), ()))
down_rows = (((0,), (0,)), ((), ()))


def passed_along(value, axis, by):
    length = lax.axis_size(axis)
    pairs = [(i, i + by) for i in range(length) if 0 <= i + by < length]
    return lax.ppermute(value, axis, pairs)


def padding(lengths, slot_count):
    position = jnp.arange(slot_count, dtype=jnp.int32)
    return (position[None, :] < lengths[:, None]).astype(jnp.float32)[..., None]


FF_CHUNK = 512
across = (((1,), (1,)), ((), ()))
down_rows = (((0,), (0,)), ((), ()))


def scaled_norm(value, gain):
    scale = lax.rsqrt(jnp.mean(value * value, -1, keepdims=True) + norm_eps)
    return scale, (value * scale * gain).astype(jnp.bfloat16)


def ffn_forward_kernel(y, gain, mask, wg, wu, wd, out, n2, acc):
    j = pl.program_id(0)

    @pl.when(j == 0)
    def _():
        n2[...] = scaled_norm(y[...], gain[...])[1]
        acc[...] = y[...]

    gate = jnp.dot(n2[...], wg[...], preferred_element_type=jnp.float32)
    up = jnp.dot(n2[...], wu[...], preferred_element_type=jnp.float32)
    hidden = (gate / (1.0 + jnp.exp(-gate)) * up).astype(jnp.bfloat16)
    acc[...] += jnp.dot(hidden, wd[...], preferred_element_type=jnp.float32)

    @pl.when(j == pl.num_programs(0) - 1)
    def _():
        out[...] = (acc[...] * mask[...]).astype(jnp.bfloat16)


def ffn_specs(tokens, width, hidden):
    steps = hidden // FF_CHUNK
    whole = pl.BlockSpec((tokens, width), lambda j: (0, 0))
    row = pl.BlockSpec((1, width), lambda j: (0, 0))
    weights = [
        pl.BlockSpec((width, FF_CHUNK), lambda j: (0, j)),
        pl.BlockSpec((width, FF_CHUNK), lambda j: (0, j + steps)),
        pl.BlockSpec((FF_CHUNK, width), lambda j: (j, 0)),
    ]
    return steps, whole, row, weights


def ffn_forward(y, gain, mask, gate_up_w, down_w):
    tokens, width = y.shape
    hidden = down_w.shape[0]
    steps, whole, row, weights = ffn_specs(tokens, width, hidden)
    return pl.pallas_call(
        ffn_forward_kernel,
        grid=(steps,),
        out_shape=jax.ShapeDtypeStruct((tokens, width), jnp.bfloat16),
        in_specs=[whole, row, pl.BlockSpec((tokens, 1), lambda j: (0, 0))] + weights,
        out_specs=whole,
        scratch_shapes=[pltpu.VMEM((tokens, width), jnp.bfloat16), pltpu.VMEM((tokens, width), jnp.float32)],
        compiler_params=pltpu.CompilerParams(vmem_limit_bytes=40 * 1024 * 1024),
        cost_estimate=pl.CostEstimate(
            flops=6 * tokens * width * hidden, bytes_accessed=6 * width * hidden, transcendentals=tokens * hidden
        ),
    )(y, gain, mask, gate_up_w, gate_up_w, down_w)


def ffn_backward_kernel(keep, y, dz, gain, mask, wg, wu, wd, dy, dyb, gain_grad, *rest):
    if keep:
        at, dgate, dup, n2t, out, n2, scale, acc, zacc = rest
    else:
        n2, scale, acc = rest
    j = pl.program_id(0)
    bf16, f32 = jnp.bfloat16, jnp.float32

    @pl.when(j == 0)
    def _():
        r, n = scaled_norm(y[...], gain[...])
        n2[...] = n
        scale[...] = r
        acc[...] = jnp.zeros_like(acc)
        if keep:
            n2t[...] = n.T
            zacc[...] = y[...]

    gate = jnp.dot(n2[...], wg[...], preferred_element_type=f32)
    up = jnp.dot(n2[...], wu[...], preferred_element_type=f32)
    grad = lax.dot_general(dz[...], wd[...], across, preferred_element_type=f32)
    sig = 1.0 / (1.0 + jnp.exp(-gate))
    silu = gate * sig
    grad_gate = (grad * up * sig * (1.0 + gate * (1.0 - sig))).astype(bf16)
    grad_up = (grad * silu).astype(bf16)
    if keep:
        hidden = (silu * up).astype(bf16)
        at[...] = hidden.T
        dgate[...] = grad_gate
        dup[...] = grad_up
        zacc[...] += jnp.dot(hidden, wd[...], preferred_element_type=f32)
    acc[...] += lax.dot_general(grad_gate, wg[...], across, preferred_element_type=f32) + lax.dot_general(
        grad_up, wu[...], across, preferred_element_type=f32
    )

    @pl.when(j == pl.num_programs(0) - 1)
    def _():
        value, r, grad_normed = y[...], scale[...], acc[...]
        scaled = grad_normed * gain[...]
        gain_grad[...] = jnp.sum(grad_normed * value * r, axis=0, keepdims=True)
        inner = jnp.mean(value * scaled, -1, keepdims=True)
        total = dz[...].astype(f32) + r * scaled - value * (r * r * r) * inner
        dy[...] = total
        dyb[...] = total.astype(bf16)
        if keep:
            out[...] = (zacc[...] * mask[...]).astype(bf16)


def ffn_backward(y, dz, gain, mask, gate_up_w, down_w, keep):
    tokens, width = y.shape
    hidden = down_w.shape[0]
    steps, whole, row, weights = ffn_specs(tokens, width, hidden)
    shape, bf16, f32 = jax.ShapeDtypeStruct, jnp.bfloat16, jnp.float32
    outs = [shape((tokens, width), f32), shape((tokens, width), bf16), shape((1, width), f32)]
    out_specs = [whole, whole, row]
    scratch = [pltpu.VMEM((tokens, width), bf16), pltpu.VMEM((tokens, 1), f32), pltpu.VMEM((tokens, width), f32)]
    if keep:
        part = pl.BlockSpec((tokens, FF_CHUNK), lambda j: (0, j))
        outs += [
            shape((hidden, tokens), bf16), shape((tokens, hidden), bf16), shape((tokens, hidden), bf16),
            shape((width, tokens), bf16), shape((tokens, width), bf16),
        ]
        out_specs += [
            pl.BlockSpec((FF_CHUNK, tokens), lambda j: (j, 0)), part, part,
            pl.BlockSpec((width, tokens), lambda j: (0, 0)), whole,
        ]
        scratch += [pltpu.VMEM((tokens, width), f32)]
    return pl.pallas_call(
        functools.partial(ffn_backward_kernel, keep),
        grid=(steps,),
        out_shape=tuple(outs),
        in_specs=[whole, whole, row, pl.BlockSpec((tokens, 1), lambda j: (0, 0))] + weights,
        out_specs=tuple(out_specs),
        scratch_shapes=scratch,
        compiler_params=pltpu.CompilerParams(vmem_limit_bytes=48 * 1024 * 1024),
        cost_estimate=pl.CostEstimate(
            flops=10 * tokens * width * hidden, bytes_accessed=6 * width * hidden, transcendentals=tokens * hidden
        ),
    )(y, dz, gain, mask, gate_up_w, gate_up_w, down_w)


def turned_tables(slots, rows):
    half_width = HD // 2
    frequency = rope_base ** (-(jnp.arange(half_width, dtype=jnp.float32) * 2.0 / HD))
    angles = frequency[:, None] * jnp.arange(slots, dtype=jnp.float32)[None, :]
    return jnp.tile(jnp.cos(angles), (1, rows)), jnp.tile(jnp.sin(angles), (1, rows))


def pair_mask(length, slots):
    groups = H // KVH
    key = lax.broadcasted_iota(jnp.int32, (slots, groups * slots), 0)
    query = lax.rem(lax.broadcasted_iota(jnp.int32, (slots, groups * slots), 1), slots)
    return (key <= query) & (key < length)


def pair_of(ref, k, row, slots):
    groups = H // KVH
    first = groups * k * HD
    return jnp.concatenate(
        [ref[first + g * HD : first + (g + 1) * HD, row * slots : (row + 1) * slots] for g in range(groups)], 1
    )


def key_value(qkvt, k, row, slots):
    tokens = slice(row * slots, (row + 1) * slots)
    keys = qkvt[(H + k) * HD : (H + k + 1) * HD, tokens]
    values = qkvt[(H + KVH + k) * HD : (H + KVH + k + 1) * HD, tokens]
    return keys, values


def pair_scores(keys, queries, mask):
    scores = lax.dot_general(keys, queries, down_rows, preferred_element_type=jnp.float32) * HD ** (-0.5)
    return jnp.where(mask, scores, masked_score)


def attention_forward_kernel(rows, info, x, gain, cosines, sines, w, wo, y, qkvt, lse, ot, n1t, n1):
    j = pl.program_id(0)
    bf16, f32 = jnp.bfloat16, jnp.float32
    slots, part, half = x.shape[0] // rows, KVH * HD, HD // 2
    groups = H // KVH

    @pl.when(j == 0)
    def _():
        n = scaled_norm(x[...].astype(f32), gain[...])[1]
        n1[...] = n
        n1t[...] = n.T

    chunk = jnp.dot(n1[...], w[...], preferred_element_type=f32).T

    @pl.when(j <= groups)
    def _():
        for h in range(KVH):
            front, back = chunk[h * HD : h * HD + half], chunk[h * HD + half : (h + 1) * HD]
            base = j * part + h * HD
            qkvt[pl.ds(pl.multiple_of(base, 16), half), :] = (front * cosines[...] - back * sines[...]).astype(bf16)
            qkvt[pl.ds(pl.multiple_of(base + half, 16), half), :] = (
                back * cosines[...] + front * sines[...]
            ).astype(bf16)

    @pl.when(j > groups)
    def _():
        qkvt[pl.ds(pl.multiple_of(j * part, 16), part), :] = chunk.astype(bf16)
        for row in range(rows):
            mask = pair_mask(info[row], slots)
            for k in range(KVH):
                keys, values = key_value(qkvt, k, row, slots)
                scores = pair_scores(keys, pair_of(qkvt, k, row, slots), mask)
                top = jnp.max(scores, 0, keepdims=True)
                total = top + jnp.log(jnp.sum(jnp.exp(scores - top), 0, keepdims=True))
                lse[row * KVH + k : row * KVH + k + 1, :] = total
                probs = jnp.exp(scores - total).astype(bf16)
                out = jnp.dot(values, probs, preferred_element_type=f32).astype(bf16)
                for g in range(groups):
                    first = (groups * k + g) * HD
                    ot[first : first + HD, row * slots : (row + 1) * slots] = out[:, g * slots : (g + 1) * slots]
        y[...] = x[...].astype(f32) + lax.dot_general(ot[...], wo[...], down_rows, preferred_element_type=f32)


def attention_backward_kernel(
    rows, keep, info, x, gain, dy, dyb, cosines, sines, qkvt, lse, wo, w, dx, *rest
):
    if keep:
        gain_grad, dqkv, dot, dqkvt, acc = rest
    else:
        dqkv, dot, dqkvt, acc = rest
    j = pl.program_id(0)
    bf16, f32 = jnp.bfloat16, jnp.float32
    slots, part, half = x.shape[0] // rows, KVH * HD, HD // 2
    groups = H // KVH

    def unrotated(grad, row, width):
        tokens = slice(row * slots, (row + 1) * slots)
        cos, sin = cosines[:, tokens], sines[:, tokens]
        if width > slots:
            cos, sin = jnp.concatenate([cos] * groups, 1), jnp.concatenate([sin] * groups, 1)
        grad = grad * HD ** (-0.5)
        front, back = grad[:half], grad[half:]
        return (front * cos + back * sin).astype(bf16), (back * cos - front * sin).astype(bf16)

    @pl.when(j == 0)
    def _():
        dot[...] = lax.dot_general(dyb[...], wo[...], across, preferred_element_type=f32).astype(bf16).T
        acc[...] = jnp.zeros_like(acc)
        for row in range(rows):
            tokens = slice(row * slots, (row + 1) * slots)
            mask = pair_mask(info[row], slots)
            for k in range(KVH):
                keys, values = key_value(qkvt, k, row, slots)
                queries, grads = pair_of(qkvt, k, row, slots), pair_of(dot, k, row, slots)
                scores = pair_scores(keys, queries, mask)
                probs = jnp.exp(scores - lse[row * KVH + k : row * KVH + k + 1, :])
                grad_probs = lax.dot_general(values, grads, down_rows, preferred_element_type=f32)
                grad_scores = (
                    probs * (grad_probs - jnp.sum(probs * grad_probs, 0, keepdims=True))
                ).astype(bf16)
                grad_values = lax.dot_general(grads, probs.astype(bf16), across, preferred_element_type=f32)
                grad_keys = lax.dot_general(queries, grad_scores, across, preferred_element_type=f32)
                grad_queries = jnp.dot(keys, grad_scores, preferred_element_type=f32)
                front, back = unrotated(grad_queries, row, groups * slots)
                for g in range(groups):
                    first = (groups * k + g) * HD
                    dqkvt[first : first + half, tokens] = front[:, g * slots : (g + 1) * slots]
                    dqkvt[first + half : first + HD, tokens] = back[:, g * slots : (g + 1) * slots]
                front, back = unrotated(grad_keys, row, slots)
                first = (H + k) * HD
                dqkvt[first : first + half, tokens] = front
                dqkvt[first + half : first + HD, tokens] = back
                first = (H + KVH + k) * HD
                dqkvt[first : first + HD, tokens] = grad_values.astype(bf16)
        for i in range(groups + 2):
            dqkv[:, i * part : (i + 1) * part] = dqkvt[i * part : (i + 1) * part, :].T

    columns = pl.ds(pl.multiple_of(j * part, 128), part)
    acc[...] += lax.dot_general(dqkv[:, columns], w[...], across, preferred_element_type=f32)

    @pl.when(j == pl.num_programs(0) - 1)
    def _():
        value, grad_normed = x[...].astype(f32), acc[...]
        r = lax.rsqrt(jnp.mean(value * value, -1, keepdims=True) + norm_eps)
        scaled = grad_normed * gain[...]
        inner = jnp.mean(value * scaled, -1, keepdims=True)
        total = dy[...] + (r * scaled - value * (r * r * r) * inner)
        if keep:
            gain_grad[...] = jnp.sum(grad_normed * value * r, axis=0, keepdims=True)
            dx[...] = jnp.where(info[rows] == 1, total, total.astype(bf16).astype(f32))
        else:
            dx[...] = total.astype(bf16)


def attention_specs(tokens, width):
    part = KVH * HD
    whole = lambda *shape: pl.BlockSpec(shape, lambda j: (0,) * len(shape))
    return part, whole, pl.BlockSpec(memory_space=pltpu.SMEM), pl.BlockSpec((width, part), lambda j: (0, j))


def attention_forward(info, x, gain, tables, qkv_w, output_weight, rows):
    tokens, width = x.shape
    cols, slots = qkv_w.shape[1], tokens // rows
    part, whole, scalars, weight = attention_specs(tokens, width)
    shape, bf16, f32 = jax.ShapeDtypeStruct, jnp.bfloat16, jnp.float32
    stats = (rows * KVH, H // KVH * slots)
    return pl.pallas_call(
        functools.partial(attention_forward_kernel, rows),
        grid=(cols // part,),
        out_shape=(
            shape((tokens, width), f32), shape((cols, tokens), bf16), shape(stats, f32),
            shape((H * HD, tokens), bf16), shape((width, tokens), bf16),
        ),
        in_specs=[
            scalars, whole(tokens, width), whole(1, width), whole(HD // 2, tokens), whole(HD // 2, tokens), weight,
            whole(H * HD, width),
        ],
        out_specs=(
            whole(tokens, width), whole(cols, tokens), whole(*stats), whole(H * HD, tokens), whole(width, tokens)
        ),
        scratch_shapes=[pltpu.VMEM((tokens, width), bf16)],
        compiler_params=pltpu.CompilerParams(vmem_limit_bytes=40 * 1024 * 1024),
        cost_estimate=pl.CostEstimate(
            flops=2 * tokens * width * (cols + H * HD), bytes_accessed=2 * width * (cols + H * HD), transcendentals=0
        ),
    )(info, x, gain, *tables, qkv_w, output_weight)


def attention_backward(info, x, gain, dy, dy_low, tables, qkvt, lse, output_weight, qkv_w, rows, keep):
    tokens, width = x.shape
    cols = qkv_w.shape[1]
    part, whole, scalars, weight = attention_specs(tokens, width)
    shape, bf16, f32 = jax.ShapeDtypeStruct, jnp.bfloat16, jnp.float32
    scratch = [pltpu.VMEM((H * HD, tokens), bf16), pltpu.VMEM((cols, tokens), bf16), pltpu.VMEM((tokens, width), f32)]
    outs, out_specs = [shape((tokens, width), f32 if keep else bf16)], [whole(tokens, width)]
    if keep:
        outs += [shape((1, width), f32), shape((tokens, cols), bf16)]
        out_specs += [whole(1, width), whole(tokens, cols)]
    else:
        scratch = [pltpu.VMEM((tokens, cols), bf16)] + scratch
    return pl.pallas_call(
        functools.partial(attention_backward_kernel, rows, keep),
        grid=(cols // part,),
        out_shape=tuple(outs),
        in_specs=[
            scalars, whole(tokens, width), whole(1, width), whole(tokens, width), whole(tokens, width),
            whole(HD // 2, tokens), whole(HD // 2, tokens), whole(cols, tokens), whole(*lse.shape), whole(H * HD, width),
            weight,
        ],
        out_specs=tuple(out_specs),
        scratch_shapes=scratch,
        compiler_params=pltpu.CompilerParams(vmem_limit_bytes=48 * 1024 * 1024),
        cost_estimate=pl.CostEstimate(
            flops=2 * tokens * width * (cols + H * HD), bytes_accessed=2 * width * (cols + H * HD), transcendentals=0
        ),
    )(info, x, gain, dy, dy_low, *tables, qkvt, lse, output_weight, qkv_w)


def flat(array):
    return array.reshape(-1, array.shape[-1])


MESH = pl.DeviceIdType.MESH
LANES = 128


def grad_plan(groups, dp, tokens, width, hidden, qkv_cols):
    pairs = dp // 2
    block = width // groups
    down_block = hidden // groups
    gate_cols = 2 * hidden // 2 // pairs
    qkv_part = qkv_cols // 2 // pairs
    pieces_gate = gate_cols // LANES
    pieces_qkv = qkv_part // LANES
    pieces = pieces_gate + pieces_qkv
    z_rows = LANES
    while down_block % z_rows or block % z_rows:
        z_rows //= 2
    row_chunks = (down_block + block) // z_rows
    half = width // 2
    z_split = max(1, pieces // row_chunks)
    while half % (z_split * LANES):
        z_split -= 1
    return dict(
        groups=groups, pairs=pairs, tokens=tokens, width=width, hidden=hidden, qkv_cols=qkv_cols, block=block,
        down_block=down_block, gate_cols=gate_cols, qkv_part=qkv_part, pieces_gate=pieces_gate, pieces=pieces,
        z_rows=z_rows, z_split=z_split, z_cols=half // z_split, z_pieces=row_chunks * z_split,
        down_chunks=down_block // z_rows, half=half,
    )


YS_RING = 4
HOP = 2
LEAD = 2


def grad_kernel(
    plan, at, ot, n2t, n1t, dz, dy, dgate, dup, dq, gp, outy, outz, outg,
    LT, RH, YS, YR, YRT, YLT, ZRT, ZLT, ZX,
    own_sem, xs, xr, ys_s, ys_r, yr_s, yr_r, yl_s, yl_r, zr_s, zr_r, zl_s, zl_r,
    zx_s, zx_r, ag_s, ag_r, sib_s, sib_r, lo,
    GC, GA, GS, GR, GL, gc_sem, ga_s, ga_r, gr_sem, gl_sem,
):
    G, A, T = plan["groups"], plan["pairs"], plan["tokens"]
    width, hidden, half = plan["width"], plan["hidden"], plan["half"]
    block, nY, nZ = plan["block"], plan["pieces"], plan["z_pieces"]
    zr, zc = plan["z_rows"], plan["z_cols"]
    s, z, d = lax.axis_index("section"), lax.axis_index("group"), lax.axis_index("dp")
    c, a = lax.rem(d, 2), lax.div(d, 2)
    sib = (s, z, 2 * a + 1 - c)
    right, left = (s, z + 1, d), (s, z - 1, d)

    def peer(k):
        return (s, z, 2 * lax.rem(a + k, A) + c)

    def remote(src, dst, ss, rs, dev):
        return pltpu.make_async_remote_copy(
            src_ref=src, dst_ref=dst, send_sem=ss, recv_sem=rs, device_id=dev, device_id_type=MESH
        )

    barrier = pltpu.get_barrier_semaphore()
    for dev in [sib, (s, lax.rem(z + 1, G), d), (s, lax.rem(z + G - 1, G), d)] + [peer(k) for k in range(1, A)]:
        pl.semaphore_signal(barrier, inc=1, device_id=dev, device_id_type=MESH)
    pl.semaphore_wait(barrier, A + 2)

    lhs = [(at, 0, hidden), (ot, hidden, width), (n2t, hidden + width, width), (n1t, hidden + 2 * width, width)]
    rhs = [(dz, 0, half), (dy, half, half), (None, width, hidden), (dq, width + hidden, plan["qkv_cols"] // 2)]
    order = [(0, 0), (2, 2), (1, 1), (3, 3)]
    own, cross = {}, {}
    for i, (ref, row, rows) in enumerate(lhs):
        own[0, i] = pltpu.make_async_copy(ref, LT.at[pl.ds(row, rows), pl.ds(0, T)], own_sem.at[i])
        cross[0, i] = remote(ref, LT.at[pl.ds(row, rows), pl.ds(T, T)], xs.at[i], xr.at[i], sib)
    for i, (ref, col, cols) in enumerate(rhs):
        if ref is None:
            continue
        mine = pl.ds(pl.multiple_of(c * cols, LANES), cols)
        theirs = pl.ds(pl.multiple_of((1 - c) * cols, LANES), cols)
        own[1, i] = pltpu.make_async_copy(ref.at[:, mine], RH.at[pl.ds(0, T), pl.ds(col, cols)], own_sem.at[4 + i])
        cross[1, i] = remote(ref.at[:, theirs], RH.at[pl.ds(T, T), pl.ds(col, cols)], xs.at[4 + i], xr.at[4 + i], sib)
    col, cols = rhs[2][1:]
    for core, (mine, theirs) in enumerate(((dgate, dup), (dup, dgate))):
        own[1, 2, core] = pltpu.make_async_copy(mine, RH.at[pl.ds(0, T), pl.ds(col, cols)], own_sem.at[6])
        cross[1, 2, core] = remote(theirs, RH.at[pl.ds(T, T), pl.ds(col, cols)], xs.at[6], xr.at[6], sib)
    own[1, 2], cross[1, 2] = own[1, 2, 0], cross[1, 2, 0]
    for i, _ in order:
        for side in (0, 1):
            if (side, i) == (1, 2):
                for core in (0, 1):
                    @pl.when(c == core)
                    def _(core=core):
                        own[1, 2, core].start()
                        cross[1, 2, core].start()
            else:
                own[side, i].start()
                cross[side, i].start()

    def operands_here(i):
        for side in (0, 1):
            own[side, i].wait()
            cross[side, i].wait_recv()

    def product(row, rows, col, cols):
        return jnp.dot(
            LT[pl.ds(row, rows), :], RH[:, pl.ds(col, cols)], preferred_element_type=jnp.float32
        )

    def y_product(q, which, b):
        is_gate = q < plan["pieces_gate"]
        row = jnp.where(is_gate, hidden + width, hidden + 2 * width) + b * block
        col = jnp.where(
            is_gate,
            width + which * plan["gate_cols"] + q * LANES,
            width + hidden + which * plan["qkv_part"] + (q - plan["pieces_gate"]) * LANES,
        )
        return product(pl.multiple_of(row, 16), block, pl.multiple_of(col, LANES), LANES)

    def z_product(p, b):
        r, h = lax.div(p, plan["z_split"]), lax.rem(p, plan["z_split"])
        is_down = r < plan["down_chunks"]
        row = jnp.where(
            is_down, b * plan["down_block"] + r * zr, hidden + b * block + (r - plan["down_chunks"]) * zr
        )
        col = jnp.where(is_down, 0, half) + h * zc
        return product(pl.multiple_of(row, 16), zr, pl.multiple_of(col, LANES), zc)

    def y_out(q, part, core):
        is_gate = q < plan["pieces_gate"]
        col = jnp.where(
            is_gate,
            core * hidden + part * plan["gate_cols"] + q * LANES,
            2 * hidden + core * (plan["qkv_cols"] // 2) + part * plan["qkv_part"] + (q - plan["pieces_gate"]) * LANES,
        )
        return outy.at[:, pl.ds(pl.multiple_of(col, LANES), LANES)]

    def z_out(p, core):
        r, h = lax.div(p, plan["z_split"]), lax.rem(p, plan["z_split"])
        return outz.at[
            pl.ds(pl.multiple_of(r * zr, 16), zr), pl.ds(pl.multiple_of(core * half + h * zc, LANES), zc)
        ]

    def y_send(q, k):
        return remote(YS.at[lax.rem(q, YS_RING), k - 1], YR.at[q, k - 1], ys_s.at[q, k - 1], ys_r.at[q, k - 1], peer(k))

    def line_copies(slots_r, slots_l, r_s, r_r, l_s, l_r, first_r, first_l, p):
        out_r, in_r, out_l, in_l = [], [], [], []
        for k in range(G):
            if k < G - 1:
                src = first_r(p) if k == 0 else slots_r.at[p, pl.ds(k, G - 1 - k)]
                out_r.append((k, remote(src, slots_r.at[p, pl.ds(k, G - 1 - k)], r_s.at[p], r_r.at[p], right)))
                held = slots_l.at[p, pl.ds(0, k + 1)]
                in_l.append((k, remote(held, held, l_s.at[p], l_r.at[p], left)))
            if k > 0:
                src = first_l(p) if k == G - 1 else slots_l.at[p, pl.ds(0, k)]
                out_l.append((k, remote(src, slots_l.at[p, pl.ds(0, k)], l_s.at[p], l_r.at[p], left)))
                held = slots_r.at[p, pl.ds(k - 1, G - k)]
                in_r.append((k, remote(held, held, r_s.at[p], r_r.at[p], right)))
        return out_r, in_r, out_l, in_l

    def at_place(copies, act):
        for k, copy in copies:
            @pl.when(z == k)
            def _(copy=copy):
                act(copy)

    def y_line(q):
        return line_copies(
            YRT, YLT, yr_s, yr_r, yl_s, yl_r,
            lambda q: YR.at[q, 0, pl.ds(1, G - 1)], lambda q: YR.at[q, 0, pl.ds(0, G - 1)], q,
        )

    def z_line(p):
        return line_copies(
            ZRT, ZLT, zr_s, zr_r, zl_s, zl_r,
            lambda p: ZRT.at[p, pl.ds(0, G - 1)], lambda p: ZLT.at[p, pl.ds(0, G - 1)], p,
        )

    def zx_copy(p, k):
        return remote(ZX.at[p, a], ZX.at[p, a], zx_s.at[p, k - 1], zx_r.at[p, k - 1], peer(k))

    def ag_copy(q, k):
        return remote(YR.at[q, 0, z], y_out(q, a, c), ag_s.at[q, k - 1], ag_r.at[q, k - 1], peer(k))

    def sib_own(q):
        return remote(YR.at[q, 0, z], y_out(q, a, c), sib_s.at[q, 0], sib_r.at[q, 0], sib)

    def sib_pass(q, k):
        part = lax.rem(a + A - k, A)
        return remote(y_out(q, part, c), y_out(q, part, c), sib_s.at[q, k], sib_r.at[q, k], sib)

    def own_y(q):
        return pltpu.make_async_copy(YR.at[q, 0, z], y_out(q, a, c), lo.at[q])

    def own_z(p):
        return pltpu.make_async_copy(ZX.at[p, a], z_out(p, c), lo.at[nY + p])

    def sib_z(p):
        return remote(ZX.at[p, a], z_out(p, c), sib_s.at[nY + p, 0], sib_r.at[nY + p, 0], sib)

    f32, bf16 = jnp.float32, jnp.bfloat16
    far = jnp.maximum(z, G - 1 - z)

    def live(index, count):
        return (index >= 0) & (index < count)

    def gain_core():
        return remote(gp, GC, gc_sem.at[0], gc_sem.at[1], sib)

    def gain_part(k):
        return remote(GA.at[a], GA.at[a], ga_s.at[k - 1], ga_r.at[k - 1], peer(k))

    def gain_right():
        return remote(GS.at[1], GR, gr_sem.at[0], gr_sem.at[1], right)

    def gain_left():
        return remote(GS.at[2], GL, gl_sem.at[0], gl_sem.at[1], left)

    def gain_step(t):
        @pl.when(t == 0)
        def _():
            gain_core().start()

        @pl.when(t == 1)
        def _():
            gain_core().wait_recv()
            GA[a] = gp[...] + GC[...]
            for k in range(1, A):
                gain_part(k).start()

        @pl.when(t == 2)
        def _():
            for k in range(1, A):
                remote(
                    GA.at[lax.rem(a + A - k, A)], GA.at[lax.rem(a + A - k, A)], ga_s.at[k - 1], ga_r.at[k - 1], peer(k)
                ).wait_recv()
            total = GA[0]
            for k in range(1, A):
                total += GA[k]
            GS[0] = total

        @pl.when(t == 2 + HOP * z)
        def _():
            @pl.when(z > 0)
            def _():
                gain_right().wait_recv()
                GS[1] = GS[0] + GR[...]

            @pl.when(z == 0)
            def _():
                GS[1] = GS[0]

            @pl.when(z < G - 1)
            def _():
                gain_right().start()

        @pl.when(t == 2 + HOP * (G - 1 - z))
        def _():
            @pl.when(z < G - 1)
            def _():
                gain_left().wait_recv()
                GS[2] = GS[0] + GL[...]

            @pl.when(z == G - 1)
            def _():
                GS[2] = GS[0]

            @pl.when(z > 0)
            def _():
                gain_left().start()

        @pl.when(t == 3 + HOP * (G - 1))
        def _():
            outg[...] = GS[1] + jnp.where(z < G - 1, GL[...], 0.0)

    def step(t, carry):
        gain_step(t)

        @pl.when(t == 0)
        def _():
            operands_here(0)
            operands_here(2)

        @pl.when(t == 1)
        def _():
            operands_here(1)
            operands_here(3)

        q1 = t

        @pl.when(live(q1, nY))
        def _():
            for k in range(1, A):
                @pl.when(q1 >= YS_RING)
                def _():
                    y_send(q1 - YS_RING, k).wait_send()

                @pl.loop(0, G)
                def _(b):
                    YS[lax.rem(q1, YS_RING), k - 1, b] = y_product(q1, lax.rem(a + k, A), b).astype(bf16)

                y_send(q1, k).start()

        pr = t - HOP * z

        @pl.when(live(pr, nZ))
        def _():
            out_r, in_r, _, _ = z_line(pr)
            at_place(in_r, lambda copy: copy.wait_recv())

            @pl.loop(0, G)
            def _(b):
                @pl.when((b > z) & (z > 0))
                def _():
                    ZRT[pr, b - 1] = (z_product(pr, b) + ZRT[pr, b - 1].astype(f32)).astype(bf16)

                @pl.when((b > z) & (z == 0))
                def _():
                    ZRT[pr, b - 1] = z_product(pr, b).astype(bf16)

            at_place(out_r, lambda copy: copy.start())

        pL = t - HOP * (G - 1 - z)

        @pl.when(live(pL, nZ))
        def _():
            _, _, out_l, in_l = z_line(pL)
            at_place(in_l, lambda copy: copy.wait_recv())

            @pl.loop(0, G)
            def _(b):
                @pl.when((b < z) & (z < G - 1))
                def _():
                    ZLT[pL, b] = (z_product(pL, b) + ZLT[pL, b].astype(f32)).astype(bf16)

                @pl.when((b < z) & (z == G - 1))
                def _():
                    ZLT[pL, b] = z_product(pL, b).astype(bf16)

            at_place(out_l, lambda copy: copy.start())

        q2 = t - LEAD

        @pl.when(live(q2, nY))
        def _():
            for k in range(1, A):
                y_send(q2, k).wait_recv()

            @pl.loop(0, G)
            def _(b):
                total = y_product(q2, a, b)
                for k in range(1, A):
                    total += YR[q2, k - 1, b].astype(f32)
                YR[q2, 0, b] = total.astype(bf16)

        qr = t - LEAD - HOP * z

        @pl.when(live(qr, nY))
        def _():
            out_r, in_r, _, _ = y_line(qr)
            at_place(in_r, lambda copy: copy.wait_recv())

            @pl.loop(0, G)
            def _(b):
                @pl.when((b > z) & (z > 0))
                def _():
                    YRT[qr, b - 1] = (YR[qr, 0, b].astype(f32) + YRT[qr, b - 1].astype(f32)).astype(bf16)

            at_place(out_r, lambda copy: copy.start())

        qL = t - LEAD - HOP * (G - 1 - z)

        @pl.when(live(qL, nY))
        def _():
            _, _, out_l, in_l = y_line(qL)
            at_place(in_l, lambda copy: copy.wait_recv())

            @pl.loop(0, G)
            def _(b):
                @pl.when((b < z) & (z < G - 1))
                def _():
                    YLT[qL, b] = (YR[qL, 0, b].astype(f32) + YLT[qL, b].astype(f32)).astype(bf16)

            at_place(out_l, lambda copy: copy.start())

        pf = t - HOP * far

        @pl.when(live(pf, nZ))
        def _():
            mine = z_product(pf, z)
            from_left = ZRT[pf, jnp.maximum(z - 1, 0)].astype(f32)
            from_right = ZLT[pf, jnp.minimum(z, G - 2)].astype(f32)
            mine = mine + jnp.where(z > 0, from_left, 0.0) + jnp.where(z < G - 1, from_right, 0.0)
            ZX[pf, a] = mine.astype(bf16)
            for k in range(1, A):
                zx_copy(pf, k).start()

        pg = t - HOP * far - LEAD

        @pl.when(live(pg, nZ))
        def _():
            for k in range(1, A):
                remote(
                    ZX.at[pg, lax.rem(a + A - k, A)], ZX.at[pg, lax.rem(a + A - k, A)],
                    zx_s.at[pg, k - 1], zx_r.at[pg, k - 1], peer(k),
                ).wait_recv()
            total = ZX[pg, 0].astype(f32)
            for k in range(1, A):
                total += ZX[pg, k].astype(f32)
            for k in range(1, A):
                zx_copy(pg, k).wait_send()
            ZX[pg, a] = total.astype(bf16)
            own_z(pg).start()
            sib_z(pg).start()

        qf = t - LEAD - HOP * far

        @pl.when(live(qf, nY))
        def _():
            total = YR[qf, 0, z].astype(f32)
            from_left = YRT[qf, jnp.maximum(z - 1, 0)].astype(f32)
            from_right = YLT[qf, jnp.minimum(z, G - 2)].astype(f32)
            total = total + jnp.where(z > 0, from_left, 0.0) + jnp.where(z < G - 1, from_right, 0.0)
            YR[qf, 0, z] = total.astype(bf16)
            for k in range(1, A):
                ag_copy(qf, k).start()
            own_y(qf).start()
            sib_own(qf).start()

        qg = t - LEAD - HOP * far - LEAD

        @pl.when(live(qg, nY))
        def _():
            for k in range(1, A):
                here = y_out(qg, lax.rem(a + A - k, A), c)
                remote(here, here, ag_s.at[qg, k - 1], ag_r.at[qg, k - 1], peer(k)).wait_recv()
                sib_pass(qg, k).start()

        return carry

    steps = max(nY, nZ) + 2 * LEAD + HOP * (G - 1)
    lax.fori_loop(0, steps, step, 0)

    gain_core().wait_send()
    for k in range(1, A):
        gain_part(k).wait_send()

    @pl.when(z < G - 1)
    def _():
        gain_right().wait_send()

    @pl.when(z > 0)
    def _():
        gain_left().wait_send()

    for i in range(4):
        for side in (0, 1):
            cross[side, i].wait_send()

    def drain_y(q, carry):
        for k in range(1, A):
            @pl.when(q >= nY - YS_RING)
            def _():
                y_send(q, k).wait_send()

            ag_copy(q, k).wait_send()
            sib_pass(q, k).wait_send()
            there = y_out(q, lax.rem(a + A - k, A), 1 - c)
            remote(there, there, sib_s.at[q, k], sib_r.at[q, k], sib).wait_recv()
        out_r, _, out_l, _ = y_line(q)
        at_place(out_r, lambda copy: copy.wait_send())
        at_place(out_l, lambda copy: copy.wait_send())
        own_y(q).wait()
        sib_own(q).wait_send()
        there = y_out(q, a, 1 - c)
        remote(there, there, sib_s.at[q, 0], sib_r.at[q, 0], sib).wait_recv()
        return carry

    lax.fori_loop(0, nY, drain_y, 0)

    def drain_z(p, carry):
        out_r, _, out_l, _ = z_line(p)
        at_place(out_r, lambda copy: copy.wait_send())
        at_place(out_l, lambda copy: copy.wait_send())
        own_z(p).wait()
        sib_z(p).wait_send()
        there = z_out(p, 1 - c)
        remote(there, there, sib_s.at[nY + p, 0], sib_r.at[nY + p, 0], sib).wait_recv()
        return carry

    lax.fori_loop(0, nZ, drain_z, 0)


def summed_grads(groups, dp, at, ot, n2t, n1t, dz, dy, dgate, dup, dq, gain_parts):
    hidden, tokens = at.shape
    width, qkv_cols = ot.shape[0], dq.shape[1]
    plan = grad_plan(groups, dp, tokens, width, hidden, qkv_cols)
    G, A, nY, nZ = groups, plan["pairs"], plan["pieces"], plan["z_pieces"]
    block, zr, zc = plan["block"], plan["z_rows"], plan["z_cols"]
    bf16, DMA = jnp.bfloat16, pltpu.SemaphoreType.DMA
    any_space = pl.BlockSpec(memory_space=pl.ANY)
    in_vmem, f32, gain_shape = pl.BlockSpec(memory_space=pltpu.VMEM), jnp.float32, gain_parts.shape
    return pl.pallas_call(
        functools.partial(grad_kernel, plan),
        out_shape=(
            jax.ShapeDtypeStruct((block, 2 * hidden + qkv_cols), bf16),
            jax.ShapeDtypeStruct((plan["down_block"] + block, width), bf16),
            jax.ShapeDtypeStruct(gain_parts.shape, f32),
        ),
        in_specs=[any_space] * 9 + [in_vmem],
        out_specs=(any_space, any_space, in_vmem),
        scratch_shapes=[
            pltpu.VMEM((hidden + 3 * width, 2 * tokens), bf16),
            pltpu.VMEM((2 * tokens, width + hidden + qkv_cols // 2), bf16),
            pltpu.VMEM((YS_RING, A - 1, G, block, LANES), bf16),
            pltpu.VMEM((nY, A - 1, G, block, LANES), bf16),
            pltpu.VMEM((nY, G - 1, block, LANES), bf16),
            pltpu.VMEM((nY, G - 1, block, LANES), bf16),
            pltpu.VMEM((nZ, G - 1, zr, zc), bf16),
            pltpu.VMEM((nZ, G - 1, zr, zc), bf16),
            pltpu.VMEM((nZ, A, zr, zc), bf16),
            DMA((8,)), DMA((8,)), DMA((8,)),
            DMA((nY, A - 1)), DMA((nY, A - 1)),
            DMA((nY,)), DMA((nY,)), DMA((nY,)), DMA((nY,)),
            DMA((nZ,)), DMA((nZ,)), DMA((nZ,)), DMA((nZ,)),
            DMA((nZ, A - 1)), DMA((nZ, A - 1)),
            DMA((nY, A - 1)), DMA((nY, A - 1)),
            DMA((nY + nZ, A)), DMA((nY + nZ, A)),
            DMA((nY + nZ,)),
            pltpu.VMEM(gain_shape, f32),
            pltpu.VMEM((A,) + gain_shape, f32),
            pltpu.VMEM((3,) + gain_shape, f32),
            pltpu.VMEM(gain_shape, f32),
            pltpu.VMEM(gain_shape, f32),
            DMA((2,)), DMA((max(A - 1, 1),)), DMA((max(A - 1, 1),)), DMA((2,)), DMA((2,)),
        ],
        compiler_params=pltpu.CompilerParams(
            collective_id=3, has_side_effects=True, vmem_limit_bytes=63 * 1024 * 1024
        ),
        cost_estimate=pl.CostEstimate(
            flops=2 * 2 * tokens * (width * (2 * hidden + qkv_cols + width) + hidden * width) // 2,
            bytes_accessed=40_000_000, transcendentals=0,
        ),
    )(at, ot, n2t, n1t, dz, dy, dgate, dup, dq, gain_parts)


W_HOP = 5
gather_families = (
    (1, True, False),
    (2, True, True),
    (1, True, False),
    (8, True, False),
    (4, False, False),
)


def gather_kernel(groups, pairs, families, *refs):
    G, A, F = groups, pairs, len(families)
    shards, wholes = refs[:F], refs[F : 2 * F]
    sems = refs[2 * F :]
    s, z, d = lax.axis_index("section"), lax.axis_index("group"), lax.axis_index("dp")
    c, a = lax.rem(d, 2), lax.div(d, 2)
    sib = (s, z, 2 * a + 1 - c)
    right, left = (s, z + 1, d), (s, z - 1, d)

    def peer(part):
        return (s, z, 2 * part + c)

    barrier = pltpu.get_barrier_semaphore()
    others = [peer(lax.rem(a + k, A)) for k in range(1, A)]
    for dev in [sib, (s, lax.rem(z + 1, G), d), (s, lax.rem(z + G - 1, G), d)] + others:
        pl.semaphore_signal(barrier, inc=1, device_id=dev, device_id_type=MESH)
    pl.semaphore_wait(barrier, A + 2)

    def cut(f, ref, i):
        pieces, by_columns, _ = families[f]
        rows, cols = ref.shape
        if pieces == 1:
            return ref
        if by_columns:
            size = cols // pieces
            return ref.at[:, pl.ds(pl.multiple_of(i * size, 128), size)]
        size = rows // pieces
        return ref.at[pl.ds(pl.multiple_of(i * size, 16), size), :]

    def placed(f, i, o, part, core):
        return cut(f, wholes[f].at[(o * A + part) * 2 + core], i)

    def copy(f, i, o, part, kind, index, dev, own=False, core=None):
        core = c if core is None else core
        there = placed(f, i, o, part, core)
        src = cut(f, shards[f], i) if own else there
        send, recv = sems[f * 9 + 2 * kind], sems[f * 9 + 2 * kind + 1]
        return pltpu.make_async_remote_copy(
            src_ref=src, dst_ref=there, send_sem=send.at[index], recv_sem=recv.at[index], device_id=dev, device_id_type=MESH
        )

    def to_right(f, i, o, part, own=False):
        return copy(f, i, o, part, 0, (i, o, lax.rem(part + A - a, A)), right, own)

    def to_left(f, i, o, part, own=False):
        return copy(f, i, o, part, 1, (i, o, lax.rem(part + A - a, A)), left, own)

    def to_part(f, i, o, k, own=False):
        return copy(f, i, o, a, 2, (i, o, k - 1), peer(lax.rem(a + k, A)), own)

    def from_part(f, i, o, k):
        return copy(f, i, o, lax.rem(a + A - k, A), 2, (i, o, k - 1), peer(lax.rem(a + A - k, A)))

    def to_core(f, i, o, part, own=False):
        return copy(f, i, o, part, 3, (i, o, lax.rem(part + A - a, A)), sib, own)

    def from_core(f, i, o, k):
        part = lax.rem(a + k, A)
        return copy(f, i, o, part, 3, (i, o, k), sib, core=1 - c)

    def own_copy(f, i):
        return pltpu.make_async_copy(cut(f, shards[f], i), placed(f, i, z, a, c), sems[f * 9 + 8].at[i])

    def along(f, i, o, part, own, go_right, go_left):
        if go_right:
            @pl.when(z < G - 1)
            def _():
                to_right(f, i, o, part, own).start()
        if go_left:
            @pl.when(z > 0)
            def _():
                to_left(f, i, o, part, own).start()

    first = []
    total = 0
    for pieces, _, _ in families:
        first.append(total)
        total += pieces

    def step(t, carry):
        for f, (pieces, _, parts_first) in enumerate(families):
            i0 = t - first[f]

            @pl.when((i0 >= 0) & (i0 < pieces))
            def _(f=f, i0=i0):
                along(f, i0, z, a, True, True, True)
                for k in range(1, A):
                    to_part(f, i0, z, k, True).start()
                to_core(f, i0, z, a, True).start()
                own_copy(f, i0).start()

        for f, (pieces, _, parts_first) in enumerate(families):
            for h in range(G):
                for k in range(A if parts_first else 1):
                    if h == 0:
                        continue
                    i = t - first[f] - W_HOP * h - (W_HOP if k > 0 else 0)
                    part = lax.rem(a + k, A)
                    for sign in (-1, 1):
                        o = z + sign * h

                        @pl.when((i >= 0) & (i < pieces) & (o >= 0) & (o < G))
                        def _(f=f, i=i, o=o, part=part, sign=sign, parts_first=parts_first):
                            if sign < 0:
                                to_right(f, i, o, part).wait_recv()
                                along(f, i, o, part, False, True, False)
                            else:
                                to_left(f, i, o, part).wait_recv()
                                along(f, i, o, part, False, False, True)
                            if not parts_first:
                                for j in range(1, A):
                                    to_part(f, i, o, j).start()
                            to_core(f, i, o, part).start()

                if parts_first and h > 0:
                    continue
                i = t - first[f] - W_HOP * (h + 1)
                for sign in (-1, 1) if h else (1,):
                    o = z + sign * h

                    @pl.when((i >= 0) & (i < pieces) & (o >= 0) & (o < G))
                    def _(f=f, i=i, o=o, parts_first=parts_first):
                        for k in range(1, A):
                            from_part(f, i, o, k).wait_recv()
                            part = lax.rem(a + A - k, A)
                            if parts_first:
                                along(f, i, o, part, False, True, True)
                            to_core(f, i, o, part).start()
        return carry

    lax.fori_loop(0, total + W_HOP * (G + 1), step, 0)

    for f, (pieces, _, parts_first) in enumerate(families):
        def drain(i, carry, f=f, parts_first=parts_first):
            own_copy(f, i).wait()

            def by_group(o, carry):
                for k in range(A):
                    part = lax.rem(a + k, A)
                    to_core(f, i, o, part).wait_send()
                    from_core(f, i, o, k).wait_recv()
                    if parts_first or k == 0:
                        @pl.when((z < G - 1) & (o <= z))
                        def _(part=part):
                            to_right(f, i, o, part).wait_send()

                        @pl.when((z > 0) & (o >= z))
                        def _(part=part):
                            to_left(f, i, o, part).wait_send()
                for k in range(1, A):
                    if parts_first:
                        @pl.when(o == z)
                        def _(k=k):
                            to_part(f, i, o, k).wait_send()
                    else:
                        to_part(f, i, o, k).wait_send()
                return carry

            return lax.fori_loop(0, G, by_group, carry)

        lax.fori_loop(0, pieces, drain, 0)


def gathered(groups, dp, shards, families):
    A, DMA = dp // 2, pltpu.SemaphoreType.DMA
    any_space = pl.BlockSpec(memory_space=pl.ANY)
    scratch = []
    for pieces, _, parts_first in families:
        on_line = (pieces, groups, A if parts_first else 1)
        scratch += [DMA(on_line)] * 4 + [DMA((pieces, groups, max(A - 1, 1)))] * 2 + [DMA((pieces, groups, A))] * 2
        scratch += [DMA((pieces,))]
    return pl.pallas_call(
        functools.partial(gather_kernel, groups, A, families),
        out_shape=tuple(jax.ShapeDtypeStruct((groups * dp,) + x.shape, x.dtype) for x in shards),
        in_specs=[any_space] * len(shards),
        out_specs=(any_space,) * len(shards),
        scratch_shapes=scratch,
        compiler_params=pltpu.CompilerParams(collective_id=5, has_side_effects=True),
    )(*shards)


def body(
    inputs_x, cotangent, lengths, attn_gain, qkv_weight, out_weight, ffn_gain, gate_up, down_weight
):
    is_first = lax.axis_index("section") == 0
    gains = jnp.concatenate([attn_gain, ffn_gain], 0)
    gains = jnp.pad(gains, ((0, 14), (0, -gains.shape[1] % 128)))
    gains, qkv_all, out_all, gate_up_all, down_all = gathered(
        lax.axis_size("group"),
        lax.axis_size("dp"),
        (gains, qkv_weight[0], out_weight[0], gate_up[0], down_weight[0]),
        gather_families,
    )
    gain_part = attn_gain.shape[1]
    weights = (
        gains[:, 0, :gain_part].reshape(-1),
        flat(qkv_all),
        flat(out_all),
        gains[:, 1, :gain_part].reshape(-1),
        flat(gate_up_all),
        flat(down_all),
    )
    rows, slots, width = inputs_x.shape
    tables = turned_tables(slots, rows)
    info = jnp.concatenate([lengths, is_first.astype(jnp.int32)[None]])
    mask = padding(lengths, slots).reshape(-1, 1)
    gain_one = weights[0].astype(jnp.float32).reshape(1, -1)
    gain_two = weights[3].astype(jnp.float32).reshape(1, -1)
    qkv_w, output_weight, _, gate_up_w, down_w = weights[1:]
    dz_given = (flat(cotangent).astype(jnp.float32) * mask).astype(jnp.bfloat16)
    after_one = attention_forward(info, flat(inputs_x), gain_one, tables, qkv_w, output_weight, rows)[0]
    first_out = ffn_forward(after_one, gain_two, mask, gate_up_w, down_w)
    recv_act = passed_along(first_out, "section", 1)
    layer_in = jnp.where(is_first, flat(inputs_x), recv_act)
    after, heads, log_total, attention_turned, normed_turned = attention_forward(
        info, layer_in, gain_one, tables, qkv_w, output_weight, rows
    )
    dy, dy_low, _ = ffn_backward(after, dz_given, gain_two, mask, gate_up_w, down_w, False)
    (second_dx,) = attention_backward(
        info, layer_in, gain_one, dy, dy_low, tables, heads, log_total, output_weight, qkv_w, rows, False
    )
    recv_grad = passed_along(second_dx, "section", -1)
    dz = jnp.where(is_first, (recv_grad.astype(jnp.float32) * mask).astype(jnp.bfloat16), dz_given)
    dy, dy_low, ffn_gain_part, hidden_turned, grad_gate, grad_up, normed_two_turned, result = ffn_backward(
        after, dz, gain_two, mask, gate_up_w, down_w, True
    )
    grad_x, attn_gain_part, grad_qkv = attention_backward(
        info, layer_in, gain_one, dy, dy_low, tables, heads, log_total, output_weight, qkv_w, rows, True
    )
    section_out = result.reshape((1,) + inputs_x.shape)
    input_grads = grad_x.reshape((1,) + inputs_x.shape)
    gain_parts = jnp.pad(jnp.concatenate([attn_gain_part, ffn_gain_part], 0), ((0, 6), (0, 0)))
    gate_qkv_sum, down_out_sum, gain_sums = summed_grads(
        lax.axis_size("group"),
        lax.axis_size("dp"),
        hidden_turned,
        attention_turned,
        normed_two_turned,
        normed_turned,
        dz,
        dy_low,
        grad_gate,
        grad_up,
        grad_qkv,
        gain_parts,
    )
    gain_cols = attn_gain.shape[1] * lax.axis_size("dp")
    gain_sums = lax.dynamic_slice_in_dim(
        gain_sums, lax.axis_index("group") * gain_cols, gain_cols, 1
    )
    gate_width = gate_up.shape[2]
    down_rows = down_weight.shape[1] * lax.axis_size("dp")
    reduced = (
        gain_sums[0],
        gate_qkv_sum[:, gate_width:].astype(jnp.float32),
        down_out_sum[down_rows:].astype(jnp.float32),
        gain_sums[1],
        gate_qkv_sum[:, :gate_width].astype(jnp.float32),
        down_out_sum[:down_rows].astype(jnp.float32),
    )
    return (section_out, input_grads) + tuple((shard_sum[None] for shard_sum in reduced))


def solution(mesh):
    placed = (
        P(("group", "dp"), None, None),
        P(("group", "dp"), None, None),
        P(("group", "dp")),
        P("section", ("group", "dp")),
        P("section", ("group", "dp"), None),
        P("section", ("group", "dp"), None),
        P("section", ("group", "dp")),
        P("section", ("group", "dp"), None),
        P("section", ("group", "dp"), None),
    )
    return jax.shard_map(
        body,
        mesh=mesh,
        in_specs=placed,
        out_specs=(
            P("section", ("group", "dp"), None, None),
            P("section", ("group", "dp"), None, None),
            P("section", "group"),
            P("section", "group", None),
            P("section", "group", None),
            P("section", "group"),
            P("section", "group", None),
            P("section", "group", None),
        ),
        check_vma=False,
    )
```

```python
import functools

import jax
import jax.numpy as jnp
from jax import lax
from jax.experimental import pallas as pl
from jax.experimental.pallas import tpu as pltpu
from jax.sharding import PartitionSpec as P

H = 16
KVH = 8
HD = 96


norm_eps = 1e-05
rope_base = 100000.0
masked_score = -1e30
across = (((1,), (1,)), ((), ()))
down_rows = (((0,), (0,)), ((), ()))


def passed_along(value, axis, by):
    length = lax.axis_size(axis)
    pairs = [(i, i + by) for i in range(length) if 0 <= i + by < length]
    return lax.ppermute(value, axis, pairs)


def padding(lengths, slot_count):
    position = jnp.arange(slot_count, dtype=jnp.int32)
    return (position[None, :] < lengths[:, None]).astype(jnp.float32)[..., None]


FF_CHUNK = 512
across = (((1,), (1,)), ((), ()))
down_rows = (((0,), (0,)), ((), ()))


def scaled_norm(value, gain):
    scale = lax.rsqrt(jnp.mean(value * value, -1, keepdims=True) + norm_eps)
    return scale, (value * scale * gain).astype(jnp.bfloat16)


def ffn_forward_kernel(y, gain, mask, wg, wu, wd, out, n2, acc):
    j = pl.program_id(0)

    @pl.when(j == 0)
    def _():
        n2[...] = scaled_norm(y[...], gain[...])[1]
        acc[...] = y[...]

    gate = jnp.dot(n2[...], wg[...], preferred_element_type=jnp.float32)
    up = jnp.dot(n2[...], wu[...], preferred_element_type=jnp.float32)
    hidden = (gate / (1.0 + jnp.exp(-gate)) * up).astype(jnp.bfloat16)
    acc[...] += jnp.dot(hidden, wd[...], preferred_element_type=jnp.float32)

    @pl.when(j == pl.num_programs(0) - 1)
    def _():
        out[...] = (acc[...] * mask[...]).astype(jnp.bfloat16)


def ffn_specs(tokens, width, hidden):
    steps = hidden // FF_CHUNK
    whole = pl.BlockSpec((tokens, width), lambda j: (0, 0))
    row = pl.BlockSpec((1, width), lambda j: (0, 0))
    weights = [
        pl.BlockSpec((width, FF_CHUNK), lambda j: (0, j)),
        pl.BlockSpec((width, FF_CHUNK), lambda j: (0, j + steps)),
        pl.BlockSpec((FF_CHUNK, width), lambda j: (j, 0)),
    ]
    return steps, whole, row, weights


def ffn_forward(y, gain, mask, gate_up_w, down_w):
    tokens, width = y.shape
    hidden = down_w.shape[0]
    steps, whole, row, weights = ffn_specs(tokens, width, hidden)
    return pl.pallas_call(
        ffn_forward_kernel,
        grid=(steps,),
        out_shape=jax.ShapeDtypeStruct((tokens, width), jnp.bfloat16),
        in_specs=[whole, row, pl.BlockSpec((tokens, 1), lambda j: (0, 0))] + weights,
        out_specs=whole,
        scratch_shapes=[pltpu.VMEM((tokens, width), jnp.bfloat16), pltpu.VMEM((tokens, width), jnp.float32)],
        compiler_params=pltpu.CompilerParams(vmem_limit_bytes=40 * 1024 * 1024),
        cost_estimate=pl.CostEstimate(
            flops=6 * tokens * width * hidden, bytes_accessed=6 * width * hidden, transcendentals=tokens * hidden
        ),
    )(y, gain, mask, gate_up_w, gate_up_w, down_w)


def ffn_backward_kernel(keep, y, dz, gain, mask, wg, wu, wd, dy, dyb, gain_grad, *rest):
    if keep:
        at, dgate, dup, n2t, out, n2, scale, acc, zacc = rest
    else:
        n2, scale, acc = rest
    j = pl.program_id(0)
    bf16, f32 = jnp.bfloat16, jnp.float32

    @pl.when(j == 0)
    def _():
        r, n = scaled_norm(y[...], gain[...])
        n2[...] = n
        scale[...] = r
        acc[...] = jnp.zeros_like(acc)
        if keep:
            n2t[...] = n.T
            zacc[...] = y[...]

    gate = jnp.dot(n2[...], wg[...], preferred_element_type=f32)
    up = jnp.dot(n2[...], wu[...], preferred_element_type=f32)
    grad = lax.dot_general(dz[...], wd[...], across, preferred_element_type=f32)
    sig = 1.0 / (1.0 + jnp.exp(-gate))
    silu = gate * sig
    grad_gate = (grad * up * sig * (1.0 + gate * (1.0 - sig))).astype(bf16)
    grad_up = (grad * silu).astype(bf16)
    if keep:
        hidden = (silu * up).astype(bf16)
        at[...] = hidden.T
        dgate[...] = grad_gate
        dup[...] = grad_up
        zacc[...] += jnp.dot(hidden, wd[...], preferred_element_type=f32)
    acc[...] += lax.dot_general(grad_gate, wg[...], across, preferred_element_type=f32) + lax.dot_general(
        grad_up, wu[...], across, preferred_element_type=f32
    )

    @pl.when(j == pl.num_programs(0) - 1)
    def _():
        value, r, grad_normed = y[...], scale[...], acc[...]
        scaled = grad_normed * gain[...]
        gain_grad[...] = jnp.sum(grad_normed * value * r, axis=0, keepdims=True)
        inner = jnp.mean(value * scaled, -1, keepdims=True)
        total = dz[...].astype(f32) + r * scaled - value * (r * r * r) * inner
        dy[...] = total
        dyb[...] = total.astype(bf16)
        if keep:
            out[...] = (zacc[...] * mask[...]).astype(bf16)


def ffn_backward(y, dz, gain, mask, gate_up_w, down_w, keep):
    tokens, width = y.shape
    hidden = down_w.shape[0]
    steps, whole, row, weights = ffn_specs(tokens, width, hidden)
    shape, bf16, f32 = jax.ShapeDtypeStruct, jnp.bfloat16, jnp.float32
    outs = [shape((tokens, width), f32), shape((tokens, width), bf16), shape((1, width), f32)]
    out_specs = [whole, whole, row]
    scratch = [pltpu.VMEM((tokens, width), bf16), pltpu.VMEM((tokens, 1), f32), pltpu.VMEM((tokens, width), f32)]
    if keep:
        part = pl.BlockSpec((tokens, FF_CHUNK), lambda j: (0, j))
        outs += [
            shape((hidden, tokens), bf16), shape((tokens, hidden), bf16), shape((tokens, hidden), bf16),
            shape((width, tokens), bf16), shape((tokens, width), bf16),
        ]
        out_specs += [
            pl.BlockSpec((FF_CHUNK, tokens), lambda j: (j, 0)), part, part,
            pl.BlockSpec((width, tokens), lambda j: (0, 0)), whole,
        ]
        scratch += [pltpu.VMEM((tokens, width), f32)]
    return pl.pallas_call(
        functools.partial(ffn_backward_kernel, keep),
        grid=(steps,),
        out_shape=tuple(outs),
        in_specs=[whole, whole, row, pl.BlockSpec((tokens, 1), lambda j: (0, 0))] + weights,
        out_specs=tuple(out_specs),
        scratch_shapes=scratch,
        compiler_params=pltpu.CompilerParams(vmem_limit_bytes=48 * 1024 * 1024),
        cost_estimate=pl.CostEstimate(
            flops=10 * tokens * width * hidden, bytes_accessed=6 * width * hidden, transcendentals=tokens * hidden
        ),
    )(y, dz, gain, mask, gate_up_w, gate_up_w, down_w)


def turned_tables(slots, rows):
    half_width = HD // 2
    frequency = rope_base ** (-(jnp.arange(half_width, dtype=jnp.float32) * 2.0 / HD))
    angles = frequency[:, None] * jnp.arange(slots, dtype=jnp.float32)[None, :]
    return jnp.tile(jnp.cos(angles), (1, rows)), jnp.tile(jnp.sin(angles), (1, rows))


def pair_mask(length, slots):
    groups = H // KVH
    key = lax.broadcasted_iota(jnp.int32, (slots, groups * slots), 0)
    query = lax.rem(lax.broadcasted_iota(jnp.int32, (slots, groups * slots), 1), slots)
    return (key <= query) & (key < length)


def pair_of(ref, k, row, slots):
    groups = H // KVH
    first = groups * k * HD
    return jnp.concatenate(
        [ref[first + g * HD : first + (g + 1) * HD, row * slots : (row + 1) * slots] for g in range(groups)], 1
    )


def key_value(qkvt, k, row, slots):
    tokens = slice(row * slots, (row + 1) * slots)
    keys = qkvt[(H + k) * HD : (H + k + 1) * HD, tokens]
    values = qkvt[(H + KVH + k) * HD : (H + KVH + k + 1) * HD, tokens]
    return keys, values


def pair_scores(keys, queries, mask):
    scores = lax.dot_general(keys, queries, down_rows, preferred_element_type=jnp.float32) * HD ** (-0.5)
    return jnp.where(mask, scores, masked_score)


def attention_forward_kernel(rows, info, x, gain, cosines, sines, w, wo, y, qkvt, lse, ot, n1t, n1):
    j = pl.program_id(0)
    bf16, f32 = jnp.bfloat16, jnp.float32
    slots, part, half = x.shape[0] // rows, KVH * HD, HD // 2
    groups = H // KVH

    @pl.when(j == 0)
    def _():
        n = scaled_norm(x[...].astype(f32), gain[...])[1]
        n1[...] = n
        n1t[...] = n.T

    chunk = jnp.dot(n1[...], w[...], preferred_element_type=f32).T

    @pl.when(j <= groups)
    def _():
        for h in range(KVH):
            front, back = chunk[h * HD : h * HD + half], chunk[h * HD + half : (h + 1) * HD]
            base = j * part + h * HD
            qkvt[pl.ds(pl.multiple_of(base, 16), half), :] = (front * cosines[...] - back * sines[...]).astype(bf16)
            qkvt[pl.ds(pl.multiple_of(base + half, 16), half), :] = (
                back * cosines[...] + front * sines[...]
            ).astype(bf16)

    @pl.when(j > groups)
    def _():
        qkvt[pl.ds(pl.multiple_of(j * part, 16), part), :] = chunk.astype(bf16)
        for row in range(rows):
            mask = pair_mask(info[row], slots)
            for k in range(KVH):
                keys, values = key_value(qkvt, k, row, slots)
                scores = pair_scores(keys, pair_of(qkvt, k, row, slots), mask)
                top = jnp.max(scores, 0, keepdims=True)
                total = top + jnp.log(jnp.sum(jnp.exp(scores - top), 0, keepdims=True))
                lse[row * KVH + k : row * KVH + k + 1, :] = total
                probs = jnp.exp(scores - total).astype(bf16)
                out = jnp.dot(values, probs, preferred_element_type=f32).astype(bf16)
                for g in range(groups):
                    first = (groups * k + g) * HD
                    ot[first : first + HD, row * slots : (row + 1) * slots] = out[:, g * slots : (g + 1) * slots]
        y[...] = x[...].astype(f32) + lax.dot_general(ot[...], wo[...], down_rows, preferred_element_type=f32)


def attention_backward_kernel(
    rows, keep, info, x, gain, dy, dyb, cosines, sines, qkvt, lse, wo, w, dx, *rest
):
    if keep:
        gain_grad, dqkv, dot, dqkvt, acc = rest
    else:
        dqkv, dot, dqkvt, acc = rest
    j = pl.program_id(0)
    bf16, f32 = jnp.bfloat16, jnp.float32
    slots, part, half = x.shape[0] // rows, KVH * HD, HD // 2
    groups = H // KVH

    def unrotated(grad, row, width):
        tokens = slice(row * slots, (row + 1) * slots)
        cos, sin = cosines[:, tokens], sines[:, tokens]
        if width > slots:
            cos, sin = jnp.concatenate([cos] * groups, 1), jnp.concatenate([sin] * groups, 1)
        grad = grad * HD ** (-0.5)
        front, back = grad[:half], grad[half:]
        return (front * cos + back * sin).astype(bf16), (back * cos - front * sin).astype(bf16)

    @pl.when(j == 0)
    def _():
        dot[...] = lax.dot_general(dyb[...], wo[...], across, preferred_element_type=f32).astype(bf16).T
        acc[...] = jnp.zeros_like(acc)
        for row in range(rows):
            tokens = slice(row * slots, (row + 1) * slots)
            mask = pair_mask(info[row], slots)
            for k in range(KVH):
                keys, values = key_value(qkvt, k, row, slots)
                queries, grads = pair_of(qkvt, k, row, slots), pair_of(dot, k, row, slots)
                scores = pair_scores(keys, queries, mask)
                probs = jnp.exp(scores - lse[row * KVH + k : row * KVH + k + 1, :])
                grad_probs = lax.dot_general(values, grads, down_rows, preferred_element_type=f32)
                grad_scores = (
                    probs * (grad_probs - jnp.sum(probs * grad_probs, 0, keepdims=True))
                ).astype(bf16)
                grad_values = lax.dot_general(grads, probs.astype(bf16), across, preferred_element_type=f32)
                grad_keys = lax.dot_general(queries, grad_scores, across, preferred_element_type=f32)
                grad_queries = jnp.dot(keys, grad_scores, preferred_element_type=f32)
                front, back = unrotated(grad_queries, row, groups * slots)
                for g in range(groups):
                    first = (groups * k + g) * HD
                    dqkvt[first : first + half, tokens] = front[:, g * slots : (g + 1) * slots]
                    dqkvt[first + half : first + HD, tokens] = back[:, g * slots : (g + 1) * slots]
                front, back = unrotated(grad_keys, row, slots)
                first = (H + k) * HD
                dqkvt[first : first + half, tokens] = front
                dqkvt[first + half : first + HD, tokens] = back
                first = (H + KVH + k) * HD
                dqkvt[first : first + HD, tokens] = grad_values.astype(bf16)
        for i in range(groups + 2):
            dqkv[:, i * part : (i + 1) * part] = dqkvt[i * part : (i + 1) * part, :].T

    columns = pl.ds(pl.multiple_of(j * part, 128), part)
    acc[...] += lax.dot_general(dqkv[:, columns], w[...], across, preferred_element_type=f32)

    @pl.when(j == pl.num_programs(0) - 1)
    def _():
        value, grad_normed = x[...].astype(f32), acc[...]
        r = lax.rsqrt(jnp.mean(value * value, -1, keepdims=True) + norm_eps)
        scaled = grad_normed * gain[...]
        inner = jnp.mean(value * scaled, -1, keepdims=True)
        total = dy[...] + (r * scaled - value * (r * r * r) * inner)
        if keep:
            gain_grad[...] = jnp.sum(grad_normed * value * r, axis=0, keepdims=True)
            dx[...] = jnp.where(info[rows] == 1, total, total.astype(bf16).astype(f32))
        else:
            dx[...] = total.astype(bf16)


def attention_specs(tokens, width):
    part = KVH * HD
    whole = lambda *shape: pl.BlockSpec(shape, lambda j: (0,) * len(shape))
    return part, whole, pl.BlockSpec(memory_space=pltpu.SMEM), pl.BlockSpec((width, part), lambda j: (0, j))


def attention_forward(info, x, gain, tables, qkv_w, output_weight, rows):
    tokens, width = x.shape
    cols, slots = qkv_w.shape[1], tokens // rows
    part, whole, scalars, weight = attention_specs(tokens, width)
    shape, bf16, f32 = jax.ShapeDtypeStruct, jnp.bfloat16, jnp.float32
    stats = (rows * KVH, H // KVH * slots)
    return pl.pallas_call(
        functools.partial(attention_forward_kernel, rows),
        grid=(cols // part,),
        out_shape=(
            shape((tokens, width), f32), shape((cols, tokens), bf16), shape(stats, f32),
            shape((H * HD, tokens), bf16), shape((width, tokens), bf16),
        ),
        in_specs=[
            scalars, whole(tokens, width), whole(1, width), whole(HD // 2, tokens), whole(HD // 2, tokens), weight,
            whole(H * HD, width),
        ],
        out_specs=(
            whole(tokens, width), whole(cols, tokens), whole(*stats), whole(H * HD, tokens), whole(width, tokens)
        ),
        scratch_shapes=[pltpu.VMEM((tokens, width), bf16)],
        compiler_params=pltpu.CompilerParams(vmem_limit_bytes=40 * 1024 * 1024),
        cost_estimate=pl.CostEstimate(
            flops=2 * tokens * width * (cols + H * HD), bytes_accessed=2 * width * (cols + H * HD), transcendentals=0
        ),
    )(info, x, gain, *tables, qkv_w, output_weight)


def attention_backward(info, x, gain, dy, dy_low, tables, qkvt, lse, output_weight, qkv_w, rows, keep):
    tokens, width = x.shape
    cols = qkv_w.shape[1]
    part, whole, scalars, weight = attention_specs(tokens, width)
    shape, bf16, f32 = jax.ShapeDtypeStruct, jnp.bfloat16, jnp.float32
    scratch = [pltpu.VMEM((H * HD, tokens), bf16), pltpu.VMEM((cols, tokens), bf16), pltpu.VMEM((tokens, width), f32)]
    outs, out_specs = [shape((tokens, width), f32 if keep else bf16)], [whole(tokens, width)]
    if keep:
        outs += [shape((1, width), f32), shape((tokens, cols), bf16)]
        out_specs += [whole(1, width), whole(tokens, cols)]
    else:
        scratch = [pltpu.VMEM((tokens, cols), bf16)] + scratch
    return pl.pallas_call(
        functools.partial(attention_backward_kernel, rows, keep),
        grid=(cols // part,),
        out_shape=tuple(outs),
        in_specs=[
            scalars, whole(tokens, width), whole(1, width), whole(tokens, width), whole(tokens, width),
            whole(HD // 2, tokens), whole(HD // 2, tokens), whole(cols, tokens), whole(*lse.shape), whole(H * HD, width),
            weight,
        ],
        out_specs=tuple(out_specs),
        scratch_shapes=scratch,
        compiler_params=pltpu.CompilerParams(vmem_limit_bytes=48 * 1024 * 1024),
        cost_estimate=pl.CostEstimate(
            flops=2 * tokens * width * (cols + H * HD), bytes_accessed=2 * width * (cols + H * HD), transcendentals=0
        ),
    )(info, x, gain, dy, dy_low, *tables, qkvt, lse, output_weight, qkv_w)


def flat(array):
    return array.reshape(-1, array.shape[-1])


MESH = pl.DeviceIdType.MESH
LANES = 128


def grad_plan(groups, dp, tokens, width, hidden, qkv_cols):
    pairs = dp // 2
    block = width // groups
    down_block = hidden // groups
    gate_cols = 2 * hidden // 2 // pairs
    qkv_part = qkv_cols // 2 // pairs
    pieces_gate = gate_cols // LANES
    pieces_qkv = qkv_part // LANES
    pieces = pieces_gate + pieces_qkv
    z_rows = LANES
    while down_block % z_rows or block % z_rows:
        z_rows //= 2
    row_chunks = (down_block + block) // z_rows
    half = width // 2
    z_split = max(1, pieces // row_chunks)
    while half % (z_split * LANES):
        z_split -= 1
    return dict(
        groups=groups, pairs=pairs, tokens=tokens, width=width, hidden=hidden, qkv_cols=qkv_cols, block=block,
        down_block=down_block, gate_cols=gate_cols, qkv_part=qkv_part, pieces_gate=pieces_gate, pieces=pieces,
        z_rows=z_rows, z_split=z_split, z_cols=half // z_split, z_pieces=row_chunks * z_split,
        down_chunks=down_block // z_rows, half=half,
    )


YS_RING = 4
HOP = 2
LEAD = 2


def grad_kernel(
    plan, at, ot, n2t, n1t, dz, dy, dgate, dup, dq, gp, outy, outz, outg,
    LT, RH, YS, YR, YRT, YLT, ZRT, ZLT, ZX,
    own_sem, xs, xr, ys_s, ys_r, yr_s, yr_r, yl_s, yl_r, zr_s, zr_r, zl_s, zl_r,
    zx_s, zx_r, ag_s, ag_r, sib_s, sib_r, lo,
    GC, GA, GS, GR, GL, gc_sem, ga_s, ga_r, gr_sem, gl_sem,
):
    G, A, T = plan["groups"], plan["pairs"], plan["tokens"]
    width, hidden, half = plan["width"], plan["hidden"], plan["half"]
    block, nY, nZ = plan["block"], plan["pieces"], plan["z_pieces"]
    zr, zc = plan["z_rows"], plan["z_cols"]
    s, z, d = lax.axis_index("section"), lax.axis_index("group"), lax.axis_index("dp")
    c, a = lax.rem(d, 2), lax.div(d, 2)
    sib = (s, z, 2 * a + 1 - c)
    right, left = (s, z + 1, d), (s, z - 1, d)

    def peer(k):
        return (s, z, 2 * lax.rem(a + k, A) + c)

    def remote(src, dst, ss, rs, dev):
        return pltpu.make_async_remote_copy(
            src_ref=src, dst_ref=dst, send_sem=ss, recv_sem=rs, device_id=dev, device_id_type=MESH
        )

    barrier = pltpu.get_barrier_semaphore()
    for dev in [sib, (s, lax.rem(z + 1, G), d), (s, lax.rem(z + G - 1, G), d)] + [peer(k) for k in range(1, A)]:
        pl.semaphore_signal(barrier, inc=1, device_id=dev, device_id_type=MESH)
    pl.semaphore_wait(barrier, A + 2)

    lhs = [(at, 0, hidden), (ot, hidden, width), (n2t, hidden + width, width), (n1t, hidden + 2 * width, width)]
    rhs = [(dz, 0, half), (dy, half, half), (None, width, hidden), (dq, width + hidden, plan["qkv_cols"] // 2)]
    order = [(0, 0), (2, 2), (1, 1), (3, 3)]
    own, cross = {}, {}
    for i, (ref, row, rows) in enumerate(lhs):
        own[0, i] = pltpu.make_async_copy(ref, LT.at[pl.ds(row, rows), pl.ds(0, T)], own_sem.at[i])
        cross[0, i] = remote(ref, LT.at[pl.ds(row, rows), pl.ds(T, T)], xs.at[i], xr.at[i], sib)
    for i, (ref, col, cols) in enumerate(rhs):
        if ref is None:
            continue
        mine = pl.ds(pl.multiple_of(c * cols, LANES), cols)
        theirs = pl.ds(pl.multiple_of((1 - c) * cols, LANES), cols)
        own[1, i] = pltpu.make_async_copy(ref.at[:, mine], RH.at[pl.ds(0, T), pl.ds(col, cols)], own_sem.at[4 + i])
        cross[1, i] = remote(ref.at[:, theirs], RH.at[pl.ds(T, T), pl.ds(col, cols)], xs.at[4 + i], xr.at[4 + i], sib)
    col, cols = rhs[2][1:]
    for core, (mine, theirs) in enumerate(((dgate, dup), (dup, dgate))):
        own[1, 2, core] = pltpu.make_async_copy(mine, RH.at[pl.ds(0, T), pl.ds(col, cols)], own_sem.at[6])
        cross[1, 2, core] = remote(theirs, RH.at[pl.ds(T, T), pl.ds(col, cols)], xs.at[6], xr.at[6], sib)
    own[1, 2], cross[1, 2] = own[1, 2, 0], cross[1, 2, 0]
    for i, _ in order:
        for side in (0, 1):
            if (side, i) == (1, 2):
                for core in (0, 1):
                    @pl.when(c == core)
                    def _(core=core):
                        own[1, 2, core].start()
                        cross[1, 2, core].start()
            else:
                own[side, i].start()
                cross[side, i].start()

    def operands_here(i):
        for side in (0, 1):
            own[side, i].wait()
            cross[side, i].wait_recv()

    def product(row, rows, col, cols):
        return jnp.dot(
            LT[pl.ds(row, rows), :], RH[:, pl.ds(col, cols)], preferred_element_type=jnp.float32
        )

    def y_product(q, which, b):
        is_gate = q < plan["pieces_gate"]
        row = jnp.where(is_gate, hidden + width, hidden + 2 * width) + b * block
        col = jnp.where(
            is_gate,
            width + which * plan["gate_cols"] + q * LANES,
            width + hidden + which * plan["qkv_part"] + (q - plan["pieces_gate"]) * LANES,
        )
        return product(pl.multiple_of(row, 16), block, pl.multiple_of(col, LANES), LANES)

    def z_product(p, b):
        r, h = lax.div(p, plan["z_split"]), lax.rem(p, plan["z_split"])
        is_down = r < plan["down_chunks"]
        row = jnp.where(
            is_down, b * plan["down_block"] + r * zr, hidden + b * block + (r - plan["down_chunks"]) * zr
        )
        col = jnp.where(is_down, 0, half) + h * zc
        return product(pl.multiple_of(row, 16), zr, pl.multiple_of(col, LANES), zc)

    def y_out(q, part, core):
        is_gate = q < plan["pieces_gate"]
        col = jnp.where(
            is_gate,
            core * hidden + part * plan["gate_cols"] + q * LANES,
            2 * hidden + core * (plan["qkv_cols"] // 2) + part * plan["qkv_part"] + (q - plan["pieces_gate"]) * LANES,
        )
        return outy.at[:, pl.ds(pl.multiple_of(col, LANES), LANES)]

    def z_out(p, core):
        r, h = lax.div(p, plan["z_split"]), lax.rem(p, plan["z_split"])
        return outz.at[
            pl.ds(pl.multiple_of(r * zr, 16), zr), pl.ds(pl.multiple_of(core * half + h * zc, LANES), zc)
        ]

    def y_send(q, k):
        return remote(YS.at[lax.rem(q, YS_RING), k - 1], YR.at[q, k - 1], ys_s.at[q, k - 1], ys_r.at[q, k - 1], peer(k))

    def line_copies(slots_r, slots_l, r_s, r_r, l_s, l_r, first_r, first_l, p):
        out_r, in_r, out_l, in_l = [], [], [], []
        for k in range(G):
            if k < G - 1:
                src = first_r(p) if k == 0 else slots_r.at[p, pl.ds(k, G - 1 - k)]
                out_r.append((k, remote(src, slots_r.at[p, pl.ds(k, G - 1 - k)], r_s.at[p], r_r.at[p], right)))
                held = slots_l.at[p, pl.ds(0, k + 1)]
                in_l.append((k, remote(held, held, l_s.at[p], l_r.at[p], left)))
            if k > 0:
                src = first_l(p) if k == G - 1 else slots_l.at[p, pl.ds(0, k)]
                out_l.append((k, remote(src, slots_l.at[p, pl.ds(0, k)], l_s.at[p], l_r.at[p], left)))
                held = slots_r.at[p, pl.ds(k - 1, G - k)]
                in_r.append((k, remote(held, held, r_s.at[p], r_r.at[p], right)))
        return out_r, in_r, out_l, in_l

    def at_place(copies, act):
        for k, copy in copies:
            @pl.when(z == k)
            def _(copy=copy):
                act(copy)

    def y_line(q):
        return line_copies(
            YRT, YLT, yr_s, yr_r, yl_s, yl_r,
            lambda q: YR.at[q, 0, pl.ds(1, G - 1)], lambda q: YR.at[q, 0, pl.ds(0, G - 1)], q,
        )

    def z_line(p):
        return line_copies(
            ZRT, ZLT, zr_s, zr_r, zl_s, zl_r,
            lambda p: ZRT.at[p, pl.ds(0, G - 1)], lambda p: ZLT.at[p, pl.ds(0, G - 1)], p,
        )

    def zx_copy(p, k):
        return remote(ZX.at[p, a], ZX.at[p, a], zx_s.at[p, k - 1], zx_r.at[p, k - 1], peer(k))

    def ag_copy(q, k):
        return remote(YR.at[q, 0, z], y_out(q, a, c), ag_s.at[q, k - 1], ag_r.at[q, k - 1], peer(k))

    def sib_own(q):
        return remote(YR.at[q, 0, z], y_out(q, a, c), sib_s.at[q, 0], sib_r.at[q, 0], sib)

    def sib_pass(q, k):
        part = lax.rem(a + A - k, A)
        return remote(y_out(q, part, c), y_out(q, part, c), sib_s.at[q, k], sib_r.at[q, k], sib)

    def own_y(q):
        return pltpu.make_async_copy(YR.at[q, 0, z], y_out(q, a, c), lo.at[q])

    def own_z(p):
        return pltpu.make_async_copy(ZX.at[p, a], z_out(p, c), lo.at[nY + p])

    def sib_z(p):
        return remote(ZX.at[p, a], z_out(p, c), sib_s.at[nY + p, 0], sib_r.at[nY + p, 0], sib)

    f32, bf16 = jnp.float32, jnp.bfloat16
    far = jnp.maximum(z, G - 1 - z)

    def live(index, count):
        return (index >= 0) & (index < count)

    def gain_core():
        return remote(gp, GC, gc_sem.at[0], gc_sem.at[1], sib)

    def gain_part(k):
        return remote(GA.at[a], GA.at[a], ga_s.at[k - 1], ga_r.at[k - 1], peer(k))

    def gain_right():
        return remote(GS.at[1], GR, gr_sem.at[0], gr_sem.at[1], right)

    def gain_left():
        return remote(GS.at[2], GL, gl_sem.at[0], gl_sem.at[1], left)

    def gain_step(t):
        @pl.when(t == 0)
        def _():
            gain_core().start()

        @pl.when(t == 1)
        def _():
            gain_core().wait_recv()
            GA[a] = gp[...] + GC[...]
            for k in range(1, A):
                gain_part(k).start()

        @pl.when(t == 2)
        def _():
            for k in range(1, A):
                remote(
                    GA.at[lax.rem(a + A - k, A)], GA.at[lax.rem(a + A - k, A)], ga_s.at[k - 1], ga_r.at[k - 1], peer(k)
                ).wait_recv()
            total = GA[0]
            for k in range(1, A):
                total += GA[k]
            GS[0] = total

        @pl.when(t == 2 + HOP * z)
        def _():
            @pl.when(z > 0)
            def _():
                gain_right().wait_recv()
                GS[1] = GS[0] + GR[...]

            @pl.when(z == 0)
            def _():
                GS[1] = GS[0]

            @pl.when(z < G - 1)
            def _():
                gain_right().start()

        @pl.when(t == 2 + HOP * (G - 1 - z))
        def _():
            @pl.when(z < G - 1)
            def _():
                gain_left().wait_recv()
                GS[2] = GS[0] + GL[...]

            @pl.when(z == G - 1)
            def _():
                GS[2] = GS[0]

            @pl.when(z > 0)
            def _():
                gain_left().start()

        @pl.when(t == 3 + HOP * (G - 1))
        def _():
            outg[...] = GS[1] + jnp.where(z < G - 1, GL[...], 0.0)

    def step(t, carry):
        gain_step(t)

        @pl.when(t == 0)
        def _():
            operands_here(0)
            operands_here(2)

        @pl.when(t == 1)
        def _():
            operands_here(1)
            operands_here(3)

        q1 = t

        @pl.when(live(q1, nY))
        def _():
            for k in range(1, A):
                @pl.when(q1 >= YS_RING)
                def _():
                    y_send(q1 - YS_RING, k).wait_send()

                @pl.loop(0, G)
                def _(b):
                    YS[lax.rem(q1, YS_RING), k - 1, b] = y_product(q1, lax.rem(a + k, A), b).astype(bf16)

                y_send(q1, k).start()

        pr = t - HOP * z

        @pl.when(live(pr, nZ))
        def _():
            out_r, in_r, _, _ = z_line(pr)
            at_place(in_r, lambda copy: copy.wait_recv())

            @pl.loop(0, G)
            def _(b):
                @pl.when((b > z) & (z > 0))
                def _():
                    ZRT[pr, b - 1] = (z_product(pr, b) + ZRT[pr, b - 1].astype(f32)).astype(bf16)

                @pl.when((b > z) & (z == 0))
                def _():
                    ZRT[pr, b - 1] = z_product(pr, b).astype(bf16)

            at_place(out_r, lambda copy: copy.start())

        pL = t - HOP * (G - 1 - z)

        @pl.when(live(pL, nZ))
        def _():
            _, _, out_l, in_l = z_line(pL)
            at_place(in_l, lambda copy: copy.wait_recv())

            @pl.loop(0, G)
            def _(b):
                @pl.when((b < z) & (z < G - 1))
                def _():
                    ZLT[pL, b] = (z_product(pL, b) + ZLT[pL, b].astype(f32)).astype(bf16)

                @pl.when((b < z) & (z == G - 1))
                def _():
                    ZLT[pL, b] = z_product(pL, b).astype(bf16)

            at_place(out_l, lambda copy: copy.start())

        q2 = t - LEAD

        @pl.when(live(q2, nY))
        def _():
            for k in range(1, A):
                y_send(q2, k).wait_recv()

            @pl.loop(0, G)
            def _(b):
                total = y_product(q2, a, b)
                for k in range(1, A):
                    total += YR[q2, k - 1, b].astype(f32)
                YR[q2, 0, b] = total.astype(bf16)

        qr = t - LEAD - HOP * z

        @pl.when(live(qr, nY))
        def _():
            out_r, in_r, _, _ = y_line(qr)
            at_place(in_r, lambda copy: copy.wait_recv())

            @pl.loop(0, G)
            def _(b):
                @pl.when((b > z) & (z > 0))
                def _():
                    YRT[qr, b - 1] = (YR[qr, 0, b].astype(f32) + YRT[qr, b - 1].astype(f32)).astype(bf16)

            at_place(out_r, lambda copy: copy.start())

        qL = t - LEAD - HOP * (G - 1 - z)

        @pl.when(live(qL, nY))
        def _():
            _, _, out_l, in_l = y_line(qL)
            at_place(in_l, lambda copy: copy.wait_recv())

            @pl.loop(0, G)
            def _(b):
                @pl.when((b < z) & (z < G - 1))
                def _():
                    YLT[qL, b] = (YR[qL, 0, b].astype(f32) + YLT[qL, b].astype(f32)).astype(bf16)

            at_place(out_l, lambda copy: copy.start())

        pf = t - HOP * far

        @pl.when(live(pf, nZ))
        def _():
            mine = z_product(pf, z)
            from_left = ZRT[pf, jnp.maximum(z - 1, 0)].astype(f32)
            from_right = ZLT[pf, jnp.minimum(z, G - 2)].astype(f32)
            mine = mine + jnp.where(z > 0, from_left, 0.0) + jnp.where(z < G - 1, from_right, 0.0)
            ZX[pf, a] = mine.astype(bf16)
            for k in range(1, A):
                zx_copy(pf, k).start()

        pg = t - HOP * far - LEAD

        @pl.when(live(pg, nZ))
        def _():
            for k in range(1, A):
                remote(
                    ZX.at[pg, lax.rem(a + A - k, A)], ZX.at[pg, lax.rem(a + A - k, A)],
                    zx_s.at[pg, k - 1], zx_r.at[pg, k - 1], peer(k),
                ).wait_recv()
            total = ZX[pg, 0].astype(f32)
            for k in range(1, A):
                total += ZX[pg, k].astype(f32)
            for k in range(1, A):
                zx_copy(pg, k).wait_send()
            ZX[pg, a] = total.astype(bf16)
            own_z(pg).start()
            sib_z(pg).start()

        qf = t - LEAD - HOP * far

        @pl.when(live(qf, nY))
        def _():
            total = YR[qf, 0, z].astype(f32)
            from_left = YRT[qf, jnp.maximum(z - 1, 0)].astype(f32)
            from_right = YLT[qf, jnp.minimum(z, G - 2)].astype(f32)
            total = total + jnp.where(z > 0, from_left, 0.0) + jnp.where(z < G - 1, from_right, 0.0)
            YR[qf, 0, z] = total.astype(bf16)
            for k in range(1, A):
                ag_copy(qf, k).start()
            own_y(qf).start()
            sib_own(qf).start()

        qg = t - LEAD - HOP * far - LEAD

        @pl.when(live(qg, nY))
        def _():
            for k in range(1, A):
                here = y_out(qg, lax.rem(a + A - k, A), c)
                remote(here, here, ag_s.at[qg, k - 1], ag_r.at[qg, k - 1], peer(k)).wait_recv()
                sib_pass(qg, k).start()

        return carry

    steps = max(nY, nZ) + 2 * LEAD + HOP * (G - 1)
    lax.fori_loop(0, steps, step, 0)

    gain_core().wait_send()
    for k in range(1, A):
        gain_part(k).wait_send()

    @pl.when(z < G - 1)
    def _():
        gain_right().wait_send()

    @pl.when(z > 0)
    def _():
        gain_left().wait_send()

    for i in range(4):
        for side in (0, 1):
            cross[side, i].wait_send()

    def drain_y(q, carry):
        for k in range(1, A):
            @pl.when(q >= nY - YS_RING)
            def _():
                y_send(q, k).wait_send()

            ag_copy(q, k).wait_send()
            sib_pass(q, k).wait_send()
            there = y_out(q, lax.rem(a + A - k, A), 1 - c)
            remote(there, there, sib_s.at[q, k], sib_r.at[q, k], sib).wait_recv()
        out_r, _, out_l, _ = y_line(q)
        at_place(out_r, lambda copy: copy.wait_send())
        at_place(out_l, lambda copy: copy.wait_send())
        own_y(q).wait()
        sib_own(q).wait_send()
        there = y_out(q, a, 1 - c)
        remote(there, there, sib_s.at[q, 0], sib_r.at[q, 0], sib).wait_recv()
        return carry

    lax.fori_loop(0, nY, drain_y, 0)

    def drain_z(p, carry):
        out_r, _, out_l, _ = z_line(p)
        at_place(out_r, lambda copy: copy.wait_send())
        at_place(out_l, lambda copy: copy.wait_send())
        own_z(p).wait()
        sib_z(p).wait_send()
        there = z_out(p, 1 - c)
        remote(there, there, sib_s.at[nY + p, 0], sib_r.at[nY + p, 0], sib).wait_recv()
        return carry

    lax.fori_loop(0, nZ, drain_z, 0)


def summed_grads(groups, dp, at, ot, n2t, n1t, dz, dy, dgate, dup, dq, gain_parts):
    hidden, tokens = at.shape
    width, qkv_cols = ot.shape[0], dq.shape[1]
    plan = grad_plan(groups, dp, tokens, width, hidden, qkv_cols)
    G, A, nY, nZ = groups, plan["pairs"], plan["pieces"], plan["z_pieces"]
    block, zr, zc = plan["block"], plan["z_rows"], plan["z_cols"]
    bf16, DMA = jnp.bfloat16, pltpu.SemaphoreType.DMA
    any_space = pl.BlockSpec(memory_space=pl.ANY)
    in_vmem, f32, gain_shape = pl.BlockSpec(memory_space=pltpu.VMEM), jnp.float32, gain_parts.shape
    return pl.pallas_call(
        functools.partial(grad_kernel, plan),
        out_shape=(
            jax.ShapeDtypeStruct((block, 2 * hidden + qkv_cols), bf16),
            jax.ShapeDtypeStruct((plan["down_block"] + block, width), bf16),
            jax.ShapeDtypeStruct(gain_parts.shape, f32),
        ),
        in_specs=[any_space] * 9 + [in_vmem],
        out_specs=(any_space, any_space, in_vmem),
        scratch_shapes=[
            pltpu.VMEM((hidden + 3 * width, 2 * tokens), bf16),
            pltpu.VMEM((2 * tokens, width + hidden + qkv_cols // 2), bf16),
            pltpu.VMEM((YS_RING, A - 1, G, block, LANES), bf16),
            pltpu.VMEM((nY, A - 1, G, block, LANES), bf16),
            pltpu.VMEM((nY, G - 1, block, LANES), bf16),
            pltpu.VMEM((nY, G - 1, block, LANES), bf16),
            pltpu.VMEM((nZ, G - 1, zr, zc), bf16),
            pltpu.VMEM((nZ, G - 1, zr, zc), bf16),
            pltpu.VMEM((nZ, A, zr, zc), bf16),
            DMA((8,)), DMA((8,)), DMA((8,)),
            DMA((nY, A - 1)), DMA((nY, A - 1)),
            DMA((nY,)), DMA((nY,)), DMA((nY,)), DMA((nY,)),
            DMA((nZ,)), DMA((nZ,)), DMA((nZ,)), DMA((nZ,)),
            DMA((nZ, A - 1)), DMA((nZ, A - 1)),
            DMA((nY, A - 1)), DMA((nY, A - 1)),
            DMA((nY + nZ, A)), DMA((nY + nZ, A)),
            DMA((nY + nZ,)),
            pltpu.VMEM(gain_shape, f32),
            pltpu.VMEM((A,) + gain_shape, f32),
            pltpu.VMEM((3,) + gain_shape, f32),
            pltpu.VMEM(gain_shape, f32),
            pltpu.VMEM(gain_shape, f32),
            DMA((2,)), DMA((max(A - 1, 1),)), DMA((max(A - 1, 1),)), DMA((2,)), DMA((2,)),
        ],
        compiler_params=pltpu.CompilerParams(
            collective_id=3, has_side_effects=True, vmem_limit_bytes=63 * 1024 * 1024
        ),
        cost_estimate=pl.CostEstimate(
            flops=2 * 2 * tokens * (width * (2 * hidden + qkv_cols + width) + hidden * width) // 2,
            bytes_accessed=40_000_000, transcendentals=0,
        ),
    )(at, ot, n2t, n1t, dz, dy, dgate, dup, dq, gain_parts)


W_HOP = 4
AFTER = 1
ROOMS = 3
gather_families = (
    (1, False, False),
    (2, False, True),
    (1, False, False),
    (8, True, False),
    (4, False, False),
)


def gather_kernel(groups, pairs, families, rows, *refs):
    G, A, F = groups, pairs, len(families)
    shards, refs = refs[:F], refs[F:]
    if rows:
        (x, mask, cosines, sines), refs = refs[:4], refs[4:]
    wholes, refs = refs[:F], refs[F:]
    if rows:
        (gain_rows, first_out), refs = refs[:2], refs[2:]
    sems, refs = refs[: 9 * F], refs[9 * F :]
    if rows:
        in_gain, in_wide, in_gate, in_down, in_sem, n1, qkvt, ot, y, n2, gate, inner = refs
    s, z, d = lax.axis_index("section"), lax.axis_index("group"), lax.axis_index("dp")
    c, a = lax.rem(d, 2), lax.div(d, 2)
    sib = (s, z, 2 * a + 1 - c)
    right, left = (s, z + 1, d), (s, z - 1, d)

    def peer(part):
        return (s, z, 2 * part + c)

    barrier = pltpu.get_barrier_semaphore()
    others = [peer(lax.rem(a + k, A)) for k in range(1, A)]
    for dev in [sib, (s, lax.rem(z + 1, G), d), (s, lax.rem(z + G - 1, G), d)] + others:
        pl.semaphore_signal(barrier, inc=1, device_id=dev, device_id_type=MESH)
    pl.semaphore_wait(barrier, A + 2)

    def columns(f, i):
        pieces, halves, _ = families[f]
        size = shards[f].shape[1] // pieces
        if halves:
            i = lax.rem(i, 2) * (pieces // 2) + lax.div(i, 2)
        return pl.ds(pl.multiple_of(i * size, 128), size)

    def cut(f, ref, i):
        return ref.at[:, columns(f, i)]

    def placed(f, i, o, part, core):
        return cut(f, wholes[f].at[(o * A + part) * 2 + core], i)

    def copy(f, i, o, part, kind, index, dev, own=False, core=None):
        core = c if core is None else core
        there = placed(f, i, o, part, core)
        src = cut(f, shards[f], i) if own else there
        send, recv = sems[f * 9 + 2 * kind], sems[f * 9 + 2 * kind + 1]
        return pltpu.make_async_remote_copy(
            src_ref=src, dst_ref=there, send_sem=send.at[index], recv_sem=recv.at[index], device_id=dev, device_id_type=MESH
        )

    def to_right(f, i, o, part, own=False):
        return copy(f, i, o, part, 0, (i, o, lax.rem(part + A - a, A)), right, own)

    def to_left(f, i, o, part, own=False):
        return copy(f, i, o, part, 1, (i, o, lax.rem(part + A - a, A)), left, own)

    def to_part(f, i, o, k, own=False):
        return copy(f, i, o, a, 2, (i, o, k - 1), peer(lax.rem(a + k, A)), own)

    def from_part(f, i, o, k):
        return copy(f, i, o, lax.rem(a + A - k, A), 2, (i, o, k - 1), peer(lax.rem(a + A - k, A)))

    def to_core(f, i, o, part, own=False):
        return copy(f, i, o, part, 3, (i, o, lax.rem(part + A - a, A)), sib, own)

    def from_core(f, i, o, k):
        part = lax.rem(a + k, A)
        return copy(f, i, o, part, 3, (i, o, k), sib, core=1 - c)

    def own_copy(f, i):
        return pltpu.make_async_copy(cut(f, shards[f], i), placed(f, i, z, a, c), sems[f * 9 + 8].at[i])

    def along(f, i, o, part, own, go_right, go_left):
        if go_right:
            @pl.when(z < G - 1)
            def _():
                to_right(f, i, o, part, own).start()
        if go_left:
            @pl.when(z > 0)
            def _():
                to_left(f, i, o, part, own).start()

    first = []
    total = 0
    for pieces, _, _ in families:
        first.append(total)
        total += pieces

    def into(f, i, room):
        return pltpu.make_async_copy(wholes[f].at[:, :, columns(f, i)], room, in_sem.at[first[f] + i])

    def arrived(f, i, room):
        own_copy(f, i).wait()

        @pl.loop(0, G)
        def _(o):
            for k in range(A):
                from_core(f, i, o, k).wait_recv()

        into(f, i, room).start()

    def one_matrix(room):
        return room.reshape(room.shape[0] * room.shape[1], room.shape[2])

    def forward(t):
        f32, bf16 = jnp.float32, jnp.bfloat16
        slots, part, half, ratio = x.shape[0] // max(rows, 1), KVH * HD, HD // 2, H // KVH
        after = W_HOP * G + AFTER
        places = [(1, i) for i in range(families[1][0])] + [(2, 0)]

        @pl.when(t == first[0] + after)
        def _():
            arrived(0, 0, in_gain)
            into(0, 0, in_gain).wait()
            turned = one_matrix(in_gain[...]).astype(f32).T
            gain_rows[...] = turned[:8]
            n1[...] = scaled_norm(x[...].astype(f32), gain_rows[0:1, :])[1]

        for slot, (f, i) in enumerate(places):
            @pl.when(t == first[f] + i + after)
            def _(slot=slot, f=f, i=i):
                arrived(f, i, in_wide.at[slot])

        i3 = t - first[3] - after

        @pl.when((i3 >= 0) & (i3 < families[3][0]))
        def _():
            arrived(3, i3, in_gate.at[lax.rem(i3, ROOMS)])

        i4 = t - first[4] - after

        @pl.when((i4 >= 0) & (i4 < families[4][0]))
        def _():
            arrived(4, i4, in_down.at[lax.rem(i4, ROOMS)])

        for i in range(families[1][0]):
            @pl.when(t == first[1] + i + after + 1)
            def _(i=i):
                into(1, i, in_wide.at[i]).wait()
                for j in range(in_wide.shape[3] // part):
                    weight = one_matrix(in_wide[i, :, :, j * part : (j + 1) * part])
                    chunk = jnp.dot(n1[...], weight, preferred_element_type=f32).T
                    top = (i * (in_wide.shape[3] // part) + j) * part
                    if top >= (H + KVH) * HD:
                        qkvt[top : top + part, :] = chunk.astype(bf16)
                        continue
                    for h in range(KVH):
                        base = top + h * HD
                        front, back = chunk[h * HD : h * HD + half], chunk[h * HD + half : (h + 1) * HD]
                        qkvt[base : base + half, :] = (front * cosines[...] - back * sines[...]).astype(bf16)
                        qkvt[base + half : base + HD, :] = (back * cosines[...] + front * sines[...]).astype(bf16)

        def heads(index, carry):
            row, k = lax.div(index, KVH), lax.rem(index, KVH)
            tokens = pl.ds(pl.multiple_of(row * slots, 128), slots)

            def band(head):
                return pl.ds(pl.multiple_of(head * HD, 16), HD)

            keys, values = qkvt[band(H + k), tokens], qkvt[band(H + KVH + k), tokens]
            queries = jnp.concatenate([qkvt[band(ratio * k + g), tokens] for g in range(ratio)], 1)
            key = lax.broadcasted_iota(jnp.int32, (slots, ratio * slots), 0)
            query = lax.rem(lax.broadcasted_iota(jnp.int32, (slots, ratio * slots), 1), slots)
            valid = mask[pl.ds(pl.multiple_of(row * slots, 128), slots), :] > 0.0
            scores = pair_scores(keys, queries, (key <= query) & valid)
            top = jnp.max(scores, 0, keepdims=True)
            total = top + jnp.log(jnp.sum(jnp.exp(scores - top), 0, keepdims=True))
            probs = jnp.exp(scores - total).astype(bf16)
            out = jnp.dot(values, probs, preferred_element_type=f32).astype(bf16)
            for g in range(ratio):
                ot[band(ratio * k + g), tokens] = out[:, g * slots : (g + 1) * slots]
            return carry

        split = rows * KVH // 2
        turn = t - first[2] - after

        @pl.when((turn >= 1) & (turn <= 2))
        def _():
            lax.fori_loop((turn - 1) * split, turn * split, heads, 0)

        @pl.when(turn == 2)
        def _():
            into(2, 0, in_wide.at[len(places) - 1]).wait()
            y[...] = x[...].astype(f32) + lax.dot_general(
                ot[...], one_matrix(in_wide[len(places) - 1]), down_rows, preferred_element_type=f32
            )
            n2[...] = scaled_norm(y[...], gain_rows[1:2, :])[1]

        c3 = i3 - 2
        size = in_gate.shape[3]

        @pl.when((c3 >= 0) & (c3 < families[3][0]))
        def _():
            room = lax.rem(c3, ROOMS)
            into(3, c3, in_gate.at[room]).wait()
            value = jnp.dot(n2[...], one_matrix(in_gate[room]), preferred_element_type=f32)

            @pl.when(lax.rem(c3, 2) == 0)
            def _():
                gate[...] = value

            @pl.when(lax.rem(c3, 2) == 1)
            def _():
                opened = gate[...]
                inner[:, pl.ds(pl.multiple_of(lax.div(c3, 2) * size, 128), size)] = (
                    opened / (1.0 + jnp.exp(-opened)) * value
                ).astype(bf16)

        c4 = i4 - 2

        @pl.when((c4 >= 0) & (c4 < families[4][0]))
        def _():
            room = lax.rem(c4, ROOMS)
            into(4, c4, in_down.at[room]).wait()
            place = columns(4, c4)
            value = y[:, place] + jnp.dot(inner[...], one_matrix(in_down[room]), preferred_element_type=f32)
            first_out[:, place] = (value * mask[...]).astype(bf16)

    def step(t, carry):
        for f, (pieces, _, parts_first) in enumerate(families):
            i0 = t - first[f]

            @pl.when((i0 >= 0) & (i0 < pieces))
            def _(f=f, i0=i0):
                along(f, i0, z, a, True, True, True)
                for k in range(1, A):
                    to_part(f, i0, z, k, True).start()
                to_core(f, i0, z, a, True).start()
                own_copy(f, i0).start()

        for f, (pieces, _, parts_first) in enumerate(families):
            for h in range(G):
                for k in range(A if parts_first else 1):
                    if h == 0:
                        continue
                    i = t - first[f] - W_HOP * h - (W_HOP if k > 0 else 0)
                    part = lax.rem(a + k, A)
                    for sign in (-1, 1):
                        o = z + sign * h

                        @pl.when((i >= 0) & (i < pieces) & (o >= 0) & (o < G))
                        def _(f=f, i=i, o=o, part=part, sign=sign, parts_first=parts_first):
                            if sign < 0:
                                to_right(f, i, o, part).wait_recv()
                                along(f, i, o, part, False, True, False)
                            else:
                                to_left(f, i, o, part).wait_recv()
                                along(f, i, o, part, False, False, True)
                            if not parts_first:
                                for j in range(1, A):
                                    to_part(f, i, o, j).start()
                            to_core(f, i, o, part).start()

                if parts_first and h > 0:
                    continue
                i = t - first[f] - W_HOP * (h + 1)
                for sign in (-1, 1) if h else (1,):
                    o = z + sign * h

                    @pl.when((i >= 0) & (i < pieces) & (o >= 0) & (o < G))
                    def _(f=f, i=i, o=o, parts_first=parts_first):
                        for k in range(1, A):
                            from_part(f, i, o, k).wait_recv()
                            part = lax.rem(a + A - k, A)
                            if parts_first:
                                along(f, i, o, part, False, True, True)
                            to_core(f, i, o, part).start()
        if rows:
            forward(t)
        return carry

    lax.fori_loop(0, total + max(W_HOP * (G + 1), W_HOP * G + AFTER + 2), step, 0)

    for f, (pieces, _, parts_first) in enumerate(families):
        def drain(i, carry, f=f, parts_first=parts_first):
            if not rows:
                own_copy(f, i).wait()

            def by_group(o, carry):
                for k in range(A):
                    part = lax.rem(a + k, A)
                    to_core(f, i, o, part).wait_send()
                    if not rows:
                        from_core(f, i, o, k).wait_recv()
                    if parts_first or k == 0:
                        @pl.when((z < G - 1) & (o <= z))
                        def _(part=part):
                            to_right(f, i, o, part).wait_send()

                        @pl.when((z > 0) & (o >= z))
                        def _(part=part):
                            to_left(f, i, o, part).wait_send()
                for k in range(1, A):
                    if parts_first:
                        @pl.when(o == z)
                        def _(k=k):
                            to_part(f, i, o, k).wait_send()
                    else:
                        to_part(f, i, o, k).wait_send()
                return carry

            return lax.fori_loop(0, G, by_group, carry)

        lax.fori_loop(0, pieces, drain, 0)


def gathered(groups, dp, shards, families, tokens):
    A, DMA, bf16, f32 = dp // 2, pltpu.SemaphoreType.DMA, jnp.bfloat16, jnp.float32
    any_space, in_vmem = pl.BlockSpec(memory_space=pl.ANY), pl.BlockSpec(memory_space=pltpu.VMEM)
    devices, shape = groups * dp, jax.ShapeDtypeStruct
    scratch = []
    for pieces, _, parts_first in families:
        on_line = (pieces, groups, A if parts_first else 1)
        scratch += [DMA(on_line)] * 4 + [DMA((pieces, groups, max(A - 1, 1)))] * 2 + [DMA((pieces, groups, A))] * 2
        scratch += [DMA((pieces,))]
    outs = tuple(shape((devices,) + x.shape, x.dtype) for x in shards)
    extra, rows = (), 0
    if tokens is not None:
        x, mask, tables, rows = tokens
        extra = (x, mask) + tables
        count, width = x.shape
        hidden = devices * shards[4].shape[0]
        outs += (shape((8, width), f32), shape((count, width), bf16))

        def room(f, rooms):
            return pltpu.VMEM((rooms, devices, shards[f].shape[0], shards[f].shape[1] // families[f][0]), bf16)

        scratch += [
            pltpu.VMEM((devices,) + shards[0].shape, bf16), room(1, families[1][0] + 1), room(3, ROOMS), room(4, ROOMS),
            DMA((sum(family[0] for family in families),)),
            pltpu.VMEM((count, width), bf16), pltpu.VMEM((shards[1].shape[1], count), bf16),
            pltpu.VMEM((width, count), bf16), pltpu.VMEM((count, width), f32), pltpu.VMEM((count, width), bf16),
            pltpu.VMEM((count, shards[3].shape[1] // families[3][0]), f32), pltpu.VMEM((count, hidden), bf16),
        ]
    return pl.pallas_call(
        functools.partial(gather_kernel, groups, A, families, rows),
        out_shape=outs,
        in_specs=[any_space] * len(shards) + [in_vmem] * len(extra),
        out_specs=(any_space,) * len(shards) + (in_vmem,) * (2 if rows else 0),
        scratch_shapes=scratch,
        compiler_params=pltpu.CompilerParams(
            collective_id=5, has_side_effects=True, vmem_limit_bytes=56 * 1024 * 1024
        ),
    )(*shards, *extra)


def body(
    inputs_x, cotangent, lengths, attn_gain, qkv_weight, out_weight, ffn_gain, gate_up, down_weight
):
    is_first = lax.axis_index("section") == 0
    rows, slots, width = inputs_x.shape
    tables = turned_tables(slots, rows)
    info = jnp.concatenate([lengths, is_first.astype(jnp.int32)[None]])
    mask = padding(lengths, slots).reshape(-1, 1)
    gains = jnp.concatenate([attn_gain, ffn_gain], 0).T
    gains = jnp.pad(gains, ((0, 0), (0, 128 - gains.shape[1])))
    shards = (gains, qkv_weight[0], out_weight[0], gate_up[0], down_weight[0])
    together = gains.shape[0] % 16 == 0
    tokens = (flat(inputs_x), mask, tables, rows) if together else None
    gathered_all = gathered(
        lax.axis_size("group"), lax.axis_size("dp"), shards, gather_families, tokens
    )
    gains_all, qkv_w, output_weight, gate_up_w, down_w = (flat(x) for x in gathered_all[:5])
    if together:
        gain_rows, first_out = gathered_all[5:]
    else:
        gain_rows = gains_all[:, :2].astype(jnp.float32).T
    gain_one, gain_two = gain_rows[0:1], gain_rows[1:2]
    dz_given = (flat(cotangent).astype(jnp.float32) * mask).astype(jnp.bfloat16)
    if not together:
        after_one = attention_forward(
            info, flat(inputs_x), gain_one, tables, qkv_w, output_weight, rows
        )[0]
        first_out = ffn_forward(after_one, gain_two, mask, gate_up_w, down_w)
    recv_act = passed_along(first_out, "section", 1)
    layer_in = jnp.where(is_first, flat(inputs_x), recv_act)
    after, heads, log_total, attention_turned, normed_turned = attention_forward(
        info, layer_in, gain_one, tables, qkv_w, output_weight, rows
    )
    dy, dy_low, _ = ffn_backward(after, dz_given, gain_two, mask, gate_up_w, down_w, False)
    (second_dx,) = attention_backward(
        info, layer_in, gain_one, dy, dy_low, tables, heads, log_total, output_weight, qkv_w, rows, False
    )
    recv_grad = passed_along(second_dx, "section", -1)
    dz = jnp.where(is_first, (recv_grad.astype(jnp.float32) * mask).astype(jnp.bfloat16), dz_given)
    dy, dy_low, ffn_gain_part, hidden_turned, grad_gate, grad_up, normed_two_turned, result = ffn_backward(
        after, dz, gain_two, mask, gate_up_w, down_w, True
    )
    grad_x, attn_gain_part, grad_qkv = attention_backward(
        info, layer_in, gain_one, dy, dy_low, tables, heads, log_total, output_weight, qkv_w, rows, True
    )
    section_out = result.reshape((1,) + inputs_x.shape)
    input_grads = grad_x.reshape((1,) + inputs_x.shape)
    gain_parts = jnp.pad(jnp.concatenate([attn_gain_part, ffn_gain_part], 0), ((0, 6), (0, 0)))
    gate_qkv_sum, down_out_sum, gain_sums = summed_grads(
        lax.axis_size("group"),
        lax.axis_size("dp"),
        hidden_turned,
        attention_turned,
        normed_two_turned,
        normed_turned,
        dz,
        dy_low,
        grad_gate,
        grad_up,
        grad_qkv,
        gain_parts,
    )
    gain_cols = attn_gain.shape[1] * lax.axis_size("dp")
    gain_sums = lax.dynamic_slice_in_dim(
        gain_sums, lax.axis_index("group") * gain_cols, gain_cols, 1
    )
    gate_width = gate_up.shape[2]
    down_rows = down_weight.shape[1] * lax.axis_size("dp")
    reduced = (
        gain_sums[0],
        gate_qkv_sum[:, gate_width:].astype(jnp.float32),
        down_out_sum[down_rows:].astype(jnp.float32),
        gain_sums[1],
        gate_qkv_sum[:, :gate_width].astype(jnp.float32),
        down_out_sum[:down_rows].astype(jnp.float32),
    )
    return (section_out, input_grads) + tuple((shard_sum[None] for shard_sum in reduced))


def solution(mesh):
    placed = (
        P(("group", "dp"), None, None),
        P(("group", "dp"), None, None),
        P(("group", "dp")),
        P("section", ("group", "dp")),
        P("section", ("group", "dp"), None),
        P("section", ("group", "dp"), None),
        P("section", ("group", "dp")),
        P("section", ("group", "dp"), None),
        P("section", ("group", "dp"), None),
    )
    return jax.shard_map(
        body,
        mesh=mesh,
        in_specs=placed,
        out_specs=(
            P("section", ("group", "dp"), None, None),
            P("section", ("group", "dp"), None, None),
            P("section", "group"),
            P("section", "group", None),
            P("section", "group", None),
            P("section", "group"),
            P("section", "group", None),
            P("section", "group", None),
        ),
        check_vma=False,
    )
```

```python
import functools

import jax
import jax.numpy as jnp
from jax import lax
from jax.experimental import pallas as pl
from jax.experimental.pallas import tpu as pltpu
from jax.sharding import PartitionSpec as P

H = 16
KVH = 8
HD = 96


norm_eps = 1e-05
rope_base = 100000.0
masked_score = -1e30
across = (((1,), (1,)), ((), ()))
down_rows = (((0,), (0,)), ((), ()))


def passed_along(value, axis, by):
    length = lax.axis_size(axis)
    pairs = [(i, i + by) for i in range(length) if 0 <= i + by < length]
    return lax.ppermute(value, axis, pairs)


def swapped(value, axis):
    return lax.ppermute(value, axis, [(i, i ^ 1) for i in range(lax.axis_size(axis))])


def padding(lengths, slot_count):
    position = jnp.arange(slot_count, dtype=jnp.int32)
    return (position[None, :] < lengths[:, None]).astype(jnp.float32)[..., None]


FF_CHUNK = 512
across = (((1,), (1,)), ((), ()))
down_rows = (((0,), (0,)), ((), ()))


def scaled_norm(value, gain):
    scale = lax.rsqrt(jnp.mean(value * value, -1, keepdims=True) + norm_eps)
    return scale, (value * scale * gain).astype(jnp.bfloat16)


def ffn_forward_kernel(y, gain, mask, wg, wu, wd, out, n2, acc):
    j = pl.program_id(0)

    @pl.when(j == 0)
    def _():
        n2[...] = scaled_norm(y[...], gain[...])[1]
        acc[...] = y[...]

    gate = jnp.dot(n2[...], wg[...], preferred_element_type=jnp.float32)
    up = jnp.dot(n2[...], wu[...], preferred_element_type=jnp.float32)
    hidden = (gate / (1.0 + jnp.exp(-gate)) * up).astype(jnp.bfloat16)
    acc[...] += jnp.dot(hidden, wd[...], preferred_element_type=jnp.float32)

    @pl.when(j == pl.num_programs(0) - 1)
    def _():
        out[...] = (acc[...] * mask[...]).astype(jnp.bfloat16)


def ffn_specs(tokens, width, hidden):
    steps = hidden // FF_CHUNK
    whole = pl.BlockSpec((tokens, width), lambda j: (0, 0))
    row = pl.BlockSpec((1, width), lambda j: (0, 0))
    weights = [
        pl.BlockSpec((width, FF_CHUNK), lambda j: (0, j)),
        pl.BlockSpec((width, FF_CHUNK), lambda j: (0, j + steps)),
        pl.BlockSpec((FF_CHUNK, width), lambda j: (j, 0)),
    ]
    return steps, whole, row, weights


def ffn_forward(y, gain, mask, gate_up_w, down_w):
    tokens, width = y.shape
    hidden = down_w.shape[0]
    steps, whole, row, weights = ffn_specs(tokens, width, hidden)
    return pl.pallas_call(
        ffn_forward_kernel,
        grid=(steps,),
        out_shape=jax.ShapeDtypeStruct((tokens, width), jnp.bfloat16),
        in_specs=[whole, row, pl.BlockSpec((tokens, 1), lambda j: (0, 0))] + weights,
        out_specs=whole,
        scratch_shapes=[pltpu.VMEM((tokens, width), jnp.bfloat16), pltpu.VMEM((tokens, width), jnp.float32)],
        compiler_params=pltpu.CompilerParams(vmem_limit_bytes=40 * 1024 * 1024),
        cost_estimate=pl.CostEstimate(
            flops=6 * tokens * width * hidden, bytes_accessed=6 * width * hidden, transcendentals=tokens * hidden
        ),
    )(y, gain, mask, gate_up_w, gate_up_w, down_w)


def ffn_prepare_kernel(y, gain, mask, wg, wu, wd, at, by_gate, by_up, n2t, out, n2, acc):
    j = pl.program_id(0)
    bf16, f32 = jnp.bfloat16, jnp.float32

    @pl.when(j == 0)
    def _():
        n = scaled_norm(y[...], gain[...])[1]
        n2[...] = n
        n2t[...] = n.T
        acc[...] = y[...]

    gate = jnp.dot(n2[...], wg[...], preferred_element_type=f32)
    up = jnp.dot(n2[...], wu[...], preferred_element_type=f32)
    sig = 1.0 / (1.0 + jnp.exp(-gate))
    silu = gate * sig
    hidden = (silu * up).astype(bf16)
    at[...] = hidden.T
    by_gate[...] = (up * sig * (1.0 + gate * (1.0 - sig))).astype(bf16)
    by_up[...] = silu.astype(bf16)
    acc[...] += jnp.dot(hidden, wd[...], preferred_element_type=f32)

    @pl.when(j == pl.num_programs(0) - 1)
    def _():
        out[...] = (acc[...] * mask[...]).astype(bf16)


def ffn_prepare(y, gain, mask, gate_up_w, down_w):
    tokens, width = y.shape
    hidden = down_w.shape[0]
    steps, whole, row, weights = ffn_specs(tokens, width, hidden)
    shape, bf16 = jax.ShapeDtypeStruct, jnp.bfloat16
    part = pl.BlockSpec((tokens, FF_CHUNK), lambda j: (0, j))
    return pl.pallas_call(
        ffn_prepare_kernel,
        grid=(steps,),
        out_shape=(
            shape((hidden, tokens), bf16), shape((tokens, hidden), bf16), shape((tokens, hidden), bf16),
            shape((width, tokens), bf16), shape((tokens, width), bf16),
        ),
        in_specs=[whole, row, pl.BlockSpec((tokens, 1), lambda j: (0, 0))] + weights,
        out_specs=(
            pl.BlockSpec((FF_CHUNK, tokens), lambda j: (j, 0)), part, part,
            pl.BlockSpec((width, tokens), lambda j: (0, 0)), whole,
        ),
        scratch_shapes=[pltpu.VMEM((tokens, width), bf16), pltpu.VMEM((tokens, width), jnp.float32)],
        compiler_params=pltpu.CompilerParams(vmem_limit_bytes=48 * 1024 * 1024),
        cost_estimate=pl.CostEstimate(
            flops=6 * tokens * width * hidden, bytes_accessed=6 * width * hidden, transcendentals=tokens * hidden
        ),
    )(y, gain, mask, gate_up_w, gate_up_w, down_w)


def ffn_backward_kernel(prepared, y, dz, gain, wg, wu, wd, *rest):
    bf16, f32 = jnp.bfloat16, jnp.float32
    if prepared:
        by_gate, by_up, dy, dyb, gain_grad, dgate, dup, acc = rest
    else:
        dy, dyb, gain_grad, n2, acc = rest
    j = pl.program_id(0)

    @pl.when(j == 0)
    def _():
        acc[...] = jnp.zeros_like(acc)
        if not prepared:
            n2[...] = scaled_norm(y[...], gain[...])[1]

    grad = lax.dot_general(dz[...], wd[...], across, preferred_element_type=f32)
    if prepared:
        grad_gate = (grad * by_gate[...].astype(f32)).astype(bf16)
        grad_up = (grad * by_up[...].astype(f32)).astype(bf16)
        dgate[...] = grad_gate
        dup[...] = grad_up
    else:
        gate = jnp.dot(n2[...], wg[...], preferred_element_type=f32)
        up = jnp.dot(n2[...], wu[...], preferred_element_type=f32)
        sig = 1.0 / (1.0 + jnp.exp(-gate))
        grad_gate = (grad * up * sig * (1.0 + gate * (1.0 - sig))).astype(bf16)
        grad_up = (grad * (gate * sig)).astype(bf16)
    acc[...] += lax.dot_general(grad_gate, wg[...], across, preferred_element_type=f32) + lax.dot_general(
        grad_up, wu[...], across, preferred_element_type=f32
    )

    @pl.when(j == pl.num_programs(0) - 1)
    def _():
        value, grad_normed = y[...], acc[...]
        r = lax.rsqrt(jnp.mean(value * value, -1, keepdims=True) + norm_eps)
        scaled = grad_normed * gain[...]
        gain_grad[...] = jnp.sum(grad_normed * value * r, axis=0, keepdims=True)
        inner = jnp.mean(value * scaled, -1, keepdims=True)
        total = dz[...].astype(f32) + r * scaled - value * (r * r * r) * inner
        dy[...] = total
        dyb[...] = total.astype(bf16)


def ffn_backward(y, dz, gain, gate_up_w, down_w, factors=()):
    tokens, width = y.shape
    hidden = down_w.shape[0]
    steps, whole, row, weights = ffn_specs(tokens, width, hidden)
    shape, bf16, f32 = jax.ShapeDtypeStruct, jnp.bfloat16, jnp.float32
    outs = [shape((tokens, width), f32), shape((tokens, width), bf16), shape((1, width), f32)]
    out_specs = [whole, whole, row]
    scratch = [pltpu.VMEM((tokens, width), f32)]
    parts = [pl.BlockSpec((tokens, FF_CHUNK), lambda j: (0, j))] * len(factors)
    if factors:
        outs += [shape((tokens, hidden), bf16)] * 2
        out_specs += parts
    else:
        scratch = [pltpu.VMEM((tokens, width), bf16)] + scratch
    return pl.pallas_call(
        functools.partial(ffn_backward_kernel, bool(factors)),
        grid=(steps,),
        out_shape=tuple(outs),
        in_specs=[whole, whole, row] + weights + parts,
        out_specs=tuple(out_specs),
        scratch_shapes=scratch,
        compiler_params=pltpu.CompilerParams(vmem_limit_bytes=48 * 1024 * 1024),
        cost_estimate=pl.CostEstimate(
            flops=10 * tokens * width * hidden, bytes_accessed=6 * width * hidden, transcendentals=tokens * hidden
        ),
    )(y, dz, gain, gate_up_w, gate_up_w, down_w, *factors)


def turned_tables(slots, rows):
    half_width = HD // 2
    frequency = rope_base ** (-(jnp.arange(half_width, dtype=jnp.float32) * 2.0 / HD))
    angles = frequency[:, None] * jnp.arange(slots, dtype=jnp.float32)[None, :]
    return jnp.tile(jnp.cos(angles), (1, rows)), jnp.tile(jnp.sin(angles), (1, rows))


def pair_mask(length, slots):
    groups = H // KVH
    key = lax.broadcasted_iota(jnp.int32, (slots, groups * slots), 0)
    query = lax.rem(lax.broadcasted_iota(jnp.int32, (slots, groups * slots), 1), slots)
    return (key <= query) & (key < length)


def pair_of(ref, k, row, slots):
    groups = H // KVH
    first = groups * k * HD
    return jnp.concatenate(
        [ref[first + g * HD : first + (g + 1) * HD, row * slots : (row + 1) * slots] for g in range(groups)], 1
    )


def key_value(qkvt, k, row, slots):
    tokens = slice(row * slots, (row + 1) * slots)
    keys = qkvt[(H + k) * HD : (H + k + 1) * HD, tokens]
    values = qkvt[(H + KVH + k) * HD : (H + KVH + k + 1) * HD, tokens]
    return keys, values


def pair_scores(keys, queries, mask):
    scores = lax.dot_general(keys, queries, down_rows, preferred_element_type=jnp.float32) * HD ** (-0.5)
    return jnp.where(mask, scores, masked_score)


def attention_forward_kernel(rows, info, x, gain, cosines, sines, w, wo, y, qkvt, lse, ot, n1t, n1):
    j = pl.program_id(0)
    bf16, f32 = jnp.bfloat16, jnp.float32
    slots, part, half = x.shape[0] // rows, KVH * HD, HD // 2
    groups = H // KVH

    @pl.when(j == 0)
    def _():
        n = scaled_norm(x[...].astype(f32), gain[...])[1]
        n1[...] = n
        n1t[...] = n.T

    chunk = jnp.dot(n1[...], w[...], preferred_element_type=f32).T

    @pl.when(j <= groups)
    def _():
        for h in range(KVH):
            front, back = chunk[h * HD : h * HD + half], chunk[h * HD + half : (h + 1) * HD]
            base = j * part + h * HD
            qkvt[pl.ds(pl.multiple_of(base, 16), half), :] = (front * cosines[...] - back * sines[...]).astype(bf16)
            qkvt[pl.ds(pl.multiple_of(base + half, 16), half), :] = (
                back * cosines[...] + front * sines[...]
            ).astype(bf16)

    @pl.when(j > groups)
    def _():
        qkvt[pl.ds(pl.multiple_of(j * part, 16), part), :] = chunk.astype(bf16)
        for row in range(rows):
            mask = pair_mask(info[row], slots)
            for k in range(KVH):
                keys, values = key_value(qkvt, k, row, slots)
                scores = pair_scores(keys, pair_of(qkvt, k, row, slots), mask)
                top = jnp.max(scores, 0, keepdims=True)
                total = top + jnp.log(jnp.sum(jnp.exp(scores - top), 0, keepdims=True))
                lse[row * KVH + k : row * KVH + k + 1, :] = total
                probs = jnp.exp(scores - total).astype(bf16)
                out = jnp.dot(values, probs, preferred_element_type=f32).astype(bf16)
                for g in range(groups):
                    first = (groups * k + g) * HD
                    ot[first : first + HD, row * slots : (row + 1) * slots] = out[:, g * slots : (g + 1) * slots]
        y[...] = x[...].astype(f32) + lax.dot_general(ot[...], wo[...], down_rows, preferred_element_type=f32)


def attention_backward_kernel(
    rows, keep, info, x, gain, dy, dyb, cosines, sines, qkvt, lse, wo, w, dx, *rest
):
    if keep:
        gain_grad, dqkv, dot, dqkvt, acc = rest
    else:
        dqkv, dot, dqkvt, acc = rest
    j = pl.program_id(0)
    bf16, f32 = jnp.bfloat16, jnp.float32
    slots, part, half = x.shape[0] // rows, KVH * HD, HD // 2
    groups = H // KVH

    def unrotated(grad, row, width):
        tokens = slice(row * slots, (row + 1) * slots)
        cos, sin = cosines[:, tokens], sines[:, tokens]
        if width > slots:
            cos, sin = jnp.concatenate([cos] * groups, 1), jnp.concatenate([sin] * groups, 1)
        grad = grad * HD ** (-0.5)
        front, back = grad[:half], grad[half:]
        return (front * cos + back * sin).astype(bf16), (back * cos - front * sin).astype(bf16)

    @pl.when(j == 0)
    def _():
        dot[...] = lax.dot_general(dyb[...], wo[...], across, preferred_element_type=f32).astype(bf16).T
        acc[...] = jnp.zeros_like(acc)
        for row in range(rows):
            tokens = slice(row * slots, (row + 1) * slots)
            mask = pair_mask(info[row], slots)
            for k in range(KVH):
                keys, values = key_value(qkvt, k, row, slots)
                queries, grads = pair_of(qkvt, k, row, slots), pair_of(dot, k, row, slots)
                scores = pair_scores(keys, queries, mask)
                probs = jnp.exp(scores - lse[row * KVH + k : row * KVH + k + 1, :])
                grad_probs = lax.dot_general(values, grads, down_rows, preferred_element_type=f32)
                grad_scores = (
                    probs * (grad_probs - jnp.sum(probs * grad_probs, 0, keepdims=True))
                ).astype(bf16)
                grad_values = lax.dot_general(grads, probs.astype(bf16), across, preferred_element_type=f32)
                grad_keys = lax.dot_general(queries, grad_scores, across, preferred_element_type=f32)
                grad_queries = jnp.dot(keys, grad_scores, preferred_element_type=f32)
                front, back = unrotated(grad_queries, row, groups * slots)
                for g in range(groups):
                    first = (groups * k + g) * HD
                    dqkvt[first : first + half, tokens] = front[:, g * slots : (g + 1) * slots]
                    dqkvt[first + half : first + HD, tokens] = back[:, g * slots : (g + 1) * slots]
                front, back = unrotated(grad_keys, row, slots)
                first = (H + k) * HD
                dqkvt[first : first + half, tokens] = front
                dqkvt[first + half : first + HD, tokens] = back
                first = (H + KVH + k) * HD
                dqkvt[first : first + HD, tokens] = grad_values.astype(bf16)
        for i in range(groups + 2):
            dqkv[:, i * part : (i + 1) * part] = dqkvt[i * part : (i + 1) * part, :].T

    columns = pl.ds(pl.multiple_of(j * part, 128), part)
    acc[...] += lax.dot_general(dqkv[:, columns], w[...], across, preferred_element_type=f32)

    @pl.when(j == pl.num_programs(0) - 1)
    def _():
        value, grad_normed = x[...].astype(f32), acc[...]
        r = lax.rsqrt(jnp.mean(value * value, -1, keepdims=True) + norm_eps)
        scaled = grad_normed * gain[...]
        inner = jnp.mean(value * scaled, -1, keepdims=True)
        total = dy[...] + (r * scaled - value * (r * r * r) * inner)
        if keep:
            gain_grad[...] = jnp.sum(grad_normed * value * r, axis=0, keepdims=True)
            dx[...] = jnp.where(info[rows] == 1, total, total.astype(bf16).astype(f32))
        else:
            dx[...] = total.astype(bf16)


def attention_specs(tokens, width):
    part = KVH * HD
    whole = lambda *shape: pl.BlockSpec(shape, lambda j: (0,) * len(shape))
    return part, whole, pl.BlockSpec(memory_space=pltpu.SMEM), pl.BlockSpec((width, part), lambda j: (0, j))


def attention_forward(info, x, gain, tables, qkv_w, output_weight, rows):
    tokens, width = x.shape
    cols, slots = qkv_w.shape[1], tokens // rows
    part, whole, scalars, weight = attention_specs(tokens, width)
    shape, bf16, f32 = jax.ShapeDtypeStruct, jnp.bfloat16, jnp.float32
    stats = (rows * KVH, H // KVH * slots)
    return pl.pallas_call(
        functools.partial(attention_forward_kernel, rows),
        grid=(cols // part,),
        out_shape=(
            shape((tokens, width), f32), shape((cols, tokens), bf16), shape(stats, f32),
            shape((H * HD, tokens), bf16), shape((width, tokens), bf16),
        ),
        in_specs=[
            scalars, whole(tokens, width), whole(1, width), whole(HD // 2, tokens), whole(HD // 2, tokens), weight,
            whole(H * HD, width),
        ],
        out_specs=(
            whole(tokens, width), whole(cols, tokens), whole(*stats), whole(H * HD, tokens), whole(width, tokens)
        ),
        scratch_shapes=[pltpu.VMEM((tokens, width), bf16)],
        compiler_params=pltpu.CompilerParams(vmem_limit_bytes=40 * 1024 * 1024),
        cost_estimate=pl.CostEstimate(
            flops=2 * tokens * width * (cols + H * HD), bytes_accessed=2 * width * (cols + H * HD), transcendentals=0
        ),
    )(info, x, gain, *tables, qkv_w, output_weight)


def attention_backward(info, x, gain, dy, dy_low, tables, qkvt, lse, output_weight, qkv_w, rows, keep):
    tokens, width = x.shape
    cols = qkv_w.shape[1]
    part, whole, scalars, weight = attention_specs(tokens, width)
    shape, bf16, f32 = jax.ShapeDtypeStruct, jnp.bfloat16, jnp.float32
    scratch = [pltpu.VMEM((H * HD, tokens), bf16), pltpu.VMEM((cols, tokens), bf16), pltpu.VMEM((tokens, width), f32)]
    outs, out_specs = [shape((tokens, width), f32 if keep else bf16)], [whole(tokens, width)]
    if keep:
        outs += [shape((1, width), f32), shape((tokens, cols), bf16)]
        out_specs += [whole(1, width), whole(tokens, cols)]
    else:
        scratch = [pltpu.VMEM((tokens, cols), bf16)] + scratch
    return pl.pallas_call(
        functools.partial(attention_backward_kernel, rows, keep),
        grid=(cols // part,),
        out_shape=tuple(outs),
        in_specs=[
            scalars, whole(tokens, width), whole(1, width), whole(tokens, width), whole(tokens, width),
            whole(HD // 2, tokens), whole(HD // 2, tokens), whole(cols, tokens), whole(*lse.shape), whole(H * HD, width),
            weight,
        ],
        out_specs=tuple(out_specs),
        scratch_shapes=scratch,
        compiler_params=pltpu.CompilerParams(vmem_limit_bytes=48 * 1024 * 1024),
        cost_estimate=pl.CostEstimate(
            flops=2 * tokens * width * (cols + H * HD), bytes_accessed=2 * width * (cols + H * HD), transcendentals=0
        ),
    )(info, x, gain, dy, dy_low, *tables, qkvt, lse, output_weight, qkv_w)


def flat(array):
    return array.reshape(-1, array.shape[-1])


MESH = pl.DeviceIdType.MESH
LANES = 128


def grad_plan(groups, dp, tokens, width, hidden, qkv_cols):
    pairs = dp // 2
    block = width // groups
    down_block = hidden // groups
    gate_cols = 2 * hidden // 2 // pairs
    qkv_part = qkv_cols // 2 // pairs
    pieces_gate = gate_cols // LANES
    pieces_qkv = qkv_part // LANES
    pieces = pieces_gate + pieces_qkv
    z_rows = LANES
    while down_block % z_rows or block % z_rows:
        z_rows //= 2
    row_chunks = (down_block + block) // z_rows
    half = width // 2
    z_split = max(1, pieces // row_chunks)
    while half % (z_split * LANES):
        z_split -= 1
    return dict(
        groups=groups, pairs=pairs, tokens=tokens, width=width, hidden=hidden, qkv_cols=qkv_cols, block=block,
        down_block=down_block, gate_cols=gate_cols, qkv_part=qkv_part, pieces_gate=pieces_gate, pieces=pieces,
        z_rows=z_rows, z_split=z_split, z_cols=half // z_split, z_pieces=row_chunks * z_split,
        down_chunks=down_block // z_rows, half=half,
    )


YS_RING = 4
HOP = 2
LEAD = 2


def grad_kernel(
    plan, at, ot, n2t, n1t, at2, ot2, n2t2, n1t2, dz, dy, dgate, dup, dq, gp, outy, outz, outg,
    LT, RH, YS, YR, YRT, YLT, ZRT, ZLT, ZX,
    own_sem, xs, xr, ys_s, ys_r, yr_s, yr_r, yl_s, yl_r, zr_s, zr_r, zl_s, zl_r,
    zx_s, zx_r, ag_s, ag_r, sib_s, sib_r, lo,
    GC, GA, GS, GR, GL, gc_sem, ga_s, ga_r, gr_sem, gl_sem,
):
    G, A, T = plan["groups"], plan["pairs"], plan["tokens"]
    width, hidden, half = plan["width"], plan["hidden"], plan["half"]
    block, nY, nZ = plan["block"], plan["pieces"], plan["z_pieces"]
    zr, zc = plan["z_rows"], plan["z_cols"]
    s, z, d = lax.axis_index("section"), lax.axis_index("group"), lax.axis_index("dp")
    c, a = lax.rem(d, 2), lax.div(d, 2)
    sib = (s, z, 2 * a + 1 - c)
    right, left = (s, z + 1, d), (s, z - 1, d)

    def peer(k):
        return (s, z, 2 * lax.rem(a + k, A) + c)

    def remote(src, dst, ss, rs, dev):
        return pltpu.make_async_remote_copy(
            src_ref=src, dst_ref=dst, send_sem=ss, recv_sem=rs, device_id=dev, device_id_type=MESH
        )

    barrier = pltpu.get_barrier_semaphore()
    for dev in [sib, (s, lax.rem(z + 1, G), d), (s, lax.rem(z + G - 1, G), d)] + [peer(k) for k in range(1, A)]:
        pl.semaphore_signal(barrier, inc=1, device_id=dev, device_id_type=MESH)
    pl.semaphore_wait(barrier, A + 2)

    lhs = [
        (at, at2, 0, hidden), (ot, ot2, hidden, width), (n2t, n2t2, hidden + width, width),
        (n1t, n1t2, hidden + 2 * width, width),
    ]
    rhs = [(dz, 0, half), (dy, half, half), (None, width, hidden), (dq, width + hidden, plan["qkv_cols"] // 2)]
    own, cross = {}, {}
    for i, (ref, theirs, row, rows) in enumerate(lhs):
        own[0, i] = pltpu.make_async_copy(ref, LT.at[pl.ds(row, rows), pl.ds(0, T)], own_sem.at[i])
        own[2, i] = pltpu.make_async_copy(theirs, LT.at[pl.ds(row, rows), pl.ds(T, T)], own_sem.at[8 + i])
    for i, (ref, col, cols) in enumerate(rhs):
        if ref is None:
            continue
        mine = pl.ds(pl.multiple_of(c * cols, LANES), cols)
        theirs = pl.ds(pl.multiple_of((1 - c) * cols, LANES), cols)
        own[1, i] = pltpu.make_async_copy(ref.at[:, mine], RH.at[pl.ds(0, T), pl.ds(col, cols)], own_sem.at[4 + i])
        cross[1, i] = remote(ref.at[:, theirs], RH.at[pl.ds(T, T), pl.ds(col, cols)], xs.at[4 + i], xr.at[4 + i], sib)
    col, cols = rhs[2][1:]
    for core, (mine, theirs) in enumerate(((dgate, dup), (dup, dgate))):
        own[1, 2, core] = pltpu.make_async_copy(mine, RH.at[pl.ds(0, T), pl.ds(col, cols)], own_sem.at[6])
        cross[1, 2, core] = remote(theirs, RH.at[pl.ds(T, T), pl.ds(col, cols)], xs.at[6], xr.at[6], sib)
    own[1, 2], cross[1, 2] = own[1, 2, 0], cross[1, 2, 0]
    def fetch(i):
        if i == 2:
            for core in (0, 1):
                @pl.when(c == core)
                def _(core=core):
                    cross[1, 2, core].start()
                    own[1, 2, core].start()
        else:
            cross[1, i].start()
            own[1, i].start()
        own[0, i].start()
        own[2, i].start()

    fetch(0)
    fetch(2)

    def operands_here(i):
        for side in (0, 2, 1):
            own[side, i].wait()
        cross[1, i].wait_recv()

    def product(row, rows, col, cols):
        return jnp.dot(
            LT[pl.ds(row, rows), :], RH[:, pl.ds(col, cols)], preferred_element_type=jnp.float32
        )

    def y_product(q, which, b):
        is_gate = q < plan["pieces_gate"]
        row = jnp.where(is_gate, hidden + width, hidden + 2 * width) + b * block
        col = jnp.where(
            is_gate,
            width + which * plan["gate_cols"] + q * LANES,
            width + hidden + which * plan["qkv_part"] + (q - plan["pieces_gate"]) * LANES,
        )
        return product(pl.multiple_of(row, 16), block, pl.multiple_of(col, LANES), LANES)

    def z_product(p, b):
        r, h = lax.div(p, plan["z_split"]), lax.rem(p, plan["z_split"])
        is_down = r < plan["down_chunks"]
        row = jnp.where(
            is_down, b * plan["down_block"] + r * zr, hidden + b * block + (r - plan["down_chunks"]) * zr
        )
        col = jnp.where(is_down, 0, half) + h * zc
        return product(pl.multiple_of(row, 16), zr, pl.multiple_of(col, LANES), zc)

    def y_out(q, part, core):
        is_gate = q < plan["pieces_gate"]
        col = jnp.where(
            is_gate,
            core * hidden + part * plan["gate_cols"] + q * LANES,
            2 * hidden + core * (plan["qkv_cols"] // 2) + part * plan["qkv_part"] + (q - plan["pieces_gate"]) * LANES,
        )
        return outy.at[:, pl.ds(pl.multiple_of(col, LANES), LANES)]

    def z_out(p, core):
        r, h = lax.div(p, plan["z_split"]), lax.rem(p, plan["z_split"])
        return outz.at[
            pl.ds(pl.multiple_of(r * zr, 16), zr), pl.ds(pl.multiple_of(core * half + h * zc, LANES), zc)
        ]

    def y_send(q, k):
        return remote(YS.at[lax.rem(q, YS_RING), k - 1], YR.at[q, k - 1], ys_s.at[q, k - 1], ys_r.at[q, k - 1], peer(k))

    def line_copies(slots_r, slots_l, r_s, r_r, l_s, l_r, first_r, first_l, p):
        out_r, in_r, out_l, in_l = [], [], [], []
        for k in range(G):
            if k < G - 1:
                src = first_r(p) if k == 0 else slots_r.at[p, pl.ds(k, G - 1 - k)]
                out_r.append((k, remote(src, slots_r.at[p, pl.ds(k, G - 1 - k)], r_s.at[p], r_r.at[p], right)))
                held = slots_l.at[p, pl.ds(0, k + 1)]
                in_l.append((k, remote(held, held, l_s.at[p], l_r.at[p], left)))
            if k > 0:
                src = first_l(p) if k == G - 1 else slots_l.at[p, pl.ds(0, k)]
                out_l.append((k, remote(src, slots_l.at[p, pl.ds(0, k)], l_s.at[p], l_r.at[p], left)))
                held = slots_r.at[p, pl.ds(k - 1, G - k)]
                in_r.append((k, remote(held, held, r_s.at[p], r_r.at[p], right)))
        return out_r, in_r, out_l, in_l

    def at_place(copies, act):
        for k, copy in copies:
            @pl.when(z == k)
            def _(copy=copy):
                act(copy)

    def y_line(q):
        return line_copies(
            YRT, YLT, yr_s, yr_r, yl_s, yl_r,
            lambda q: YR.at[q, 0, pl.ds(1, G - 1)], lambda q: YR.at[q, 0, pl.ds(0, G - 1)], q,
        )

    def z_line(p):
        return line_copies(
            ZRT, ZLT, zr_s, zr_r, zl_s, zl_r,
            lambda p: ZRT.at[p, pl.ds(0, G - 1)], lambda p: ZLT.at[p, pl.ds(0, G - 1)], p,
        )

    def zx_copy(p, k):
        return remote(ZX.at[p, a], ZX.at[p, a], zx_s.at[p, k - 1], zx_r.at[p, k - 1], peer(k))

    def ag_copy(q, k):
        return remote(YR.at[q, 0, z], y_out(q, a, c), ag_s.at[q, k - 1], ag_r.at[q, k - 1], peer(k))

    def sib_own(q):
        return remote(YR.at[q, 0, z], y_out(q, a, c), sib_s.at[q, 0], sib_r.at[q, 0], sib)

    def sib_pass(q, k):
        part = lax.rem(a + A - k, A)
        return remote(y_out(q, part, c), y_out(q, part, c), sib_s.at[q, k], sib_r.at[q, k], sib)

    def own_y(q):
        return pltpu.make_async_copy(YR.at[q, 0, z], y_out(q, a, c), lo.at[q])

    def own_z(p):
        return pltpu.make_async_copy(ZX.at[p, a], z_out(p, c), lo.at[nY + p])

    def sib_z(p):
        return remote(ZX.at[p, a], z_out(p, c), sib_s.at[nY + p, 0], sib_r.at[nY + p, 0], sib)

    f32, bf16 = jnp.float32, jnp.bfloat16
    far = jnp.maximum(z, G - 1 - z)

    def live(index, count):
        return (index >= 0) & (index < count)

    def gain_core():
        return remote(gp, GC, gc_sem.at[0], gc_sem.at[1], sib)

    def gain_part(k):
        return remote(GA.at[a], GA.at[a], ga_s.at[k - 1], ga_r.at[k - 1], peer(k))

    def gain_right():
        return remote(GS.at[1], GR, gr_sem.at[0], gr_sem.at[1], right)

    def gain_left():
        return remote(GS.at[2], GL, gl_sem.at[0], gl_sem.at[1], left)

    def gain_step(t):
        @pl.when(t == 0)
        def _():
            gain_core().start()

        @pl.when(t == 1)
        def _():
            gain_core().wait_recv()
            GA[a] = gp[...] + GC[...]
            for k in range(1, A):
                gain_part(k).start()

        @pl.when(t == 2)
        def _():
            for k in range(1, A):
                remote(
                    GA.at[lax.rem(a + A - k, A)], GA.at[lax.rem(a + A - k, A)], ga_s.at[k - 1], ga_r.at[k - 1], peer(k)
                ).wait_recv()
            total = GA[0]
            for k in range(1, A):
                total += GA[k]
            GS[0] = total

        @pl.when(t == 2 + HOP * z)
        def _():
            @pl.when(z > 0)
            def _():
                gain_right().wait_recv()
                GS[1] = GS[0] + GR[...]

            @pl.when(z == 0)
            def _():
                GS[1] = GS[0]

            @pl.when(z < G - 1)
            def _():
                gain_right().start()

        @pl.when(t == 2 + HOP * (G - 1 - z))
        def _():
            @pl.when(z < G - 1)
            def _():
                gain_left().wait_recv()
                GS[2] = GS[0] + GL[...]

            @pl.when(z == G - 1)
            def _():
                GS[2] = GS[0]

            @pl.when(z > 0)
            def _():
                gain_left().start()

        @pl.when(t == 3 + HOP * (G - 1))
        def _():
            outg[...] = GS[1] + jnp.where(z < G - 1, GL[...], 0.0)

    def step(t, carry):
        gain_step(t)

        @pl.when(t == 0)
        def _():
            operands_here(0)
            operands_here(2)
            fetch(1)
            fetch(3)

        @pl.when(t == jnp.minimum(plan["pieces_gate"], plan["down_chunks"] * plan["z_split"]) - 1)
        def _():
            operands_here(1)
            operands_here(3)

        q1 = t

        @pl.when(live(q1, nY))
        def _():
            for k in range(1, A):
                @pl.when(q1 >= YS_RING)
                def _():
                    y_send(q1 - YS_RING, k).wait_send()

                @pl.loop(0, G)
                def _(b):
                    YS[lax.rem(q1, YS_RING), k - 1, b] = y_product(q1, lax.rem(a + k, A), b).astype(bf16)

                y_send(q1, k).start()

        pr = t - HOP * z

        @pl.when(live(pr, nZ))
        def _():
            out_r, in_r, _, _ = z_line(pr)
            at_place(in_r, lambda copy: copy.wait_recv())

            @pl.loop(0, G)
            def _(b):
                @pl.when((b > z) & (z > 0))
                def _():
                    ZRT[pr, b - 1] = (z_product(pr, b) + ZRT[pr, b - 1].astype(f32)).astype(bf16)

                @pl.when((b > z) & (z == 0))
                def _():
                    ZRT[pr, b - 1] = z_product(pr, b).astype(bf16)

            at_place(out_r, lambda copy: copy.start())

        pL = t - HOP * (G - 1 - z)

        @pl.when(live(pL, nZ))
        def _():
            _, _, out_l, in_l = z_line(pL)
            at_place(in_l, lambda copy: copy.wait_recv())

            @pl.loop(0, G)
            def _(b):
                @pl.when((b < z) & (z < G - 1))
                def _():
                    ZLT[pL, b] = (z_product(pL, b) + ZLT[pL, b].astype(f32)).astype(bf16)

                @pl.when((b < z) & (z == G - 1))
                def _():
                    ZLT[pL, b] = z_product(pL, b).astype(bf16)

            at_place(out_l, lambda copy: copy.start())

        q2 = t - LEAD

        @pl.when(live(q2, nY))
        def _():
            for k in range(1, A):
                y_send(q2, k).wait_recv()

            @pl.loop(0, G)
            def _(b):
                total = y_product(q2, a, b)
                for k in range(1, A):
                    total += YR[q2, k - 1, b].astype(f32)
                YR[q2, 0, b] = total.astype(bf16)

        qr = t - LEAD - HOP * z

        @pl.when(live(qr, nY))
        def _():
            out_r, in_r, _, _ = y_line(qr)
            at_place(in_r, lambda copy: copy.wait_recv())

            @pl.loop(0, G)
            def _(b):
                @pl.when((b > z) & (z > 0))
                def _():
                    YRT[qr, b - 1] = (YR[qr, 0, b].astype(f32) + YRT[qr, b - 1].astype(f32)).astype(bf16)

            at_place(out_r, lambda copy: copy.start())

        qL = t - LEAD - HOP * (G - 1 - z)

        @pl.when(live(qL, nY))
        def _():
            _, _, out_l, in_l = y_line(qL)
            at_place(in_l, lambda copy: copy.wait_recv())

            @pl.loop(0, G)
            def _(b):
                @pl.when((b < z) & (z < G - 1))
                def _():
                    YLT[qL, b] = (YR[qL, 0, b].astype(f32) + YLT[qL, b].astype(f32)).astype(bf16)

            at_place(out_l, lambda copy: copy.start())

        pf = t - HOP * far

        @pl.when(live(pf, nZ))
        def _():
            mine = z_product(pf, z)
            from_left = ZRT[pf, jnp.maximum(z - 1, 0)].astype(f32)
            from_right = ZLT[pf, jnp.minimum(z, G - 2)].astype(f32)
            mine = mine + jnp.where(z > 0, from_left, 0.0) + jnp.where(z < G - 1, from_right, 0.0)
            ZX[pf, a] = mine.astype(bf16)
            for k in range(1, A):
                zx_copy(pf, k).start()

        pg = t - HOP * far - LEAD

        @pl.when(live(pg, nZ))
        def _():
            for k in range(1, A):
                remote(
                    ZX.at[pg, lax.rem(a + A - k, A)], ZX.at[pg, lax.rem(a + A - k, A)],
                    zx_s.at[pg, k - 1], zx_r.at[pg, k - 1], peer(k),
                ).wait_recv()
            total = ZX[pg, 0].astype(f32)
            for k in range(1, A):
                total += ZX[pg, k].astype(f32)
            for k in range(1, A):
                zx_copy(pg, k).wait_send()
            ZX[pg, a] = total.astype(bf16)
            own_z(pg).start()
            sib_z(pg).start()

        qf = t - LEAD - HOP * far

        @pl.when(live(qf, nY))
        def _():
            total = YR[qf, 0, z].astype(f32)
            from_left = YRT[qf, jnp.maximum(z - 1, 0)].astype(f32)
            from_right = YLT[qf, jnp.minimum(z, G - 2)].astype(f32)
            total = total + jnp.where(z > 0, from_left, 0.0) + jnp.where(z < G - 1, from_right, 0.0)
            YR[qf, 0, z] = total.astype(bf16)
            for k in range(1, A):
                ag_copy(qf, k).start()
            own_y(qf).start()
            sib_own(qf).start()

        qg = t - LEAD - HOP * far - LEAD

        @pl.when(live(qg, nY))
        def _():
            for k in range(1, A):
                here = y_out(qg, lax.rem(a + A - k, A), c)
                remote(here, here, ag_s.at[qg, k - 1], ag_r.at[qg, k - 1], peer(k)).wait_recv()
                sib_pass(qg, k).start()

        return carry

    steps = max(nY, nZ) + 2 * LEAD + HOP * (G - 1)
    lax.fori_loop(0, steps, step, 0)

    gain_core().wait_send()
    for k in range(1, A):
        gain_part(k).wait_send()

    @pl.when(z < G - 1)
    def _():
        gain_right().wait_send()

    @pl.when(z > 0)
    def _():
        gain_left().wait_send()

    for i in range(4):
        cross[1, i].wait_send()

    def drain_y(q, carry):
        for k in range(1, A):
            @pl.when(q >= nY - YS_RING)
            def _():
                y_send(q, k).wait_send()

            ag_copy(q, k).wait_send()
            sib_pass(q, k).wait_send()
            there = y_out(q, lax.rem(a + A - k, A), 1 - c)
            remote(there, there, sib_s.at[q, k], sib_r.at[q, k], sib).wait_recv()
        out_r, _, out_l, _ = y_line(q)
        at_place(out_r, lambda copy: copy.wait_send())
        at_place(out_l, lambda copy: copy.wait_send())
        own_y(q).wait()
        sib_own(q).wait_send()
        there = y_out(q, a, 1 - c)
        remote(there, there, sib_s.at[q, 0], sib_r.at[q, 0], sib).wait_recv()
        return carry

    lax.fori_loop(0, nY, drain_y, 0)

    def drain_z(p, carry):
        out_r, _, out_l, _ = z_line(p)
        at_place(out_r, lambda copy: copy.wait_send())
        at_place(out_l, lambda copy: copy.wait_send())
        own_z(p).wait()
        sib_z(p).wait_send()
        there = z_out(p, 1 - c)
        remote(there, there, sib_s.at[nY + p, 0], sib_r.at[nY + p, 0], sib).wait_recv()
        return carry

    lax.fori_loop(0, nZ, drain_z, 0)


def summed_grads(groups, dp, activations, others, dz, dy, dgate, dup, dq, gain_parts):
    hidden, tokens = activations[0].shape
    width, qkv_cols = dz.shape[1], dq.shape[1]
    plan = grad_plan(groups, dp, tokens, width, hidden, qkv_cols)
    G, A, nY, nZ = groups, plan["pairs"], plan["pieces"], plan["z_pieces"]
    block, zr, zc = plan["block"], plan["z_rows"], plan["z_cols"]
    bf16, DMA = jnp.bfloat16, pltpu.SemaphoreType.DMA
    any_space = pl.BlockSpec(memory_space=pl.ANY)
    in_vmem, f32, gain_shape = pl.BlockSpec(memory_space=pltpu.VMEM), jnp.float32, gain_parts.shape
    return pl.pallas_call(
        functools.partial(grad_kernel, plan),
        out_shape=(
            jax.ShapeDtypeStruct((block, 2 * hidden + qkv_cols), bf16),
            jax.ShapeDtypeStruct((plan["down_block"] + block, width), bf16),
            jax.ShapeDtypeStruct(gain_parts.shape, f32),
        ),
        in_specs=[any_space] * 13 + [in_vmem],
        out_specs=(any_space, any_space, in_vmem),
        scratch_shapes=[
            pltpu.VMEM((hidden + 3 * width, 2 * tokens), bf16),
            pltpu.VMEM((2 * tokens, width + hidden + qkv_cols // 2), bf16),
            pltpu.VMEM((YS_RING, A - 1, G, block, LANES), bf16),
            pltpu.VMEM((nY, A - 1, G, block, LANES), bf16),
            pltpu.VMEM((nY, G - 1, block, LANES), bf16),
            pltpu.VMEM((nY, G - 1, block, LANES), bf16),
            pltpu.VMEM((nZ, G - 1, zr, zc), bf16),
            pltpu.VMEM((nZ, G - 1, zr, zc), bf16),
            pltpu.VMEM((nZ, A, zr, zc), bf16),
            DMA((12,)), DMA((8,)), DMA((8,)),
            DMA((nY, A - 1)), DMA((nY, A - 1)),
            DMA((nY,)), DMA((nY,)), DMA((nY,)), DMA((nY,)),
            DMA((nZ,)), DMA((nZ,)), DMA((nZ,)), DMA((nZ,)),
            DMA((nZ, A - 1)), DMA((nZ, A - 1)),
            DMA((nY, A - 1)), DMA((nY, A - 1)),
            DMA((nY + nZ, A)), DMA((nY + nZ, A)),
            DMA((nY + nZ,)),
            pltpu.VMEM(gain_shape, f32),
            pltpu.VMEM((A,) + gain_shape, f32),
            pltpu.VMEM((3,) + gain_shape, f32),
            pltpu.VMEM(gain_shape, f32),
            pltpu.VMEM(gain_shape, f32),
            DMA((2,)), DMA((max(A - 1, 1),)), DMA((max(A - 1, 1),)), DMA((2,)), DMA((2,)),
        ],
        compiler_params=pltpu.CompilerParams(
            collective_id=3, has_side_effects=True, vmem_limit_bytes=63 * 1024 * 1024
        ),
        cost_estimate=pl.CostEstimate(
            flops=2 * 2 * tokens * (width * (2 * hidden + qkv_cols + width) + hidden * width) // 2,
            bytes_accessed=40_000_000, transcendentals=0,
        ),
    )(*activations, *others, dz, dy, dgate, dup, dq, gain_parts)


W_HOP = 4
AFTER = 1
ROOMS = 3
gather_families = (
    (1, False, False),
    (2, False, True),
    (1, False, False),
    (8, True, False),
    (4, False, False),
)


def gather_kernel(groups, pairs, families, rows, *refs):
    G, A, F = groups, pairs, len(families)
    shards, refs = refs[:F], refs[F:]
    if rows:
        (x, mask, cosines, sines), refs = refs[:4], refs[4:]
    wholes, refs = refs[:F], refs[F:]
    if rows:
        (gain_rows, first_out, handed), refs = refs[:3], refs[3:]
    sems, refs = refs[: 9 * F], refs[9 * F :]
    if rows:
        in_gain, in_wide, in_gate, in_down, in_sem, hand_s, hand_r, n1, qkvt, ot, y, n2, gate, inner = refs
    s, z, d = lax.axis_index("section"), lax.axis_index("group"), lax.axis_index("dp")
    c, a = lax.rem(d, 2), lax.div(d, 2)
    sib = (s, z, 2 * a + 1 - c)
    right, left = (s, z + 1, d), (s, z - 1, d)

    def peer(part):
        return (s, z, 2 * part + c)

    barrier = pltpu.get_barrier_semaphore()
    others = [peer(lax.rem(a + k, A)) for k in range(1, A)]
    if rows:
        others.append((1 - s, z, d))
    others += [sib, (s, lax.rem(z + 1, G), d), (s, lax.rem(z + G - 1, G), d)]
    for dev in others:
        pl.semaphore_signal(barrier, inc=1, device_id=dev, device_id_type=MESH)
    pl.semaphore_wait(barrier, len(others))

    def columns(f, i):
        pieces, halves, _ = families[f]
        size = shards[f].shape[1] // pieces
        if halves:
            i = lax.rem(i, 2) * (pieces // 2) + lax.div(i, 2)
        return pl.ds(pl.multiple_of(i * size, 128), size)

    def cut(f, ref, i):
        return ref.at[:, columns(f, i)]

    def placed(f, i, o, part, core):
        return cut(f, wholes[f].at[(o * A + part) * 2 + core], i)

    def copy(f, i, o, part, kind, index, dev, own=False, core=None):
        core = c if core is None else core
        there = placed(f, i, o, part, core)
        src = cut(f, shards[f], i) if own else there
        send, recv = sems[f * 9 + 2 * kind], sems[f * 9 + 2 * kind + 1]
        return pltpu.make_async_remote_copy(
            src_ref=src, dst_ref=there, send_sem=send.at[index], recv_sem=recv.at[index], device_id=dev, device_id_type=MESH
        )

    def to_right(f, i, o, part, own=False):
        return copy(f, i, o, part, 0, (i, o, lax.rem(part + A - a, A)), right, own)

    def to_left(f, i, o, part, own=False):
        return copy(f, i, o, part, 1, (i, o, lax.rem(part + A - a, A)), left, own)

    def to_part(f, i, o, k, own=False):
        return copy(f, i, o, a, 2, (i, o, k - 1), peer(lax.rem(a + k, A)), own)

    def from_part(f, i, o, k):
        return copy(f, i, o, lax.rem(a + A - k, A), 2, (i, o, k - 1), peer(lax.rem(a + A - k, A)))

    def to_core(f, i, o, part, own=False):
        return copy(f, i, o, part, 3, (i, o, lax.rem(part + A - a, A)), sib, own)

    def from_core(f, i, o, k):
        part = lax.rem(a + k, A)
        return copy(f, i, o, part, 3, (i, o, k), sib, core=1 - c)

    def own_copy(f, i):
        return pltpu.make_async_copy(cut(f, shards[f], i), placed(f, i, z, a, c), sems[f * 9 + 8].at[i])

    def along(f, i, o, part, own, go_right, go_left):
        if go_right:
            @pl.when(z < G - 1)
            def _():
                to_right(f, i, o, part, own).start()
        if go_left:
            @pl.when(z > 0)
            def _():
                to_left(f, i, o, part, own).start()

    first = []
    total = 0
    for pieces, _, _ in families:
        first.append(total)
        total += pieces

    def into(f, i, room):
        return pltpu.make_async_copy(wholes[f].at[:, :, columns(f, i)], room, in_sem.at[first[f] + i])

    def arrived(f, i, room):
        own_copy(f, i).wait()

        @pl.loop(0, G)
        def _(o):
            for k in range(A):
                from_core(f, i, o, k).wait_recv()

        into(f, i, room).start()

    def hand_over(i):
        place = columns(4, i)
        return pltpu.make_async_remote_copy(
            src_ref=first_out.at[:, place], dst_ref=handed.at[:, place], send_sem=hand_s.at[i], recv_sem=hand_r.at[i],
            device_id=(1 - s, z, d), device_id_type=MESH,
        )

    def one_matrix(room):
        return room.reshape(room.shape[0] * room.shape[1], room.shape[2])

    def forward(t):
        f32, bf16 = jnp.float32, jnp.bfloat16
        slots, part, half, ratio = x.shape[0] // max(rows, 1), KVH * HD, HD // 2, H // KVH
        after = W_HOP * G + AFTER
        places = [(1, i) for i in range(families[1][0])] + [(2, 0)]

        @pl.when(t == first[0] + after)
        def _():
            arrived(0, 0, in_gain)
            into(0, 0, in_gain).wait()
            turned = one_matrix(in_gain[...]).astype(f32).T
            gain_rows[...] = turned[:8]
            n1[...] = scaled_norm(x[...].astype(f32), gain_rows[0:1, :])[1]

        for slot, (f, i) in enumerate(places):
            @pl.when(t == first[f] + i + after)
            def _(slot=slot, f=f, i=i):
                arrived(f, i, in_wide.at[slot])

        i3 = t - first[3] - after

        @pl.when((i3 >= 0) & (i3 < families[3][0]))
        def _():
            arrived(3, i3, in_gate.at[lax.rem(i3, ROOMS)])

        i4 = t - first[4] - after

        @pl.when((i4 >= 0) & (i4 < families[4][0]))
        def _():
            arrived(4, i4, in_down.at[lax.rem(i4, ROOMS)])

        for i in range(families[1][0]):
            @pl.when(t == first[1] + i + after + 1)
            def _(i=i):
                into(1, i, in_wide.at[i]).wait()
                for j in range(in_wide.shape[3] // part):
                    weight = one_matrix(in_wide[i, :, :, j * part : (j + 1) * part])
                    chunk = jnp.dot(n1[...], weight, preferred_element_type=f32).T
                    top = (i * (in_wide.shape[3] // part) + j) * part
                    if top >= (H + KVH) * HD:
                        qkvt[top : top + part, :] = chunk.astype(bf16)
                        continue
                    for h in range(KVH):
                        base = top + h * HD
                        front, back = chunk[h * HD : h * HD + half], chunk[h * HD + half : (h + 1) * HD]
                        qkvt[base : base + half, :] = (front * cosines[...] - back * sines[...]).astype(bf16)
                        qkvt[base + half : base + HD, :] = (back * cosines[...] + front * sines[...]).astype(bf16)

        def heads(index, carry):
            row, k = lax.div(index, KVH), lax.rem(index, KVH)
            tokens = pl.ds(pl.multiple_of(row * slots, 128), slots)

            def band(head):
                return pl.ds(pl.multiple_of(head * HD, 16), HD)

            keys, values = qkvt[band(H + k), tokens], qkvt[band(H + KVH + k), tokens]
            queries = jnp.concatenate([qkvt[band(ratio * k + g), tokens] for g in range(ratio)], 1)
            key = lax.broadcasted_iota(jnp.int32, (slots, ratio * slots), 0)
            query = lax.rem(lax.broadcasted_iota(jnp.int32, (slots, ratio * slots), 1), slots)
            valid = mask[pl.ds(pl.multiple_of(row * slots, 128), slots), :] > 0.0
            scores = pair_scores(keys, queries, (key <= query) & valid)
            top = jnp.max(scores, 0, keepdims=True)
            total = top + jnp.log(jnp.sum(jnp.exp(scores - top), 0, keepdims=True))
            probs = jnp.exp(scores - total).astype(bf16)
            out = jnp.dot(values, probs, preferred_element_type=f32).astype(bf16)
            for g in range(ratio):
                ot[band(ratio * k + g), tokens] = out[:, g * slots : (g + 1) * slots]
            return carry

        split = rows * KVH // 2
        turn = t - first[2] - after

        @pl.when((turn >= 1) & (turn <= 2))
        def _():
            lax.fori_loop((turn - 1) * split, turn * split, heads, 0)

        @pl.when(turn == 2)
        def _():
            into(2, 0, in_wide.at[len(places) - 1]).wait()
            y[...] = x[...].astype(f32) + lax.dot_general(
                ot[...], one_matrix(in_wide[len(places) - 1]), down_rows, preferred_element_type=f32
            )
            n2[...] = scaled_norm(y[...], gain_rows[1:2, :])[1]

        c3 = i3 - 2
        size = in_gate.shape[3]

        @pl.when((c3 >= 0) & (c3 < families[3][0]))
        def _():
            room = lax.rem(c3, ROOMS)
            into(3, c3, in_gate.at[room]).wait()
            value = jnp.dot(n2[...], one_matrix(in_gate[room]), preferred_element_type=f32)

            @pl.when(lax.rem(c3, 2) == 0)
            def _():
                gate[...] = value

            @pl.when(lax.rem(c3, 2) == 1)
            def _():
                opened = gate[...]
                inner[:, pl.ds(pl.multiple_of(lax.div(c3, 2) * size, 128), size)] = (
                    opened / (1.0 + jnp.exp(-opened)) * value
                ).astype(bf16)

        c4 = i4 - 2

        @pl.when((c4 >= 0) & (c4 < families[4][0]))
        def _():
            room = lax.rem(c4, ROOMS)
            into(4, c4, in_down.at[room]).wait()
            place = columns(4, c4)
            value = y[:, place] + jnp.dot(inner[...], one_matrix(in_down[room]), preferred_element_type=f32)
            first_out[:, place] = (value * mask[...]).astype(bf16)
            hand_over(c4).start()

    def step(t, carry):
        for f, (pieces, _, parts_first) in enumerate(families):
            i0 = t - first[f]

            @pl.when((i0 >= 0) & (i0 < pieces))
            def _(f=f, i0=i0):
                along(f, i0, z, a, True, True, True)
                for k in range(1, A):
                    to_part(f, i0, z, k, True).start()
                to_core(f, i0, z, a, True).start()
                own_copy(f, i0).start()

        for f, (pieces, _, parts_first) in enumerate(families):
            for h in range(G):
                for k in range(A if parts_first else 1):
                    if h == 0:
                        continue
                    i = t - first[f] - W_HOP * h - (W_HOP if k > 0 else 0)
                    part = lax.rem(a + k, A)
                    for sign in (-1, 1):
                        o = z + sign * h

                        @pl.when((i >= 0) & (i < pieces) & (o >= 0) & (o < G))
                        def _(f=f, i=i, o=o, part=part, sign=sign, parts_first=parts_first):
                            if sign < 0:
                                to_right(f, i, o, part).wait_recv()
                                along(f, i, o, part, False, True, False)
                            else:
                                to_left(f, i, o, part).wait_recv()
                                along(f, i, o, part, False, False, True)
                            if not parts_first:
                                for j in range(1, A):
                                    to_part(f, i, o, j).start()
                            to_core(f, i, o, part).start()

                if parts_first and h > 0:
                    continue
                i = t - first[f] - W_HOP * (h + 1)
                for sign in (-1, 1) if h else (1,):
                    o = z + sign * h

                    @pl.when((i >= 0) & (i < pieces) & (o >= 0) & (o < G))
                    def _(f=f, i=i, o=o, parts_first=parts_first):
                        for k in range(1, A):
                            from_part(f, i, o, k).wait_recv()
                            part = lax.rem(a + A - k, A)
                            if parts_first:
                                along(f, i, o, part, False, True, True)
                            to_core(f, i, o, part).start()
        if rows:
            forward(t)
        return carry

    lax.fori_loop(0, total + max(W_HOP * (G + 1), W_HOP * G + AFTER + 2), step, 0)

    if rows:
        for i in range(families[4][0]):
            hand_over(i).wait()

    for f, (pieces, _, parts_first) in enumerate(families):
        def drain(i, carry, f=f, parts_first=parts_first):
            if not rows:
                own_copy(f, i).wait()

            def by_group(o, carry):
                for k in range(A):
                    part = lax.rem(a + k, A)
                    to_core(f, i, o, part).wait_send()
                    if not rows:
                        from_core(f, i, o, k).wait_recv()
                    if parts_first or k == 0:
                        @pl.when((z < G - 1) & (o <= z))
                        def _(part=part):
                            to_right(f, i, o, part).wait_send()

                        @pl.when((z > 0) & (o >= z))
                        def _(part=part):
                            to_left(f, i, o, part).wait_send()
                for k in range(1, A):
                    if parts_first:
                        @pl.when(o == z)
                        def _(k=k):
                            to_part(f, i, o, k).wait_send()
                    else:
                        to_part(f, i, o, k).wait_send()
                return carry

            return lax.fori_loop(0, G, by_group, carry)

        lax.fori_loop(0, pieces, drain, 0)


def gathered(groups, dp, shards, families, tokens):
    A, DMA, bf16, f32 = dp // 2, pltpu.SemaphoreType.DMA, jnp.bfloat16, jnp.float32
    any_space, in_vmem = pl.BlockSpec(memory_space=pl.ANY), pl.BlockSpec(memory_space=pltpu.VMEM)
    devices, shape = groups * dp, jax.ShapeDtypeStruct
    scratch = []
    for pieces, _, parts_first in families:
        on_line = (pieces, groups, A if parts_first else 1)
        scratch += [DMA(on_line)] * 4 + [DMA((pieces, groups, max(A - 1, 1)))] * 2 + [DMA((pieces, groups, A))] * 2
        scratch += [DMA((pieces,))]
    outs = tuple(shape((devices,) + x.shape, x.dtype) for x in shards)
    extra, rows = (), 0
    if tokens is not None:
        x, mask, tables, rows = tokens
        extra = (x, mask) + tables
        count, width = x.shape
        hidden = devices * shards[4].shape[0]
        outs += (shape((8, width), f32), shape((count, width), bf16), shape((count, width), bf16))

        def room(f, rooms):
            return pltpu.VMEM((rooms, devices, shards[f].shape[0], shards[f].shape[1] // families[f][0]), bf16)

        scratch += [
            pltpu.VMEM((devices,) + shards[0].shape, bf16), room(1, families[1][0] + 1), room(3, ROOMS), room(4, ROOMS),
            DMA((sum(family[0] for family in families),)), DMA((families[4][0],)), DMA((families[4][0],)),
            pltpu.VMEM((count, width), bf16), pltpu.VMEM((shards[1].shape[1], count), bf16),
            pltpu.VMEM((width, count), bf16), pltpu.VMEM((count, width), f32), pltpu.VMEM((count, width), bf16),
            pltpu.VMEM((count, shards[3].shape[1] // families[3][0]), f32), pltpu.VMEM((count, hidden), bf16),
        ]
    return pl.pallas_call(
        functools.partial(gather_kernel, groups, A, families, rows),
        out_shape=outs,
        in_specs=[any_space] * len(shards) + [in_vmem] * len(extra),
        out_specs=(any_space,) * len(shards) + ((in_vmem, in_vmem, any_space) if rows else ()),
        scratch_shapes=scratch,
        compiler_params=pltpu.CompilerParams(
            collective_id=5, has_side_effects=True, vmem_limit_bytes=56 * 1024 * 1024
        ),
    )(*shards, *extra)


def body(
    inputs_x, cotangent, lengths, attn_gain, qkv_weight, out_weight, ffn_gain, gate_up, down_weight
):
    is_first = lax.axis_index("section") == 0
    rows, slots, width = inputs_x.shape
    tables = turned_tables(slots, rows)
    info = jnp.concatenate([lengths, is_first.astype(jnp.int32)[None]])
    mask = padding(lengths, slots).reshape(-1, 1)
    gains = jnp.concatenate([attn_gain, ffn_gain], 0).T
    gains = jnp.pad(gains, ((0, 0), (0, 128 - gains.shape[1])))
    shards = (gains, qkv_weight[0], out_weight[0], gate_up[0], down_weight[0])
    together = gains.shape[0] % 16 == 0
    tokens = (flat(inputs_x), mask, tables, rows) if together else None
    gathered_all = gathered(
        lax.axis_size("group"), lax.axis_size("dp"), shards, gather_families, tokens
    )
    gains_all, qkv_w, output_weight, gate_up_w, down_w = (flat(x) for x in gathered_all[:5])
    if together:
        gain_rows, _, recv_act = gathered_all[5:]
    else:
        gain_rows = gains_all[:, :2].astype(jnp.float32).T
    gain_one, gain_two = gain_rows[0:1], gain_rows[1:2]
    dz_given = (flat(cotangent).astype(jnp.float32) * mask).astype(jnp.bfloat16)
    if not together:
        after_one = attention_forward(
            info, flat(inputs_x), gain_one, tables, qkv_w, output_weight, rows
        )[0]
        first_out = ffn_forward(after_one, gain_two, mask, gate_up_w, down_w)
        recv_act = passed_along(first_out, "section", 1)
    layer_in = jnp.where(is_first, flat(inputs_x), recv_act)
    after, heads, log_total, attention_turned, normed_turned = attention_forward(
        info, layer_in, gain_one, tables, qkv_w, output_weight, rows
    )
    dy, dy_low, _ = ffn_backward(after, dz_given, gain_two, gate_up_w, down_w)
    (second_dx,) = attention_backward(
        info, layer_in, gain_one, dy, dy_low, tables, heads, log_total, output_weight, qkv_w, rows, False
    )
    recv_grad = passed_along(second_dx, "section", -1)
    after, second_dx = lax.optimization_barrier((after, second_dx))
    hidden_turned, by_gate, by_up, normed_two_turned, result = ffn_prepare(
        after, gain_two, mask, gate_up_w, down_w
    )
    activations = (hidden_turned, attention_turned, normed_two_turned, normed_turned)
    recv_grad, activations, by_gate = lax.optimization_barrier((recv_grad, activations, by_gate))
    others = tuple(swapped(x, "dp") for x in activations)
    dz = jnp.where(is_first, (recv_grad.astype(jnp.float32) * mask).astype(jnp.bfloat16), dz_given)
    dy, dy_low, ffn_gain_part, grad_gate, grad_up = ffn_backward(
        after, dz, gain_two, gate_up_w, down_w, (by_gate, by_up)
    )
    grad_x, attn_gain_part, grad_qkv = attention_backward(
        info, layer_in, gain_one, dy, dy_low, tables, heads, log_total, output_weight, qkv_w, rows, True
    )
    section_out = result.reshape((1,) + inputs_x.shape)
    input_grads = grad_x.reshape((1,) + inputs_x.shape)
    gain_parts = jnp.pad(jnp.concatenate([attn_gain_part, ffn_gain_part], 0), ((0, 6), (0, 0)))
    gate_qkv_sum, down_out_sum, gain_sums = summed_grads(
        lax.axis_size("group"),
        lax.axis_size("dp"),
        activations,
        others,
        dz,
        dy_low,
        grad_gate,
        grad_up,
        grad_qkv,
        gain_parts,
    )
    gain_cols = attn_gain.shape[1] * lax.axis_size("dp")
    gain_sums = lax.dynamic_slice_in_dim(
        gain_sums, lax.axis_index("group") * gain_cols, gain_cols, 1
    )
    gate_width = gate_up.shape[2]
    down_rows = down_weight.shape[1] * lax.axis_size("dp")
    reduced = (
        gain_sums[0],
        gate_qkv_sum[:, gate_width:].astype(jnp.float32),
        down_out_sum[down_rows:].astype(jnp.float32),
        gain_sums[1],
        gate_qkv_sum[:, :gate_width].astype(jnp.float32),
        down_out_sum[:down_rows].astype(jnp.float32),
    )
    return (section_out, input_grads) + tuple((shard_sum[None] for shard_sum in reduced))


def solution(mesh):
    placed = (
        P(("group", "dp"), None, None),
        P(("group", "dp"), None, None),
        P(("group", "dp")),
        P("section", ("group", "dp")),
        P("section", ("group", "dp"), None),
        P("section", ("group", "dp"), None),
        P("section", ("group", "dp")),
        P("section", ("group", "dp"), None),
        P("section", ("group", "dp"), None),
    )
    return jax.shard_map(
        body,
        mesh=mesh,
        in_specs=placed,
        out_specs=(
            P("section", ("group", "dp"), None, None),
            P("section", ("group", "dp"), None, None),
            P("section", "group"),
            P("section", "group", None),
            P("section", "group", None),
            P("section", "group"),
            P("section", "group", None),
            P("section", "group", None),
        ),
        check_vma=False,
    )
```

```python
import functools

import jax
import jax.numpy as jnp
from jax import lax
from jax.experimental import pallas as pl
from jax.experimental.pallas import tpu as pltpu
from jax.sharding import PartitionSpec as P

H = 16
KVH = 8
HD = 96


norm_eps = 1e-05
rope_base = 100000.0
masked_score = -1e30
across = (((1,), (1,)), ((), ()))
down_rows = (((0,), (0,)), ((), ()))


def passed_along(value, axis, by):
    length = lax.axis_size(axis)
    pairs = [(i, i + by) for i in range(length) if 0 <= i + by < length]
    return lax.ppermute(value, axis, pairs)


def swapped(value, axis):
    return lax.ppermute(value, axis, [(i, i ^ 1) for i in range(lax.axis_size(axis))])


def padding(lengths, slot_count):
    position = jnp.arange(slot_count, dtype=jnp.int32)
    return (position[None, :] < lengths[:, None]).astype(jnp.float32)[..., None]


FF_CHUNK = 1024
across = (((1,), (1,)), ((), ()))
down_rows = (((0,), (0,)), ((), ()))


def scaled_norm(value, gain):
    scale = lax.rsqrt(jnp.mean(value * value, -1, keepdims=True) + norm_eps)
    return scale, (value * scale * gain).astype(jnp.bfloat16)


def ffn_forward_kernel(y, gain, mask, wg, wu, wd, out, n2, acc):
    j = pl.program_id(0)

    @pl.when(j == 0)
    def _():
        n2[...] = scaled_norm(y[...], gain[...])[1]
        acc[...] = y[...]

    gate = jnp.dot(n2[...], wg[...], preferred_element_type=jnp.float32)
    up = jnp.dot(n2[...], wu[...], preferred_element_type=jnp.float32)
    hidden = (gate / (1.0 + jnp.exp(-gate)) * up).astype(jnp.bfloat16)
    acc[...] += jnp.dot(hidden, wd[...], preferred_element_type=jnp.float32)

    @pl.when(j == pl.num_programs(0) - 1)
    def _():
        out[...] = (acc[...] * mask[...]).astype(jnp.bfloat16)


def ffn_specs(tokens, width, hidden):
    steps = hidden // FF_CHUNK
    whole = pl.BlockSpec((tokens, width), lambda j: (0, 0))
    row = pl.BlockSpec((1, width), lambda j: (0, 0))
    weights = [
        pl.BlockSpec((width, FF_CHUNK), lambda j: (0, j)),
        pl.BlockSpec((width, FF_CHUNK), lambda j: (0, j + steps)),
        pl.BlockSpec((FF_CHUNK, width), lambda j: (j, 0)),
    ]
    return steps, whole, row, weights


def ffn_forward(y, gain, mask, gate_up_w, down_w):
    tokens, width = y.shape
    hidden = down_w.shape[0]
    steps, whole, row, weights = ffn_specs(tokens, width, hidden)
    return pl.pallas_call(
        ffn_forward_kernel,
        grid=(steps,),
        out_shape=jax.ShapeDtypeStruct((tokens, width), jnp.bfloat16),
        in_specs=[whole, row, pl.BlockSpec((tokens, 1), lambda j: (0, 0))] + weights,
        out_specs=whole,
        scratch_shapes=[pltpu.VMEM((tokens, width), jnp.bfloat16), pltpu.VMEM((tokens, width), jnp.float32)],
        compiler_params=pltpu.CompilerParams(vmem_limit_bytes=40 * 1024 * 1024),
        cost_estimate=pl.CostEstimate(
            flops=6 * tokens * width * hidden, bytes_accessed=6 * width * hidden, transcendentals=tokens * hidden
        ),
    )(y, gain, mask, gate_up_w, gate_up_w, down_w)


def ffn_prepare_kernel(y, gain, mask, wg, wu, wd, at, by_gate, by_up, n2t, out, n2, acc):
    j = pl.program_id(0)
    bf16, f32 = jnp.bfloat16, jnp.float32

    @pl.when(j == 0)
    def _():
        n = scaled_norm(y[...], gain[...])[1]
        n2[...] = n
        n2t[...] = n.T
        acc[...] = y[...]

    gate = jnp.dot(n2[...], wg[...], preferred_element_type=f32)
    up = jnp.dot(n2[...], wu[...], preferred_element_type=f32)
    sig = 1.0 / (1.0 + jnp.exp(-gate))
    silu = gate * sig
    hidden = (silu * up).astype(bf16)
    at[...] = hidden.T
    by_gate[...] = (up * sig * (1.0 + gate * (1.0 - sig))).astype(bf16)
    by_up[...] = silu.astype(bf16)
    acc[...] += jnp.dot(hidden, wd[...], preferred_element_type=f32)

    @pl.when(j == pl.num_programs(0) - 1)
    def _():
        out[...] = (acc[...] * mask[...]).astype(bf16)


def ffn_prepare(y, gain, mask, gate_up_w, down_w):
    tokens, width = y.shape
    hidden = down_w.shape[0]
    steps, whole, row, weights = ffn_specs(tokens, width, hidden)
    shape, bf16 = jax.ShapeDtypeStruct, jnp.bfloat16
    part = pl.BlockSpec((tokens, FF_CHUNK), lambda j: (0, j))
    return pl.pallas_call(
        ffn_prepare_kernel,
        grid=(steps,),
        out_shape=(
            shape((hidden, tokens), bf16), shape((tokens, hidden), bf16), shape((tokens, hidden), bf16),
            shape((width, tokens), bf16), shape((tokens, width), bf16),
        ),
        in_specs=[whole, row, pl.BlockSpec((tokens, 1), lambda j: (0, 0))] + weights,
        out_specs=(
            pl.BlockSpec((FF_CHUNK, tokens), lambda j: (j, 0)), part, part,
            pl.BlockSpec((width, tokens), lambda j: (0, 0)), whole,
        ),
        scratch_shapes=[pltpu.VMEM((tokens, width), bf16), pltpu.VMEM((tokens, width), jnp.float32)],
        compiler_params=pltpu.CompilerParams(vmem_limit_bytes=48 * 1024 * 1024),
        cost_estimate=pl.CostEstimate(
            flops=6 * tokens * width * hidden, bytes_accessed=6 * width * hidden, transcendentals=tokens * hidden
        ),
    )(y, gain, mask, gate_up_w, gate_up_w, down_w)


def ffn_backward_kernel(prepared, y, dz, gain, wg, wu, wd, *rest):
    bf16, f32 = jnp.bfloat16, jnp.float32
    if prepared:
        by_gate, by_up, dy, dyb, gain_grad, dgate, dup, acc = rest
    else:
        dy, dyb, gain_grad, n2, acc = rest
    j = pl.program_id(0)

    @pl.when(j == 0)
    def _():
        acc[...] = jnp.zeros_like(acc)
        if not prepared:
            n2[...] = scaled_norm(y[...], gain[...])[1]

    grad = lax.dot_general(dz[...], wd[...], across, preferred_element_type=f32)
    if prepared:
        grad_gate = (grad * by_gate[...].astype(f32)).astype(bf16)
        grad_up = (grad * by_up[...].astype(f32)).astype(bf16)
        dgate[...] = grad_gate
        dup[...] = grad_up
    else:
        gate = jnp.dot(n2[...], wg[...], preferred_element_type=f32)
        up = jnp.dot(n2[...], wu[...], preferred_element_type=f32)
        sig = 1.0 / (1.0 + jnp.exp(-gate))
        grad_gate = (grad * up * sig * (1.0 + gate * (1.0 - sig))).astype(bf16)
        grad_up = (grad * (gate * sig)).astype(bf16)
    acc[...] += lax.dot_general(grad_gate, wg[...], across, preferred_element_type=f32) + lax.dot_general(
        grad_up, wu[...], across, preferred_element_type=f32
    )

    @pl.when(j == pl.num_programs(0) - 1)
    def _():
        value, grad_normed = y[...], acc[...]
        r = lax.rsqrt(jnp.mean(value * value, -1, keepdims=True) + norm_eps)
        scaled = grad_normed * gain[...]
        gain_grad[...] = jnp.sum(grad_normed * value * r, axis=0, keepdims=True)
        inner = jnp.mean(value * scaled, -1, keepdims=True)
        total = dz[...].astype(f32) + r * scaled - value * (r * r * r) * inner
        dy[...] = total
        dyb[...] = total.astype(bf16)


def ffn_backward(y, dz, gain, gate_up_w, down_w, factors=()):
    tokens, width = y.shape
    hidden = down_w.shape[0]
    steps, whole, row, weights = ffn_specs(tokens, width, hidden)
    shape, bf16, f32 = jax.ShapeDtypeStruct, jnp.bfloat16, jnp.float32
    outs = [shape((tokens, width), f32), shape((tokens, width), bf16), shape((1, width), f32)]
    out_specs = [whole, whole, row]
    scratch = [pltpu.VMEM((tokens, width), f32)]
    parts = [pl.BlockSpec((tokens, FF_CHUNK), lambda j: (0, j))] * len(factors)
    if factors:
        outs += [shape((tokens, hidden), bf16)] * 2
        out_specs += parts
    else:
        scratch = [pltpu.VMEM((tokens, width), bf16)] + scratch
    return pl.pallas_call(
        functools.partial(ffn_backward_kernel, bool(factors)),
        grid=(steps,),
        out_shape=tuple(outs),
        in_specs=[whole, whole, row] + weights + parts,
        out_specs=tuple(out_specs),
        scratch_shapes=scratch,
        compiler_params=pltpu.CompilerParams(vmem_limit_bytes=48 * 1024 * 1024),
        cost_estimate=pl.CostEstimate(
            flops=10 * tokens * width * hidden, bytes_accessed=6 * width * hidden, transcendentals=tokens * hidden
        ),
    )(y, dz, gain, gate_up_w, gate_up_w, down_w, *factors)


def turned_tables(slots, rows):
    half_width = HD // 2
    frequency = rope_base ** (-(jnp.arange(half_width, dtype=jnp.float32) * 2.0 / HD))
    angles = frequency[:, None] * jnp.arange(slots, dtype=jnp.float32)[None, :]
    return jnp.tile(jnp.cos(angles), (1, rows)), jnp.tile(jnp.sin(angles), (1, rows))


def pair_mask(length, slots):
    groups = H // KVH
    key = lax.broadcasted_iota(jnp.int32, (slots, groups * slots), 0)
    query = lax.rem(lax.broadcasted_iota(jnp.int32, (slots, groups * slots), 1), slots)
    return (key <= query) & (key < length)


def pair_of(ref, k, row, slots):
    groups = H // KVH
    first = groups * k * HD
    return jnp.concatenate(
        [ref[first + g * HD : first + (g + 1) * HD, row * slots : (row + 1) * slots] for g in range(groups)], 1
    )


def key_value(qkvt, k, row, slots):
    tokens = slice(row * slots, (row + 1) * slots)
    keys = qkvt[(H + k) * HD : (H + k + 1) * HD, tokens]
    values = qkvt[(H + KVH + k) * HD : (H + KVH + k + 1) * HD, tokens]
    return keys, values


def pair_scores(keys, queries, mask):
    scores = lax.dot_general(keys, queries, down_rows, preferred_element_type=jnp.float32) * HD ** (-0.5)
    return jnp.where(mask, scores, masked_score)


def attention_forward_kernel(rows, info, x, gain, cosines, sines, w, wo, y, qkvt, lse, ot, n1t, n1):
    j = pl.program_id(0)
    bf16, f32 = jnp.bfloat16, jnp.float32
    slots, part, half = x.shape[0] // rows, KVH * HD, HD // 2
    groups = H // KVH

    @pl.when(j == 0)
    def _():
        n = scaled_norm(x[...].astype(f32), gain[...])[1]
        n1[...] = n
        n1t[...] = n.T

    chunk = jnp.dot(n1[...], w[...], preferred_element_type=f32).T

    @pl.when(j <= groups)
    def _():
        for h in range(KVH):
            front, back = chunk[h * HD : h * HD + half], chunk[h * HD + half : (h + 1) * HD]
            base = j * part + h * HD
            qkvt[pl.ds(pl.multiple_of(base, 16), half), :] = (front * cosines[...] - back * sines[...]).astype(bf16)
            qkvt[pl.ds(pl.multiple_of(base + half, 16), half), :] = (
                back * cosines[...] + front * sines[...]
            ).astype(bf16)

    @pl.when(j > groups)
    def _():
        qkvt[pl.ds(pl.multiple_of(j * part, 16), part), :] = chunk.astype(bf16)
        for row in range(rows):
            mask = pair_mask(info[row], slots)
            for k in range(KVH):
                keys, values = key_value(qkvt, k, row, slots)
                scores = pair_scores(keys, pair_of(qkvt, k, row, slots), mask)
                top = jnp.max(scores, 0, keepdims=True)
                total = top + jnp.log(jnp.sum(jnp.exp(scores - top), 0, keepdims=True))
                lse[row * KVH + k : row * KVH + k + 1, :] = total
                probs = jnp.exp(scores - total).astype(bf16)
                out = jnp.dot(values, probs, preferred_element_type=f32).astype(bf16)
                for g in range(groups):
                    first = (groups * k + g) * HD
                    ot[first : first + HD, row * slots : (row + 1) * slots] = out[:, g * slots : (g + 1) * slots]
        y[...] = x[...].astype(f32) + lax.dot_general(ot[...], wo[...], down_rows, preferred_element_type=f32)


def attention_backward_kernel(
    rows, keep, info, x, gain, dy, dyb, cosines, sines, qkvt, lse, wo, w, dx, *rest
):
    if keep:
        gain_grad, dqkv, dot, dqkvt, acc = rest
    else:
        dqkv, dot, dqkvt, acc = rest
    j = pl.program_id(0)
    bf16, f32 = jnp.bfloat16, jnp.float32
    slots, part, half = x.shape[0] // rows, KVH * HD, HD // 2
    groups = H // KVH

    def unrotated(grad, row, width):
        tokens = slice(row * slots, (row + 1) * slots)
        cos, sin = cosines[:, tokens], sines[:, tokens]
        if width > slots:
            cos, sin = jnp.concatenate([cos] * groups, 1), jnp.concatenate([sin] * groups, 1)
        grad = grad * HD ** (-0.5)
        front, back = grad[:half], grad[half:]
        return (front * cos + back * sin).astype(bf16), (back * cos - front * sin).astype(bf16)

    @pl.when(j == 0)
    def _():
        dot[...] = lax.dot_general(dyb[...], wo[...], across, preferred_element_type=f32).astype(bf16).T
        acc[...] = jnp.zeros_like(acc)
        for row in range(rows):
            tokens = slice(row * slots, (row + 1) * slots)
            mask = pair_mask(info[row], slots)
            for k in range(KVH):
                keys, values = key_value(qkvt, k, row, slots)
                queries, grads = pair_of(qkvt, k, row, slots), pair_of(dot, k, row, slots)
                scores = pair_scores(keys, queries, mask)
                probs = jnp.exp(scores - lse[row * KVH + k : row * KVH + k + 1, :])
                grad_probs = lax.dot_general(values, grads, down_rows, preferred_element_type=f32)
                grad_scores = (
                    probs * (grad_probs - jnp.sum(probs * grad_probs, 0, keepdims=True))
                ).astype(bf16)
                grad_values = lax.dot_general(grads, probs.astype(bf16), across, preferred_element_type=f32)
                grad_keys = lax.dot_general(queries, grad_scores, across, preferred_element_type=f32)
                grad_queries = jnp.dot(keys, grad_scores, preferred_element_type=f32)
                front, back = unrotated(grad_queries, row, groups * slots)
                for g in range(groups):
                    first = (groups * k + g) * HD
                    dqkvt[first : first + half, tokens] = front[:, g * slots : (g + 1) * slots]
                    dqkvt[first + half : first + HD, tokens] = back[:, g * slots : (g + 1) * slots]
                front, back = unrotated(grad_keys, row, slots)
                first = (H + k) * HD
                dqkvt[first : first + half, tokens] = front
                dqkvt[first + half : first + HD, tokens] = back
                first = (H + KVH + k) * HD
                dqkvt[first : first + HD, tokens] = grad_values.astype(bf16)
        for i in range(groups + 2):
            dqkv[:, i * part : (i + 1) * part] = dqkvt[i * part : (i + 1) * part, :].T

    columns = pl.ds(pl.multiple_of(j * part, 128), part)
    acc[...] += lax.dot_general(dqkv[:, columns], w[...], across, preferred_element_type=f32)

    @pl.when(j == pl.num_programs(0) - 1)
    def _():
        value, grad_normed = x[...].astype(f32), acc[...]
        r = lax.rsqrt(jnp.mean(value * value, -1, keepdims=True) + norm_eps)
        scaled = grad_normed * gain[...]
        inner = jnp.mean(value * scaled, -1, keepdims=True)
        total = dy[...] + (r * scaled - value * (r * r * r) * inner)
        if keep:
            gain_grad[...] = jnp.sum(grad_normed * value * r, axis=0, keepdims=True)
            dx[...] = jnp.where(info[rows] == 1, total, total.astype(bf16).astype(f32))
        else:
            dx[...] = total.astype(bf16)


def attention_specs(tokens, width):
    part = KVH * HD
    whole = lambda *shape: pl.BlockSpec(shape, lambda j: (0,) * len(shape))
    return part, whole, pl.BlockSpec(memory_space=pltpu.SMEM), pl.BlockSpec((width, part), lambda j: (0, j))


def attention_forward(info, x, gain, tables, qkv_w, output_weight, rows):
    tokens, width = x.shape
    cols, slots = qkv_w.shape[1], tokens // rows
    part, whole, scalars, weight = attention_specs(tokens, width)
    shape, bf16, f32 = jax.ShapeDtypeStruct, jnp.bfloat16, jnp.float32
    stats = (rows * KVH, H // KVH * slots)
    return pl.pallas_call(
        functools.partial(attention_forward_kernel, rows),
        grid=(cols // part,),
        out_shape=(
            shape((tokens, width), f32), shape((cols, tokens), bf16), shape(stats, f32),
            shape((H * HD, tokens), bf16), shape((width, tokens), bf16),
        ),
        in_specs=[
            scalars, whole(tokens, width), whole(1, width), whole(HD // 2, tokens), whole(HD // 2, tokens), weight,
            whole(H * HD, width),
        ],
        out_specs=(
            whole(tokens, width), whole(cols, tokens), whole(*stats), whole(H * HD, tokens), whole(width, tokens)
        ),
        scratch_shapes=[pltpu.VMEM((tokens, width), bf16)],
        compiler_params=pltpu.CompilerParams(vmem_limit_bytes=40 * 1024 * 1024),
        cost_estimate=pl.CostEstimate(
            flops=2 * tokens * width * (cols + H * HD), bytes_accessed=2 * width * (cols + H * HD), transcendentals=0
        ),
    )(info, x, gain, *tables, qkv_w, output_weight)


def attention_backward(info, x, gain, dy, dy_low, tables, qkvt, lse, output_weight, qkv_w, rows, keep):
    tokens, width = x.shape
    cols = qkv_w.shape[1]
    part, whole, scalars, weight = attention_specs(tokens, width)
    shape, bf16, f32 = jax.ShapeDtypeStruct, jnp.bfloat16, jnp.float32
    scratch = [pltpu.VMEM((H * HD, tokens), bf16), pltpu.VMEM((cols, tokens), bf16), pltpu.VMEM((tokens, width), f32)]
    outs, out_specs = [shape((tokens, width), f32 if keep else bf16)], [whole(tokens, width)]
    if keep:
        outs += [shape((1, width), f32), shape((tokens, cols), bf16)]
        out_specs += [whole(1, width), whole(tokens, cols)]
    else:
        scratch = [pltpu.VMEM((tokens, cols), bf16)] + scratch
    return pl.pallas_call(
        functools.partial(attention_backward_kernel, rows, keep),
        grid=(cols // part,),
        out_shape=tuple(outs),
        in_specs=[
            scalars, whole(tokens, width), whole(1, width), whole(tokens, width), whole(tokens, width),
            whole(HD // 2, tokens), whole(HD // 2, tokens), whole(cols, tokens), whole(*lse.shape), whole(H * HD, width),
            weight,
        ],
        out_specs=tuple(out_specs),
        scratch_shapes=scratch,
        compiler_params=pltpu.CompilerParams(vmem_limit_bytes=48 * 1024 * 1024),
        cost_estimate=pl.CostEstimate(
            flops=2 * tokens * width * (cols + H * HD), bytes_accessed=2 * width * (cols + H * HD), transcendentals=0
        ),
    )(info, x, gain, dy, dy_low, *tables, qkvt, lse, output_weight, qkv_w)


def flat(array):
    return array.reshape(-1, array.shape[-1])


MESH = pl.DeviceIdType.MESH
LANES = 128


def grad_plan(groups, dp, tokens, width, hidden, qkv_cols):
    pairs = dp // 2
    block = width // groups
    down_block = hidden // groups
    gate_cols = 2 * hidden // 2 // pairs
    qkv_part = qkv_cols // 2 // pairs
    pieces_gate = gate_cols // LANES
    pieces_qkv = qkv_part // LANES
    pieces = pieces_gate + pieces_qkv
    z_rows = LANES
    while down_block % z_rows or block % z_rows:
        z_rows //= 2
    row_chunks = (down_block + block) // z_rows
    half = width // 2
    z_split = max(1, pieces // row_chunks)
    while half % (z_split * LANES):
        z_split -= 1
    return dict(
        groups=groups, pairs=pairs, tokens=tokens, width=width, hidden=hidden, qkv_cols=qkv_cols, block=block,
        down_block=down_block, gate_cols=gate_cols, qkv_part=qkv_part, pieces_gate=pieces_gate, pieces=pieces,
        z_rows=z_rows, z_split=z_split, z_cols=half // z_split, z_pieces=row_chunks * z_split,
        down_chunks=down_block // z_rows, half=half,
    )


YS_RING = 4
HOP = 2
LEAD = 2


def grad_kernel(
    plan, at, ot, n2t, n1t, at2, ot2, n2t2, n1t2, dz, dy, dgate, dup, dq, gp, outy, outz, outg,
    LT, RH, YS, YR, YRT, YLT, ZRT, ZLT, ZX,
    own_sem, xs, xr, ys_s, ys_r, yr_s, yr_r, yl_s, yl_r, zr_s, zr_r, zl_s, zl_r,
    zx_s, zx_r, ag_s, ag_r, sib_s, sib_r, lo,
    GC, GA, GS, GR, GL, gc_sem, ga_s, ga_r, gr_sem, gl_sem,
):
    G, A, T = plan["groups"], plan["pairs"], plan["tokens"]
    width, hidden, half = plan["width"], plan["hidden"], plan["half"]
    block, nY, nZ = plan["block"], plan["pieces"], plan["z_pieces"]
    zr, zc = plan["z_rows"], plan["z_cols"]
    s, z, d = lax.axis_index("section"), lax.axis_index("group"), lax.axis_index("dp")
    c, a = lax.rem(d, 2), lax.div(d, 2)
    sib = (s, z, 2 * a + 1 - c)
    right, left = (s, z + 1, d), (s, z - 1, d)

    def peer(k):
        return (s, z, 2 * lax.rem(a + k, A) + c)

    def remote(src, dst, ss, rs, dev):
        return pltpu.make_async_remote_copy(
            src_ref=src, dst_ref=dst, send_sem=ss, recv_sem=rs, device_id=dev, device_id_type=MESH
        )

    barrier = pltpu.get_barrier_semaphore()
    for dev in [sib, (s, lax.rem(z + 1, G), d), (s, lax.rem(z + G - 1, G), d)] + [peer(k) for k in range(1, A)]:
        pl.semaphore_signal(barrier, inc=1, device_id=dev, device_id_type=MESH)
    pl.semaphore_wait(barrier, A + 2)

    lhs = [
        (at, at2, 0, hidden), (ot, ot2, hidden, width), (n2t, n2t2, hidden + width, width),
        (n1t, n1t2, hidden + 2 * width, width),
    ]
    rhs = [(dz, 0, half), (dy, half, half), (None, width, hidden), (dq, width + hidden, plan["qkv_cols"] // 2)]
    own, cross = {}, {}
    for i, (ref, theirs, row, rows) in enumerate(lhs):
        own[0, i] = pltpu.make_async_copy(ref, LT.at[pl.ds(row, rows), pl.ds(0, T)], own_sem.at[i])
        own[2, i] = pltpu.make_async_copy(theirs, LT.at[pl.ds(row, rows), pl.ds(T, T)], own_sem.at[8 + i])
    for i, (ref, col, cols) in enumerate(rhs):
        if ref is None:
            continue
        mine = pl.ds(pl.multiple_of(c * cols, LANES), cols)
        theirs = pl.ds(pl.multiple_of((1 - c) * cols, LANES), cols)
        own[1, i] = pltpu.make_async_copy(ref.at[:, mine], RH.at[pl.ds(0, T), pl.ds(col, cols)], own_sem.at[4 + i])
        cross[1, i] = remote(ref.at[:, theirs], RH.at[pl.ds(T, T), pl.ds(col, cols)], xs.at[4 + i], xr.at[4 + i], sib)
    col, cols = rhs[2][1:]
    for core, (mine, theirs) in enumerate(((dgate, dup), (dup, dgate))):
        own[1, 2, core] = pltpu.make_async_copy(mine, RH.at[pl.ds(0, T), pl.ds(col, cols)], own_sem.at[6])
        cross[1, 2, core] = remote(theirs, RH.at[pl.ds(T, T), pl.ds(col, cols)], xs.at[6], xr.at[6], sib)
    own[1, 2], cross[1, 2] = own[1, 2, 0], cross[1, 2, 0]
    def fetch(i):
        if i == 2:
            for core in (0, 1):
                @pl.when(c == core)
                def _(core=core):
                    cross[1, 2, core].start()
                    own[1, 2, core].start()
        else:
            cross[1, i].start()
            own[1, i].start()
        own[0, i].start()
        own[2, i].start()

    fetch(0)
    fetch(2)

    def operands_here(i):
        for side in (0, 2, 1):
            own[side, i].wait()
        cross[1, i].wait_recv()

    def product(row, rows, col, cols):
        return jnp.dot(
            LT[pl.ds(row, rows), :], RH[:, pl.ds(col, cols)], preferred_element_type=jnp.float32
        )

    def y_product(q, which, b):
        is_gate = q < plan["pieces_gate"]
        row = jnp.where(is_gate, hidden + width, hidden + 2 * width) + b * block
        col = jnp.where(
            is_gate,
            width + which * plan["gate_cols"] + q * LANES,
            width + hidden + which * plan["qkv_part"] + (q - plan["pieces_gate"]) * LANES,
        )
        return product(pl.multiple_of(row, 16), block, pl.multiple_of(col, LANES), LANES)

    def z_product(p, b):
        r, h = lax.div(p, plan["z_split"]), lax.rem(p, plan["z_split"])
        is_down = r < plan["down_chunks"]
        row = jnp.where(
            is_down, b * plan["down_block"] + r * zr, hidden + b * block + (r - plan["down_chunks"]) * zr
        )
        col = jnp.where(is_down, 0, half) + h * zc
        return product(pl.multiple_of(row, 16), zr, pl.multiple_of(col, LANES), zc)

    def y_out(q, part, core):
        is_gate = q < plan["pieces_gate"]
        col = jnp.where(
            is_gate,
            core * hidden + part * plan["gate_cols"] + q * LANES,
            2 * hidden + core * (plan["qkv_cols"] // 2) + part * plan["qkv_part"] + (q - plan["pieces_gate"]) * LANES,
        )
        return outy.at[:, pl.ds(pl.multiple_of(col, LANES), LANES)]

    def z_out(p, core):
        r, h = lax.div(p, plan["z_split"]), lax.rem(p, plan["z_split"])
        return outz.at[
            pl.ds(pl.multiple_of(r * zr, 16), zr), pl.ds(pl.multiple_of(core * half + h * zc, LANES), zc)
        ]

    def y_send(q, k):
        return remote(YS.at[lax.rem(q, YS_RING), k - 1], YR.at[q, k - 1], ys_s.at[q, k - 1], ys_r.at[q, k - 1], peer(k))

    def line_copies(slots_r, slots_l, r_s, r_r, l_s, l_r, first_r, first_l, p):
        out_r, in_r, out_l, in_l = [], [], [], []
        for k in range(G):
            if k < G - 1:
                src = first_r(p) if k == 0 else slots_r.at[p, pl.ds(k, G - 1 - k)]
                out_r.append((k, remote(src, slots_r.at[p, pl.ds(k, G - 1 - k)], r_s.at[p], r_r.at[p], right)))
                held = slots_l.at[p, pl.ds(0, k + 1)]
                in_l.append((k, remote(held, held, l_s.at[p], l_r.at[p], left)))
            if k > 0:
                src = first_l(p) if k == G - 1 else slots_l.at[p, pl.ds(0, k)]
                out_l.append((k, remote(src, slots_l.at[p, pl.ds(0, k)], l_s.at[p], l_r.at[p], left)))
                held = slots_r.at[p, pl.ds(k - 1, G - k)]
                in_r.append((k, remote(held, held, r_s.at[p], r_r.at[p], right)))
        return out_r, in_r, out_l, in_l

    def at_place(copies, act):
        for k, copy in copies:
            @pl.when(z == k)
            def _(copy=copy):
                act(copy)

    def y_line(q):
        return line_copies(
            YRT, YLT, yr_s, yr_r, yl_s, yl_r,
            lambda q: YR.at[q, 0, pl.ds(1, G - 1)], lambda q: YR.at[q, 0, pl.ds(0, G - 1)], q,
        )

    def z_line(p):
        return line_copies(
            ZRT, ZLT, zr_s, zr_r, zl_s, zl_r,
            lambda p: ZRT.at[p, pl.ds(0, G - 1)], lambda p: ZLT.at[p, pl.ds(0, G - 1)], p,
        )

    def zx_copy(p, k):
        return remote(ZX.at[p, a], ZX.at[p, a], zx_s.at[p, k - 1], zx_r.at[p, k - 1], peer(k))

    def ag_copy(q, k):
        return remote(YR.at[q, 0, z], y_out(q, a, c), ag_s.at[q, k - 1], ag_r.at[q, k - 1], peer(k))

    def sib_own(q):
        return remote(YR.at[q, 0, z], y_out(q, a, c), sib_s.at[q, 0], sib_r.at[q, 0], sib)

    def sib_pass(q, k):
        part = lax.rem(a + A - k, A)
        return remote(y_out(q, part, c), y_out(q, part, c), sib_s.at[q, k], sib_r.at[q, k], sib)

    def own_y(q):
        return pltpu.make_async_copy(YR.at[q, 0, z], y_out(q, a, c), lo.at[q])

    def own_z(p):
        return pltpu.make_async_copy(ZX.at[p, a], z_out(p, c), lo.at[nY + p])

    def sib_z(p):
        return remote(ZX.at[p, a], z_out(p, c), sib_s.at[nY + p, 0], sib_r.at[nY + p, 0], sib)

    f32, bf16 = jnp.float32, jnp.bfloat16
    far = jnp.maximum(z, G - 1 - z)

    def live(index, count):
        return (index >= 0) & (index < count)

    def gain_core():
        return remote(gp, GC, gc_sem.at[0], gc_sem.at[1], sib)

    def gain_part(k):
        return remote(GA.at[a], GA.at[a], ga_s.at[k - 1], ga_r.at[k - 1], peer(k))

    def gain_right():
        return remote(GS.at[1], GR, gr_sem.at[0], gr_sem.at[1], right)

    def gain_left():
        return remote(GS.at[2], GL, gl_sem.at[0], gl_sem.at[1], left)

    def gain_step(t):
        @pl.when(t == 0)
        def _():
            gain_core().start()

        @pl.when(t == 1)
        def _():
            gain_core().wait_recv()
            GA[a] = gp[...] + GC[...]
            for k in range(1, A):
                gain_part(k).start()

        @pl.when(t == 2)
        def _():
            for k in range(1, A):
                remote(
                    GA.at[lax.rem(a + A - k, A)], GA.at[lax.rem(a + A - k, A)], ga_s.at[k - 1], ga_r.at[k - 1], peer(k)
                ).wait_recv()
            total = GA[0]
            for k in range(1, A):
                total += GA[k]
            GS[0] = total

        @pl.when(t == 2 + HOP * z)
        def _():
            @pl.when(z > 0)
            def _():
                gain_right().wait_recv()
                GS[1] = GS[0] + GR[...]

            @pl.when(z == 0)
            def _():
                GS[1] = GS[0]

            @pl.when(z < G - 1)
            def _():
                gain_right().start()

        @pl.when(t == 2 + HOP * (G - 1 - z))
        def _():
            @pl.when(z < G - 1)
            def _():
                gain_left().wait_recv()
                GS[2] = GS[0] + GL[...]

            @pl.when(z == G - 1)
            def _():
                GS[2] = GS[0]

            @pl.when(z > 0)
            def _():
                gain_left().start()

        @pl.when(t == 3 + HOP * (G - 1))
        def _():
            outg[...] = GS[1] + jnp.where(z < G - 1, GL[...], 0.0)

    def step(t, carry):
        gain_step(t)

        @pl.when(t == 0)
        def _():
            operands_here(0)
            operands_here(2)
            fetch(1)
            fetch(3)

        @pl.when(t == jnp.minimum(plan["pieces_gate"], plan["down_chunks"] * plan["z_split"]) - 1)
        def _():
            operands_here(1)
            operands_here(3)

        q1 = t

        @pl.when(live(q1, nY))
        def _():
            for k in range(1, A):
                @pl.when(q1 >= YS_RING)
                def _():
                    y_send(q1 - YS_RING, k).wait_send()

                @pl.loop(0, G)
                def _(b):
                    YS[lax.rem(q1, YS_RING), k - 1, b] = y_product(q1, lax.rem(a + k, A), b).astype(bf16)

                y_send(q1, k).start()

        pr = t - HOP * z

        @pl.when(live(pr, nZ))
        def _():
            out_r, in_r, _, _ = z_line(pr)
            at_place(in_r, lambda copy: copy.wait_recv())

            @pl.loop(0, G)
            def _(b):
                @pl.when((b > z) & (z > 0))
                def _():
                    ZRT[pr, b - 1] = (z_product(pr, b) + ZRT[pr, b - 1].astype(f32)).astype(bf16)

                @pl.when((b > z) & (z == 0))
                def _():
                    ZRT[pr, b - 1] = z_product(pr, b).astype(bf16)

            at_place(out_r, lambda copy: copy.start())

        pL = t - HOP * (G - 1 - z)

        @pl.when(live(pL, nZ))
        def _():
            _, _, out_l, in_l = z_line(pL)
            at_place(in_l, lambda copy: copy.wait_recv())

            @pl.loop(0, G)
            def _(b):
                @pl.when((b < z) & (z < G - 1))
                def _():
                    ZLT[pL, b] = (z_product(pL, b) + ZLT[pL, b].astype(f32)).astype(bf16)

                @pl.when((b < z) & (z == G - 1))
                def _():
                    ZLT[pL, b] = z_product(pL, b).astype(bf16)

            at_place(out_l, lambda copy: copy.start())

        q2 = t - LEAD

        @pl.when(live(q2, nY))
        def _():
            for k in range(1, A):
                y_send(q2, k).wait_recv()

            @pl.loop(0, G)
            def _(b):
                total = y_product(q2, a, b)
                for k in range(1, A):
                    total += YR[q2, k - 1, b].astype(f32)
                YR[q2, 0, b] = total.astype(bf16)

        qr = t - LEAD - HOP * z

        @pl.when(live(qr, nY))
        def _():
            out_r, in_r, _, _ = y_line(qr)
            at_place(in_r, lambda copy: copy.wait_recv())

            @pl.loop(0, G)
            def _(b):
                @pl.when((b > z) & (z > 0))
                def _():
                    YRT[qr, b - 1] = (YR[qr, 0, b].astype(f32) + YRT[qr, b - 1].astype(f32)).astype(bf16)

            at_place(out_r, lambda copy: copy.start())

        qL = t - LEAD - HOP * (G - 1 - z)

        @pl.when(live(qL, nY))
        def _():
            _, _, out_l, in_l = y_line(qL)
            at_place(in_l, lambda copy: copy.wait_recv())

            @pl.loop(0, G)
            def _(b):
                @pl.when((b < z) & (z < G - 1))
                def _():
                    YLT[qL, b] = (YR[qL, 0, b].astype(f32) + YLT[qL, b].astype(f32)).astype(bf16)

            at_place(out_l, lambda copy: copy.start())

        pf = t - HOP * far

        @pl.when(live(pf, nZ))
        def _():
            mine = z_product(pf, z)
            from_left = ZRT[pf, jnp.maximum(z - 1, 0)].astype(f32)
            from_right = ZLT[pf, jnp.minimum(z, G - 2)].astype(f32)
            mine = mine + jnp.where(z > 0, from_left, 0.0) + jnp.where(z < G - 1, from_right, 0.0)
            ZX[pf, a] = mine.astype(bf16)
            for k in range(1, A):
                zx_copy(pf, k).start()

        pg = t - HOP * far - LEAD

        @pl.when(live(pg, nZ))
        def _():
            for k in range(1, A):
                remote(
                    ZX.at[pg, lax.rem(a + A - k, A)], ZX.at[pg, lax.rem(a + A - k, A)],
                    zx_s.at[pg, k - 1], zx_r.at[pg, k - 1], peer(k),
                ).wait_recv()
            total = ZX[pg, 0].astype(f32)
            for k in range(1, A):
                total += ZX[pg, k].astype(f32)
            for k in range(1, A):
                zx_copy(pg, k).wait_send()
            ZX[pg, a] = total.astype(bf16)
            own_z(pg).start()
            sib_z(pg).start()

        qf = t - LEAD - HOP * far

        @pl.when(live(qf, nY))
        def _():
            total = YR[qf, 0, z].astype(f32)
            from_left = YRT[qf, jnp.maximum(z - 1, 0)].astype(f32)
            from_right = YLT[qf, jnp.minimum(z, G - 2)].astype(f32)
            total = total + jnp.where(z > 0, from_left, 0.0) + jnp.where(z < G - 1, from_right, 0.0)
            YR[qf, 0, z] = total.astype(bf16)
            for k in range(1, A):
                ag_copy(qf, k).start()
            own_y(qf).start()
            sib_own(qf).start()

        qg = t - LEAD - HOP * far - LEAD

        @pl.when(live(qg, nY))
        def _():
            for k in range(1, A):
                here = y_out(qg, lax.rem(a + A - k, A), c)
                remote(here, here, ag_s.at[qg, k - 1], ag_r.at[qg, k - 1], peer(k)).wait_recv()
                sib_pass(qg, k).start()

        return carry

    steps = max(nY, nZ) + 2 * LEAD + HOP * (G - 1)
    lax.fori_loop(0, steps, step, 0)

    gain_core().wait_send()
    for k in range(1, A):
        gain_part(k).wait_send()

    @pl.when(z < G - 1)
    def _():
        gain_right().wait_send()

    @pl.when(z > 0)
    def _():
        gain_left().wait_send()

    for i in range(4):
        cross[1, i].wait_send()

    def drain_y(q, carry):
        for k in range(1, A):
            @pl.when(q >= nY - YS_RING)
            def _():
                y_send(q, k).wait_send()

            ag_copy(q, k).wait_send()
            sib_pass(q, k).wait_send()
            there = y_out(q, lax.rem(a + A - k, A), 1 - c)
            remote(there, there, sib_s.at[q, k], sib_r.at[q, k], sib).wait_recv()
        out_r, _, out_l, _ = y_line(q)
        at_place(out_r, lambda copy: copy.wait_send())
        at_place(out_l, lambda copy: copy.wait_send())
        own_y(q).wait()
        sib_own(q).wait_send()
        there = y_out(q, a, 1 - c)
        remote(there, there, sib_s.at[q, 0], sib_r.at[q, 0], sib).wait_recv()
        return carry

    lax.fori_loop(0, nY, drain_y, 0)

    def drain_z(p, carry):
        out_r, _, out_l, _ = z_line(p)
        at_place(out_r, lambda copy: copy.wait_send())
        at_place(out_l, lambda copy: copy.wait_send())
        own_z(p).wait()
        sib_z(p).wait_send()
        there = z_out(p, 1 - c)
        remote(there, there, sib_s.at[nY + p, 0], sib_r.at[nY + p, 0], sib).wait_recv()
        return carry

    lax.fori_loop(0, nZ, drain_z, 0)


def summed_grads(groups, dp, activations, others, dz, dy, dgate, dup, dq, gain_parts):
    hidden, tokens = activations[0].shape
    width, qkv_cols = dz.shape[1], dq.shape[1]
    plan = grad_plan(groups, dp, tokens, width, hidden, qkv_cols)
    G, A, nY, nZ = groups, plan["pairs"], plan["pieces"], plan["z_pieces"]
    block, zr, zc = plan["block"], plan["z_rows"], plan["z_cols"]
    bf16, DMA = jnp.bfloat16, pltpu.SemaphoreType.DMA
    any_space = pl.BlockSpec(memory_space=pl.ANY)
    in_vmem, f32, gain_shape = pl.BlockSpec(memory_space=pltpu.VMEM), jnp.float32, gain_parts.shape
    return pl.pallas_call(
        functools.partial(grad_kernel, plan),
        out_shape=(
            jax.ShapeDtypeStruct((block, 2 * hidden + qkv_cols), bf16),
            jax.ShapeDtypeStruct((plan["down_block"] + block, width), bf16),
            jax.ShapeDtypeStruct(gain_parts.shape, f32),
        ),
        in_specs=[any_space] * 13 + [in_vmem],
        out_specs=(any_space, any_space, in_vmem),
        scratch_shapes=[
            pltpu.VMEM((hidden + 3 * width, 2 * tokens), bf16),
            pltpu.VMEM((2 * tokens, width + hidden + qkv_cols // 2), bf16),
            pltpu.VMEM((YS_RING, A - 1, G, block, LANES), bf16),
            pltpu.VMEM((nY, A - 1, G, block, LANES), bf16),
            pltpu.VMEM((nY, G - 1, block, LANES), bf16),
            pltpu.VMEM((nY, G - 1, block, LANES), bf16),
            pltpu.VMEM((nZ, G - 1, zr, zc), bf16),
            pltpu.VMEM((nZ, G - 1, zr, zc), bf16),
            pltpu.VMEM((nZ, A, zr, zc), bf16),
            DMA((12,)), DMA((8,)), DMA((8,)),
            DMA((nY, A - 1)), DMA((nY, A - 1)),
            DMA((nY,)), DMA((nY,)), DMA((nY,)), DMA((nY,)),
            DMA((nZ,)), DMA((nZ,)), DMA((nZ,)), DMA((nZ,)),
            DMA((nZ, A - 1)), DMA((nZ, A - 1)),
            DMA((nY, A - 1)), DMA((nY, A - 1)),
            DMA((nY + nZ, A)), DMA((nY + nZ, A)),
            DMA((nY + nZ,)),
            pltpu.VMEM(gain_shape, f32),
            pltpu.VMEM((A,) + gain_shape, f32),
            pltpu.VMEM((3,) + gain_shape, f32),
            pltpu.VMEM(gain_shape, f32),
            pltpu.VMEM(gain_shape, f32),
            DMA((2,)), DMA((max(A - 1, 1),)), DMA((max(A - 1, 1),)), DMA((2,)), DMA((2,)),
        ],
        compiler_params=pltpu.CompilerParams(
            collective_id=3, has_side_effects=True, vmem_limit_bytes=63 * 1024 * 1024
        ),
        cost_estimate=pl.CostEstimate(
            flops=2 * 2 * tokens * (width * (2 * hidden + qkv_cols + width) + hidden * width) // 2,
            bytes_accessed=40_000_000, transcendentals=0,
        ),
    )(*activations, *others, dz, dy, dgate, dup, dq, gain_parts)


W_HOP = 4
AFTER = 1
ROOMS = 3
gather_families = (
    (1, False, False),
    (2, False, True),
    (1, False, False),
    (8, True, False),
    (6, False, False),
)


def gather_kernel(groups, pairs, families, rows, *refs):
    G, A, F = groups, pairs, len(families)
    shards, refs = refs[:F], refs[F:]
    if rows:
        (x, mask, cosines, sines), refs = refs[:4], refs[4:]
    wholes, refs = refs[:F], refs[F:]
    if rows:
        (gain_rows, first_out, handed), refs = refs[:3], refs[3:]
    sems, refs = refs[: 9 * F], refs[9 * F :]
    if rows:
        in_gain, in_wide, in_gate, in_down, in_sem, hand_s, hand_r, n1, qkvt, ot, y, n2, gate, inner = refs
    s, z, d = lax.axis_index("section"), lax.axis_index("group"), lax.axis_index("dp")
    c, a = lax.rem(d, 2), lax.div(d, 2)
    sib = (s, z, 2 * a + 1 - c)
    right, left = (s, z + 1, d), (s, z - 1, d)

    def peer(part):
        return (s, z, 2 * part + c)

    barrier = pltpu.get_barrier_semaphore()
    others = [peer(lax.rem(a + k, A)) for k in range(1, A)]
    if rows:
        others.append((1 - s, z, d))
    others += [sib, (s, lax.rem(z + 1, G), d), (s, lax.rem(z + G - 1, G), d)]
    for dev in others:
        pl.semaphore_signal(barrier, inc=1, device_id=dev, device_id_type=MESH)
    pl.semaphore_wait(barrier, len(others))

    def columns(f, i):
        pieces, halves, _ = families[f]
        size = shards[f].shape[1] // pieces
        if halves:
            i = lax.rem(i, 2) * (pieces // 2) + lax.div(i, 2)
        return pl.ds(pl.multiple_of(i * size, 128), size)

    def cut(f, ref, i):
        return ref.at[:, columns(f, i)]

    def placed(f, i, o, part, core):
        return cut(f, wholes[f].at[(o * A + part) * 2 + core], i)

    def copy(f, i, o, part, kind, index, dev, own=False, core=None):
        core = c if core is None else core
        there = placed(f, i, o, part, core)
        src = cut(f, shards[f], i) if own else there
        send, recv = sems[f * 9 + 2 * kind], sems[f * 9 + 2 * kind + 1]
        return pltpu.make_async_remote_copy(
            src_ref=src, dst_ref=there, send_sem=send.at[index], recv_sem=recv.at[index], device_id=dev, device_id_type=MESH
        )

    def to_right(f, i, o, part, own=False):
        return copy(f, i, o, part, 0, (i, o, lax.rem(part + A - a, A)), right, own)

    def to_left(f, i, o, part, own=False):
        return copy(f, i, o, part, 1, (i, o, lax.rem(part + A - a, A)), left, own)

    def to_part(f, i, o, k, own=False):
        return copy(f, i, o, a, 2, (i, o, k - 1), peer(lax.rem(a + k, A)), own)

    def from_part(f, i, o, k):
        return copy(f, i, o, lax.rem(a + A - k, A), 2, (i, o, k - 1), peer(lax.rem(a + A - k, A)))

    def to_core(f, i, o, part, own=False):
        return copy(f, i, o, part, 3, (i, o, lax.rem(part + A - a, A)), sib, own)

    def from_core(f, i, o, k):
        part = lax.rem(a + k, A)
        return copy(f, i, o, part, 3, (i, o, k), sib, core=1 - c)

    def own_copy(f, i):
        return pltpu.make_async_copy(cut(f, shards[f], i), placed(f, i, z, a, c), sems[f * 9 + 8].at[i])

    def along(f, i, o, part, own, go_right, go_left):
        if go_right:
            @pl.when(z < G - 1)
            def _():
                to_right(f, i, o, part, own).start()
        if go_left:
            @pl.when(z > 0)
            def _():
                to_left(f, i, o, part, own).start()

    first = []
    total = 0
    for pieces, _, _ in families:
        first.append(total)
        total += pieces

    def into(f, i, room):
        return pltpu.make_async_copy(wholes[f].at[:, :, columns(f, i)], room, in_sem.at[first[f] + i])

    def arrived(f, i, room):
        own_copy(f, i).wait()

        @pl.loop(0, G)
        def _(o):
            for k in range(A):
                from_core(f, i, o, k).wait_recv()

        into(f, i, room).start()

    def hand_over(i):
        place = columns(4, i)
        return pltpu.make_async_remote_copy(
            src_ref=first_out.at[:, place], dst_ref=handed.at[:, place], send_sem=hand_s.at[i], recv_sem=hand_r.at[i],
            device_id=(1 - s, z, d), device_id_type=MESH,
        )

    def one_matrix(room):
        return room.reshape(room.shape[0] * room.shape[1], room.shape[2])

    def forward(t):
        f32, bf16 = jnp.float32, jnp.bfloat16
        slots, part, half, ratio = x.shape[0] // max(rows, 1), KVH * HD, HD // 2, H // KVH
        after = W_HOP * G + AFTER
        places = [(1, i) for i in range(families[1][0])] + [(2, 0)]

        @pl.when(t == first[0] + after)
        def _():
            arrived(0, 0, in_gain)
            into(0, 0, in_gain).wait()
            turned = one_matrix(in_gain[...]).astype(f32).T
            gain_rows[...] = turned[:8]
            n1[...] = scaled_norm(x[...].astype(f32), gain_rows[0:1, :])[1]

        for slot, (f, i) in enumerate(places):
            @pl.when(t == first[f] + i + after)
            def _(slot=slot, f=f, i=i):
                arrived(f, i, in_wide.at[slot])

        i3 = t - first[3] - after

        @pl.when((i3 >= 0) & (i3 < families[3][0]))
        def _():
            arrived(3, i3, in_gate.at[lax.rem(i3, ROOMS)])

        i4 = t - first[4] - after

        @pl.when((i4 >= 0) & (i4 < families[4][0]))
        def _():
            arrived(4, i4, in_down.at[lax.rem(i4, ROOMS)])

        for i in range(families[1][0]):
            @pl.when(t == first[1] + i + after + 1)
            def _(i=i):
                into(1, i, in_wide.at[i]).wait()
                for j in range(in_wide.shape[3] // part):
                    weight = one_matrix(in_wide[i, :, :, j * part : (j + 1) * part])
                    chunk = jnp.dot(n1[...], weight, preferred_element_type=f32).T
                    top = (i * (in_wide.shape[3] // part) + j) * part
                    if top >= (H + KVH) * HD:
                        qkvt[top : top + part, :] = chunk.astype(bf16)
                        continue
                    for h in range(KVH):
                        base = top + h * HD
                        front, back = chunk[h * HD : h * HD + half], chunk[h * HD + half : (h + 1) * HD]
                        qkvt[base : base + half, :] = (front * cosines[...] - back * sines[...]).astype(bf16)
                        qkvt[base + half : base + HD, :] = (back * cosines[...] + front * sines[...]).astype(bf16)

        def heads(index, carry):
            row, k = lax.div(index, KVH), lax.rem(index, KVH)
            tokens = pl.ds(pl.multiple_of(row * slots, 128), slots)

            def band(head):
                return pl.ds(pl.multiple_of(head * HD, 16), HD)

            keys, values = qkvt[band(H + k), tokens], qkvt[band(H + KVH + k), tokens]
            queries = jnp.concatenate([qkvt[band(ratio * k + g), tokens] for g in range(ratio)], 1)
            key = lax.broadcasted_iota(jnp.int32, (slots, ratio * slots), 0)
            query = lax.rem(lax.broadcasted_iota(jnp.int32, (slots, ratio * slots), 1), slots)
            valid = mask[pl.ds(pl.multiple_of(row * slots, 128), slots), :] > 0.0
            scores = pair_scores(keys, queries, (key <= query) & valid)
            top = jnp.max(scores, 0, keepdims=True)
            total = top + jnp.log(jnp.sum(jnp.exp(scores - top), 0, keepdims=True))
            probs = jnp.exp(scores - total).astype(bf16)
            out = jnp.dot(values, probs, preferred_element_type=f32).astype(bf16)
            for g in range(ratio):
                ot[band(ratio * k + g), tokens] = out[:, g * slots : (g + 1) * slots]
            return carry

        split = rows * KVH // 2
        turn = t - first[2] - after

        @pl.when((turn >= 1) & (turn <= 2))
        def _():
            lax.fori_loop((turn - 1) * split, turn * split, heads, 0)

        @pl.when(turn == 2)
        def _():
            into(2, 0, in_wide.at[len(places) - 1]).wait()
            y[...] = x[...].astype(f32) + lax.dot_general(
                ot[...], one_matrix(in_wide[len(places) - 1]), down_rows, preferred_element_type=f32
            )
            n2[...] = scaled_norm(y[...], gain_rows[1:2, :])[1]

        c3 = i3 - 2
        size = in_gate.shape[3]

        @pl.when((c3 >= 0) & (c3 < families[3][0]))
        def _():
            room = lax.rem(c3, ROOMS)
            into(3, c3, in_gate.at[room]).wait()
            value = jnp.dot(n2[...], one_matrix(in_gate[room]), preferred_element_type=f32)

            @pl.when(lax.rem(c3, 2) == 0)
            def _():
                gate[...] = value

            @pl.when(lax.rem(c3, 2) == 1)
            def _():
                opened = gate[...]
                inner[:, pl.ds(pl.multiple_of(lax.div(c3, 2) * size, 128), size)] = (
                    opened / (1.0 + jnp.exp(-opened)) * value
                ).astype(bf16)

        c4 = i4 - 2

        @pl.when((c4 >= 0) & (c4 < families[4][0]))
        def _():
            room = lax.rem(c4, ROOMS)
            into(4, c4, in_down.at[room]).wait()
            place = columns(4, c4)
            value = y[:, place] + jnp.dot(inner[...], one_matrix(in_down[room]), preferred_element_type=f32)
            first_out[:, place] = (value * mask[...]).astype(bf16)
            hand_over(c4).start()

    def step(t, carry):
        for f, (pieces, _, parts_first) in enumerate(families):
            i0 = t - first[f]

            @pl.when((i0 >= 0) & (i0 < pieces))
            def _(f=f, i0=i0):
                along(f, i0, z, a, True, True, True)
                for k in range(1, A):
                    to_part(f, i0, z, k, True).start()
                to_core(f, i0, z, a, True).start()
                own_copy(f, i0).start()

        for f, (pieces, _, parts_first) in enumerate(families):
            for h in range(G):
                for k in range(A if parts_first else 1):
                    if h == 0:
                        continue
                    i = t - first[f] - W_HOP * h - (W_HOP if k > 0 else 0)
                    part = lax.rem(a + k, A)
                    for sign in (-1, 1):
                        o = z + sign * h

                        @pl.when((i >= 0) & (i < pieces) & (o >= 0) & (o < G))
                        def _(f=f, i=i, o=o, part=part, sign=sign, parts_first=parts_first):
                            if sign < 0:
                                to_right(f, i, o, part).wait_recv()
                                along(f, i, o, part, False, True, False)
                            else:
                                to_left(f, i, o, part).wait_recv()
                                along(f, i, o, part, False, False, True)
                            if not parts_first:
                                for j in range(1, A):
                                    to_part(f, i, o, j).start()
                            to_core(f, i, o, part).start()

                if parts_first and h > 0:
                    continue
                i = t - first[f] - W_HOP * (h + 1)
                for sign in (-1, 1) if h else (1,):
                    o = z + sign * h

                    @pl.when((i >= 0) & (i < pieces) & (o >= 0) & (o < G))
                    def _(f=f, i=i, o=o, parts_first=parts_first):
                        for k in range(1, A):
                            from_part(f, i, o, k).wait_recv()
                            part = lax.rem(a + A - k, A)
                            if parts_first:
                                along(f, i, o, part, False, True, True)
                            to_core(f, i, o, part).start()
        if rows:
            forward(t)
        return carry

    lax.fori_loop(0, total + max(W_HOP * (G + 1), W_HOP * G + AFTER + 2), step, 0)

    if rows:
        for i in range(families[4][0]):
            hand_over(i).wait()

    for f, (pieces, _, parts_first) in enumerate(families):
        def drain(i, carry, f=f, parts_first=parts_first):
            if not rows:
                own_copy(f, i).wait()

            def by_group(o, carry):
                for k in range(A):
                    part = lax.rem(a + k, A)
                    to_core(f, i, o, part).wait_send()
                    if not rows:
                        from_core(f, i, o, k).wait_recv()
                    if parts_first or k == 0:
                        @pl.when((z < G - 1) & (o <= z))
                        def _(part=part):
                            to_right(f, i, o, part).wait_send()

                        @pl.when((z > 0) & (o >= z))
                        def _(part=part):
                            to_left(f, i, o, part).wait_send()
                for k in range(1, A):
                    if parts_first:
                        @pl.when(o == z)
                        def _(k=k):
                            to_part(f, i, o, k).wait_send()
                    else:
                        to_part(f, i, o, k).wait_send()
                return carry

            return lax.fori_loop(0, G, by_group, carry)

        lax.fori_loop(0, pieces, drain, 0)


def gathered(groups, dp, shards, families, tokens):
    A, DMA, bf16, f32 = dp // 2, pltpu.SemaphoreType.DMA, jnp.bfloat16, jnp.float32
    any_space, in_vmem = pl.BlockSpec(memory_space=pl.ANY), pl.BlockSpec(memory_space=pltpu.VMEM)
    devices, shape = groups * dp, jax.ShapeDtypeStruct
    scratch = []
    for pieces, _, parts_first in families:
        on_line = (pieces, groups, A if parts_first else 1)
        scratch += [DMA(on_line)] * 4 + [DMA((pieces, groups, max(A - 1, 1)))] * 2 + [DMA((pieces, groups, A))] * 2
        scratch += [DMA((pieces,))]
    outs = tuple(shape((devices,) + x.shape, x.dtype) for x in shards)
    extra, rows = (), 0
    if tokens is not None:
        x, mask, tables, rows = tokens
        extra = (x, mask) + tables
        count, width = x.shape
        hidden = devices * shards[4].shape[0]
        outs += (shape((8, width), f32), shape((count, width), bf16), shape((count, width), bf16))

        def room(f, rooms):
            return pltpu.VMEM((rooms, devices, shards[f].shape[0], shards[f].shape[1] // families[f][0]), bf16)

        scratch += [
            pltpu.VMEM((devices,) + shards[0].shape, bf16), room(1, families[1][0] + 1), room(3, ROOMS), room(4, ROOMS),
            DMA((sum(family[0] for family in families),)), DMA((families[4][0],)), DMA((families[4][0],)),
            pltpu.VMEM((count, width), bf16), pltpu.VMEM((shards[1].shape[1], count), bf16),
            pltpu.VMEM((width, count), bf16), pltpu.VMEM((count, width), f32), pltpu.VMEM((count, width), bf16),
            pltpu.VMEM((count, shards[3].shape[1] // families[3][0]), f32), pltpu.VMEM((count, hidden), bf16),
        ]
    return pl.pallas_call(
        functools.partial(gather_kernel, groups, A, families, rows),
        out_shape=outs,
        in_specs=[any_space] * len(shards) + [in_vmem] * len(extra),
        out_specs=(any_space,) * len(shards) + ((in_vmem, in_vmem, any_space) if rows else ()),
        scratch_shapes=scratch,
        compiler_params=pltpu.CompilerParams(
            collective_id=5, has_side_effects=True, vmem_limit_bytes=56 * 1024 * 1024
        ),
    )(*shards, *extra)


def body(
    inputs_x, cotangent, lengths, attn_gain, qkv_weight, out_weight, ffn_gain, gate_up, down_weight
):
    is_first = lax.axis_index("section") == 0
    rows, slots, width = inputs_x.shape
    tables = turned_tables(slots, rows)
    info = jnp.concatenate([lengths, is_first.astype(jnp.int32)[None]])
    mask = padding(lengths, slots).reshape(-1, 1)
    gains = jnp.concatenate([attn_gain, ffn_gain], 0).T
    gains = jnp.pad(gains, ((0, 0), (0, 128 - gains.shape[1])))
    shards = (gains, qkv_weight[0], out_weight[0], gate_up[0], down_weight[0])
    together = gains.shape[0] % 16 == 0
    tokens = (flat(inputs_x), mask, tables, rows) if together else None
    gathered_all = gathered(
        lax.axis_size("group"), lax.axis_size("dp"), shards, gather_families, tokens
    )
    gains_all, qkv_w, output_weight, gate_up_w, down_w = (flat(x) for x in gathered_all[:5])
    if together:
        gain_rows, _, recv_act = gathered_all[5:]
    else:
        gain_rows = gains_all[:, :2].astype(jnp.float32).T
    gain_one, gain_two = gain_rows[0:1], gain_rows[1:2]
    dz_given = (flat(cotangent).astype(jnp.float32) * mask).astype(jnp.bfloat16)
    if not together:
        after_one = attention_forward(
            info, flat(inputs_x), gain_one, tables, qkv_w, output_weight, rows
        )[0]
        first_out = ffn_forward(after_one, gain_two, mask, gate_up_w, down_w)
        recv_act = passed_along(first_out, "section", 1)
    layer_in = jnp.where(is_first, flat(inputs_x), recv_act)
    after, heads, log_total, attention_turned, normed_turned = attention_forward(
        info, layer_in, gain_one, tables, qkv_w, output_weight, rows
    )
    dy, dy_low, _ = ffn_backward(after, dz_given, gain_two, gate_up_w, down_w)
    (second_dx,) = attention_backward(
        info, layer_in, gain_one, dy, dy_low, tables, heads, log_total, output_weight, qkv_w, rows, False
    )
    recv_grad = passed_along(second_dx, "section", -1)
    after, second_dx = lax.optimization_barrier((after, second_dx))
    hidden_turned, by_gate, by_up, normed_two_turned, result = ffn_prepare(
        after, gain_two, mask, gate_up_w, down_w
    )
    activations = (hidden_turned, attention_turned, normed_two_turned, normed_turned)
    recv_grad, activations, by_gate = lax.optimization_barrier((recv_grad, activations, by_gate))
    others = tuple(swapped(x, "dp") for x in activations)
    dz = jnp.where(is_first, (recv_grad.astype(jnp.float32) * mask).astype(jnp.bfloat16), dz_given)
    dy, dy_low, ffn_gain_part, grad_gate, grad_up = ffn_backward(
        after, dz, gain_two, gate_up_w, down_w, (by_gate, by_up)
    )
    grad_x, attn_gain_part, grad_qkv = attention_backward(
        info, layer_in, gain_one, dy, dy_low, tables, heads, log_total, output_weight, qkv_w, rows, True
    )
    section_out = result.reshape((1,) + inputs_x.shape)
    input_grads = grad_x.reshape((1,) + inputs_x.shape)
    gain_parts = jnp.pad(jnp.concatenate([attn_gain_part, ffn_gain_part], 0), ((0, 6), (0, 0)))
    gate_qkv_sum, down_out_sum, gain_sums = summed_grads(
        lax.axis_size("group"),
        lax.axis_size("dp"),
        activations,
        others,
        dz,
        dy_low,
        grad_gate,
        grad_up,
        grad_qkv,
        gain_parts,
    )
    gain_cols = attn_gain.shape[1] * lax.axis_size("dp")
    gain_sums = lax.dynamic_slice_in_dim(
        gain_sums, lax.axis_index("group") * gain_cols, gain_cols, 1
    )
    gate_width = gate_up.shape[2]
    down_rows = down_weight.shape[1] * lax.axis_size("dp")
    reduced = (
        gain_sums[0],
        gate_qkv_sum[:, gate_width:].astype(jnp.float32),
        down_out_sum[down_rows:].astype(jnp.float32),
        gain_sums[1],
        gate_qkv_sum[:, :gate_width].astype(jnp.float32),
        down_out_sum[:down_rows].astype(jnp.float32),
    )
    return (section_out, input_grads) + tuple((shard_sum[None] for shard_sum in reduced))


def solution(mesh):
    placed = (
        P(("group", "dp"), None, None),
        P(("group", "dp"), None, None),
        P(("group", "dp")),
        P("section", ("group", "dp")),
        P("section", ("group", "dp"), None),
        P("section", ("group", "dp"), None),
        P("section", ("group", "dp")),
        P("section", ("group", "dp"), None),
        P("section", ("group", "dp"), None),
    )
    return jax.shard_map(
        body,
        mesh=mesh,
        in_specs=placed,
        out_specs=(
            P("section", ("group", "dp"), None, None),
            P("section", ("group", "dp"), None, None),
            P("section", "group"),
            P("section", "group", None),
            P("section", "group", None),
            P("section", "group"),
            P("section", "group", None),
            P("section", "group", None),
        ),
        check_vma=False,
    )
```

```python
import functools

import jax
import jax.numpy as jnp
from jax import lax
from jax.experimental import pallas as pl
from jax.experimental.pallas import tpu as pltpu
from jax.sharding import PartitionSpec as P

H = 16
KVH = 8
HD = 96


norm_eps = 1e-05
rope_base = 100000.0
masked_score = -1e30
across = (((1,), (1,)), ((), ()))
down_rows = (((0,), (0,)), ((), ()))


def passed_along(value, axis, by):
    length = lax.axis_size(axis)
    pairs = [(i, i + by) for i in range(length) if 0 <= i + by < length]
    return lax.ppermute(value, axis, pairs)


def swapped(value, axis):
    return lax.ppermute(value, axis, [(i, i ^ 1) for i in range(lax.axis_size(axis))])


def padding(lengths, slot_count):
    position = jnp.arange(slot_count, dtype=jnp.int32)
    return (position[None, :] < lengths[:, None]).astype(jnp.float32)[..., None]


FF_CHUNK = 1024
across = (((1,), (1,)), ((), ()))
down_rows = (((0,), (0,)), ((), ()))


def scaled_norm(value, gain):
    scale = lax.rsqrt(jnp.mean(value * value, -1, keepdims=True) + norm_eps)
    return scale, (value * scale * gain).astype(jnp.bfloat16)


def ffn_forward_kernel(y, gain, mask, wg, wu, wd, out, n2, acc):
    j = pl.program_id(0)

    @pl.when(j == 0)
    def _():
        n2[...] = scaled_norm(y[...], gain[...])[1]
        acc[...] = y[...]

    gate = jnp.dot(n2[...], wg[...], preferred_element_type=jnp.float32)
    up = jnp.dot(n2[...], wu[...], preferred_element_type=jnp.float32)
    hidden = (gate / (1.0 + jnp.exp(-gate)) * up).astype(jnp.bfloat16)
    acc[...] += jnp.dot(hidden, wd[...], preferred_element_type=jnp.float32)

    @pl.when(j == pl.num_programs(0) - 1)
    def _():
        out[...] = (acc[...] * mask[...]).astype(jnp.bfloat16)


def ffn_specs(tokens, width, hidden):
    steps = hidden // FF_CHUNK
    whole = pl.BlockSpec((tokens, width), lambda j: (0, 0))
    row = pl.BlockSpec((1, width), lambda j: (0, 0))
    weights = [
        pl.BlockSpec((width, FF_CHUNK), lambda j: (0, j)),
        pl.BlockSpec((width, FF_CHUNK), lambda j: (0, j + steps)),
        pl.BlockSpec((FF_CHUNK, width), lambda j: (j, 0)),
    ]
    return steps, whole, row, weights


def ffn_forward(y, gain, mask, gate_up_w, down_w):
    tokens, width = y.shape
    hidden = down_w.shape[0]
    steps, whole, row, weights = ffn_specs(tokens, width, hidden)
    return pl.pallas_call(
        ffn_forward_kernel,
        grid=(steps,),
        out_shape=jax.ShapeDtypeStruct((tokens, width), jnp.bfloat16),
        in_specs=[whole, row, pl.BlockSpec((tokens, 1), lambda j: (0, 0))] + weights,
        out_specs=whole,
        scratch_shapes=[pltpu.VMEM((tokens, width), jnp.bfloat16), pltpu.VMEM((tokens, width), jnp.float32)],
        compiler_params=pltpu.CompilerParams(vmem_limit_bytes=40 * 1024 * 1024),
        cost_estimate=pl.CostEstimate(
            flops=6 * tokens * width * hidden, bytes_accessed=6 * width * hidden, transcendentals=tokens * hidden
        ),
    )(y, gain, mask, gate_up_w, gate_up_w, down_w)


def ffn_prepare_kernel(y, gain, mask, wg, wu, wd, at, by_gate, by_up, n2t, out, n2, acc):
    j = pl.program_id(0)
    bf16, f32 = jnp.bfloat16, jnp.float32

    @pl.when(j == 0)
    def _():
        n = scaled_norm(y[...], gain[...])[1]
        n2[...] = n
        n2t[...] = n.T
        acc[...] = y[...]

    gate = jnp.dot(n2[...], wg[...], preferred_element_type=f32)
    up = jnp.dot(n2[...], wu[...], preferred_element_type=f32)
    sig = 1.0 / (1.0 + jnp.exp(-gate))
    silu = gate * sig
    hidden = (silu * up).astype(bf16)
    at[...] = hidden.T
    by_gate[...] = (up * sig * (1.0 + gate * (1.0 - sig))).astype(bf16)
    by_up[...] = silu.astype(bf16)
    acc[...] += jnp.dot(hidden, wd[...], preferred_element_type=f32)

    @pl.when(j == pl.num_programs(0) - 1)
    def _():
        out[...] = (acc[...] * mask[...]).astype(bf16)


def ffn_prepare(y, gain, mask, gate_up_w, down_w):
    tokens, width = y.shape
    hidden = down_w.shape[0]
    steps, whole, row, weights = ffn_specs(tokens, width, hidden)
    shape, bf16 = jax.ShapeDtypeStruct, jnp.bfloat16
    part = pl.BlockSpec((tokens, FF_CHUNK), lambda j: (0, j))
    return pl.pallas_call(
        ffn_prepare_kernel,
        grid=(steps,),
        out_shape=(
            shape((hidden, tokens), bf16), shape((tokens, hidden), bf16), shape((tokens, hidden), bf16),
            shape((width, tokens), bf16), shape((tokens, width), bf16),
        ),
        in_specs=[whole, row, pl.BlockSpec((tokens, 1), lambda j: (0, 0))] + weights,
        out_specs=(
            pl.BlockSpec((FF_CHUNK, tokens), lambda j: (j, 0)), part, part,
            pl.BlockSpec((width, tokens), lambda j: (0, 0)), whole,
        ),
        scratch_shapes=[pltpu.VMEM((tokens, width), bf16), pltpu.VMEM((tokens, width), jnp.float32)],
        compiler_params=pltpu.CompilerParams(vmem_limit_bytes=48 * 1024 * 1024),
        cost_estimate=pl.CostEstimate(
            flops=6 * tokens * width * hidden, bytes_accessed=6 * width * hidden, transcendentals=tokens * hidden
        ),
    )(y, gain, mask, gate_up_w, gate_up_w, down_w)


def ffn_backward_kernel(prepared, y, dz, gain, wg, wu, wd, *rest):
    bf16, f32 = jnp.bfloat16, jnp.float32
    if prepared:
        by_gate, by_up, dy, dyb, gain_grad, dgate, dup, acc = rest
    else:
        dy, dyb, gain_grad, n2, acc = rest
    j = pl.program_id(0)

    @pl.when(j == 0)
    def _():
        acc[...] = jnp.zeros_like(acc)
        if not prepared:
            n2[...] = scaled_norm(y[...], gain[...])[1]

    grad = lax.dot_general(dz[...], wd[...], across, preferred_element_type=f32)
    if prepared:
        grad_gate = (grad * by_gate[...].astype(f32)).astype(bf16)
        grad_up = (grad * by_up[...].astype(f32)).astype(bf16)
        dgate[...] = grad_gate
        dup[...] = grad_up
    else:
        gate = jnp.dot(n2[...], wg[...], preferred_element_type=f32)
        up = jnp.dot(n2[...], wu[...], preferred_element_type=f32)
        sig = 1.0 / (1.0 + jnp.exp(-gate))
        grad_gate = (grad * up * sig * (1.0 + gate * (1.0 - sig))).astype(bf16)
        grad_up = (grad * (gate * sig)).astype(bf16)
    acc[...] += lax.dot_general(grad_gate, wg[...], across, preferred_element_type=f32) + lax.dot_general(
        grad_up, wu[...], across, preferred_element_type=f32
    )

    @pl.when(j == pl.num_programs(0) - 1)
    def _():
        value, grad_normed = y[...], acc[...]
        r = lax.rsqrt(jnp.mean(value * value, -1, keepdims=True) + norm_eps)
        scaled = grad_normed * gain[...]
        gain_grad[...] = jnp.sum(grad_normed * value * r, axis=0, keepdims=True)
        inner = jnp.mean(value * scaled, -1, keepdims=True)
        total = dz[...].astype(f32) + r * scaled - value * (r * r * r) * inner
        dy[...] = total
        dyb[...] = total.astype(bf16)


def ffn_backward(y, dz, gain, gate_up_w, down_w, factors=()):
    tokens, width = y.shape
    hidden = down_w.shape[0]
    steps, whole, row, weights = ffn_specs(tokens, width, hidden)
    shape, bf16, f32 = jax.ShapeDtypeStruct, jnp.bfloat16, jnp.float32
    outs = [shape((tokens, width), f32), shape((tokens, width), bf16), shape((1, width), f32)]
    out_specs = [whole, whole, row]
    scratch = [pltpu.VMEM((tokens, width), f32)]
    parts = [pl.BlockSpec((tokens, FF_CHUNK), lambda j: (0, j))] * len(factors)
    if factors:
        outs += [shape((tokens, hidden), bf16)] * 2
        out_specs += parts
    else:
        scratch = [pltpu.VMEM((tokens, width), bf16)] + scratch
    return pl.pallas_call(
        functools.partial(ffn_backward_kernel, bool(factors)),
        grid=(steps,),
        out_shape=tuple(outs),
        in_specs=[whole, whole, row] + weights + parts,
        out_specs=tuple(out_specs),
        scratch_shapes=scratch,
        compiler_params=pltpu.CompilerParams(vmem_limit_bytes=48 * 1024 * 1024),
        cost_estimate=pl.CostEstimate(
            flops=10 * tokens * width * hidden, bytes_accessed=6 * width * hidden, transcendentals=tokens * hidden
        ),
    )(y, dz, gain, gate_up_w, gate_up_w, down_w, *factors)


def turned_tables(slots, rows):
    half_width = HD // 2
    frequency = rope_base ** (-(jnp.arange(half_width, dtype=jnp.float32) * 2.0 / HD))
    angles = frequency[:, None] * jnp.arange(slots, dtype=jnp.float32)[None, :]
    return jnp.tile(jnp.cos(angles), (1, rows)), jnp.tile(jnp.sin(angles), (1, rows))


def pair_mask(length, slots):
    groups = H // KVH
    key = lax.broadcasted_iota(jnp.int32, (slots, groups * slots), 0)
    query = lax.rem(lax.broadcasted_iota(jnp.int32, (slots, groups * slots), 1), slots)
    return (key <= query) & (key < length)


def pair_of(ref, k, row, slots):
    groups = H // KVH
    first = groups * k * HD
    return jnp.concatenate(
        [ref[first + g * HD : first + (g + 1) * HD, row * slots : (row + 1) * slots] for g in range(groups)], 1
    )


def key_value(qkvt, k, row, slots):
    tokens = slice(row * slots, (row + 1) * slots)
    keys = qkvt[(H + k) * HD : (H + k + 1) * HD, tokens]
    values = qkvt[(H + KVH + k) * HD : (H + KVH + k + 1) * HD, tokens]
    return keys, values


def pair_scores(keys, queries, mask):
    scores = lax.dot_general(keys, queries, down_rows, preferred_element_type=jnp.float32) * HD ** (-0.5)
    return jnp.where(mask, scores, masked_score)


def attention_forward_kernel(rows, info, x, gain, cosines, sines, w, wo, y, qkvt, lse, ot, n1t, n1):
    j = pl.program_id(0)
    bf16, f32 = jnp.bfloat16, jnp.float32
    slots, part, half = x.shape[0] // rows, KVH * HD, HD // 2
    groups = H // KVH

    @pl.when(j == 0)
    def _():
        n = scaled_norm(x[...].astype(f32), gain[...])[1]
        n1[...] = n
        n1t[...] = n.T

    chunk = jnp.dot(n1[...], w[...], preferred_element_type=f32).T

    @pl.when(j <= groups)
    def _():
        for h in range(KVH):
            front, back = chunk[h * HD : h * HD + half], chunk[h * HD + half : (h + 1) * HD]
            base = j * part + h * HD
            qkvt[pl.ds(pl.multiple_of(base, 16), half), :] = (front * cosines[...] - back * sines[...]).astype(bf16)
            qkvt[pl.ds(pl.multiple_of(base + half, 16), half), :] = (
                back * cosines[...] + front * sines[...]
            ).astype(bf16)

    @pl.when(j > groups)
    def _():
        qkvt[pl.ds(pl.multiple_of(j * part, 16), part), :] = chunk.astype(bf16)
        for row in range(rows):
            mask = pair_mask(info[row], slots)
            for k in range(KVH):
                keys, values = key_value(qkvt, k, row, slots)
                scores = pair_scores(keys, pair_of(qkvt, k, row, slots), mask)
                top = jnp.max(scores, 0, keepdims=True)
                total = top + jnp.log(jnp.sum(jnp.exp(scores - top), 0, keepdims=True))
                lse[row * KVH + k : row * KVH + k + 1, :] = total
                probs = jnp.exp(scores - total).astype(bf16)
                out = jnp.dot(values, probs, preferred_element_type=f32).astype(bf16)
                for g in range(groups):
                    first = (groups * k + g) * HD
                    ot[first : first + HD, row * slots : (row + 1) * slots] = out[:, g * slots : (g + 1) * slots]
        y[...] = x[...].astype(f32) + lax.dot_general(ot[...], wo[...], down_rows, preferred_element_type=f32)


def attention_backward_kernel(
    rows, keep, info, x, gain, dy, dyb, cosines, sines, qkvt, lse, wo, w, dx, *rest
):
    if keep:
        gain_grad, dqkv, dot, dqkvt, acc = rest
    else:
        dqkv, dot, dqkvt, acc = rest
    j = pl.program_id(0)
    bf16, f32 = jnp.bfloat16, jnp.float32
    slots, part, half = x.shape[0] // rows, KVH * HD, HD // 2
    groups = H // KVH

    def unrotated(grad, row, width):
        tokens = slice(row * slots, (row + 1) * slots)
        cos, sin = cosines[:, tokens], sines[:, tokens]
        if width > slots:
            cos, sin = jnp.concatenate([cos] * groups, 1), jnp.concatenate([sin] * groups, 1)
        grad = grad * HD ** (-0.5)
        front, back = grad[:half], grad[half:]
        return (front * cos + back * sin).astype(bf16), (back * cos - front * sin).astype(bf16)

    @pl.when(j == 0)
    def _():
        dot[...] = lax.dot_general(dyb[...], wo[...], across, preferred_element_type=f32).astype(bf16).T
        acc[...] = jnp.zeros_like(acc)
        for row in range(rows):
            tokens = slice(row * slots, (row + 1) * slots)
            mask = pair_mask(info[row], slots)
            for k in range(KVH):
                keys, values = key_value(qkvt, k, row, slots)
                queries, grads = pair_of(qkvt, k, row, slots), pair_of(dot, k, row, slots)
                scores = pair_scores(keys, queries, mask)
                probs = jnp.exp(scores - lse[row * KVH + k : row * KVH + k + 1, :])
                grad_probs = lax.dot_general(values, grads, down_rows, preferred_element_type=f32)
                grad_scores = (
                    probs * (grad_probs - jnp.sum(probs * grad_probs, 0, keepdims=True))
                ).astype(bf16)
                grad_values = lax.dot_general(grads, probs.astype(bf16), across, preferred_element_type=f32)
                grad_keys = lax.dot_general(queries, grad_scores, across, preferred_element_type=f32)
                grad_queries = jnp.dot(keys, grad_scores, preferred_element_type=f32)
                front, back = unrotated(grad_queries, row, groups * slots)
                for g in range(groups):
                    first = (groups * k + g) * HD
                    dqkvt[first : first + half, tokens] = front[:, g * slots : (g + 1) * slots]
                    dqkvt[first + half : first + HD, tokens] = back[:, g * slots : (g + 1) * slots]
                front, back = unrotated(grad_keys, row, slots)
                first = (H + k) * HD
                dqkvt[first : first + half, tokens] = front
                dqkvt[first + half : first + HD, tokens] = back
                first = (H + KVH + k) * HD
                dqkvt[first : first + HD, tokens] = grad_values.astype(bf16)
        for i in range(groups + 2):
            dqkv[:, i * part : (i + 1) * part] = dqkvt[i * part : (i + 1) * part, :].T

    columns = pl.ds(pl.multiple_of(j * part, 128), part)
    acc[...] += lax.dot_general(dqkv[:, columns], w[...], across, preferred_element_type=f32)

    @pl.when(j == pl.num_programs(0) - 1)
    def _():
        value, grad_normed = x[...].astype(f32), acc[...]
        r = lax.rsqrt(jnp.mean(value * value, -1, keepdims=True) + norm_eps)
        scaled = grad_normed * gain[...]
        inner = jnp.mean(value * scaled, -1, keepdims=True)
        total = dy[...] + (r * scaled - value * (r * r * r) * inner)
        if keep:
            gain_grad[...] = jnp.sum(grad_normed * value * r, axis=0, keepdims=True)
            dx[...] = jnp.where(info[rows] == 1, total, total.astype(bf16).astype(f32))
        else:
            dx[...] = total.astype(bf16)


def attention_specs(tokens, width):
    part = KVH * HD
    whole = lambda *shape: pl.BlockSpec(shape, lambda j: (0,) * len(shape))
    return part, whole, pl.BlockSpec(memory_space=pltpu.SMEM), pl.BlockSpec((width, part), lambda j: (0, j))


def attention_forward(info, x, gain, tables, qkv_w, output_weight, rows):
    tokens, width = x.shape
    cols, slots = qkv_w.shape[1], tokens // rows
    part, whole, scalars, weight = attention_specs(tokens, width)
    shape, bf16, f32 = jax.ShapeDtypeStruct, jnp.bfloat16, jnp.float32
    stats = (rows * KVH, H // KVH * slots)
    return pl.pallas_call(
        functools.partial(attention_forward_kernel, rows),
        grid=(cols // part,),
        out_shape=(
            shape((tokens, width), f32), shape((cols, tokens), bf16), shape(stats, f32),
            shape((H * HD, tokens), bf16), shape((width, tokens), bf16),
        ),
        in_specs=[
            scalars, whole(tokens, width), whole(1, width), whole(HD // 2, tokens), whole(HD // 2, tokens), weight,
            whole(H * HD, width),
        ],
        out_specs=(
            whole(tokens, width), whole(cols, tokens), whole(*stats), whole(H * HD, tokens), whole(width, tokens)
        ),
        scratch_shapes=[pltpu.VMEM((tokens, width), bf16)],
        compiler_params=pltpu.CompilerParams(vmem_limit_bytes=40 * 1024 * 1024),
        cost_estimate=pl.CostEstimate(
            flops=2 * tokens * width * (cols + H * HD), bytes_accessed=2 * width * (cols + H * HD), transcendentals=0
        ),
    )(info, x, gain, *tables, qkv_w, output_weight)


def attention_backward(info, x, gain, dy, dy_low, tables, qkvt, lse, output_weight, qkv_w, rows, keep):
    tokens, width = x.shape
    cols = qkv_w.shape[1]
    part, whole, scalars, weight = attention_specs(tokens, width)
    shape, bf16, f32 = jax.ShapeDtypeStruct, jnp.bfloat16, jnp.float32
    scratch = [pltpu.VMEM((H * HD, tokens), bf16), pltpu.VMEM((cols, tokens), bf16), pltpu.VMEM((tokens, width), f32)]
    outs, out_specs = [shape((tokens, width), f32 if keep else bf16)], [whole(tokens, width)]
    if keep:
        outs += [shape((1, width), f32), shape((tokens, cols), bf16)]
        out_specs += [whole(1, width), whole(tokens, cols)]
    else:
        scratch = [pltpu.VMEM((tokens, cols), bf16)] + scratch
    return pl.pallas_call(
        functools.partial(attention_backward_kernel, rows, keep),
        grid=(cols // part,),
        out_shape=tuple(outs),
        in_specs=[
            scalars, whole(tokens, width), whole(1, width), whole(tokens, width), whole(tokens, width),
            whole(HD // 2, tokens), whole(HD // 2, tokens), whole(cols, tokens), whole(*lse.shape), whole(H * HD, width),
            weight,
        ],
        out_specs=tuple(out_specs),
        scratch_shapes=scratch,
        compiler_params=pltpu.CompilerParams(vmem_limit_bytes=48 * 1024 * 1024),
        cost_estimate=pl.CostEstimate(
            flops=2 * tokens * width * (cols + H * HD), bytes_accessed=2 * width * (cols + H * HD), transcendentals=0
        ),
    )(info, x, gain, dy, dy_low, *tables, qkvt, lse, output_weight, qkv_w)


def flat(array):
    return array.reshape(-1, array.shape[-1])


MESH = pl.DeviceIdType.MESH
LANES = 128


def grad_plan(groups, dp, tokens, width, hidden, qkv_cols):
    pairs = dp // 2
    block = width // groups
    down_block = hidden // groups
    gate_cols = 2 * hidden // 2 // pairs
    qkv_part = qkv_cols // 2 // pairs
    pieces_gate = gate_cols // LANES
    pieces_qkv = qkv_part // LANES
    pieces = pieces_gate + pieces_qkv
    z_rows = LANES
    while down_block % z_rows or block % z_rows:
        z_rows //= 2
    row_chunks = (down_block + block) // z_rows
    half = width // 2
    z_split = max(1, pieces // row_chunks)
    while half % (z_split * LANES):
        z_split -= 1
    return dict(
        groups=groups, pairs=pairs, tokens=tokens, width=width, hidden=hidden, qkv_cols=qkv_cols, block=block,
        down_block=down_block, gate_cols=gate_cols, qkv_part=qkv_part, pieces_gate=pieces_gate, pieces=pieces,
        z_rows=z_rows, z_split=z_split, z_cols=half // z_split, z_pieces=row_chunks * z_split,
        down_chunks=down_block // z_rows, half=half,
    )


YS_RING = 4
HOP = 2
LEAD = 2
YLAG = 2


def grad_kernel(
    plan, at, ot, n2t, n1t, at2, ot2, n2t2, n1t2, dz, dy, dgate, dup, dq, gp, outy, outz, outg,
    LT, RH, YS, YR, YRT, YLT, ZRT, ZLT, ZX,
    own_sem, xs, xr, ys_s, ys_r, yr_s, yr_r, yl_s, yl_r, zr_s, zr_r, zl_s, zl_r,
    zx_s, zx_r, ag_s, ag_r, sib_s, sib_r, lo,
    GC, GA, GS, GR, GL, gc_sem, ga_s, ga_r, gr_sem, gl_sem,
):
    G, A, T = plan["groups"], plan["pairs"], plan["tokens"]
    width, hidden, half = plan["width"], plan["hidden"], plan["half"]
    block, nY, nZ = plan["block"], plan["pieces"], plan["z_pieces"]
    zr, zc = plan["z_rows"], plan["z_cols"]
    s, z, d = lax.axis_index("section"), lax.axis_index("group"), lax.axis_index("dp")
    c, a = lax.rem(d, 2), lax.div(d, 2)
    sib = (s, z, 2 * a + 1 - c)
    right, left = (s, z + 1, d), (s, z - 1, d)

    def peer(k):
        return (s, z, 2 * lax.rem(a + k, A) + c)

    def remote(src, dst, ss, rs, dev):
        return pltpu.make_async_remote_copy(
            src_ref=src, dst_ref=dst, send_sem=ss, recv_sem=rs, device_id=dev, device_id_type=MESH
        )

    barrier = pltpu.get_barrier_semaphore()
    for dev in [sib, (s, lax.rem(z + 1, G), d), (s, lax.rem(z + G - 1, G), d)] + [peer(k) for k in range(1, A)]:
        pl.semaphore_signal(barrier, inc=1, device_id=dev, device_id_type=MESH)
    pl.semaphore_wait(barrier, A + 2)

    lhs = [
        (at, at2, 0, hidden), (ot, ot2, hidden, width), (n2t, n2t2, hidden + width, width),
        (n1t, n1t2, hidden + 2 * width, width),
    ]
    rhs = [(dz, 0, half), (dy, half, half), (None, width, hidden), (dq, width + hidden, plan["qkv_cols"] // 2)]
    own, cross = {}, {}
    for i, (ref, theirs, row, rows) in enumerate(lhs):
        own[0, i] = pltpu.make_async_copy(ref, LT.at[pl.ds(row, rows), pl.ds(0, T)], own_sem.at[i])
        own[2, i] = pltpu.make_async_copy(theirs, LT.at[pl.ds(row, rows), pl.ds(T, T)], own_sem.at[8 + i])
    for i, (ref, col, cols) in enumerate(rhs):
        if ref is None:
            continue
        mine = pl.ds(pl.multiple_of(c * cols, LANES), cols)
        theirs = pl.ds(pl.multiple_of((1 - c) * cols, LANES), cols)
        own[1, i] = pltpu.make_async_copy(ref.at[:, mine], RH.at[pl.ds(0, T), pl.ds(col, cols)], own_sem.at[4 + i])
        cross[1, i] = remote(ref.at[:, theirs], RH.at[pl.ds(T, T), pl.ds(col, cols)], xs.at[4 + i], xr.at[4 + i], sib)
    col, cols = rhs[2][1:]
    for core, (mine, theirs) in enumerate(((dgate, dup), (dup, dgate))):
        own[1, 2, core] = pltpu.make_async_copy(mine, RH.at[pl.ds(0, T), pl.ds(col, cols)], own_sem.at[6])
        cross[1, 2, core] = remote(theirs, RH.at[pl.ds(T, T), pl.ds(col, cols)], xs.at[6], xr.at[6], sib)
    own[1, 2], cross[1, 2] = own[1, 2, 0], cross[1, 2, 0]
    def fetch(i):
        if i == 2:
            for core in (0, 1):
                @pl.when(c == core)
                def _(core=core):
                    cross[1, 2, core].start()
                    own[1, 2, core].start()
        else:
            cross[1, i].start()
            own[1, i].start()
        own[0, i].start()
        own[2, i].start()

    fetch(0)
    fetch(2)

    def operands_here(i):
        for side in (0, 2, 1):
            own[side, i].wait()
        cross[1, i].wait_recv()

    def product(row, rows, col, cols):
        return jnp.dot(
            LT[pl.ds(row, rows), :], RH[:, pl.ds(col, cols)], preferred_element_type=jnp.float32
        )

    def y_product(q, which, b):
        is_gate = q < plan["pieces_gate"]
        row = jnp.where(is_gate, hidden + width, hidden + 2 * width) + b * block
        col = jnp.where(
            is_gate,
            width + which * plan["gate_cols"] + q * LANES,
            width + hidden + which * plan["qkv_part"] + (q - plan["pieces_gate"]) * LANES,
        )
        return product(pl.multiple_of(row, 16), block, pl.multiple_of(col, LANES), LANES)

    def z_product(p, b):
        r, h = lax.div(p, plan["z_split"]), lax.rem(p, plan["z_split"])
        is_down = r < plan["down_chunks"]
        row = jnp.where(
            is_down, b * plan["down_block"] + r * zr, hidden + b * block + (r - plan["down_chunks"]) * zr
        )
        col = jnp.where(is_down, 0, half) + h * zc
        return product(pl.multiple_of(row, 16), zr, pl.multiple_of(col, LANES), zc)

    def y_out(q, part, core):
        is_gate = q < plan["pieces_gate"]
        col = jnp.where(
            is_gate,
            core * hidden + part * plan["gate_cols"] + q * LANES,
            2 * hidden + core * (plan["qkv_cols"] // 2) + part * plan["qkv_part"] + (q - plan["pieces_gate"]) * LANES,
        )
        return outy.at[:, pl.ds(pl.multiple_of(col, LANES), LANES)]

    def z_out(p, core):
        r, h = lax.div(p, plan["z_split"]), lax.rem(p, plan["z_split"])
        return outz.at[
            pl.ds(pl.multiple_of(r * zr, 16), zr), pl.ds(pl.multiple_of(core * half + h * zc, LANES), zc)
        ]

    def y_send(q, k):
        return remote(YS.at[lax.rem(q, YS_RING), k - 1], YR.at[q, k - 1], ys_s.at[q, k - 1], ys_r.at[q, k - 1], peer(k))

    def line_copies(slots_r, slots_l, r_s, r_r, l_s, l_r, first_r, first_l, p):
        out_r, in_r, out_l, in_l = [], [], [], []
        for k in range(G):
            if k < G - 1:
                src = first_r(p) if k == 0 else slots_r.at[p, pl.ds(k, G - 1 - k)]
                out_r.append((k, remote(src, slots_r.at[p, pl.ds(k, G - 1 - k)], r_s.at[p], r_r.at[p], right)))
                held = slots_l.at[p, pl.ds(0, k + 1)]
                in_l.append((k, remote(held, held, l_s.at[p], l_r.at[p], left)))
            if k > 0:
                src = first_l(p) if k == G - 1 else slots_l.at[p, pl.ds(0, k)]
                out_l.append((k, remote(src, slots_l.at[p, pl.ds(0, k)], l_s.at[p], l_r.at[p], left)))
                held = slots_r.at[p, pl.ds(k - 1, G - k)]
                in_r.append((k, remote(held, held, r_s.at[p], r_r.at[p], right)))
        return out_r, in_r, out_l, in_l

    def at_place(copies, act):
        for k, copy in copies:
            @pl.when(z == k)
            def _(copy=copy):
                act(copy)

    def y_line(q):
        return line_copies(
            YRT, YLT, yr_s, yr_r, yl_s, yl_r,
            lambda q: YR.at[q, 0, pl.ds(1, G - 1)], lambda q: YR.at[q, 0, pl.ds(0, G - 1)], q,
        )

    def z_line(p):
        return line_copies(
            ZRT, ZLT, zr_s, zr_r, zl_s, zl_r,
            lambda p: ZRT.at[p, pl.ds(0, G - 1)], lambda p: ZLT.at[p, pl.ds(0, G - 1)], p,
        )

    def zx_copy(p, k):
        return remote(ZX.at[p, a], ZX.at[p, a], zx_s.at[p, k - 1], zx_r.at[p, k - 1], peer(k))

    def ag_copy(q, k):
        return remote(YR.at[q, 0, z], y_out(q, a, c), ag_s.at[q, k - 1], ag_r.at[q, k - 1], peer(k))

    def sib_own(q):
        return remote(YR.at[q, 0, z], y_out(q, a, c), sib_s.at[q, 0], sib_r.at[q, 0], sib)

    def sib_pass(q, k):
        part = lax.rem(a + A - k, A)
        return remote(y_out(q, part, c), y_out(q, part, c), sib_s.at[q, k], sib_r.at[q, k], sib)

    def own_y(q):
        return pltpu.make_async_copy(YR.at[q, 0, z], y_out(q, a, c), lo.at[q])

    def own_z(p):
        return pltpu.make_async_copy(ZX.at[p, a], z_out(p, c), lo.at[nY + p])

    def sib_z(p):
        return remote(ZX.at[p, a], z_out(p, c), sib_s.at[nY + p, 0], sib_r.at[nY + p, 0], sib)

    f32, bf16 = jnp.float32, jnp.bfloat16
    far = jnp.maximum(z, G - 1 - z)

    def live(index, count):
        return (index >= 0) & (index < count)

    def gain_core():
        return remote(gp, GC, gc_sem.at[0], gc_sem.at[1], sib)

    def gain_part(k):
        return remote(GA.at[a], GA.at[a], ga_s.at[k - 1], ga_r.at[k - 1], peer(k))

    def gain_right():
        return remote(GS.at[1], GR, gr_sem.at[0], gr_sem.at[1], right)

    def gain_left():
        return remote(GS.at[2], GL, gl_sem.at[0], gl_sem.at[1], left)

    def gain_step(t):
        @pl.when(t == 0)
        def _():
            gain_core().start()

        @pl.when(t == 1)
        def _():
            gain_core().wait_recv()
            GA[a] = gp[...] + GC[...]
            for k in range(1, A):
                gain_part(k).start()

        @pl.when(t == 2)
        def _():
            for k in range(1, A):
                remote(
                    GA.at[lax.rem(a + A - k, A)], GA.at[lax.rem(a + A - k, A)], ga_s.at[k - 1], ga_r.at[k - 1], peer(k)
                ).wait_recv()
            total = GA[0]
            for k in range(1, A):
                total += GA[k]
            GS[0] = total

        @pl.when(t == 2 + HOP * z)
        def _():
            @pl.when(z > 0)
            def _():
                gain_right().wait_recv()
                GS[1] = GS[0] + GR[...]

            @pl.when(z == 0)
            def _():
                GS[1] = GS[0]

            @pl.when(z < G - 1)
            def _():
                gain_right().start()

        @pl.when(t == 2 + HOP * (G - 1 - z))
        def _():
            @pl.when(z < G - 1)
            def _():
                gain_left().wait_recv()
                GS[2] = GS[0] + GL[...]

            @pl.when(z == G - 1)
            def _():
                GS[2] = GS[0]

            @pl.when(z > 0)
            def _():
                gain_left().start()

        @pl.when(t == 3 + HOP * (G - 1))
        def _():
            outg[...] = GS[1] + jnp.where(z < G - 1, GL[...], 0.0)

    def step(t, carry):
        gain_step(t)

        @pl.when(t == 0)
        def _():
            operands_here(0)
            operands_here(2)
            fetch(1)
            fetch(3)

        @pl.when(t == jnp.minimum(plan["pieces_gate"], plan["down_chunks"] * plan["z_split"]) - 1)
        def _():
            operands_here(1)
            operands_here(3)

        q1 = t - YLAG

        @pl.when(live(q1, nY))
        def _():
            for k in range(1, A):
                @pl.when(q1 >= YS_RING)
                def _():
                    y_send(q1 - YS_RING, k).wait_send()

                @pl.loop(0, G)
                def _(b):
                    YS[lax.rem(q1, YS_RING), k - 1, b] = y_product(q1, lax.rem(a + k, A), b).astype(bf16)

                y_send(q1, k).start()

        pr = t - HOP * z

        @pl.when(live(pr, nZ))
        def _():
            out_r, in_r, _, _ = z_line(pr)
            at_place(in_r, lambda copy: copy.wait_recv())

            @pl.loop(0, G)
            def _(b):
                @pl.when((b > z) & (z > 0))
                def _():
                    ZRT[pr, b - 1] = (z_product(pr, b) + ZRT[pr, b - 1].astype(f32)).astype(bf16)

                @pl.when((b > z) & (z == 0))
                def _():
                    ZRT[pr, b - 1] = z_product(pr, b).astype(bf16)

            at_place(out_r, lambda copy: copy.start())

        pL = t - HOP * (G - 1 - z)

        @pl.when(live(pL, nZ))
        def _():
            _, _, out_l, in_l = z_line(pL)
            at_place(in_l, lambda copy: copy.wait_recv())

            @pl.loop(0, G)
            def _(b):
                @pl.when((b < z) & (z < G - 1))
                def _():
                    ZLT[pL, b] = (z_product(pL, b) + ZLT[pL, b].astype(f32)).astype(bf16)

                @pl.when((b < z) & (z == G - 1))
                def _():
                    ZLT[pL, b] = z_product(pL, b).astype(bf16)

            at_place(out_l, lambda copy: copy.start())

        q2 = t - YLAG - LEAD

        @pl.when(live(q2, nY))
        def _():
            for k in range(1, A):
                y_send(q2, k).wait_recv()

            @pl.loop(0, G)
            def _(b):
                total = y_product(q2, a, b)
                for k in range(1, A):
                    total += YR[q2, k - 1, b].astype(f32)
                YR[q2, 0, b] = total.astype(bf16)

        qr = t - YLAG - LEAD - HOP * z

        @pl.when(live(qr, nY))
        def _():
            out_r, in_r, _, _ = y_line(qr)
            at_place(in_r, lambda copy: copy.wait_recv())

            @pl.loop(0, G)
            def _(b):
                @pl.when((b > z) & (z > 0))
                def _():
                    YRT[qr, b - 1] = (YR[qr, 0, b].astype(f32) + YRT[qr, b - 1].astype(f32)).astype(bf16)

            at_place(out_r, lambda copy: copy.start())

        qL = t - YLAG - LEAD - HOP * (G - 1 - z)

        @pl.when(live(qL, nY))
        def _():
            _, _, out_l, in_l = y_line(qL)
            at_place(in_l, lambda copy: copy.wait_recv())

            @pl.loop(0, G)
            def _(b):
                @pl.when((b < z) & (z < G - 1))
                def _():
                    YLT[qL, b] = (YR[qL, 0, b].astype(f32) + YLT[qL, b].astype(f32)).astype(bf16)

            at_place(out_l, lambda copy: copy.start())

        pf = t - HOP * far

        @pl.when(live(pf, nZ))
        def _():
            mine = z_product(pf, z)
            from_left = ZRT[pf, jnp.maximum(z - 1, 0)].astype(f32)
            from_right = ZLT[pf, jnp.minimum(z, G - 2)].astype(f32)
            mine = mine + jnp.where(z > 0, from_left, 0.0) + jnp.where(z < G - 1, from_right, 0.0)
            ZX[pf, a] = mine.astype(bf16)
            for k in range(1, A):
                zx_copy(pf, k).start()

        pg = t - HOP * far - LEAD

        @pl.when(live(pg, nZ))
        def _():
            for k in range(1, A):
                remote(
                    ZX.at[pg, lax.rem(a + A - k, A)], ZX.at[pg, lax.rem(a + A - k, A)],
                    zx_s.at[pg, k - 1], zx_r.at[pg, k - 1], peer(k),
                ).wait_recv()
            total = ZX[pg, 0].astype(f32)
            for k in range(1, A):
                total += ZX[pg, k].astype(f32)
            for k in range(1, A):
                zx_copy(pg, k).wait_send()
            ZX[pg, a] = total.astype(bf16)
            own_z(pg).start()
            sib_z(pg).start()

        qf = t - YLAG - LEAD - HOP * far

        @pl.when(live(qf, nY))
        def _():
            total = YR[qf, 0, z].astype(f32)
            from_left = YRT[qf, jnp.maximum(z - 1, 0)].astype(f32)
            from_right = YLT[qf, jnp.minimum(z, G - 2)].astype(f32)
            total = total + jnp.where(z > 0, from_left, 0.0) + jnp.where(z < G - 1, from_right, 0.0)
            YR[qf, 0, z] = total.astype(bf16)
            for k in range(1, A):
                ag_copy(qf, k).start()
            own_y(qf).start()
            sib_own(qf).start()

        qg = t - YLAG - LEAD - HOP * far - LEAD

        @pl.when(live(qg, nY))
        def _():
            for k in range(1, A):
                here = y_out(qg, lax.rem(a + A - k, A), c)
                remote(here, here, ag_s.at[qg, k - 1], ag_r.at[qg, k - 1], peer(k)).wait_recv()
                sib_pass(qg, k).start()

        return carry

    steps = max(nY + YLAG, nZ) + 2 * LEAD + HOP * (G - 1)
    lax.fori_loop(0, steps, step, 0)

    gain_core().wait_send()
    for k in range(1, A):
        gain_part(k).wait_send()

    @pl.when(z < G - 1)
    def _():
        gain_right().wait_send()

    @pl.when(z > 0)
    def _():
        gain_left().wait_send()

    for i in range(4):
        cross[1, i].wait_send()

    def drain_y(q, carry):
        for k in range(1, A):
            @pl.when(q >= nY - YS_RING)
            def _():
                y_send(q, k).wait_send()

            ag_copy(q, k).wait_send()
            sib_pass(q, k).wait_send()
            there = y_out(q, lax.rem(a + A - k, A), 1 - c)
            remote(there, there, sib_s.at[q, k], sib_r.at[q, k], sib).wait_recv()
        out_r, _, out_l, _ = y_line(q)
        at_place(out_r, lambda copy: copy.wait_send())
        at_place(out_l, lambda copy: copy.wait_send())
        own_y(q).wait()
        sib_own(q).wait_send()
        there = y_out(q, a, 1 - c)
        remote(there, there, sib_s.at[q, 0], sib_r.at[q, 0], sib).wait_recv()
        return carry

    lax.fori_loop(0, nY, drain_y, 0)

    def drain_z(p, carry):
        out_r, _, out_l, _ = z_line(p)
        at_place(out_r, lambda copy: copy.wait_send())
        at_place(out_l, lambda copy: copy.wait_send())
        own_z(p).wait()
        sib_z(p).wait_send()
        there = z_out(p, 1 - c)
        remote(there, there, sib_s.at[nY + p, 0], sib_r.at[nY + p, 0], sib).wait_recv()
        return carry

    lax.fori_loop(0, nZ, drain_z, 0)


def summed_grads(groups, dp, activations, others, dz, dy, dgate, dup, dq, gain_parts):
    hidden, tokens = activations[0].shape
    width, qkv_cols = dz.shape[1], dq.shape[1]
    plan = grad_plan(groups, dp, tokens, width, hidden, qkv_cols)
    G, A, nY, nZ = groups, plan["pairs"], plan["pieces"], plan["z_pieces"]
    block, zr, zc = plan["block"], plan["z_rows"], plan["z_cols"]
    bf16, DMA = jnp.bfloat16, pltpu.SemaphoreType.DMA
    any_space = pl.BlockSpec(memory_space=pl.ANY)
    in_vmem, f32, gain_shape = pl.BlockSpec(memory_space=pltpu.VMEM), jnp.float32, gain_parts.shape
    return pl.pallas_call(
        functools.partial(grad_kernel, plan),
        out_shape=(
            jax.ShapeDtypeStruct((block, 2 * hidden + qkv_cols), bf16),
            jax.ShapeDtypeStruct((plan["down_block"] + block, width), bf16),
            jax.ShapeDtypeStruct(gain_parts.shape, f32),
        ),
        in_specs=[any_space] * 13 + [in_vmem],
        out_specs=(any_space, any_space, in_vmem),
        scratch_shapes=[
            pltpu.VMEM((hidden + 3 * width, 2 * tokens), bf16),
            pltpu.VMEM((2 * tokens, width + hidden + qkv_cols // 2), bf16),
            pltpu.VMEM((YS_RING, A - 1, G, block, LANES), bf16),
            pltpu.VMEM((nY, A - 1, G, block, LANES), bf16),
            pltpu.VMEM((nY, G - 1, block, LANES), bf16),
            pltpu.VMEM((nY, G - 1, block, LANES), bf16),
            pltpu.VMEM((nZ, G - 1, zr, zc), bf16),
            pltpu.VMEM((nZ, G - 1, zr, zc), bf16),
            pltpu.VMEM((nZ, A, zr, zc), bf16),
            DMA((12,)), DMA((8,)), DMA((8,)),
            DMA((nY, A - 1)), DMA((nY, A - 1)),
            DMA((nY,)), DMA((nY,)), DMA((nY,)), DMA((nY,)),
            DMA((nZ,)), DMA((nZ,)), DMA((nZ,)), DMA((nZ,)),
            DMA((nZ, A - 1)), DMA((nZ, A - 1)),
            DMA((nY, A - 1)), DMA((nY, A - 1)),
            DMA((nY + nZ, A)), DMA((nY + nZ, A)),
            DMA((nY + nZ,)),
            pltpu.VMEM(gain_shape, f32),
            pltpu.VMEM((A,) + gain_shape, f32),
            pltpu.VMEM((3,) + gain_shape, f32),
            pltpu.VMEM(gain_shape, f32),
            pltpu.VMEM(gain_shape, f32),
            DMA((2,)), DMA((max(A - 1, 1),)), DMA((max(A - 1, 1),)), DMA((2,)), DMA((2,)),
        ],
        compiler_params=pltpu.CompilerParams(
            collective_id=3, has_side_effects=True, vmem_limit_bytes=63 * 1024 * 1024
        ),
        cost_estimate=pl.CostEstimate(
            flops=2 * 2 * tokens * (width * (2 * hidden + qkv_cols + width) + hidden * width) // 2,
            bytes_accessed=40_000_000, transcendentals=0,
        ),
    )(*activations, *others, dz, dy, dgate, dup, dq, gain_parts)


W_HOP = 4
AFTER = 1
ROOMS = 3
gather_families = (
    (1, False, False),
    (2, False, True),
    (1, False, False),
    (8, True, False),
    (6, False, False),
)


def gather_kernel(groups, pairs, families, rows, *refs):
    G, A, F = groups, pairs, len(families)
    shards, refs = refs[:F], refs[F:]
    if rows:
        (x, mask, cosines, sines), refs = refs[:4], refs[4:]
    wholes, refs = refs[:F], refs[F:]
    if rows:
        (gain_rows, first_out, handed), refs = refs[:3], refs[3:]
    sems, refs = refs[: 9 * F], refs[9 * F :]
    if rows:
        in_gain, in_wide, in_gate, in_down, in_sem, hand_s, hand_r, n1, qkvt, ot, y, n2, gate, inner = refs
    s, z, d = lax.axis_index("section"), lax.axis_index("group"), lax.axis_index("dp")
    c, a = lax.rem(d, 2), lax.div(d, 2)
    sib = (s, z, 2 * a + 1 - c)
    right, left = (s, z + 1, d), (s, z - 1, d)

    def peer(part):
        return (s, z, 2 * part + c)

    barrier = pltpu.get_barrier_semaphore()
    others = [peer(lax.rem(a + k, A)) for k in range(1, A)]
    if rows:
        others.append((1 - s, z, d))
    others += [sib, (s, lax.rem(z + 1, G), d), (s, lax.rem(z + G - 1, G), d)]
    for dev in others:
        pl.semaphore_signal(barrier, inc=1, device_id=dev, device_id_type=MESH)
    pl.semaphore_wait(barrier, len(others))

    def columns(f, i):
        pieces, halves, _ = families[f]
        size = shards[f].shape[1] // pieces
        if halves:
            i = lax.rem(i, 2) * (pieces // 2) + lax.div(i, 2)
        return pl.ds(pl.multiple_of(i * size, 128), size)

    def cut(f, ref, i):
        return ref.at[:, columns(f, i)]

    def placed(f, i, o, part, core):
        return cut(f, wholes[f].at[(o * A + part) * 2 + core], i)

    def copy(f, i, o, part, kind, index, dev, own=False, core=None):
        core = c if core is None else core
        there = placed(f, i, o, part, core)
        src = cut(f, shards[f], i) if own else there
        send, recv = sems[f * 9 + 2 * kind], sems[f * 9 + 2 * kind + 1]
        return pltpu.make_async_remote_copy(
            src_ref=src, dst_ref=there, send_sem=send.at[index], recv_sem=recv.at[index], device_id=dev, device_id_type=MESH
        )

    def to_right(f, i, o, part, own=False):
        return copy(f, i, o, part, 0, (i, o, lax.rem(part + A - a, A)), right, own)

    def to_left(f, i, o, part, own=False):
        return copy(f, i, o, part, 1, (i, o, lax.rem(part + A - a, A)), left, own)

    def to_part(f, i, o, k, own=False):
        return copy(f, i, o, a, 2, (i, o, k - 1), peer(lax.rem(a + k, A)), own)

    def from_part(f, i, o, k):
        return copy(f, i, o, lax.rem(a + A - k, A), 2, (i, o, k - 1), peer(lax.rem(a + A - k, A)))

    def to_core(f, i, o, part, own=False):
        return copy(f, i, o, part, 3, (i, o, lax.rem(part + A - a, A)), sib, own)

    def from_core(f, i, o, k):
        part = lax.rem(a + k, A)
        return copy(f, i, o, part, 3, (i, o, k), sib, core=1 - c)

    def own_copy(f, i):
        return pltpu.make_async_copy(cut(f, shards[f], i), placed(f, i, z, a, c), sems[f * 9 + 8].at[i])

    def along(f, i, o, part, own, go_right, go_left):
        if go_right:
            @pl.when(z < G - 1)
            def _():
                to_right(f, i, o, part, own).start()
        if go_left:
            @pl.when(z > 0)
            def _():
                to_left(f, i, o, part, own).start()

    first = []
    total = 0
    for pieces, _, _ in families:
        first.append(total)
        total += pieces

    def into(f, i, room):
        return pltpu.make_async_copy(wholes[f].at[:, :, columns(f, i)], room, in_sem.at[first[f] + i])

    def arrived(f, i, room):
        own_copy(f, i).wait()

        @pl.loop(0, G)
        def _(o):
            for k in range(A):
                from_core(f, i, o, k).wait_recv()

        into(f, i, room).start()

    def hand_over(i):
        place = columns(4, i)
        return pltpu.make_async_remote_copy(
            src_ref=first_out.at[:, place], dst_ref=handed.at[:, place], send_sem=hand_s.at[i], recv_sem=hand_r.at[i],
            device_id=(1 - s, z, d), device_id_type=MESH,
        )

    def one_matrix(room):
        return room.reshape(room.shape[0] * room.shape[1], room.shape[2])

    def forward(t):
        f32, bf16 = jnp.float32, jnp.bfloat16
        slots, part, half, ratio = x.shape[0] // max(rows, 1), KVH * HD, HD // 2, H // KVH
        after = W_HOP * G + AFTER
        places = [(1, i) for i in range(families[1][0])] + [(2, 0)]

        @pl.when(t == first[0] + after)
        def _():
            arrived(0, 0, in_gain)
            into(0, 0, in_gain).wait()
            turned = one_matrix(in_gain[...]).astype(f32).T
            gain_rows[...] = turned[:8]
            n1[...] = scaled_norm(x[...].astype(f32), gain_rows[0:1, :])[1]

        for slot, (f, i) in enumerate(places):
            @pl.when(t == first[f] + i + after)
            def _(slot=slot, f=f, i=i):
                arrived(f, i, in_wide.at[slot])

        i3 = t - first[3] - after

        @pl.when((i3 >= 0) & (i3 < families[3][0]))
        def _():
            arrived(3, i3, in_gate.at[lax.rem(i3, ROOMS)])

        i4 = t - first[4] - after

        @pl.when((i4 >= 0) & (i4 < families[4][0]))
        def _():
            arrived(4, i4, in_down.at[lax.rem(i4, ROOMS)])

        for i in range(families[1][0]):
            @pl.when(t == first[1] + i + after + 1)
            def _(i=i):
                into(1, i, in_wide.at[i]).wait()
                for j in range(in_wide.shape[3] // part):
                    weight = one_matrix(in_wide[i, :, :, j * part : (j + 1) * part])
                    chunk = jnp.dot(n1[...], weight, preferred_element_type=f32).T
                    top = (i * (in_wide.shape[3] // part) + j) * part
                    if top >= (H + KVH) * HD:
                        qkvt[top : top + part, :] = chunk.astype(bf16)
                        continue
                    for h in range(KVH):
                        base = top + h * HD
                        front, back = chunk[h * HD : h * HD + half], chunk[h * HD + half : (h + 1) * HD]
                        qkvt[base : base + half, :] = (front * cosines[...] - back * sines[...]).astype(bf16)
                        qkvt[base + half : base + HD, :] = (back * cosines[...] + front * sines[...]).astype(bf16)

        def heads(index, carry):
            row, k = lax.div(index, KVH), lax.rem(index, KVH)
            tokens = pl.ds(pl.multiple_of(row * slots, 128), slots)

            def band(head):
                return pl.ds(pl.multiple_of(head * HD, 16), HD)

            keys, values = qkvt[band(H + k), tokens], qkvt[band(H + KVH + k), tokens]
            queries = jnp.concatenate([qkvt[band(ratio * k + g), tokens] for g in range(ratio)], 1)
            key = lax.broadcasted_iota(jnp.int32, (slots, ratio * slots), 0)
            query = lax.rem(lax.broadcasted_iota(jnp.int32, (slots, ratio * slots), 1), slots)
            valid = mask[pl.ds(pl.multiple_of(row * slots, 128), slots), :] > 0.0
            scores = pair_scores(keys, queries, (key <= query) & valid)
            top = jnp.max(scores, 0, keepdims=True)
            total = top + jnp.log(jnp.sum(jnp.exp(scores - top), 0, keepdims=True))
            probs = jnp.exp(scores - total).astype(bf16)
            out = jnp.dot(values, probs, preferred_element_type=f32).astype(bf16)
            for g in range(ratio):
                ot[band(ratio * k + g), tokens] = out[:, g * slots : (g + 1) * slots]
            return carry

        split = rows * KVH // 2
        turn = t - first[2] - after

        @pl.when((turn >= 1) & (turn <= 2))
        def _():
            lax.fori_loop((turn - 1) * split, turn * split, heads, 0)

        @pl.when(turn == 2)
        def _():
            into(2, 0, in_wide.at[len(places) - 1]).wait()
            y[...] = x[...].astype(f32) + lax.dot_general(
                ot[...], one_matrix(in_wide[len(places) - 1]), down_rows, preferred_element_type=f32
            )
            n2[...] = scaled_norm(y[...], gain_rows[1:2, :])[1]

        c3 = i3 - 2
        size = in_gate.shape[3]

        @pl.when((c3 >= 0) & (c3 < families[3][0]))
        def _():
            room = lax.rem(c3, ROOMS)
            into(3, c3, in_gate.at[room]).wait()
            value = jnp.dot(n2[...], one_matrix(in_gate[room]), preferred_element_type=f32)

            @pl.when(lax.rem(c3, 2) == 0)
            def _():
                gate[...] = value

            @pl.when(lax.rem(c3, 2) == 1)
            def _():
                opened = gate[...]
                inner[:, pl.ds(pl.multiple_of(lax.div(c3, 2) * size, 128), size)] = (
                    opened / (1.0 + jnp.exp(-opened)) * value
                ).astype(bf16)

        c4 = i4 - 2

        @pl.when((c4 >= 0) & (c4 < families[4][0]))
        def _():
            room = lax.rem(c4, ROOMS)
            into(4, c4, in_down.at[room]).wait()
            place = columns(4, c4)
            value = y[:, place] + jnp.dot(inner[...], one_matrix(in_down[room]), preferred_element_type=f32)
            first_out[:, place] = (value * mask[...]).astype(bf16)
            hand_over(c4).start()

    def step(t, carry):
        for f, (pieces, _, parts_first) in enumerate(families):
            i0 = t - first[f]

            @pl.when((i0 >= 0) & (i0 < pieces))
            def _(f=f, i0=i0):
                along(f, i0, z, a, True, True, True)
                for k in range(1, A):
                    to_part(f, i0, z, k, True).start()
                to_core(f, i0, z, a, True).start()
                own_copy(f, i0).start()

        for f, (pieces, _, parts_first) in enumerate(families):
            for h in range(G):
                for k in range(A if parts_first else 1):
                    if h == 0:
                        continue
                    i = t - first[f] - W_HOP * h - (W_HOP if k > 0 else 0)
                    part = lax.rem(a + k, A)
                    for sign in (-1, 1):
                        o = z + sign * h

                        @pl.when((i >= 0) & (i < pieces) & (o >= 0) & (o < G))
                        def _(f=f, i=i, o=o, part=part, sign=sign, parts_first=parts_first):
                            if sign < 0:
                                to_right(f, i, o, part).wait_recv()
                                along(f, i, o, part, False, True, False)
                            else:
                                to_left(f, i, o, part).wait_recv()
                                along(f, i, o, part, False, False, True)
                            if not parts_first:
                                for j in range(1, A):
                                    to_part(f, i, o, j).start()
                            to_core(f, i, o, part).start()

                if parts_first and h > 0:
                    continue
                i = t - first[f] - W_HOP * (h + 1)
                for sign in (-1, 1) if h else (1,):
                    o = z + sign * h

                    @pl.when((i >= 0) & (i < pieces) & (o >= 0) & (o < G))
                    def _(f=f, i=i, o=o, parts_first=parts_first):
                        for k in range(1, A):
                            from_part(f, i, o, k).wait_recv()
                            part = lax.rem(a + A - k, A)
                            if parts_first:
                                along(f, i, o, part, False, True, True)
                            to_core(f, i, o, part).start()
        if rows:
            forward(t)
        return carry

    lax.fori_loop(0, total + max(W_HOP * (G + 1), W_HOP * G + AFTER + 2), step, 0)

    if rows:
        for i in range(families[4][0]):
            hand_over(i).wait()

    for f, (pieces, _, parts_first) in enumerate(families):
        def drain(i, carry, f=f, parts_first=parts_first):
            if not rows:
                own_copy(f, i).wait()

            def by_group(o, carry):
                for k in range(A):
                    part = lax.rem(a + k, A)
                    to_core(f, i, o, part).wait_send()
                    if not rows:
                        from_core(f, i, o, k).wait_recv()
                    if parts_first or k == 0:
                        @pl.when((z < G - 1) & (o <= z))
                        def _(part=part):
                            to_right(f, i, o, part).wait_send()

                        @pl.when((z > 0) & (o >= z))
                        def _(part=part):
                            to_left(f, i, o, part).wait_send()
                for k in range(1, A):
                    if parts_first:
                        @pl.when(o == z)
                        def _(k=k):
                            to_part(f, i, o, k).wait_send()
                    else:
                        to_part(f, i, o, k).wait_send()
                return carry

            return lax.fori_loop(0, G, by_group, carry)

        lax.fori_loop(0, pieces, drain, 0)


def gathered(groups, dp, shards, families, tokens):
    A, DMA, bf16, f32 = dp // 2, pltpu.SemaphoreType.DMA, jnp.bfloat16, jnp.float32
    any_space, in_vmem = pl.BlockSpec(memory_space=pl.ANY), pl.BlockSpec(memory_space=pltpu.VMEM)
    devices, shape = groups * dp, jax.ShapeDtypeStruct
    scratch = []
    for pieces, _, parts_first in families:
        on_line = (pieces, groups, A if parts_first else 1)
        scratch += [DMA(on_line)] * 4 + [DMA((pieces, groups, max(A - 1, 1)))] * 2 + [DMA((pieces, groups, A))] * 2
        scratch += [DMA((pieces,))]
    outs = tuple(shape((devices,) + x.shape, x.dtype) for x in shards)
    extra, rows = (), 0
    if tokens is not None:
        x, mask, tables, rows = tokens
        extra = (x, mask) + tables
        count, width = x.shape
        hidden = devices * shards[4].shape[0]
        outs += (shape((8, width), f32), shape((count, width), bf16), shape((count, width), bf16))

        def room(f, rooms):
            return pltpu.VMEM((rooms, devices, shards[f].shape[0], shards[f].shape[1] // families[f][0]), bf16)

        scratch += [
            pltpu.VMEM((devices,) + shards[0].shape, bf16), room(1, families[1][0] + 1), room(3, ROOMS), room(4, ROOMS),
            DMA((sum(family[0] for family in families),)), DMA((families[4][0],)), DMA((families[4][0],)),
            pltpu.VMEM((count, width), bf16), pltpu.VMEM((shards[1].shape[1], count), bf16),
            pltpu.VMEM((width, count), bf16), pltpu.VMEM((count, width), f32), pltpu.VMEM((count, width), bf16),
            pltpu.VMEM((count, shards[3].shape[1] // families[3][0]), f32), pltpu.VMEM((count, hidden), bf16),
        ]
    return pl.pallas_call(
        functools.partial(gather_kernel, groups, A, families, rows),
        out_shape=outs,
        in_specs=[any_space] * len(shards) + [in_vmem] * len(extra),
        out_specs=(any_space,) * len(shards) + ((in_vmem, in_vmem, any_space) if rows else ()),
        scratch_shapes=scratch,
        compiler_params=pltpu.CompilerParams(
            collective_id=5, has_side_effects=True, vmem_limit_bytes=56 * 1024 * 1024
        ),
    )(*shards, *extra)


def widen_kernel(source, *parts):
    start = 0
    for part in parts:
        part[...] = source[:, start : start + part.shape[1]].astype(jnp.float32)
        start += part.shape[1]


def widened(source, widths):
    rows, cols = source.shape
    band = 32 if rows % 32 == 0 else 16
    return pl.pallas_call(
        widen_kernel,
        grid=(rows // band,),
        out_shape=tuple(jax.ShapeDtypeStruct((rows, width), jnp.float32) for width in widths),
        in_specs=[pl.BlockSpec((band, cols), lambda i: (i, 0))],
        out_specs=tuple(pl.BlockSpec((band, width), lambda i: (i, 0)) for width in widths),
        compiler_params=pltpu.CompilerParams(vmem_limit_bytes=32 * 1024 * 1024),
        cost_estimate=pl.CostEstimate(flops=0, bytes_accessed=6 * rows * cols, transcendentals=0),
    )(source)


def body(
    inputs_x, cotangent, lengths, attn_gain, qkv_weight, out_weight, ffn_gain, gate_up, down_weight
):
    is_first = lax.axis_index("section") == 0
    rows, slots, width = inputs_x.shape
    tables = turned_tables(slots, rows)
    info = jnp.concatenate([lengths, is_first.astype(jnp.int32)[None]])
    mask = padding(lengths, slots).reshape(-1, 1)
    gains = jnp.concatenate([attn_gain, ffn_gain], 0).T
    gains = jnp.pad(gains, ((0, 0), (0, 128 - gains.shape[1])))
    shards = (gains, qkv_weight[0], out_weight[0], gate_up[0], down_weight[0])
    together = gains.shape[0] % 16 == 0
    tokens = (flat(inputs_x), mask, tables, rows) if together else None
    gathered_all = gathered(
        lax.axis_size("group"), lax.axis_size("dp"), shards, gather_families, tokens
    )
    gains_all, qkv_w, output_weight, gate_up_w, down_w = (flat(x) for x in gathered_all[:5])
    if together:
        gain_rows, _, recv_act = gathered_all[5:]
    else:
        gain_rows = gains_all[:, :2].astype(jnp.float32).T
    gain_one, gain_two = gain_rows[0:1], gain_rows[1:2]
    dz_given = (flat(cotangent).astype(jnp.float32) * mask).astype(jnp.bfloat16)
    if not together:
        after_one = attention_forward(
            info, flat(inputs_x), gain_one, tables, qkv_w, output_weight, rows
        )[0]
        first_out = ffn_forward(after_one, gain_two, mask, gate_up_w, down_w)
        recv_act = passed_along(first_out, "section", 1)
    layer_in = jnp.where(is_first, flat(inputs_x), recv_act)
    after, heads, log_total, attention_turned, normed_turned = attention_forward(
        info, layer_in, gain_one, tables, qkv_w, output_weight, rows
    )
    dy, dy_low, _ = ffn_backward(after, dz_given, gain_two, gate_up_w, down_w)
    (second_dx,) = attention_backward(
        info, layer_in, gain_one, dy, dy_low, tables, heads, log_total, output_weight, qkv_w, rows, False
    )
    recv_grad = passed_along(second_dx, "section", -1)
    after, second_dx = lax.optimization_barrier((after, second_dx))
    hidden_turned, by_gate, by_up, normed_two_turned, result = ffn_prepare(
        after, gain_two, mask, gate_up_w, down_w
    )
    activations = (hidden_turned, attention_turned, normed_two_turned, normed_turned)
    recv_grad, activations, by_gate = lax.optimization_barrier((recv_grad, activations, by_gate))
    others = tuple(swapped(x, "dp") for x in activations)
    dz = jnp.where(is_first, (recv_grad.astype(jnp.float32) * mask).astype(jnp.bfloat16), dz_given)
    dy, dy_low, ffn_gain_part, grad_gate, grad_up = ffn_backward(
        after, dz, gain_two, gate_up_w, down_w, (by_gate, by_up)
    )
    grad_x, attn_gain_part, grad_qkv = attention_backward(
        info, layer_in, gain_one, dy, dy_low, tables, heads, log_total, output_weight, qkv_w, rows, True
    )
    section_out = result.reshape((1,) + inputs_x.shape)
    input_grads = grad_x.reshape((1,) + inputs_x.shape)
    gain_parts = jnp.pad(jnp.concatenate([attn_gain_part, ffn_gain_part], 0), ((0, 6), (0, 0)))
    gate_qkv_sum, down_out_sum, gain_sums = summed_grads(
        lax.axis_size("group"),
        lax.axis_size("dp"),
        activations,
        others,
        dz,
        dy_low,
        grad_gate,
        grad_up,
        grad_qkv,
        gain_parts,
    )
    gain_cols = attn_gain.shape[1] * lax.axis_size("dp")
    gain_sums = lax.dynamic_slice_in_dim(
        gain_sums, lax.axis_index("group") * gain_cols, gain_cols, 1
    )
    gate_sum, qkv_sum = widened(gate_qkv_sum, (gate_up.shape[2], qkv_weight.shape[2]))
    down_rows = down_weight.shape[1] * lax.axis_size("dp")
    reduced = (
        gain_sums[0],
        qkv_sum,
        down_out_sum[down_rows:].astype(jnp.float32),
        gain_sums[1],
        gate_sum,
        down_out_sum[:down_rows].astype(jnp.float32),
    )
    return (section_out, input_grads) + tuple((shard_sum[None] for shard_sum in reduced))


def solution(mesh):
    placed = (
        P(("group", "dp"), None, None),
        P(("group", "dp"), None, None),
        P(("group", "dp")),
        P("section", ("group", "dp")),
        P("section", ("group", "dp"), None),
        P("section", ("group", "dp"), None),
        P("section", ("group", "dp")),
        P("section", ("group", "dp"), None),
        P("section", ("group", "dp"), None),
    )
    return jax.shard_map(
        body,
        mesh=mesh,
        in_specs=placed,
        out_specs=(
            P("section", ("group", "dp"), None, None),
            P("section", ("group", "dp"), None, None),
            P("section", "group"),
            P("section", "group", None),
            P("section", "group", None),
            P("section", "group"),
            P("section", "group", None),
            P("section", "group", None),
        ),
        check_vma=False,
    )
```

```python
import functools

import jax
import jax.numpy as jnp
from jax import lax
from jax.experimental import pallas as pl
from jax.experimental.pallas import tpu as pltpu
from jax.sharding import PartitionSpec as P

H = 16
KVH = 8
HD = 96


norm_eps = 1e-05
rope_base = 100000.0
masked_score = -1e30
across = (((1,), (1,)), ((), ()))
down_rows = (((0,), (0,)), ((), ()))


def passed_along(value, axis, by):
    length = lax.axis_size(axis)
    pairs = [(i, i + by) for i in range(length) if 0 <= i + by < length]
    return lax.ppermute(value, axis, pairs)


def swapped(value, axis):
    return lax.ppermute(value, axis, [(i, i ^ 1) for i in range(lax.axis_size(axis))])


def padding(lengths, slot_count):
    position = jnp.arange(slot_count, dtype=jnp.int32)
    return (position[None, :] < lengths[:, None]).astype(jnp.float32)[..., None]


FF_CHUNK = 1024
across = (((1,), (1,)), ((), ()))
down_rows = (((0,), (0,)), ((), ()))


def scaled_norm(value, gain):
    scale = lax.rsqrt(jnp.mean(value * value, -1, keepdims=True) + norm_eps)
    return scale, (value * scale * gain).astype(jnp.bfloat16)


def ffn_forward_kernel(y, gain, mask, wg, wu, wd, out, n2, acc):
    j = pl.program_id(0)

    @pl.when(j == 0)
    def _():
        n2[...] = scaled_norm(y[...], gain[...])[1]
        acc[...] = y[...]

    gate = jnp.dot(n2[...], wg[...], preferred_element_type=jnp.float32)
    up = jnp.dot(n2[...], wu[...], preferred_element_type=jnp.float32)
    hidden = (gate / (1.0 + jnp.exp(-gate)) * up).astype(jnp.bfloat16)
    acc[...] += jnp.dot(hidden, wd[...], preferred_element_type=jnp.float32)

    @pl.when(j == pl.num_programs(0) - 1)
    def _():
        out[...] = (acc[...] * mask[...]).astype(jnp.bfloat16)


def ffn_specs(tokens, width, hidden):
    steps = hidden // FF_CHUNK
    whole = pl.BlockSpec((tokens, width), lambda j: (0, 0))
    row = pl.BlockSpec((1, width), lambda j: (0, 0))
    weights = [
        pl.BlockSpec((width, FF_CHUNK), lambda j: (0, j)),
        pl.BlockSpec((width, FF_CHUNK), lambda j: (0, j + steps)),
        pl.BlockSpec((FF_CHUNK, width), lambda j: (j, 0)),
    ]
    return steps, whole, row, weights


def ffn_forward(y, gain, mask, gate_up_w, down_w):
    tokens, width = y.shape
    hidden = down_w.shape[0]
    steps, whole, row, weights = ffn_specs(tokens, width, hidden)
    return pl.pallas_call(
        ffn_forward_kernel,
        grid=(steps,),
        out_shape=jax.ShapeDtypeStruct((tokens, width), jnp.bfloat16),
        in_specs=[whole, row, pl.BlockSpec((tokens, 1), lambda j: (0, 0))] + weights,
        out_specs=whole,
        scratch_shapes=[pltpu.VMEM((tokens, width), jnp.bfloat16), pltpu.VMEM((tokens, width), jnp.float32)],
        compiler_params=pltpu.CompilerParams(vmem_limit_bytes=40 * 1024 * 1024),
        cost_estimate=pl.CostEstimate(
            flops=6 * tokens * width * hidden, bytes_accessed=6 * width * hidden, transcendentals=tokens * hidden
        ),
    )(y, gain, mask, gate_up_w, gate_up_w, down_w)


def ffn_prepare_kernel(y, gain, mask, wg, wu, wd, at, by_gate, by_up, n2t, out, n2, acc):
    j = pl.program_id(0)
    bf16, f32 = jnp.bfloat16, jnp.float32

    @pl.when(j == 0)
    def _():
        n = scaled_norm(y[...], gain[...])[1]
        n2[...] = n
        n2t[...] = n.T
        acc[...] = y[...]

    gate = jnp.dot(n2[...], wg[...], preferred_element_type=f32)
    up = jnp.dot(n2[...], wu[...], preferred_element_type=f32)
    sig = 1.0 / (1.0 + jnp.exp(-gate))
    silu = gate * sig
    hidden = (silu * up).astype(bf16)
    at[...] = hidden.T
    by_gate[...] = (up * sig * (1.0 + gate * (1.0 - sig))).astype(bf16)
    by_up[...] = silu.astype(bf16)
    acc[...] += jnp.dot(hidden, wd[...], preferred_element_type=f32)

    @pl.when(j == pl.num_programs(0) - 1)
    def _():
        out[...] = (acc[...] * mask[...]).astype(bf16)


def ffn_prepare(y, gain, mask, gate_up_w, down_w):
    tokens, width = y.shape
    hidden = down_w.shape[0]
    steps, whole, row, weights = ffn_specs(tokens, width, hidden)
    shape, bf16 = jax.ShapeDtypeStruct, jnp.bfloat16
    part = pl.BlockSpec((tokens, FF_CHUNK), lambda j: (0, j))
    return pl.pallas_call(
        ffn_prepare_kernel,
        grid=(steps,),
        out_shape=(
            shape((hidden, tokens), bf16), shape((tokens, hidden), bf16), shape((tokens, hidden), bf16),
            shape((width, tokens), bf16), shape((tokens, width), bf16),
        ),
        in_specs=[whole, row, pl.BlockSpec((tokens, 1), lambda j: (0, 0))] + weights,
        out_specs=(
            pl.BlockSpec((FF_CHUNK, tokens), lambda j: (j, 0)), part, part,
            pl.BlockSpec((width, tokens), lambda j: (0, 0)), whole,
        ),
        scratch_shapes=[pltpu.VMEM((tokens, width), bf16), pltpu.VMEM((tokens, width), jnp.float32)],
        compiler_params=pltpu.CompilerParams(vmem_limit_bytes=48 * 1024 * 1024),
        cost_estimate=pl.CostEstimate(
            flops=6 * tokens * width * hidden, bytes_accessed=6 * width * hidden, transcendentals=tokens * hidden
        ),
    )(y, gain, mask, gate_up_w, gate_up_w, down_w)


def ffn_backward_kernel(prepared, y, dz, gain, wg, wu, wd, *rest):
    bf16, f32 = jnp.bfloat16, jnp.float32
    if prepared:
        by_gate, by_up, dy, dyb, gain_grad, dgate, dup, acc = rest
    else:
        dy, dyb, gain_grad, n2, acc = rest
    j = pl.program_id(0)

    @pl.when(j == 0)
    def _():
        acc[...] = jnp.zeros_like(acc)
        if not prepared:
            n2[...] = scaled_norm(y[...], gain[...])[1]

    grad = lax.dot_general(dz[...], wd[...], across, preferred_element_type=f32)
    if prepared:
        grad_gate = (grad * by_gate[...].astype(f32)).astype(bf16)
        grad_up = (grad * by_up[...].astype(f32)).astype(bf16)
        dgate[...] = grad_gate
        dup[...] = grad_up
    else:
        gate = jnp.dot(n2[...], wg[...], preferred_element_type=f32)
        up = jnp.dot(n2[...], wu[...], preferred_element_type=f32)
        sig = 1.0 / (1.0 + jnp.exp(-gate))
        grad_gate = (grad * up * sig * (1.0 + gate * (1.0 - sig))).astype(bf16)
        grad_up = (grad * (gate * sig)).astype(bf16)
    acc[...] += lax.dot_general(grad_gate, wg[...], across, preferred_element_type=f32) + lax.dot_general(
        grad_up, wu[...], across, preferred_element_type=f32
    )

    @pl.when(j == pl.num_programs(0) - 1)
    def _():
        value, grad_normed = y[...], acc[...]
        r = lax.rsqrt(jnp.mean(value * value, -1, keepdims=True) + norm_eps)
        scaled = grad_normed * gain[...]
        gain_grad[...] = jnp.sum(grad_normed * value * r, axis=0, keepdims=True)
        inner = jnp.mean(value * scaled, -1, keepdims=True)
        total = dz[...].astype(f32) + r * scaled - value * (r * r * r) * inner
        dy[...] = total
        dyb[...] = total.astype(bf16)


def ffn_backward(y, dz, gain, gate_up_w, down_w, factors=()):
    tokens, width = y.shape
    hidden = down_w.shape[0]
    steps, whole, row, weights = ffn_specs(tokens, width, hidden)
    shape, bf16, f32 = jax.ShapeDtypeStruct, jnp.bfloat16, jnp.float32
    outs = [shape((tokens, width), f32), shape((tokens, width), bf16), shape((1, width), f32)]
    out_specs = [whole, whole, row]
    scratch = [pltpu.VMEM((tokens, width), f32)]
    parts = [pl.BlockSpec((tokens, FF_CHUNK), lambda j: (0, j))] * len(factors)
    if factors:
        outs += [shape((tokens, hidden), bf16)] * 2
        out_specs += parts
    else:
        scratch = [pltpu.VMEM((tokens, width), bf16)] + scratch
    return pl.pallas_call(
        functools.partial(ffn_backward_kernel, bool(factors)),
        grid=(steps,),
        out_shape=tuple(outs),
        in_specs=[whole, whole, row] + weights + parts,
        out_specs=tuple(out_specs),
        scratch_shapes=scratch,
        compiler_params=pltpu.CompilerParams(vmem_limit_bytes=48 * 1024 * 1024),
        cost_estimate=pl.CostEstimate(
            flops=10 * tokens * width * hidden, bytes_accessed=6 * width * hidden, transcendentals=tokens * hidden
        ),
    )(y, dz, gain, gate_up_w, gate_up_w, down_w, *factors)


def turned_tables(slots, rows):
    half_width = HD // 2
    frequency = rope_base ** (-(jnp.arange(half_width, dtype=jnp.float32) * 2.0 / HD))
    angles = frequency[:, None] * jnp.arange(slots, dtype=jnp.float32)[None, :]
    return jnp.tile(jnp.cos(angles), (1, rows)), jnp.tile(jnp.sin(angles), (1, rows))


def pair_mask(length, slots):
    groups = H // KVH
    key = lax.broadcasted_iota(jnp.int32, (slots, groups * slots), 0)
    query = lax.rem(lax.broadcasted_iota(jnp.int32, (slots, groups * slots), 1), slots)
    return (key <= query) & (key < length)


def pair_of(ref, k, row, slots):
    groups = H // KVH
    first = groups * k * HD
    return jnp.concatenate(
        [ref[first + g * HD : first + (g + 1) * HD, row * slots : (row + 1) * slots] for g in range(groups)], 1
    )


def key_value(qkvt, k, row, slots):
    tokens = slice(row * slots, (row + 1) * slots)
    keys = qkvt[(H + k) * HD : (H + k + 1) * HD, tokens]
    values = qkvt[(H + KVH + k) * HD : (H + KVH + k + 1) * HD, tokens]
    return keys, values


def pair_scores(keys, queries, mask):
    scores = lax.dot_general(keys, queries, down_rows, preferred_element_type=jnp.float32) * HD ** (-0.5)
    return jnp.where(mask, scores, masked_score)


def attention_forward_kernel(rows, info, x, gain, cosines, sines, w, wo, y, qkvt, lse, ot, n1t, n1):
    j = pl.program_id(0)
    bf16, f32 = jnp.bfloat16, jnp.float32
    slots, part, half = x.shape[0] // rows, KVH * HD, HD // 2
    groups = H // KVH

    @pl.when(j == 0)
    def _():
        n = scaled_norm(x[...].astype(f32), gain[...])[1]
        n1[...] = n
        n1t[...] = n.T

    chunk = jnp.dot(n1[...], w[...], preferred_element_type=f32).T

    @pl.when(j <= groups)
    def _():
        for h in range(KVH):
            front, back = chunk[h * HD : h * HD + half], chunk[h * HD + half : (h + 1) * HD]
            base = j * part + h * HD
            qkvt[pl.ds(pl.multiple_of(base, 16), half), :] = (front * cosines[...] - back * sines[...]).astype(bf16)
            qkvt[pl.ds(pl.multiple_of(base + half, 16), half), :] = (
                back * cosines[...] + front * sines[...]
            ).astype(bf16)

    @pl.when(j > groups)
    def _():
        qkvt[pl.ds(pl.multiple_of(j * part, 16), part), :] = chunk.astype(bf16)
        for row in range(rows):
            mask = pair_mask(info[row], slots)
            for k in range(KVH):
                keys, values = key_value(qkvt, k, row, slots)
                scores = pair_scores(keys, pair_of(qkvt, k, row, slots), mask)
                top = jnp.max(scores, 0, keepdims=True)
                total = top + jnp.log(jnp.sum(jnp.exp(scores - top), 0, keepdims=True))
                lse[row * KVH + k : row * KVH + k + 1, :] = total
                probs = jnp.exp(scores - total).astype(bf16)
                out = jnp.dot(values, probs, preferred_element_type=f32).astype(bf16)
                for g in range(groups):
                    first = (groups * k + g) * HD
                    ot[first : first + HD, row * slots : (row + 1) * slots] = out[:, g * slots : (g + 1) * slots]
        y[...] = x[...].astype(f32) + lax.dot_general(ot[...], wo[...], down_rows, preferred_element_type=f32)


def attention_backward_kernel(
    rows, keep, info, x, gain, dy, dyb, cosines, sines, qkvt, lse, wo, w, dx, *rest
):
    if keep:
        gain_grad, dqkv, dot, dqkvt, acc = rest
    else:
        dqkv, dot, dqkvt, acc = rest
    j = pl.program_id(0)
    bf16, f32 = jnp.bfloat16, jnp.float32
    slots, part, half = x.shape[0] // rows, KVH * HD, HD // 2
    groups = H // KVH

    def unrotated(grad, row, width):
        tokens = slice(row * slots, (row + 1) * slots)
        cos, sin = cosines[:, tokens], sines[:, tokens]
        if width > slots:
            cos, sin = jnp.concatenate([cos] * groups, 1), jnp.concatenate([sin] * groups, 1)
        grad = grad * HD ** (-0.5)
        front, back = grad[:half], grad[half:]
        return (front * cos + back * sin).astype(bf16), (back * cos - front * sin).astype(bf16)

    @pl.when(j == 0)
    def _():
        dot[...] = lax.dot_general(dyb[...], wo[...], across, preferred_element_type=f32).astype(bf16).T
        acc[...] = jnp.zeros_like(acc)
        for row in range(rows):
            tokens = slice(row * slots, (row + 1) * slots)
            mask = pair_mask(info[row], slots)
            for k in range(KVH):
                keys, values = key_value(qkvt, k, row, slots)
                queries, grads = pair_of(qkvt, k, row, slots), pair_of(dot, k, row, slots)
                scores = pair_scores(keys, queries, mask)
                probs = jnp.exp(scores - lse[row * KVH + k : row * KVH + k + 1, :])
                grad_probs = lax.dot_general(values, grads, down_rows, preferred_element_type=f32)
                grad_scores = (
                    probs * (grad_probs - jnp.sum(probs * grad_probs, 0, keepdims=True))
                ).astype(bf16)
                grad_values = lax.dot_general(grads, probs.astype(bf16), across, preferred_element_type=f32)
                grad_keys = lax.dot_general(queries, grad_scores, across, preferred_element_type=f32)
                grad_queries = jnp.dot(keys, grad_scores, preferred_element_type=f32)
                front, back = unrotated(grad_queries, row, groups * slots)
                for g in range(groups):
                    first = (groups * k + g) * HD
                    dqkvt[first : first + half, tokens] = front[:, g * slots : (g + 1) * slots]
                    dqkvt[first + half : first + HD, tokens] = back[:, g * slots : (g + 1) * slots]
                front, back = unrotated(grad_keys, row, slots)
                first = (H + k) * HD
                dqkvt[first : first + half, tokens] = front
                dqkvt[first + half : first + HD, tokens] = back
                first = (H + KVH + k) * HD
                dqkvt[first : first + HD, tokens] = grad_values.astype(bf16)
        for i in range(groups + 2):
            dqkv[:, i * part : (i + 1) * part] = dqkvt[i * part : (i + 1) * part, :].T

    columns = pl.ds(pl.multiple_of(j * part, 128), part)
    acc[...] += lax.dot_general(dqkv[:, columns], w[...], across, preferred_element_type=f32)

    @pl.when(j == pl.num_programs(0) - 1)
    def _():
        value, grad_normed = x[...].astype(f32), acc[...]
        r = lax.rsqrt(jnp.mean(value * value, -1, keepdims=True) + norm_eps)
        scaled = grad_normed * gain[...]
        inner = jnp.mean(value * scaled, -1, keepdims=True)
        total = dy[...] + (r * scaled - value * (r * r * r) * inner)
        if keep:
            gain_grad[...] = jnp.sum(grad_normed * value * r, axis=0, keepdims=True)
            dx[...] = jnp.where(info[rows] == 1, total, total.astype(bf16).astype(f32))
        else:
            dx[...] = total.astype(bf16)


def attention_specs(tokens, width):
    part = KVH * HD
    whole = lambda *shape: pl.BlockSpec(shape, lambda j: (0,) * len(shape))
    return part, whole, pl.BlockSpec(memory_space=pltpu.SMEM), pl.BlockSpec((width, part), lambda j: (0, j))


def attention_forward(info, x, gain, tables, qkv_w, output_weight, rows):
    tokens, width = x.shape
    cols, slots = qkv_w.shape[1], tokens // rows
    part, whole, scalars, weight = attention_specs(tokens, width)
    shape, bf16, f32 = jax.ShapeDtypeStruct, jnp.bfloat16, jnp.float32
    stats = (rows * KVH, H // KVH * slots)
    return pl.pallas_call(
        functools.partial(attention_forward_kernel, rows),
        grid=(cols // part,),
        out_shape=(
            shape((tokens, width), f32), shape((cols, tokens), bf16), shape(stats, f32),
            shape((H * HD, tokens), bf16), shape((width, tokens), bf16),
        ),
        in_specs=[
            scalars, whole(tokens, width), whole(1, width), whole(HD // 2, tokens), whole(HD // 2, tokens), weight,
            whole(H * HD, width),
        ],
        out_specs=(
            whole(tokens, width), whole(cols, tokens), whole(*stats), whole(H * HD, tokens), whole(width, tokens)
        ),
        scratch_shapes=[pltpu.VMEM((tokens, width), bf16)],
        compiler_params=pltpu.CompilerParams(vmem_limit_bytes=40 * 1024 * 1024),
        cost_estimate=pl.CostEstimate(
            flops=2 * tokens * width * (cols + H * HD), bytes_accessed=2 * width * (cols + H * HD), transcendentals=0
        ),
    )(info, x, gain, *tables, qkv_w, output_weight)


def attention_backward(info, x, gain, dy, dy_low, tables, qkvt, lse, output_weight, qkv_w, rows, keep):
    tokens, width = x.shape
    cols = qkv_w.shape[1]
    part, whole, scalars, weight = attention_specs(tokens, width)
    shape, bf16, f32 = jax.ShapeDtypeStruct, jnp.bfloat16, jnp.float32
    scratch = [pltpu.VMEM((H * HD, tokens), bf16), pltpu.VMEM((cols, tokens), bf16), pltpu.VMEM((tokens, width), f32)]
    outs, out_specs = [shape((tokens, width), f32 if keep else bf16)], [whole(tokens, width)]
    if keep:
        outs += [shape((1, width), f32), shape((tokens, cols), bf16)]
        out_specs += [whole(1, width), whole(tokens, cols)]
    else:
        scratch = [pltpu.VMEM((tokens, cols), bf16)] + scratch
    return pl.pallas_call(
        functools.partial(attention_backward_kernel, rows, keep),
        grid=(cols // part,),
        out_shape=tuple(outs),
        in_specs=[
            scalars, whole(tokens, width), whole(1, width), whole(tokens, width), whole(tokens, width),
            whole(HD // 2, tokens), whole(HD // 2, tokens), whole(cols, tokens), whole(*lse.shape), whole(H * HD, width),
            weight,
        ],
        out_specs=tuple(out_specs),
        scratch_shapes=scratch,
        compiler_params=pltpu.CompilerParams(vmem_limit_bytes=48 * 1024 * 1024),
        cost_estimate=pl.CostEstimate(
            flops=2 * tokens * width * (cols + H * HD), bytes_accessed=2 * width * (cols + H * HD), transcendentals=0
        ),
    )(info, x, gain, dy, dy_low, *tables, qkvt, lse, output_weight, qkv_w)


def flat(array):
    return array.reshape(-1, array.shape[-1])


MESH = pl.DeviceIdType.MESH
LANES = 128


def grad_plan(groups, dp, tokens, width, hidden, qkv_cols):
    pairs = dp // 2
    block = width // groups
    down_block = hidden // groups
    gate_cols = 2 * hidden // 2 // pairs
    qkv_part = qkv_cols // 2 // pairs
    pieces_gate = gate_cols // LANES
    pieces_qkv = qkv_part // LANES
    pieces = pieces_gate + pieces_qkv
    z_rows = LANES
    while down_block % z_rows or block % z_rows:
        z_rows //= 2
    row_chunks = (down_block + block) // z_rows
    half = width // 2
    z_split = max(1, pieces // row_chunks)
    while half % (z_split * LANES):
        z_split -= 1
    return dict(
        groups=groups, pairs=pairs, tokens=tokens, width=width, hidden=hidden, qkv_cols=qkv_cols, block=block,
        down_block=down_block, gate_cols=gate_cols, qkv_part=qkv_part, pieces_gate=pieces_gate, pieces=pieces,
        z_rows=z_rows, z_split=z_split, z_cols=half // z_split, z_pieces=row_chunks * z_split,
        down_chunks=down_block // z_rows, half=half,
    )


YS_RING = 4
HOP = 2
LEAD = 2
YLAG = 2


def grad_kernel(
    plan, at, ot, n2t, n1t, at2, ot2, n2t2, n1t2, dz, dy, dgate, dup, dq, gp, outy, outz, outg,
    LT, RH, YS, YR, YRT, YLT, ZRT, ZLT, ZX,
    own_sem, xs, xr, ys_s, ys_r, yr_s, yr_r, yl_s, yl_r, zr_s, zr_r, zl_s, zl_r,
    zx_s, zx_r, ag_s, ag_r, sib_s, sib_r, lo,
    GC, GA, GS, GR, GL, gc_sem, ga_s, ga_r, gr_sem, gl_sem,
):
    G, A, T = plan["groups"], plan["pairs"], plan["tokens"]
    width, hidden, half = plan["width"], plan["hidden"], plan["half"]
    block, nY, nZ = plan["block"], plan["pieces"], plan["z_pieces"]
    zr, zc = plan["z_rows"], plan["z_cols"]
    s, z, d = lax.axis_index("section"), lax.axis_index("group"), lax.axis_index("dp")
    c, a = lax.rem(d, 2), lax.div(d, 2)
    sib = (s, z, 2 * a + 1 - c)
    right, left = (s, z + 1, d), (s, z - 1, d)

    def peer(k):
        return (s, z, 2 * lax.rem(a + k, A) + c)

    def remote(src, dst, ss, rs, dev):
        return pltpu.make_async_remote_copy(
            src_ref=src, dst_ref=dst, send_sem=ss, recv_sem=rs, device_id=dev, device_id_type=MESH
        )

    barrier = pltpu.get_barrier_semaphore()
    for dev in [sib, (s, lax.rem(z + 1, G), d), (s, lax.rem(z + G - 1, G), d)] + [peer(k) for k in range(1, A)]:
        pl.semaphore_signal(barrier, inc=1, device_id=dev, device_id_type=MESH)
    pl.semaphore_wait(barrier, A + 2)

    lhs = [
        (at, at2, 0, hidden), (ot, ot2, hidden, width), (n2t, n2t2, hidden + width, width),
        (n1t, n1t2, hidden + 2 * width, width),
    ]
    rhs = [(dz, 0, half), (dy, half, half), (None, width, hidden), (dq, width + hidden, plan["qkv_cols"] // 2)]
    own, cross = {}, {}
    for i, (ref, theirs, row, rows) in enumerate(lhs):
        own[0, i] = pltpu.make_async_copy(ref, LT.at[pl.ds(row, rows), pl.ds(0, T)], own_sem.at[i])
        own[2, i] = pltpu.make_async_copy(theirs, LT.at[pl.ds(row, rows), pl.ds(T, T)], own_sem.at[8 + i])
    for i, (ref, col, cols) in enumerate(rhs):
        if ref is None:
            continue
        mine = pl.ds(pl.multiple_of(c * cols, LANES), cols)
        theirs = pl.ds(pl.multiple_of((1 - c) * cols, LANES), cols)
        own[1, i] = pltpu.make_async_copy(ref.at[:, mine], RH.at[pl.ds(0, T), pl.ds(col, cols)], own_sem.at[4 + i])
        cross[1, i] = remote(ref.at[:, theirs], RH.at[pl.ds(T, T), pl.ds(col, cols)], xs.at[4 + i], xr.at[4 + i], sib)
    col, cols = rhs[2][1:]
    for core, (mine, theirs) in enumerate(((dgate, dup), (dup, dgate))):
        own[1, 2, core] = pltpu.make_async_copy(mine, RH.at[pl.ds(0, T), pl.ds(col, cols)], own_sem.at[6])
        cross[1, 2, core] = remote(theirs, RH.at[pl.ds(T, T), pl.ds(col, cols)], xs.at[6], xr.at[6], sib)
    own[1, 2], cross[1, 2] = own[1, 2, 0], cross[1, 2, 0]
    def fetch(i):
        if i == 2:
            for core in (0, 1):
                @pl.when(c == core)
                def _(core=core):
                    cross[1, 2, core].start()
                    own[1, 2, core].start()
        else:
            cross[1, i].start()
            own[1, i].start()
        own[0, i].start()
        own[2, i].start()

    fetch(0)
    fetch(2)

    def operands_here(i):
        for side in (0, 2, 1):
            own[side, i].wait()
        cross[1, i].wait_recv()

    def product(row, rows, col, cols):
        return jnp.dot(
            LT[pl.ds(row, rows), :], RH[:, pl.ds(col, cols)], preferred_element_type=jnp.float32
        )

    def y_product(q, which, b):
        is_gate = q < plan["pieces_gate"]
        row = jnp.where(is_gate, hidden + width, hidden + 2 * width) + b * block
        col = jnp.where(
            is_gate,
            width + which * plan["gate_cols"] + q * LANES,
            width + hidden + which * plan["qkv_part"] + (q - plan["pieces_gate"]) * LANES,
        )
        return product(pl.multiple_of(row, 16), block, pl.multiple_of(col, LANES), LANES)

    def z_product(p, b):
        r, h = lax.div(p, plan["z_split"]), lax.rem(p, plan["z_split"])
        is_down = r < plan["down_chunks"]
        row = jnp.where(
            is_down, b * plan["down_block"] + r * zr, hidden + b * block + (r - plan["down_chunks"]) * zr
        )
        col = jnp.where(is_down, 0, half) + h * zc
        return product(pl.multiple_of(row, 16), zr, pl.multiple_of(col, LANES), zc)

    def y_out(q, part, core):
        is_gate = q < plan["pieces_gate"]
        col = jnp.where(
            is_gate,
            core * hidden + part * plan["gate_cols"] + q * LANES,
            2 * hidden + core * (plan["qkv_cols"] // 2) + part * plan["qkv_part"] + (q - plan["pieces_gate"]) * LANES,
        )
        return outy.at[:, pl.ds(pl.multiple_of(col, LANES), LANES)]

    def z_out(p, core):
        r, h = lax.div(p, plan["z_split"]), lax.rem(p, plan["z_split"])
        return outz.at[
            pl.ds(pl.multiple_of(r * zr, 16), zr), pl.ds(pl.multiple_of(core * half + h * zc, LANES), zc)
        ]

    def y_send(q, k):
        return remote(YS.at[lax.rem(q, YS_RING), k - 1], YR.at[q, k - 1], ys_s.at[q, k - 1], ys_r.at[q, k - 1], peer(k))

    def line_copies(slots_r, slots_l, r_s, r_r, l_s, l_r, first_r, first_l, p):
        out_r, in_r, out_l, in_l = [], [], [], []
        for k in range(G):
            if k < G - 1:
                src = first_r(p) if k == 0 else slots_r.at[p, pl.ds(k, G - 1 - k)]
                out_r.append((k, remote(src, slots_r.at[p, pl.ds(k, G - 1 - k)], r_s.at[p], r_r.at[p], right)))
                held = slots_l.at[p, pl.ds(0, k + 1)]
                in_l.append((k, remote(held, held, l_s.at[p], l_r.at[p], left)))
            if k > 0:
                src = first_l(p) if k == G - 1 else slots_l.at[p, pl.ds(0, k)]
                out_l.append((k, remote(src, slots_l.at[p, pl.ds(0, k)], l_s.at[p], l_r.at[p], left)))
                held = slots_r.at[p, pl.ds(k - 1, G - k)]
                in_r.append((k, remote(held, held, r_s.at[p], r_r.at[p], right)))
        return out_r, in_r, out_l, in_l

    def at_place(copies, act):
        for k, copy in copies:
            @pl.when(z == k)
            def _(copy=copy):
                act(copy)

    def y_line(q):
        return line_copies(
            YRT, YLT, yr_s, yr_r, yl_s, yl_r,
            lambda q: YR.at[q, 0, pl.ds(1, G - 1)], lambda q: YR.at[q, 0, pl.ds(0, G - 1)], q,
        )

    def z_line(p):
        return line_copies(
            ZRT, ZLT, zr_s, zr_r, zl_s, zl_r,
            lambda p: ZRT.at[p, pl.ds(0, G - 1)], lambda p: ZLT.at[p, pl.ds(0, G - 1)], p,
        )

    def zx_copy(p, k):
        return remote(ZX.at[p, a], ZX.at[p, a], zx_s.at[p, k - 1], zx_r.at[p, k - 1], peer(k))

    def ag_copy(q, k):
        return remote(YR.at[q, 0, z], y_out(q, a, c), ag_s.at[q, k - 1], ag_r.at[q, k - 1], peer(k))

    def sib_own(q):
        return remote(YR.at[q, 0, z], y_out(q, a, c), sib_s.at[q, 0], sib_r.at[q, 0], sib)

    def sib_pass(q, k):
        part = lax.rem(a + A - k, A)
        return remote(y_out(q, part, c), y_out(q, part, c), sib_s.at[q, k], sib_r.at[q, k], sib)

    def own_y(q):
        return pltpu.make_async_copy(YR.at[q, 0, z], y_out(q, a, c), lo.at[q])

    def own_z(p):
        return pltpu.make_async_copy(ZX.at[p, a], z_out(p, c), lo.at[nY + p])

    def sib_z(p):
        return remote(ZX.at[p, a], z_out(p, c), sib_s.at[nY + p, 0], sib_r.at[nY + p, 0], sib)

    f32, bf16 = jnp.float32, jnp.bfloat16
    far = jnp.maximum(z, G - 1 - z)

    def live(index, count):
        return (index >= 0) & (index < count)

    def gain_core():
        return remote(gp, GC, gc_sem.at[0], gc_sem.at[1], sib)

    def gain_part(k):
        return remote(GA.at[a], GA.at[a], ga_s.at[k - 1], ga_r.at[k - 1], peer(k))

    def gain_right():
        return remote(GS.at[1], GR, gr_sem.at[0], gr_sem.at[1], right)

    def gain_left():
        return remote(GS.at[2], GL, gl_sem.at[0], gl_sem.at[1], left)

    def gain_step(t):
        @pl.when(t == 0)
        def _():
            gain_core().start()

        @pl.when(t == 1)
        def _():
            gain_core().wait_recv()
            GA[a] = gp[...] + GC[...]
            for k in range(1, A):
                gain_part(k).start()

        @pl.when(t == 2)
        def _():
            for k in range(1, A):
                remote(
                    GA.at[lax.rem(a + A - k, A)], GA.at[lax.rem(a + A - k, A)], ga_s.at[k - 1], ga_r.at[k - 1], peer(k)
                ).wait_recv()
            total = GA[0]
            for k in range(1, A):
                total += GA[k]
            GS[0] = total

        @pl.when(t == 2 + HOP * z)
        def _():
            @pl.when(z > 0)
            def _():
                gain_right().wait_recv()
                GS[1] = GS[0] + GR[...]

            @pl.when(z == 0)
            def _():
                GS[1] = GS[0]

            @pl.when(z < G - 1)
            def _():
                gain_right().start()

        @pl.when(t == 2 + HOP * (G - 1 - z))
        def _():
            @pl.when(z < G - 1)
            def _():
                gain_left().wait_recv()
                GS[2] = GS[0] + GL[...]

            @pl.when(z == G - 1)
            def _():
                GS[2] = GS[0]

            @pl.when(z > 0)
            def _():
                gain_left().start()

        @pl.when(t == 3 + HOP * (G - 1))
        def _():
            outg[...] = GS[1] + jnp.where(z < G - 1, GL[...], 0.0)

    def step(t, carry):
        gain_step(t)

        @pl.when(t == 0)
        def _():
            operands_here(0)
            operands_here(2)
            fetch(1)
            fetch(3)

        @pl.when(t == jnp.minimum(plan["pieces_gate"], plan["down_chunks"] * plan["z_split"]) - 1)
        def _():
            operands_here(1)
            operands_here(3)

        q1 = t - YLAG

        @pl.when(live(q1, nY))
        def _():
            for k in range(1, A):
                @pl.when(q1 >= YS_RING)
                def _():
                    y_send(q1 - YS_RING, k).wait_send()

                @pl.loop(0, G)
                def _(b):
                    YS[lax.rem(q1, YS_RING), k - 1, b] = y_product(q1, lax.rem(a + k, A), b).astype(bf16)

                y_send(q1, k).start()

        pr = t - HOP * z

        @pl.when(live(pr, nZ))
        def _():
            out_r, in_r, _, _ = z_line(pr)
            at_place(in_r, lambda copy: copy.wait_recv())

            @pl.loop(0, G)
            def _(b):
                @pl.when((b > z) & (z > 0))
                def _():
                    ZRT[pr, b - 1] = (z_product(pr, b) + ZRT[pr, b - 1].astype(f32)).astype(bf16)

                @pl.when((b > z) & (z == 0))
                def _():
                    ZRT[pr, b - 1] = z_product(pr, b).astype(bf16)

            at_place(out_r, lambda copy: copy.start())

        pL = t - HOP * (G - 1 - z)

        @pl.when(live(pL, nZ))
        def _():
            _, _, out_l, in_l = z_line(pL)
            at_place(in_l, lambda copy: copy.wait_recv())

            @pl.loop(0, G)
            def _(b):
                @pl.when((b < z) & (z < G - 1))
                def _():
                    ZLT[pL, b] = (z_product(pL, b) + ZLT[pL, b].astype(f32)).astype(bf16)

                @pl.when((b < z) & (z == G - 1))
                def _():
                    ZLT[pL, b] = z_product(pL, b).astype(bf16)

            at_place(out_l, lambda copy: copy.start())

        q2 = t - YLAG - LEAD

        @pl.when(live(q2, nY))
        def _():
            for k in range(1, A):
                y_send(q2, k).wait_recv()

            @pl.loop(0, G)
            def _(b):
                total = y_product(q2, a, b)
                for k in range(1, A):
                    total += YR[q2, k - 1, b].astype(f32)
                YR[q2, 0, b] = total.astype(bf16)

        qr = t - YLAG - LEAD - HOP * z

        @pl.when(live(qr, nY))
        def _():
            out_r, in_r, _, _ = y_line(qr)
            at_place(in_r, lambda copy: copy.wait_recv())

            @pl.loop(0, G)
            def _(b):
                @pl.when((b > z) & (z > 0))
                def _():
                    YRT[qr, b - 1] = (YR[qr, 0, b].astype(f32) + YRT[qr, b - 1].astype(f32)).astype(bf16)

            at_place(out_r, lambda copy: copy.start())

        qL = t - YLAG - LEAD - HOP * (G - 1 - z)

        @pl.when(live(qL, nY))
        def _():
            _, _, out_l, in_l = y_line(qL)
            at_place(in_l, lambda copy: copy.wait_recv())

            @pl.loop(0, G)
            def _(b):
                @pl.when((b < z) & (z < G - 1))
                def _():
                    YLT[qL, b] = (YR[qL, 0, b].astype(f32) + YLT[qL, b].astype(f32)).astype(bf16)

            at_place(out_l, lambda copy: copy.start())

        pf = t - HOP * far

        @pl.when(live(pf, nZ))
        def _():
            mine = z_product(pf, z)
            from_left = ZRT[pf, jnp.maximum(z - 1, 0)].astype(f32)
            from_right = ZLT[pf, jnp.minimum(z, G - 2)].astype(f32)
            mine = mine + jnp.where(z > 0, from_left, 0.0) + jnp.where(z < G - 1, from_right, 0.0)
            ZX[pf, a] = mine.astype(bf16)
            for k in range(1, A):
                zx_copy(pf, k).start()

        pg = t - HOP * far - LEAD

        @pl.when(live(pg, nZ))
        def _():
            for k in range(1, A):
                remote(
                    ZX.at[pg, lax.rem(a + A - k, A)], ZX.at[pg, lax.rem(a + A - k, A)],
                    zx_s.at[pg, k - 1], zx_r.at[pg, k - 1], peer(k),
                ).wait_recv()
            total = ZX[pg, 0].astype(f32)
            for k in range(1, A):
                total += ZX[pg, k].astype(f32)
            for k in range(1, A):
                zx_copy(pg, k).wait_send()
            ZX[pg, a] = total.astype(bf16)
            own_z(pg).start()
            sib_z(pg).start()

        qf = t - YLAG - LEAD - HOP * far

        @pl.when(live(qf, nY))
        def _():
            total = YR[qf, 0, z].astype(f32)
            from_left = YRT[qf, jnp.maximum(z - 1, 0)].astype(f32)
            from_right = YLT[qf, jnp.minimum(z, G - 2)].astype(f32)
            total = total + jnp.where(z > 0, from_left, 0.0) + jnp.where(z < G - 1, from_right, 0.0)
            YR[qf, 0, z] = total.astype(bf16)
            for k in range(1, A):
                ag_copy(qf, k).start()
            own_y(qf).start()
            sib_own(qf).start()

        qg = t - YLAG - LEAD - HOP * far - LEAD

        @pl.when(live(qg, nY))
        def _():
            for k in range(1, A):
                here = y_out(qg, lax.rem(a + A - k, A), c)
                remote(here, here, ag_s.at[qg, k - 1], ag_r.at[qg, k - 1], peer(k)).wait_recv()
                sib_pass(qg, k).start()

        return carry

    steps = max(nY + YLAG, nZ) + 2 * LEAD + HOP * (G - 1)
    lax.fori_loop(0, steps, step, 0)

    gain_core().wait_send()
    for k in range(1, A):
        gain_part(k).wait_send()

    @pl.when(z < G - 1)
    def _():
        gain_right().wait_send()

    @pl.when(z > 0)
    def _():
        gain_left().wait_send()

    for i in range(4):
        cross[1, i].wait_send()

    def drain_y(q, carry):
        for k in range(1, A):
            @pl.when(q >= nY - YS_RING)
            def _():
                y_send(q, k).wait_send()

            ag_copy(q, k).wait_send()
            sib_pass(q, k).wait_send()
            there = y_out(q, lax.rem(a + A - k, A), 1 - c)
            remote(there, there, sib_s.at[q, k], sib_r.at[q, k], sib).wait_recv()
        out_r, _, out_l, _ = y_line(q)
        at_place(out_r, lambda copy: copy.wait_send())
        at_place(out_l, lambda copy: copy.wait_send())
        own_y(q).wait()
        sib_own(q).wait_send()
        there = y_out(q, a, 1 - c)
        remote(there, there, sib_s.at[q, 0], sib_r.at[q, 0], sib).wait_recv()
        return carry

    lax.fori_loop(0, nY, drain_y, 0)

    def drain_z(p, carry):
        out_r, _, out_l, _ = z_line(p)
        at_place(out_r, lambda copy: copy.wait_send())
        at_place(out_l, lambda copy: copy.wait_send())
        own_z(p).wait()
        sib_z(p).wait_send()
        there = z_out(p, 1 - c)
        remote(there, there, sib_s.at[nY + p, 0], sib_r.at[nY + p, 0], sib).wait_recv()
        return carry

    lax.fori_loop(0, nZ, drain_z, 0)


def summed_grads(groups, dp, activations, others, dz, dy, dgate, dup, dq, gain_parts):
    hidden, tokens = activations[0].shape
    width, qkv_cols = dz.shape[1], dq.shape[1]
    plan = grad_plan(groups, dp, tokens, width, hidden, qkv_cols)
    G, A, nY, nZ = groups, plan["pairs"], plan["pieces"], plan["z_pieces"]
    block, zr, zc = plan["block"], plan["z_rows"], plan["z_cols"]
    bf16, DMA = jnp.bfloat16, pltpu.SemaphoreType.DMA
    any_space = pl.BlockSpec(memory_space=pl.ANY)
    in_vmem, f32, gain_shape = pl.BlockSpec(memory_space=pltpu.VMEM), jnp.float32, gain_parts.shape
    return pl.pallas_call(
        functools.partial(grad_kernel, plan),
        out_shape=(
            jax.ShapeDtypeStruct((block, 2 * hidden + qkv_cols), bf16),
            jax.ShapeDtypeStruct((plan["down_block"] + block, width), bf16),
            jax.ShapeDtypeStruct(gain_parts.shape, f32),
        ),
        in_specs=[any_space] * 13 + [in_vmem],
        out_specs=(any_space, any_space, in_vmem),
        scratch_shapes=[
            pltpu.VMEM((hidden + 3 * width, 2 * tokens), bf16),
            pltpu.VMEM((2 * tokens, width + hidden + qkv_cols // 2), bf16),
            pltpu.VMEM((YS_RING, A - 1, G, block, LANES), bf16),
            pltpu.VMEM((nY, A - 1, G, block, LANES), bf16),
            pltpu.VMEM((nY, G - 1, block, LANES), bf16),
            pltpu.VMEM((nY, G - 1, block, LANES), bf16),
            pltpu.VMEM((nZ, G - 1, zr, zc), bf16),
            pltpu.VMEM((nZ, G - 1, zr, zc), bf16),
            pltpu.VMEM((nZ, A, zr, zc), bf16),
            DMA((12,)), DMA((8,)), DMA((8,)),
            DMA((nY, A - 1)), DMA((nY, A - 1)),
            DMA((nY,)), DMA((nY,)), DMA((nY,)), DMA((nY,)),
            DMA((nZ,)), DMA((nZ,)), DMA((nZ,)), DMA((nZ,)),
            DMA((nZ, A - 1)), DMA((nZ, A - 1)),
            DMA((nY, A - 1)), DMA((nY, A - 1)),
            DMA((nY + nZ, A)), DMA((nY + nZ, A)),
            DMA((nY + nZ,)),
            pltpu.VMEM(gain_shape, f32),
            pltpu.VMEM((A,) + gain_shape, f32),
            pltpu.VMEM((3,) + gain_shape, f32),
            pltpu.VMEM(gain_shape, f32),
            pltpu.VMEM(gain_shape, f32),
            DMA((2,)), DMA((max(A - 1, 1),)), DMA((max(A - 1, 1),)), DMA((2,)), DMA((2,)),
        ],
        compiler_params=pltpu.CompilerParams(
            collective_id=3, has_side_effects=True, vmem_limit_bytes=63 * 1024 * 1024
        ),
        cost_estimate=pl.CostEstimate(
            flops=2 * 2 * tokens * (width * (2 * hidden + qkv_cols + width) + hidden * width) // 2,
            bytes_accessed=40_000_000, transcendentals=0,
        ),
    )(*activations, *others, dz, dy, dgate, dup, dq, gain_parts)


W_HOP = 4
AFTER = 1
ROOMS = 3
gather_families = (
    (1, False, False),
    (2, False, True),
    (1, False, False),
    (8, True, False),
    (6, False, False),
)


def gather_kernel(groups, pairs, families, rows, *refs):
    G, A, F = groups, pairs, len(families)
    shards, refs = refs[:F], refs[F:]
    if rows:
        (x, mask, cosines, sines), refs = refs[:4], refs[4:]
    wholes, refs = refs[:F], refs[F:]
    if rows:
        (gain_rows, first_out, handed), refs = refs[:3], refs[3:]
    sems, refs = refs[: 9 * F], refs[9 * F :]
    if rows:
        in_gain, in_wide, in_gate, in_down, in_sem, hand_s, hand_r, n1, qkvt, ot, y, n2, gate, inner = refs
    s, z, d = lax.axis_index("section"), lax.axis_index("group"), lax.axis_index("dp")
    c, a = lax.rem(d, 2), lax.div(d, 2)
    sib = (s, z, 2 * a + 1 - c)
    right, left = (s, z + 1, d), (s, z - 1, d)

    def peer(part):
        return (s, z, 2 * part + c)

    barrier = pltpu.get_barrier_semaphore()
    others = [peer(lax.rem(a + k, A)) for k in range(1, A)]
    if rows:
        others.append((1 - s, z, d))
    others += [sib, (s, lax.rem(z + 1, G), d), (s, lax.rem(z + G - 1, G), d)]
    for dev in others:
        pl.semaphore_signal(barrier, inc=1, device_id=dev, device_id_type=MESH)
    pl.semaphore_wait(barrier, len(others))

    def columns(f, i):
        pieces, halves, _ = families[f]
        size = shards[f].shape[1] // pieces
        if halves:
            i = lax.rem(i, 2) * (pieces // 2) + lax.div(i, 2)
        return pl.ds(pl.multiple_of(i * size, 128), size)

    def cut(f, ref, i):
        return ref.at[:, columns(f, i)]

    def placed(f, i, o, part, core):
        return cut(f, wholes[f].at[(o * A + part) * 2 + core], i)

    def copy(f, i, o, part, kind, index, dev, own=False, core=None):
        core = c if core is None else core
        there = placed(f, i, o, part, core)
        src = cut(f, shards[f], i) if own else there
        send, recv = sems[f * 9 + 2 * kind], sems[f * 9 + 2 * kind + 1]
        return pltpu.make_async_remote_copy(
            src_ref=src, dst_ref=there, send_sem=send.at[index], recv_sem=recv.at[index], device_id=dev, device_id_type=MESH
        )

    def to_right(f, i, o, part, own=False):
        return copy(f, i, o, part, 0, (i, o, lax.rem(part + A - a, A)), right, own)

    def to_left(f, i, o, part, own=False):
        return copy(f, i, o, part, 1, (i, o, lax.rem(part + A - a, A)), left, own)

    def to_part(f, i, o, k, own=False):
        return copy(f, i, o, a, 2, (i, o, k - 1), peer(lax.rem(a + k, A)), own)

    def from_part(f, i, o, k):
        return copy(f, i, o, lax.rem(a + A - k, A), 2, (i, o, k - 1), peer(lax.rem(a + A - k, A)))

    def to_core(f, i, o, part, own=False):
        return copy(f, i, o, part, 3, (i, o, lax.rem(part + A - a, A)), sib, own)

    def from_core(f, i, o, k):
        part = lax.rem(a + k, A)
        return copy(f, i, o, part, 3, (i, o, k), sib, core=1 - c)

    def own_copy(f, i):
        return pltpu.make_async_copy(cut(f, shards[f], i), placed(f, i, z, a, c), sems[f * 9 + 8].at[i])

    def along(f, i, o, part, own, go_right, go_left):
        if go_right:
            @pl.when(z < G - 1)
            def _():
                to_right(f, i, o, part, own).start()
        if go_left:
            @pl.when(z > 0)
            def _():
                to_left(f, i, o, part, own).start()

    first = []
    total = 0
    for pieces, _, _ in families:
        first.append(total)
        total += pieces

    def into(f, i, room):
        return pltpu.make_async_copy(wholes[f].at[:, :, columns(f, i)], room, in_sem.at[first[f] + i])

    def arrived(f, i, room):
        own_copy(f, i).wait()

        @pl.loop(0, G)
        def _(o):
            for k in range(A):
                from_core(f, i, o, k).wait_recv()

        into(f, i, room).start()

    def hand_over(i):
        place = columns(4, i)
        return pltpu.make_async_remote_copy(
            src_ref=first_out.at[:, place], dst_ref=handed.at[:, place], send_sem=hand_s.at[i], recv_sem=hand_r.at[i],
            device_id=(1 - s, z, d), device_id_type=MESH,
        )

    def one_matrix(room):
        return room.reshape(room.shape[0] * room.shape[1], room.shape[2])

    def forward(t):
        f32, bf16 = jnp.float32, jnp.bfloat16
        slots, part, half, ratio = x.shape[0] // max(rows, 1), KVH * HD, HD // 2, H // KVH
        after = W_HOP * G + AFTER
        places = [(1, i) for i in range(families[1][0])] + [(2, 0)]

        @pl.when(t == first[0] + after)
        def _():
            arrived(0, 0, in_gain)
            into(0, 0, in_gain).wait()
            turned = one_matrix(in_gain[...]).astype(f32).T
            gain_rows[...] = turned[:8]
            n1[...] = scaled_norm(x[...].astype(f32), gain_rows[0:1, :])[1]

        for slot, (f, i) in enumerate(places):
            @pl.when(t == first[f] + i + after)
            def _(slot=slot, f=f, i=i):
                arrived(f, i, in_wide.at[slot])

        i3 = t - first[3] - after

        @pl.when((i3 >= 0) & (i3 < families[3][0]))
        def _():
            arrived(3, i3, in_gate.at[lax.rem(i3, ROOMS)])

        i4 = t - first[4] - after

        @pl.when((i4 >= 0) & (i4 < families[4][0]))
        def _():
            arrived(4, i4, in_down.at[lax.rem(i4, ROOMS)])

        for i in range(families[1][0]):
            @pl.when(t == first[1] + i + after + 1)
            def _(i=i):
                into(1, i, in_wide.at[i]).wait()
                for j in range(in_wide.shape[3] // part):
                    weight = one_matrix(in_wide[i, :, :, j * part : (j + 1) * part])
                    chunk = jnp.dot(n1[...], weight, preferred_element_type=f32).T
                    top = (i * (in_wide.shape[3] // part) + j) * part
                    if top >= (H + KVH) * HD:
                        qkvt[top : top + part, :] = chunk.astype(bf16)
                        continue
                    for h in range(KVH):
                        base = top + h * HD
                        front, back = chunk[h * HD : h * HD + half], chunk[h * HD + half : (h + 1) * HD]
                        qkvt[base : base + half, :] = (front * cosines[...] - back * sines[...]).astype(bf16)
                        qkvt[base + half : base + HD, :] = (back * cosines[...] + front * sines[...]).astype(bf16)

        def heads(index, carry):
            row, k = lax.div(index, KVH), lax.rem(index, KVH)
            tokens = pl.ds(pl.multiple_of(row * slots, 128), slots)

            def band(head):
                return pl.ds(pl.multiple_of(head * HD, 16), HD)

            keys, values = qkvt[band(H + k), tokens], qkvt[band(H + KVH + k), tokens]
            queries = jnp.concatenate([qkvt[band(ratio * k + g), tokens] for g in range(ratio)], 1)
            key = lax.broadcasted_iota(jnp.int32, (slots, ratio * slots), 0)
            query = lax.rem(lax.broadcasted_iota(jnp.int32, (slots, ratio * slots), 1), slots)
            valid = mask[pl.ds(pl.multiple_of(row * slots, 128), slots), :] > 0.0
            scores = pair_scores(keys, queries, (key <= query) & valid)
            top = jnp.max(scores, 0, keepdims=True)
            total = top + jnp.log(jnp.sum(jnp.exp(scores - top), 0, keepdims=True))
            probs = jnp.exp(scores - total).astype(bf16)
            out = jnp.dot(values, probs, preferred_element_type=f32).astype(bf16)
            for g in range(ratio):
                ot[band(ratio * k + g), tokens] = out[:, g * slots : (g + 1) * slots]
            return carry

        split = rows * KVH // 2
        turn = t - first[2] - after

        @pl.when((turn >= 1) & (turn <= 2))
        def _():
            lax.fori_loop((turn - 1) * split, turn * split, heads, 0)

        @pl.when(turn == 2)
        def _():
            into(2, 0, in_wide.at[len(places) - 1]).wait()
            y[...] = x[...].astype(f32) + lax.dot_general(
                ot[...], one_matrix(in_wide[len(places) - 1]), down_rows, preferred_element_type=f32
            )
            n2[...] = scaled_norm(y[...], gain_rows[1:2, :])[1]

        c3 = i3 - 2
        size = in_gate.shape[3]

        @pl.when((c3 >= 0) & (c3 < families[3][0]))
        def _():
            room = lax.rem(c3, ROOMS)
            into(3, c3, in_gate.at[room]).wait()
            value = jnp.dot(n2[...], one_matrix(in_gate[room]), preferred_element_type=f32)

            @pl.when(lax.rem(c3, 2) == 0)
            def _():
                gate[...] = value

            @pl.when(lax.rem(c3, 2) == 1)
            def _():
                opened = gate[...]
                inner[:, pl.ds(pl.multiple_of(lax.div(c3, 2) * size, 128), size)] = (
                    opened / (1.0 + jnp.exp(-opened)) * value
                ).astype(bf16)

        c4 = i4 - 2

        @pl.when((c4 >= 0) & (c4 < families[4][0]))
        def _():
            room = lax.rem(c4, ROOMS)
            into(4, c4, in_down.at[room]).wait()
            place = columns(4, c4)
            value = y[:, place] + jnp.dot(inner[...], one_matrix(in_down[room]), preferred_element_type=f32)
            first_out[:, place] = (value * mask[...]).astype(bf16)
            hand_over(c4).start()

    def step(t, carry):
        for f, (pieces, _, parts_first) in enumerate(families):
            i0 = t - first[f]

            @pl.when((i0 >= 0) & (i0 < pieces))
            def _(f=f, i0=i0):
                along(f, i0, z, a, True, True, True)
                for k in range(1, A):
                    to_part(f, i0, z, k, True).start()
                to_core(f, i0, z, a, True).start()
                own_copy(f, i0).start()

        for f, (pieces, _, parts_first) in enumerate(families):
            for h in range(G):
                for k in range(A if parts_first else 1):
                    if h == 0:
                        continue
                    i = t - first[f] - W_HOP * h - (W_HOP if k > 0 else 0)
                    part = lax.rem(a + k, A)
                    for sign in (-1, 1):
                        o = z + sign * h

                        @pl.when((i >= 0) & (i < pieces) & (o >= 0) & (o < G))
                        def _(f=f, i=i, o=o, part=part, sign=sign, parts_first=parts_first):
                            if sign < 0:
                                to_right(f, i, o, part).wait_recv()
                                along(f, i, o, part, False, True, False)
                            else:
                                to_left(f, i, o, part).wait_recv()
                                along(f, i, o, part, False, False, True)
                            if not parts_first:
                                for j in range(1, A):
                                    to_part(f, i, o, j).start()
                            to_core(f, i, o, part).start()

                if parts_first and h > 0:
                    continue
                i = t - first[f] - W_HOP * (h + 1)
                for sign in (-1, 1) if h else (1,):
                    o = z + sign * h

                    @pl.when((i >= 0) & (i < pieces) & (o >= 0) & (o < G))
                    def _(f=f, i=i, o=o, parts_first=parts_first):
                        for k in range(1, A):
                            from_part(f, i, o, k).wait_recv()
                            part = lax.rem(a + A - k, A)
                            if parts_first:
                                along(f, i, o, part, False, True, True)
                            to_core(f, i, o, part).start()
        if rows:
            forward(t)
        return carry

    lax.fori_loop(0, total + max(W_HOP * (G + 1), W_HOP * G + AFTER + 2), step, 0)

    if rows:
        for i in range(families[4][0]):
            hand_over(i).wait()

    for f, (pieces, _, parts_first) in enumerate(families):
        def drain(i, carry, f=f, parts_first=parts_first):
            if not rows:
                own_copy(f, i).wait()

            def by_group(o, carry):
                for k in range(A):
                    part = lax.rem(a + k, A)
                    to_core(f, i, o, part).wait_send()
                    if not rows:
                        from_core(f, i, o, k).wait_recv()
                    if parts_first or k == 0:
                        @pl.when((z < G - 1) & (o <= z))
                        def _(part=part):
                            to_right(f, i, o, part).wait_send()

                        @pl.when((z > 0) & (o >= z))
                        def _(part=part):
                            to_left(f, i, o, part).wait_send()
                for k in range(1, A):
                    if parts_first:
                        @pl.when(o == z)
                        def _(k=k):
                            to_part(f, i, o, k).wait_send()
                    else:
                        to_part(f, i, o, k).wait_send()
                return carry

            return lax.fori_loop(0, G, by_group, carry)

        lax.fori_loop(0, pieces, drain, 0)


def gathered(groups, dp, shards, families, tokens):
    A, DMA, bf16, f32 = dp // 2, pltpu.SemaphoreType.DMA, jnp.bfloat16, jnp.float32
    any_space, in_vmem = pl.BlockSpec(memory_space=pl.ANY), pl.BlockSpec(memory_space=pltpu.VMEM)
    devices, shape = groups * dp, jax.ShapeDtypeStruct
    scratch = []
    for pieces, _, parts_first in families:
        on_line = (pieces, groups, A if parts_first else 1)
        scratch += [DMA(on_line)] * 4 + [DMA((pieces, groups, max(A - 1, 1)))] * 2 + [DMA((pieces, groups, A))] * 2
        scratch += [DMA((pieces,))]
    outs = tuple(shape((devices,) + x.shape, x.dtype) for x in shards)
    extra, rows = (), 0
    if tokens is not None:
        x, mask, tables, rows = tokens
        extra = (x, mask) + tables
        count, width = x.shape
        hidden = devices * shards[4].shape[0]
        outs += (shape((8, width), f32), shape((count, width), bf16), shape((count, width), bf16))

        def room(f, rooms):
            return pltpu.VMEM((rooms, devices, shards[f].shape[0], shards[f].shape[1] // families[f][0]), bf16)

        scratch += [
            pltpu.VMEM((devices,) + shards[0].shape, bf16), room(1, families[1][0] + 1), room(3, ROOMS), room(4, ROOMS),
            DMA((sum(family[0] for family in families),)), DMA((families[4][0],)), DMA((families[4][0],)),
            pltpu.VMEM((count, width), bf16), pltpu.VMEM((shards[1].shape[1], count), bf16),
            pltpu.VMEM((width, count), bf16), pltpu.VMEM((count, width), f32), pltpu.VMEM((count, width), bf16),
            pltpu.VMEM((count, shards[3].shape[1] // families[3][0]), f32), pltpu.VMEM((count, hidden), bf16),
        ]
    return pl.pallas_call(
        functools.partial(gather_kernel, groups, A, families, rows),
        out_shape=outs,
        in_specs=[any_space] * len(shards) + [in_vmem] * len(extra),
        out_specs=(any_space,) * len(shards) + ((in_vmem, in_vmem, any_space) if rows else ()),
        scratch_shapes=scratch,
        compiler_params=pltpu.CompilerParams(
            collective_id=5, has_side_effects=True, vmem_limit_bytes=56 * 1024 * 1024
        ),
    )(*shards, *extra)


def widen_kernel(source, *parts):
    start = 0
    for part in parts:
        part[...] = source[:, start : start + part.shape[1]].astype(jnp.float32)
        start += part.shape[1]


def widened(source, widths):
    rows, cols = source.shape
    band = 64 if rows % 64 == 0 else 16
    return pl.pallas_call(
        widen_kernel,
        grid=(rows // band,),
        out_shape=tuple(jax.ShapeDtypeStruct((rows, width), jnp.float32) for width in widths),
        in_specs=[pl.BlockSpec((band, cols), lambda i: (i, 0))],
        out_specs=tuple(pl.BlockSpec((band, width), lambda i: (i, 0)) for width in widths),
        compiler_params=pltpu.CompilerParams(vmem_limit_bytes=32 * 1024 * 1024),
        cost_estimate=pl.CostEstimate(flops=0, bytes_accessed=6 * rows * cols, transcendentals=0),
    )(source)


def body(
    inputs_x, cotangent, lengths, attn_gain, qkv_weight, out_weight, ffn_gain, gate_up, down_weight
):
    is_first = lax.axis_index("section") == 0
    rows, slots, width = inputs_x.shape
    tables = turned_tables(slots, rows)
    info = jnp.concatenate([lengths, is_first.astype(jnp.int32)[None]])
    mask = padding(lengths, slots).reshape(-1, 1)
    gains = jnp.concatenate([attn_gain, ffn_gain], 0).T
    gains = jnp.pad(gains, ((0, 0), (0, 128 - gains.shape[1])))
    shards = (gains, qkv_weight[0], out_weight[0], gate_up[0], down_weight[0])
    together = gains.shape[0] % 16 == 0
    tokens = (flat(inputs_x), mask, tables, rows) if together else None
    gathered_all = gathered(
        lax.axis_size("group"), lax.axis_size("dp"), shards, gather_families, tokens
    )
    gains_all, qkv_w, output_weight, gate_up_w, down_w = (flat(x) for x in gathered_all[:5])
    if together:
        gain_rows, _, recv_act = gathered_all[5:]
    else:
        gain_rows = gains_all[:, :2].astype(jnp.float32).T
    gain_one, gain_two = gain_rows[0:1], gain_rows[1:2]
    dz_given = (flat(cotangent).astype(jnp.float32) * mask).astype(jnp.bfloat16)
    if not together:
        after_one = attention_forward(
            info, flat(inputs_x), gain_one, tables, qkv_w, output_weight, rows
        )[0]
        first_out = ffn_forward(after_one, gain_two, mask, gate_up_w, down_w)
        recv_act = passed_along(first_out, "section", 1)
    layer_in = jnp.where(is_first, flat(inputs_x), recv_act)
    after, heads, log_total, attention_turned, normed_turned = attention_forward(
        info, layer_in, gain_one, tables, qkv_w, output_weight, rows
    )
    dy, dy_low, _ = ffn_backward(after, dz_given, gain_two, gate_up_w, down_w)
    (second_dx,) = attention_backward(
        info, layer_in, gain_one, dy, dy_low, tables, heads, log_total, output_weight, qkv_w, rows, False
    )
    recv_grad = passed_along(second_dx, "section", -1)
    after, second_dx = lax.optimization_barrier((after, second_dx))
    hidden_turned, by_gate, by_up, normed_two_turned, result = ffn_prepare(
        after, gain_two, mask, gate_up_w, down_w
    )
    activations = (hidden_turned, attention_turned, normed_two_turned, normed_turned)
    recv_grad, activations, by_gate = lax.optimization_barrier((recv_grad, activations, by_gate))
    others = tuple(swapped(x, "dp") for x in activations)
    dz = jnp.where(is_first, (recv_grad.astype(jnp.float32) * mask).astype(jnp.bfloat16), dz_given)
    dy, dy_low, ffn_gain_part, grad_gate, grad_up = ffn_backward(
        after, dz, gain_two, gate_up_w, down_w, (by_gate, by_up)
    )
    grad_x, attn_gain_part, grad_qkv = attention_backward(
        info, layer_in, gain_one, dy, dy_low, tables, heads, log_total, output_weight, qkv_w, rows, True
    )
    section_out = result.reshape((1,) + inputs_x.shape)
    input_grads = grad_x.reshape((1,) + inputs_x.shape)
    gain_parts = jnp.pad(jnp.concatenate([attn_gain_part, ffn_gain_part], 0), ((0, 6), (0, 0)))
    gate_qkv_sum, down_out_sum, gain_sums = summed_grads(
        lax.axis_size("group"),
        lax.axis_size("dp"),
        activations,
        others,
        dz,
        dy_low,
        grad_gate,
        grad_up,
        grad_qkv,
        gain_parts,
    )
    gain_cols = attn_gain.shape[1] * lax.axis_size("dp")
    gain_sums = lax.dynamic_slice_in_dim(
        gain_sums, lax.axis_index("group") * gain_cols, gain_cols, 1
    )
    gate_sum, qkv_sum = widened(gate_qkv_sum, (gate_up.shape[2], qkv_weight.shape[2]))
    down_rows = down_weight.shape[1] * lax.axis_size("dp")
    reduced = (
        gain_sums[0],
        qkv_sum,
        down_out_sum[down_rows:].astype(jnp.float32),
        gain_sums[1],
        gate_sum,
        down_out_sum[:down_rows].astype(jnp.float32),
    )
    return (section_out, input_grads) + tuple((shard_sum[None] for shard_sum in reduced))


def solution(mesh):
    placed = (
        P(("group", "dp"), None, None),
        P(("group", "dp"), None, None),
        P(("group", "dp")),
        P("section", ("group", "dp")),
        P("section", ("group", "dp"), None),
        P("section", ("group", "dp"), None),
        P("section", ("group", "dp")),
        P("section", ("group", "dp"), None),
        P("section", ("group", "dp"), None),
    )
    return jax.shard_map(
        body,
        mesh=mesh,
        in_specs=placed,
        out_specs=(
            P("section", ("group", "dp"), None, None),
            P("section", ("group", "dp"), None, None),
            P("section", "group"),
            P("section", "group", None),
            P("section", "group", None),
            P("section", "group"),
            P("section", "group", None),
            P("section", "group", None),
        ),
        check_vma=False,
    )
```
